32 devices in a mesh: seq: 16 (over z, x, core), head: 2 (over y).
Axes of the slice: x: 2, y: 2, z: 4, core: 2. Of those that a mesh axis runs over, the one named last changes fastest.
Arguments:
- tokens: bfloat16 [16384, 1152], P(('seq', 'head')), may hold values from -6 to 6
- cotangent: bfloat16 [16384, 1152], P(('seq', 'head')), may hold values from -6 to 6
- buckets: int32 [16], P('seq'), may hold values from 0 to 7
- timesteps: int32 [16], P('seq'), may hold values from 0 to 999
- labels: int32 [16], P('seq'), may hold values from 0 to 999
- class_table: bfloat16 [1000, 1152], replicated, may hold values from -6 to 6
- step_count: int32 [], replicated, may hold values from 2 to 20
- modulate_master: float32 [1152, 6912], P('seq', 'head'), may hold values from -0.1875 to 0.1875
- modulate_first: float32 [1152, 6912], P('seq', 'head'), may hold values from -0.0008544922 to 0.0008544922
- modulate_second: float32 [1152, 6912], P('seq', 'head'), may hold values from 2.049866e-08 to 8.199464e-08
- attend_master: float32 [1152, 3456], P('seq', 'head'), may hold values from -0.1875 to 0.1875
- attend_first: float32 [1152, 3456], P('seq', 'head'), may hold values from -0.00048828125 to 0.00048828125
- attend_second: float32 [1152, 3456], P('seq', 'head'), may hold values from 6.6934405e-09 to 2.6773762e-08
- project_master: float32 [1152, 1152], P('seq', 'head'), may hold values from -0.1875 to 0.1875
- project_first: float32 [1152, 1152], P('seq', 'head'), may hold values from -0.0012207031 to 0.0012207031
- project_second: float32 [1152, 1152], P('seq', 'head'), may hold values from 4.1834003e-08 to 1.6733601e-07
- expand_master: float32 [1152, 4608], P('seq', 'head'), may hold values from -0.1875 to 0.1875
- expand_first: float32 [1152, 4608], P('seq', 'head'), may hold values from -0.0007324219 to 0.0007324219
- expand_second: float32 [1152, 4608], P('seq', 'head'), may hold values from 1.5060241e-08 to 6.0240964e-08
- reduce_master: float32 [4608, 1152], P('seq', 'head'), may hold values from -0.09375 to 0.09375
- reduce_first: float32 [4608, 1152], P('seq', 'head'), may hold values from -0.0012207031 to 0.0012207031
- reduce_second: float32 [4608, 1152], P('seq', 'head'), may hold values from 4.1834003e-08 to 1.6733601e-07
- biases_master: float32 [16128], replicated, may hold values from -1 to 1
- biases_first: float32 [16128], replicated, may hold values from -0.0009765625 to 0.0009765625
- biases_second: float32 [16128], replicated, may hold values from 2.6773762e-08 to 1.0709505e-07
Outputs:
- output: bfloat16 [16384, 1152], P(('seq', 'head'))
- input_grad: float32 [16384, 1152], P(('seq', 'head'))
- grad_norm: float32 [], replicated
- modulate_updated: float32 [1152, 6912], P('seq', 'head')
- modulate_momentum: float32 [1152, 6912], P('seq', 'head')
- modulate_variance: float32 [1152, 6912], P('seq', 'head')
- attend_updated: float32 [1152, 3456], P('seq', 'head')
- attend_momentum: float32 [1152, 3456], P('seq', 'head')
- attend_variance: float32 [1152, 3456], P('seq', 'head')
- project_updated: float32 [1152, 1152], P('seq', 'head')
- project_momentum: float32 [1152, 1152], P('seq', 'head')
- project_variance: float32 [1152, 1152], P('seq', 'head')
- expand_updated: float32 [1152, 4608], P('seq', 'head')
- expand_momentum: float32 [1152, 4608], P('seq', 'head')
- expand_variance: float32 [1152, 4608], P('seq', 'head')
- reduce_updated: float32 [4608, 1152], P('seq', 'head')
- reduce_momentum: float32 [4608, 1152], P('seq', 'head')
- reduce_variance: float32 [4608, 1152], P('seq', 'head')
- biases_updated: float32 [16128], replicated
- biases_momentum: float32 [16128], replicated
- biases_variance: float32 [16128], replicated
The draws below stay inside these ranges and needn't reach their ends.
Inputs may be any that keep to these rules, and one draw needn't show every extreme that they name: `buckets`: bucket ids index the table of grid shapes in the reference program.
All inputs are finite; a program needn't handle non-finite values.
Results may differ from the reference program's by a relative error of at most 0.035.
Values may be sent and summed in bfloat16 or wider, within the bound.
A program may use at most 256 MiB of HBM per device.

```python
import math
import jax
import jax.numpy as jnp
from jax import lax

D = 1152
HEADS = 16
HEAD_DIM = 72
FF = 4608
NCLASS = 1000
SIDE = 32
NBUCKET = 8
NSTEPS = 1000
IMG_GRP = 1
LMAX = 1024
IMAGES = 16
TOKENS = 16384
NB = 16128
NPARAM = 23904000


def with_ends(drawn, stream_key, smallest, high):
    extent = drawn.shape
    spot = [jax.random.randint(jax.random.fold_in(stream_key, axis), (), 0, extent[axis]) for axis in range(len(extent))]
    drawn = drawn.at[tuple(spot)].set(smallest)
    longest = extent.index(max(extent))
    spot[longest] = (spot[longest] + 1) % extent[longest]
    return drawn.at[tuple(spot)].set(high)


def levels(stream_key, shape, shards, low, top_value):
    level = 1.0
    for dim, parts in shards:
        steps = jax.random.uniform(jax.random.fold_in(jax.random.fold_in(stream_key, 6), dim), (parts,), jnp.float32, low / len(shards), top_value / len(shards))
        level = level * jnp.repeat(jnp.exp(steps), shape[dim] // parts).reshape((-1,) + (1,) * (len(shape) - 1 - dim))
    return level


def noise(stream_key, shape, scale, bound, cuts=(), held_as=jnp.bfloat16):
    factor_of = levels(stream_key, shape, cuts, -0.22, 0.18) if cuts else 1.0
    drawn = jax.random.normal(stream_key, shape, jnp.float32) * scale * factor_of
    return jnp.minimum(jnp.maximum(drawn, -bound), bound).astype(held_as)


def setup_inputs(seed: int = 0) -> dict:
    keys = jax.random.split(jax.random.key(seed), 26)
    tokens = noise(keys[0], (TOKENS, D), 1.0, 6.0, ((0, 32),))
    cotangent = noise(keys[1], (TOKENS, D), 1.0, 6.0, ((0, 32),))
    buckets = with_ends(jax.random.randint(keys[2], (IMAGES,), 0, NBUCKET), jax.random.fold_in(keys[2], 1), 0, NBUCKET - 1).astype(jnp.int32)
    timesteps = with_ends(jax.random.randint(keys[3], (IMAGES,), 0, NSTEPS), jax.random.fold_in(keys[3], 1), 0, NSTEPS - 1).astype(jnp.int32)
    labels = with_ends(jax.random.randint(keys[4], (IMAGES,), 0, NCLASS), jax.random.fold_in(keys[4], 1), 0, NCLASS - 1).astype(jnp.int32)
    class_table = noise(keys[5], (NCLASS, D), 1.0, 6.0)
    step_count = jax.random.randint(keys[6], (), 2, 21).astype(jnp.int32)
    modulate_master = noise(keys[7], (D, 6 * D), D ** -0.5, 0.1875, ((0, 16), (1, 2)), jnp.float32)
    modulate_first = noise(keys[8], (D, 6 * D), (0.7 * NPARAM ** -0.5), 0.0008544922, ((0, 16), (1, 2)), jnp.float32)
    modulate_second = jnp.clip(jnp.exp(math.log(8.199464218705543e-08) - 1.3862944 * jax.random.uniform(keys[9], (D, 6 * D), jnp.float32) ** levels(keys[9], (D, 6 * D), ((0, 16), (1, 2)), -0.2, 0.2)), 2.0498660546763858e-08, 8.199464218705543e-08)
    attend_master = noise(keys[10], (D, 3 * D), D ** -0.5, 0.1875, ((0, 16), (1, 2)), jnp.float32)
    attend_first = noise(keys[11], (D, 3 * D), (0.4 * NPARAM ** -0.5), 0.00048828125, ((0, 16), (1, 2)), jnp.float32)
    attend_second = jnp.clip(jnp.exp(math.log(2.6773761874210322e-08) - 1.3862944 * jax.random.uniform(keys[12], (D, 3 * D), jnp.float32) ** levels(keys[12], (D, 3 * D), ((0, 16), (1, 2)), -0.2, 0.2)), 6.6934404685525806e-09, 2.6773761874210322e-08)
    project_master = noise(keys[13], (D, D), D ** -0.5, 0.1875, ((0, 16), (1, 2)), jnp.float32)
    project_first = noise(keys[14], (D, D), (1.0 * NPARAM ** -0.5), 0.0012207031, ((0, 16), (1, 2)), jnp.float32)
    project_second = jnp.clip(jnp.exp(math.log(1.6733601171381451e-07) - 1.3862944 * jax.random.uniform(keys[15], (D, D), jnp.float32) ** levels(keys[15], (D, D), ((0, 16), (1, 2)), -0.2, 0.2)), 4.183400292845363e-08, 1.6733601171381451e-07)
    expand_master = noise(keys[16], (D, FF), D ** -0.5, 0.1875, ((0, 16), (1, 2)), jnp.float32)
    expand_first = noise(keys[17], (D, FF), (0.6 * NPARAM ** -0.5), 0.0007324219, ((0, 16), (1, 2)), jnp.float32)
    expand_second = jnp.clip(jnp.exp(math.log(6.024096421697323e-08) - 1.3862944 * jax.random.uniform(keys[18], (D, FF), jnp.float32) ** levels(keys[18], (D, FF), ((0, 16), (1, 2)), -0.2, 0.2)), 1.5060241054243306e-08, 6.024096421697323e-08)
    reduce_master = noise(keys[19], (FF, D), FF ** -0.5, 0.09375, ((0, 16), (1, 2)), jnp.float32)
    reduce_first = noise(keys[20], (FF, D), (1.0 * NPARAM ** -0.5), 0.0012207031, ((0, 16), (1, 2)), jnp.float32)
    reduce_second = jnp.clip(jnp.exp(math.log(1.6733601171381451e-07) - 1.3862944 * jax.random.uniform(keys[21], (FF, D), jnp.float32) ** levels(keys[21], (FF, D), ((0, 16), (1, 2)), -0.2, 0.2)), 4.183400292845363e-08, 1.6733601171381451e-07)
    biases_master = noise(keys[22], (NB,), 0.2, 1.0, (), jnp.float32)
    biases_first = noise(keys[23], (NB,), (0.8 * NPARAM ** -0.5), 0.0009765625, (), jnp.float32)
    biases_second = jnp.clip(jnp.exp(jax.random.uniform(keys[24], (NB,), jnp.float32, math.log(2.6773761874210322e-08), math.log(1.0709504749684129e-07))), 2.6773761874210322e-08, 1.0709504749684129e-07)
    return {"tokens": tokens, "cotangent": cotangent, "buckets": buckets, "timesteps": timesteps, "labels": labels, "class_table": class_table, "step_count": step_count, "modulate_master": modulate_master, "modulate_first": modulate_first, "modulate_second": modulate_second, "attend_master": attend_master, "attend_first": attend_first, "attend_second": attend_second, "project_master": project_master, "project_first": project_first, "project_second": project_second, "expand_master": expand_master, "expand_first": expand_first, "expand_second": expand_second, "reduce_master": reduce_master, "reduce_first": reduce_first, "reduce_second": reduce_second, "biases_master": biases_master, "biases_first": biases_first, "biases_second": biases_second}


highest = lax.Precision.HIGHEST
row_units = (8, 4, 16, 6, 10, 7, 4, 6)
col_units = (8, 16, 4, 10, 6, 9, 8, 6)

@jax.custom_vjp
def low(v):
    return lax.optimization_barrier(v.astype(jnp.bfloat16)).astype(jnp.float32)

@jax.custom_vjp
def low_back(v):
    return v

def low_keep(v):
    return (low(v), None)

def low_pass(kept, grad):
    return (grad,)

def back_keep(v):
    return (v, None)

def back_low(kept, grad):
    return (low(grad),)
low.defvjp(low_keep, low_pass)
low_back.defvjp(back_keep, back_low)

def table_pick(indices, entries):
    matches = indices[..., None] == jnp.arange(len(entries), dtype=jnp.int32)
    return lax.optimization_barrier(jnp.sum(jnp.where(matches, jnp.array(entries, jnp.int32), 0), axis=-1)).astype(jnp.int32)

def layer_norm(value):
    average = lax.optimization_barrier(jnp.mean(value, axis=-1, keepdims=True))
    centred = value - average
    spread = lax.optimization_barrier(jnp.mean(centred * centred, axis=-1, keepdims=True))
    return centred * lax.rsqrt(spread + 1e-06)

def time_features(moments, width):
    half_width = width // 2
    frequency = jnp.exp(-math.log(10000.0) * jnp.arange(half_width, dtype=jnp.float32) / half_width)
    angles = moments.astype(jnp.float32)[:, None] * frequency[None, :]
    return jnp.concatenate([jnp.cos(angles), jnp.sin(angles)], axis=1)

def grid_features(position, row_wide, width):
    quarter = width // 4
    omegas = jnp.exp(-math.log(10000.0) * jnp.arange(quarter, dtype=jnp.float32) / quarter)
    row_angle = (position // row_wide).astype(jnp.float32)[:, None] * omegas[None, :]
    col_angle = (position % row_wide).astype(jnp.float32)[:, None] * omegas[None, :]
    return jnp.concatenate([jnp.sin(row_angle), jnp.cos(row_angle), jnp.sin(col_angle), jnp.cos(col_angle)], axis=1)

def image_attention(queries, key_rows, value_rows, live_keys):
    block_rows = min(512, LMAX)
    score_scale = HEAD_DIM ** (-0.5)
    key_heads = key_rows.reshape(LMAX, HEADS, HEAD_DIM)
    value_heads = value_rows.reshape(LMAX, HEADS, HEAD_DIM)

    def one_block(query_block):
        scores = low_back(jnp.einsum('qhe,khe->hqk', query_block, key_heads, precision=highest) * score_scale)
        scores = jnp.where(live_keys[None, None, :], scores, -1e+30)
        maximum = lax.optimization_barrier(jnp.max(scores, axis=-1, keepdims=True))
        weights = jnp.exp(scores - maximum)
        probability = weights / lax.optimization_barrier(jnp.sum(weights, axis=-1, keepdims=True))
        return jnp.einsum('hqk,khe->qhe', low(probability), value_heads, precision=highest)
    blocks = queries.reshape(LMAX // block_rows, block_rows, HEADS, HEAD_DIM)
    result = lax.map(jax.checkpoint(one_block), blocks)
    return result.reshape(LMAX, HEADS * HEAD_DIM)

def block_forward(group_tokens, mod_weight, attend_weight, project_weight, expand_weight, reduce_weight, bias_vector, condition, live_keys, grid_cells):
    image_count = condition.shape[0]
    modulation = low_back(jnp.dot(condition, mod_weight, precision=highest) + bias_vector[:6 * D])
    mod_rows = jnp.repeat(modulation, LMAX, axis=0)
    shift_one, scale_one, gating_one, shift_two, scale_two, gating_two = jnp.split(mod_rows, 6, axis=1)
    offset_base = 6 * D
    bias_query = bias_vector[offset_base:offset_base + D]
    bias_value = bias_vector[offset_base + D:offset_base + 2 * D]
    bias_proj = bias_vector[offset_base + 2 * D:offset_base + 3 * D]
    bias_hidden = bias_vector[offset_base + 3 * D:offset_base + 3 * D + FF]
    bias_output = bias_vector[offset_base + 3 * D + FF:]
    residual_zero = group_tokens + grid_cells
    hidden_attend = low(layer_norm(residual_zero) * (1.0 + scale_one) + shift_one)
    packed = jnp.dot(hidden_attend, attend_weight, precision=highest)
    queries = low_back(low(packed[:, :D] + bias_query))
    key_rows = low_back(low(packed[:, D:2 * D]))
    value_rows = low_back(low(packed[:, 2 * D:] + bias_value))
    attention = lax.map(lambda packed_in: image_attention(packed_in[0], packed_in[1], packed_in[2], packed_in[3]), (queries.reshape(image_count, LMAX, D), key_rows.reshape(image_count, LMAX, D), value_rows.reshape(image_count, LMAX, D), live_keys))
    attention = low_back(low(attention.reshape(image_count * LMAX, D)))
    branch_attend = low_back(jnp.dot(attention, project_weight, precision=highest) + bias_proj)
    residual_one = residual_zero + gating_one * branch_attend
    hidden_expand = low(layer_norm(residual_one) * (1.0 + scale_two) + shift_two)
    widened = low_back(jnp.dot(hidden_expand, expand_weight, precision=highest) + bias_hidden)
    activated = low(jax.nn.gelu(widened, approximate=True))
    branch_expand = low_back(jnp.dot(activated, reduce_weight, precision=highest) + bias_output)
    return residual_one + gating_two * branch_expand

def adam_update(master, first_moment, second_moment, gradient, learn_rate, clip_factor, correction):
    clipped = gradient * clip_factor
    first_new = 0.5 * first_moment + 0.5 * clipped
    second_new = 0.5 * second_moment + 0.5 * clipped * clipped
    direction = first_new / correction / (jnp.sqrt(second_new / correction) + 1e-08)
    return (master - learn_rate * (direction + 0.1 * master), first_new, second_new)

def reference(tokens, cotangent, buckets, timesteps, labels, class_table, step_count, modulate_master, modulate_first, modulate_second, attend_master, attend_first, attend_second, project_master, project_first, project_second, expand_master, expand_first, expand_second, reduce_master, reduce_first, reduce_second, biases_master, biases_first, biases_second):
    masters = (modulate_master, attend_master, project_master, expand_master, reduce_master, biases_master)
    params = tuple((master.astype(jnp.bfloat16).astype(jnp.float32) for master in masters))
    condition = low(jax.nn.silu(class_table.astype(jnp.float32)[labels] + time_features(timesteps, D)))
    unit_cells = SIDE // 8
    heights = table_pick(buckets, row_units) * unit_cells
    widths = table_pick(buckets, col_units) * unit_cells
    group_count = IMAGES // IMG_GRP
    row_count = IMG_GRP * LMAX
    position = jnp.arange(LMAX, dtype=jnp.int32)
    scan_inputs = (tokens.reshape(group_count, row_count, D), cotangent.reshape(group_count, row_count, D), condition.reshape(group_count, IMG_GRP, D), heights.reshape(group_count, IMG_GRP), widths.reshape(group_count, IMG_GRP))

    def group_step(totals, inputs):
        group_tokens, group_cot, group_cond, group_height, group_wide = inputs
        live_keys = position[None, :] < (group_height * group_wide)[:, None]
        grid_cells = grid_features(jnp.tile(position, IMG_GRP), jnp.repeat(group_wide, LMAX), D)

        def forward(group_in, mod_weight, attend_weight, project_weight, expand_weight, reduce_weight, bias_vector):
            return block_forward(group_in, mod_weight, attend_weight, project_weight, expand_weight, reduce_weight, bias_vector, group_cond, live_keys, grid_cells)
        result, pullback = jax.vjp(forward, group_tokens.astype(jnp.float32), params[0], params[1], params[2], params[3], params[4], params[5])
        live_rows = live_keys.reshape(row_count, 1).astype(jnp.float32)
        gradients = pullback(group_cot.astype(jnp.float32) * live_rows)
        totals = tuple((running + gradient for running, gradient in zip(totals, gradients[1:])))
        return (totals, (result.astype(jnp.bfloat16), gradients[0]))
    initial = tuple((jnp.zeros(param.shape, jnp.float32) for param in params))
    totals, (results, input_grads) = lax.scan(group_step, initial, scan_inputs)
    square_total = sum((jnp.sum(gradient * gradient) for gradient in totals))
    grad_norm = jnp.sqrt(square_total)
    clip_factor = jnp.minimum(1.0, 1.0 / (grad_norm + 1e-06))
    correction = 1.0 - jnp.power(0.5, step_count.astype(jnp.float32))
    modulate_new = adam_update(modulate_master, modulate_first, modulate_second, totals[0], 0.5 * D ** (-0.5), clip_factor, correction)
    attend_new = adam_update(attend_master, attend_first, attend_second, totals[1], 0.5 * D ** (-0.5), clip_factor, correction)
    project_new = adam_update(project_master, project_first, project_second, totals[2], 0.5 * D ** (-0.5), clip_factor, correction)
    expand_new = adam_update(expand_master, expand_first, expand_second, totals[3], 0.5 * D ** (-0.5), clip_factor, correction)
    reduce_new = adam_update(reduce_master, reduce_first, reduce_second, totals[4], 0.5 * FF ** (-0.5), clip_factor, correction)
    biases_new = adam_update(biases_master, biases_first, biases_second, totals[5], 0.1, clip_factor, correction)
    return (results.reshape(TOKENS, D), input_grads.reshape(TOKENS, D), grad_norm, modulate_new[0], modulate_new[1], modulate_new[2], attend_new[0], attend_new[1], attend_new[2], project_new[0], project_new[1], project_new[2], expand_new[0], expand_new[1], expand_new[2], reduce_new[0], reduce_new[1], reduce_new[2], biases_new[0], biases_new[1], biases_new[2])
```

```python
import functools
import math

import jax
import jax.numpy as jnp
from jax import lax
from jax.experimental import pallas as pl
from jax.experimental.pallas import tpu as pltpu
from jax.sharding import Mesh
from jax.sharding import PartitionSpec as P

D = 1152
HEAD_DIM = 72
FF = 4608
SIDE = 32
LMAX = 1024


highest = lax.Precision.HIGHEST
row_units = (8, 4, 16, 6, 10, 7, 4, 6)
col_units = (8, 16, 4, 10, 6, 9, 8, 6)


def table_pick(indices, entries):
    matches = indices[..., None] == jnp.arange(len(entries), dtype=jnp.int32)
    return jnp.sum(jnp.where(matches, jnp.array(entries, jnp.int32), 0), axis=-1)


def layer_norm(value):
    average = jnp.mean(value, axis=-1, keepdims=True)
    centred = value - average
    spread = jnp.mean(centred * centred, axis=-1, keepdims=True)
    return centred * lax.rsqrt(spread + 1e-06)


def modulate(value, shift, scaling):
    return layer_norm(value) * (1.0 + scaling) + shift


def time_features(moments, width):
    half_width = width // 2
    frequency = jnp.exp(-math.log(10000.0) * jnp.arange(half_width, dtype=jnp.float32) / half_width)
    angles = moments.astype(jnp.float32)[:, None] * frequency[None, :]
    return jnp.concatenate([jnp.cos(angles), jnp.sin(angles)], axis=1)


def grid_features(position, row_wide, width):
    quarter = width // 4
    omegas = jnp.exp(-math.log(10000.0) * jnp.arange(quarter, dtype=jnp.float32) / quarter)
    row_angle = (position // row_wide).astype(jnp.float32)[:, None] * omegas[None, :]
    col_angle = (position % row_wide).astype(jnp.float32)[:, None] * omegas[None, :]
    return jnp.concatenate(
        [jnp.sin(row_angle), jnp.cos(row_angle), jnp.sin(col_angle), jnp.cos(col_angle)], axis=1
    )


def fold_rows(left_side, weight_slab):
    return jnp.dot(
        left_side,
        lax.all_gather(weight_slab, "seq", axis=0, tiled=True),
        preferred_element_type=jnp.float32,
    )


def back_cols(gradient, weight_slab):
    return lax.dot_general(
        gradient,
        lax.all_gather(weight_slab, "seq", axis=0, tiled=True),
        (((1,), (1,)), ((), ())),
        preferred_element_type=jnp.float32,
    )


def rows_seq(left_side, right_side):
    return lax.psum_scatter(
        lax.dot_general(
            left_side, right_side, (((0,), (0,)), ((), ())), preferred_element_type=jnp.float32
        ).astype(jnp.bfloat16),
        "seq",
        scatter_dimension=0,
        tiled=True,
    ).astype(jnp.float32)


def attend(queries, key_rows, value_rows, lengths):
    heads_here = queries.shape[1] // HEAD_DIM
    block_rows = min(512, LMAX)
    score_scale = HEAD_DIM ** (-0.5)
    image_count = lengths.shape[0]

    def per_image(packed):
        query_image, key_image, value_image, length = packed
        key_heads = key_image.reshape(LMAX, heads_here, HEAD_DIM)
        value_heads = value_image.reshape(LMAX, heads_here, HEAD_DIM)
        live_keys = jnp.arange(LMAX, dtype=jnp.int32) < length

        def per_block(query_block):
            scores = (
                jnp.einsum(
                    "qhe,khe->hqk", query_block, key_heads, preferred_element_type=jnp.float32
                )
                * score_scale
            )
            scores = jnp.where(live_keys[None, None, :], scores, -1e30)
            maximum = jnp.max(scores, axis=-1, keepdims=True)
            weights = jnp.exp(scores - maximum)
            totals = jnp.sum(weights, axis=-1, keepdims=True)
            probability = (weights / totals).astype(jnp.bfloat16)
            result = jnp.einsum(
                "hqk,khe->qhe", probability, value_heads, preferred_element_type=jnp.float32
            )
            return (result.astype(jnp.bfloat16), (maximum + jnp.log(totals))[:, :, 0])

        blocks = query_image.reshape(LMAX // block_rows, block_rows, heads_here, HEAD_DIM)
        result, log_sums = lax.map(per_block, blocks)
        return (result.reshape(LMAX, heads_here * HEAD_DIM), log_sums)

    stacked = (
        queries.reshape(image_count, LMAX, -1),
        key_rows.reshape(image_count, LMAX, -1),
        value_rows.reshape(image_count, LMAX, -1),
        lengths,
    )
    result, log_sums = lax.map(per_image, stacked)
    return (result.reshape(image_count * LMAX, -1), log_sums)


def attend_back(queries, key_rows, value_rows, grad_rows, log_sums, lengths):
    heads_here = queries.shape[1] // HEAD_DIM
    block_rows = min(512, LMAX)
    score_scale = HEAD_DIM ** (-0.5)
    image_count = lengths.shape[0]

    def per_image(packed):
        query_image, key_image, value_image, grad_image, logsum_image, length = packed
        key_heads = key_image.reshape(LMAX, heads_here, HEAD_DIM)
        value_heads = value_image.reshape(LMAX, heads_here, HEAD_DIM)
        live_keys = jnp.arange(LMAX, dtype=jnp.int32) < length

        def per_block(running, inputs):
            key_grad, value_grad = running
            query_block, grad_block, logsum_block = inputs
            scores = (
                jnp.einsum(
                    "qhe,khe->hqk", query_block, key_heads, preferred_element_type=jnp.float32
                )
                * score_scale
            )
            scores = jnp.where(live_keys[None, None, :], scores, -1e30)
            probability = jnp.exp(scores - logsum_block[:, :, None])
            grad_prob = jnp.einsum(
                "qhe,khe->hqk", grad_block, value_heads, preferred_element_type=jnp.float32
            )
            inner_sum = jnp.sum(probability * grad_prob, axis=-1, keepdims=True)
            grad_score = (probability * (grad_prob - inner_sum)).astype(jnp.bfloat16)
            query_grad = (
                jnp.einsum(
                    "hqk,khe->qhe", grad_score, key_heads, preferred_element_type=jnp.float32
                )
                * score_scale
            )
            key_grad = (
                key_grad
                + jnp.einsum(
                    "hqk,qhe->khe", grad_score, query_block, preferred_element_type=jnp.float32
                )
                * score_scale
            )
            value_grad = value_grad + jnp.einsum(
                "hqk,qhe->khe",
                probability.astype(jnp.bfloat16),
                grad_block,
                preferred_element_type=jnp.float32,
            )
            return ((key_grad, value_grad), query_grad.astype(jnp.bfloat16))

        initial = (
            jnp.zeros((LMAX, heads_here, HEAD_DIM), jnp.float32),
            jnp.zeros((LMAX, heads_here, HEAD_DIM), jnp.float32),
        )
        blocks = (
            query_image.reshape(LMAX // block_rows, block_rows, heads_here, HEAD_DIM),
            grad_image.reshape(LMAX // block_rows, block_rows, heads_here, HEAD_DIM),
            logsum_image,
        )
        (key_grad, value_grad), query_grad = lax.scan(per_block, initial, blocks)
        return (
            query_grad.reshape(LMAX, -1),
            key_grad.reshape(LMAX, -1).astype(jnp.bfloat16),
            value_grad.reshape(LMAX, -1).astype(jnp.bfloat16),
        )

    stacked = (
        queries.reshape(image_count, LMAX, -1),
        key_rows.reshape(image_count, LMAX, -1),
        value_rows.reshape(image_count, LMAX, -1),
        grad_rows.reshape(image_count, LMAX, -1),
        log_sums,
        lengths,
    )
    query_grad, key_grad, value_grad = lax.map(per_image, stacked)
    return (
        query_grad.reshape(image_count * LMAX, -1),
        key_grad.reshape(image_count * LMAX, -1),
        value_grad.reshape(image_count * LMAX, -1),
    )


def adam_update(master, first_moment, second_moment, gradient, learn_rate, clip_factor, correction):
    clipped = gradient * clip_factor
    first_new = 0.5 * first_moment + 0.5 * clipped
    second_new = 0.5 * second_moment + 0.5 * clipped * clipped
    direction = first_new / correction / (jnp.sqrt(second_new / correction) + 1e-08)
    return (master - learn_rate * (direction + 0.1 * master), first_new, second_new)


def on_device(
    tokens,
    cotangent,
    buckets,
    timesteps,
    labels,
    class_table,
    step_count,
    modulate_master,
    modulate_first,
    modulate_second,
    attend_master,
    attend_first,
    attend_second,
    project_master,
    project_first,
    project_second,
    expand_master,
    expand_first,
    expand_second,
    reduce_master,
    reduce_first,
    reduce_second,
    biases_master,
    biases_first,
    biases_second,
):
    head_index = lax.axis_index("head")
    head_count = lax.axis_size("head")
    tok_rows = tokens.shape[0]
    image_count = buckets.shape[0]
    unit_cells = SIDE // 8
    heights = table_pick(buckets, row_units) * unit_cells
    widths = table_pick(buckets, col_units) * unit_cells
    lengths = heights * widths
    row_index = head_index * tok_rows + jnp.arange(tok_rows, dtype=jnp.int32)
    image_of = row_index // LMAX
    position = row_index % LMAX
    choose = image_of[:, None] == jnp.arange(image_count, dtype=jnp.int32)[None, :]
    pick_rows = choose.astype(jnp.float32)
    row_wide = jnp.sum(jnp.where(choose, widths[None, :], 0), axis=1)
    row_length = jnp.sum(jnp.where(choose, lengths[None, :], 0), axis=1)
    live_rows = (position < row_length).astype(jnp.float32)
    grid_cells = grid_features(position, row_wide, D)
    class_pick = (
        labels[:, None] == jnp.arange(class_table.shape[0], dtype=jnp.int32)[None, :]
    ).astype(jnp.bfloat16)
    class_rows = jnp.dot(class_pick, class_table, preferred_element_type=jnp.float32)
    condition = jax.nn.silu(class_rows + time_features(timesteps, D)).astype(jnp.bfloat16)
    bias_low = biases_master.astype(jnp.bfloat16).astype(jnp.float32)
    offset_base = 6 * D
    bias_query = bias_low[offset_base : offset_base + D]
    bias_value = bias_low[offset_base + D : offset_base + 2 * D]
    bias_proj = bias_low[offset_base + 2 * D : offset_base + 3 * D]
    bias_hidden = bias_low[offset_base + 3 * D : offset_base + 3 * D + FF]
    bias_output = bias_low[offset_base + 3 * D + FF :]
    head_slabs = (
        lax.all_gather(attend_master.astype(jnp.bfloat16), "head", axis=1, tiled=True),
        lax.all_gather(project_master.astype(jnp.bfloat16), "head", axis=1, tiled=True),
        lax.all_gather(expand_master.astype(jnp.bfloat16), "head", axis=1, tiled=True),
        lax.all_gather(reduce_master.astype(jnp.bfloat16), "head", axis=1, tiled=True),
    )
    attend_slab, project_slab, expand_slab, reduce_slab = head_slabs
    mod_width = 6 * D // head_count
    mod_share = fold_rows(condition, modulate_master.astype(jnp.bfloat16))
    mod_share = mod_share + lax.dynamic_slice_in_dim(bias_low, head_index * mod_width, mod_width)
    modulation = lax.all_gather(mod_share, "head", axis=1, tiled=True)
    mod_rows = jnp.dot(pick_rows, modulation, precision=highest)
    shift_one, scale_one, gating_one, shift_two, scale_two, gating_two = jnp.split(
        mod_rows, 6, axis=1
    )
    residual_zero = tokens.astype(jnp.float32) + grid_cells
    hidden_attend = modulate(residual_zero, shift_one, scale_one).astype(jnp.bfloat16)
    packed = fold_rows(hidden_attend, attend_slab)
    queries = (packed[:, :D] + bias_query).astype(jnp.bfloat16)
    key_rows = packed[:, D : 2 * D].astype(jnp.bfloat16)
    value_rows = (packed[:, 2 * D :] + bias_value).astype(jnp.bfloat16)
    query_heads, key_heads, value_heads = (
        lax.all_to_all(queries, "head", split_axis=1, concat_axis=0, tiled=True),
        lax.all_to_all(key_rows, "head", split_axis=1, concat_axis=0, tiled=True),
        lax.all_to_all(value_rows, "head", split_axis=1, concat_axis=0, tiled=True),
    )
    head_out, log_sums = attend(query_heads, key_heads, value_heads, lengths)
    attention = lax.all_to_all(head_out, "head", split_axis=0, concat_axis=1, tiled=True)
    branch_attend = fold_rows(attention, project_slab) + bias_proj
    residual_one = residual_zero + gating_one * branch_attend
    hidden_expand = modulate(residual_one, shift_two, scale_two).astype(jnp.bfloat16)
    widened = fold_rows(hidden_expand, expand_slab) + bias_hidden
    activated = jax.nn.gelu(widened, approximate=True).astype(jnp.bfloat16)
    branch_expand = fold_rows(activated, reduce_slab) + bias_output
    output = (residual_one + gating_two * branch_expand).astype(jnp.bfloat16)
    outer_grad = cotangent.astype(jnp.float32) * live_rows[:, None]
    gating_later = outer_grad * branch_expand
    closing_grad = (outer_grad * gating_two).astype(jnp.bfloat16)
    active_grad = back_cols(closing_grad, reduce_slab)
    gelu_value, gelu_pullback = jax.vjp(lambda inner: jax.nn.gelu(inner, approximate=True), widened)
    widened_grad = gelu_pullback(active_grad)[0].astype(jnp.bfloat16)
    hidden_grad = back_cols(widened_grad, expand_slab)
    later_value, later_pullback = jax.vjp(modulate, residual_one, shift_two, scale_two)
    residual_part, shift_later, scale_later = later_pullback(hidden_grad)
    middle_grad = outer_grad + residual_part
    gating_early = middle_grad * branch_attend
    branch_grad = (middle_grad * gating_one).astype(jnp.bfloat16)
    attend_grad = back_cols(branch_grad, project_slab).astype(jnp.bfloat16)
    heads_grad = lax.all_to_all(attend_grad, "head", split_axis=1, concat_axis=0, tiled=True)
    query_grad, keyrow_grad, value_grad = attend_back(
        query_heads, key_heads, value_heads, heads_grad, log_sums, lengths
    )
    query_back, keys_back, values_back = (
        lax.all_to_all(query_grad, "head", split_axis=0, concat_axis=1, tiled=True),
        lax.all_to_all(keyrow_grad, "head", split_axis=0, concat_axis=1, tiled=True),
        lax.all_to_all(value_grad, "head", split_axis=0, concat_axis=1, tiled=True),
    )
    packed_grad = jnp.concatenate([query_back, keys_back, values_back], axis=1)
    normed_grad = back_cols(packed_grad, attend_slab)
    early_value, early_pullback = jax.vjp(modulate, residual_zero, shift_one, scale_one)
    input_part, shift_early, scale_early = early_pullback(normed_grad)
    input_grad = middle_grad + input_part
    mod_token_grad = jnp.concatenate(
        [shift_early, scale_early, gating_early, shift_later, scale_later, gating_later], axis=1
    )
    mod_grad = lax.dot_general(
        pick_rows, mod_token_grad, (((0,), (0,)), ((), ())), precision=highest
    )
    mod_summed = lax.psum_scatter(mod_grad, "head", scatter_dimension=1, tiled=True)
    mod_rounded = mod_summed.astype(jnp.bfloat16)
    grad_mod = rows_seq(condition, mod_rounded)
    mod_slot = lax.dynamic_update_slice_in_dim(
        jnp.zeros((6 * D,), jnp.float32),
        jnp.sum(mod_rounded.astype(jnp.float32), axis=0),
        head_index * mod_width,
        0,
    )
    bias_share = jnp.concatenate(
        [
            mod_slot,
            jnp.sum(query_back.astype(jnp.float32), axis=0),
            jnp.sum(values_back.astype(jnp.float32), axis=0),
            jnp.sum(branch_grad.astype(jnp.float32), axis=0),
            jnp.sum(widened_grad.astype(jnp.float32), axis=0),
            jnp.sum(closing_grad.astype(jnp.float32), axis=0),
        ]
    )
    operand_pairs = (
        (hidden_attend, packed_grad),
        (attention, branch_grad),
        (hidden_expand, widened_grad),
        (activated, closing_grad),
    )
    term_slabs = tuple((rows_seq(left_side, right_side) for left_side, right_side in operand_pairs))
    reduced = (
        lax.psum_scatter(
            term_slabs[0].astype(jnp.bfloat16), "head", scatter_dimension=1, tiled=True
        ).astype(jnp.float32),
        lax.psum_scatter(
            term_slabs[1].astype(jnp.bfloat16), "head", scatter_dimension=1, tiled=True
        ).astype(jnp.float32),
        lax.psum_scatter(
            term_slabs[2].astype(jnp.bfloat16), "head", scatter_dimension=1, tiled=True
        ).astype(jnp.float32),
        lax.psum_scatter(
            term_slabs[3].astype(jnp.bfloat16), "head", scatter_dimension=1, tiled=True
        ).astype(jnp.float32),
    )
    grad_attend, grad_project, grad_expand, grad_reduce = reduced
    local_squares = jnp.sum(grad_mod * grad_mod) + sum(
        (jnp.sum(gradient * gradient) for gradient in reduced)
    )
    bias_total, square_total = lax.psum((bias_share, local_squares), ("seq", "head"))
    grad_norm = jnp.sqrt(square_total + jnp.sum(bias_total * bias_total))
    clip_factor = jnp.minimum(1.0, 1.0 / (grad_norm + 1e-06))
    correction = 1.0 - jnp.power(0.5, step_count.astype(jnp.float32))
    modulate_new = adam_update(
        modulate_master,
        modulate_first,
        modulate_second,
        grad_mod,
        0.5 * D ** (-0.5),
        clip_factor,
        correction,
    )
    attend_new = adam_update(
        attend_master,
        attend_first,
        attend_second,
        grad_attend,
        0.5 * D ** (-0.5),
        clip_factor,
        correction,
    )
    project_new = adam_update(
        project_master,
        project_first,
        project_second,
        grad_project,
        0.5 * D ** (-0.5),
        clip_factor,
        correction,
    )
    expand_new = adam_update(
        expand_master,
        expand_first,
        expand_second,
        grad_expand,
        0.5 * D ** (-0.5),
        clip_factor,
        correction,
    )
    reduce_new = adam_update(
        reduce_master,
        reduce_first,
        reduce_second,
        grad_reduce,
        0.5 * FF ** (-0.5),
        clip_factor,
        correction,
    )
    biases_new = adam_update(
        biases_master, biases_first, biases_second, bias_total, 0.1, clip_factor, correction
    )
    return (
        output,
        input_grad,
        grad_norm,
        modulate_new[0],
        modulate_new[1],
        modulate_new[2],
        attend_new[0],
        attend_new[1],
        attend_new[2],
        project_new[0],
        project_new[1],
        project_new[2],
        expand_new[0],
        expand_new[1],
        expand_new[2],
        reduce_new[0],
        reduce_new[1],
        reduce_new[2],
        biases_new[0],
        biases_new[1],
        biases_new[2],
    )


MESH = pl.DeviceIdType.MESH
PIECES = {"q": (144, 864, 96), "p": (72, 576, None), "u": (144, 1152, 96), "d": (288, 576, 192)}
NAMES = ("q", "p", "u", "d")


def place():
    return tuple(lax.axis_index(a) for a in ("z", "x", "c", "y"))


def at_z(k):
    z = lax.axis_index("z")
    return (z + 1 - 2 * (z % 2), (z + 2) % 4, 3 - z)[k - 1]


def rdma(src, dst, send, recv, to):
    return pltpu.make_async_remote_copy(
        src_ref=src, dst_ref=dst, send_sem=send, recv_sem=recv, device_id=to, device_id_type=MESH
    )


def greet(partners):
    barrier = pltpu.get_barrier_semaphore()
    for to in partners:
        pl.semaphore_signal(barrier, inc=1, device_id=to, device_id_type=MESH)
    pl.semaphore_wait(barrier, len(partners))


def parts_of(rows, cut, k):
    if cut is None:
        return ((0, rows), None) if k % 2 == 0 else (None, (0, rows))
    return (0, cut), (cut, rows - cut)


def gather_kernel(*refs):
    own, full = refs[0:4], refs[4:8]
    lsem, zs, zr, xs, xr, ys, yr, fs, fr = refs[8:]
    z, x, c, y = place()
    xn, yn = (z, 1 - x, c, y), (z, x, c, 1 - y)
    zn = [None] + [(at_z(k), x, c, y) for k in (1, 2, 3)]
    greet([xn, yn] + zn[1:])
    pending = []
    for w in range(4):
        mine = full[w].at[y, z, x]
        pltpu.make_async_copy(own[w], mine, lsem.at[w]).start()
        for k in (1, 2, 3):
            d = rdma(own[w], mine, zs.at[w, k], zr.at[w, k], zn[k])
            d.start()
            pending.append(d)
        for to, s, r in ((xn, xs, xr), (yn, ys, yr)):
            d = rdma(own[w], mine, s.at[w, 0], r.at[w, 0], to)
            d.start()
            pending.append(d)
    for w in range(4):
        rows, _, cut = PIECES[NAMES[w]]
        for k in (1, 2, 3):
            piece = full[w].at[y, at_z(k), x]
            rdma(piece, piece, zs.at[w, k], zr.at[w, k], zn[k]).wait_recv()
            for to, s, r in ((xn, xs, xr), (yn, ys, yr)):
                d = rdma(piece, piece, s.at[w, k], r.at[w, k], to)
                d.start()
                pending.append(d)
        for k in range(4):
            zk = z if k == 0 else at_z(k)
            by_x, by_y = parts_of(rows, cut, k)
            piece = full[w].at[y, zk, 1 - x]
            rdma(piece, piece, xs.at[w, k], xr.at[w, k], xn).wait_recv()
            if by_x is not None:
                part = full[w].at[y, zk, 1 - x, pl.ds(*by_x)]
                d = rdma(part, part, fs.at[w, k, 0], fr.at[w, k, 0], yn)
                d.start()
                pending.append(d)
            piece = full[w].at[1 - y, zk, x]
            rdma(piece, piece, ys.at[w, k], yr.at[w, k], yn).wait_recv()
            if by_y is not None:
                part = full[w].at[1 - y, zk, x, pl.ds(*by_y)]
                d = rdma(part, part, fs.at[w, k, 1], fr.at[w, k, 1], xn)
                d.start()
                pending.append(d)
    for w in range(4):
        rows, _, cut = PIECES[NAMES[w]]
        pltpu.make_async_copy(own[w], full[w].at[y, z, x], lsem.at[w]).wait()
        for k in range(4):
            zk = z if k == 0 else at_z(k)
            for i, span in enumerate(parts_of(rows, cut, k)):
                if span is not None:
                    part = full[w].at[1 - y, zk, 1 - x, pl.ds(*span)]
                    rdma(part, part, fs.at[w, k, i], fr.at[w, k, i], xn).wait_recv()
    for d in pending:
        d.wait_send()


def gather_weights(own):
    any_space = pl.BlockSpec(memory_space=pl.ANY)
    dma = pltpu.SemaphoreType.DMA
    return pl.pallas_call(
        gather_kernel,
        out_shape=[
            jax.ShapeDtypeStruct((2, 4, 2) + PIECES[n][:2], jnp.bfloat16) for n in NAMES
        ],
        in_specs=[any_space] * 4,
        out_specs=[any_space] * 4,
        scratch_shapes=[dma((4,))] + [dma((4, 4))] * 6 + [dma((4, 4, 2))] * 2,
        compiler_params=pltpu.CompilerParams(collective_id=0, has_side_effects=True),
        name="gather_weights",
    )(*own)


def scatter_kernel(*refs):
    grads, outs = refs[0:4], refs[4:8]
    held, diag, by_x, by_y, by_z = (refs[8 + 4 * i : 12 + 4 * i] for i in range(5))
    lsem, fs, fr, xs, xr, ys, yr, zs, zr = refs[28:]
    z, x, c, y = place()
    xn, yn = (z, 1 - x, c, y), (z, x, c, 1 - y)
    zn = [None] + [(at_z(k), x, c, y) for k in (1, 2, 3)]
    f32 = jnp.float32
    for w in range(4):
        pltpu.make_async_copy(grads[w], held[w], lsem.at[w]).start()
    greet([xn, yn] + zn[1:])
    pending = []
    order = (3, 2, 1, 0)

    def z_of(k):
        return z if k == 0 else at_z(k)

    for w in range(4):
        rows, _, cut = PIECES[NAMES[w]]
        pltpu.make_async_copy(grads[w], held[w], lsem.at[w]).wait()
        for k in order:
            spans = parts_of(rows, cut, k)
            for i, (span, to) in enumerate(zip(spans, (yn, xn))):
                if span is not None:
                    d = rdma(
                        held[w].at[1 - y, z_of(k), 1 - x, pl.ds(*span)],
                        diag[w].at[k, pl.ds(*span)],
                        fs.at[w, k, i],
                        fr.at[w, k, i],
                        to,
                    )
                    d.start()
                    pending.append(d)
    for w in range(4):
        rows, _, cut = PIECES[NAMES[w]]
        for k in order:
            spans = parts_of(rows, cut, k)
            for i, span in enumerate(spans):
                piece = held[w].at[(y, z_of(k), 1 - x) if i == 0 else (1 - y, z_of(k), x)]
                if span is not None:
                    part = diag[w].at[k, pl.ds(*span)]
                    rdma(part, part, fs.at[w, k, i], fr.at[w, k, i], xn).wait_recv()
                    target = piece.at[pl.ds(*span)]
                    target[...] = (target[...].astype(f32) + part[...].astype(f32)).astype(
                        jnp.bfloat16
                    )
                box, to, s, r = ((by_x, xn, xs, xr), (by_y, yn, ys, yr))[i]
                d = rdma(piece, box[w].at[k], s.at[w, k], r.at[w, k], to)
                d.start()
                pending.append(d)
    for w in range(4):
        for k in order:
            for box, s, r in ((by_x, xs, xr), (by_y, ys, yr)):
                part = box[w].at[k]
                rdma(part, part, s.at[w, k], r.at[w, k], xn).wait_recv()
            piece = held[w].at[y, z_of(k), x]
            total = piece[...].astype(f32) + by_x[w][k].astype(f32) + by_y[w][k].astype(f32)
            if k == 0:
                outs[w][...] = total
            else:
                piece[...] = total.astype(jnp.bfloat16)
                d = rdma(piece, by_z[w].at[k - 1], zs.at[w, k - 1], zr.at[w, k - 1], zn[k])
                d.start()
                pending.append(d)
    for w in range(4):
        total = outs[w][...]
        for k in (1, 2, 3):
            part = by_z[w].at[k - 1]
            rdma(part, part, zs.at[w, k - 1], zr.at[w, k - 1], zn[k]).wait_recv()
            total = total + part[...].astype(f32)
        outs[w][...] = total
    for d in pending:
        d.wait_send()


def scatter_grads(grads):
    dma = pltpu.SemaphoreType.DMA
    shapes = [PIECES[n][:2] for n in NAMES]

    def boxes(*lead):
        return [pltpu.VMEM(lead + s, jnp.bfloat16) for s in shapes]

    return pl.pallas_call(
        scatter_kernel,
        out_shape=[jax.ShapeDtypeStruct(s, jnp.float32) for s in shapes],
        in_specs=[pl.BlockSpec(memory_space=pl.ANY)] * 4,
        out_specs=[pl.BlockSpec(memory_space=pltpu.VMEM)] * 4,
        scratch_shapes=boxes(2, 4, 2)
        + boxes(4)
        + boxes(4)
        + boxes(4)
        + boxes(3)
        + [dma((4,))]
        + [dma((4, 4, 2))] * 2
        + [dma((4, 4))] * 6,
        compiler_params=pltpu.CompilerParams(
            collective_id=1, has_side_effects=True, vmem_limit_bytes=56 * 2**20
        ),
        name="scatter_grads",
    )(*grads)


def mod_kernel(cond_ref, weight_ref, out_ref, lhs, conds, part, got_z, mid, got_x, near, got_c, s, r):
    z, x, c, y = place()
    xn, yn, twin = (z, 1 - x, c, y), (z, x, c, 1 - y), (z, x, 1 - c, y)
    zn = [None] + [(at_z(k), x, c, y) for k in (1, 2, 3)]
    greet([xn, yn, twin] + zn[1:])
    conds[z, x, c] = cond_ref[...]
    d = rdma(conds.at[z, x, c], conds.at[z, x, c], s.at[0], r.at[0], twin)
    d.start()
    d.wait()
    d = rdma(conds.at[z, x], conds.at[z, x], s.at[1], r.at[1], xn)
    d.start()
    d.wait()
    ds = [rdma(conds.at[z], conds.at[z], s.at[1 + k], r.at[1 + k], zn[k]) for k in (1, 2, 3)]
    for d in ds:
        d.start()
    for d in ds:
        d.wait()
    me = (z * 2 + x) * 2 + c
    for i in range(16):
        lhs[pl.ds(i, 1), :] = conds[i // 4, i // 2 % 2, i % 2, pl.ds(me, 1), :]
    result = jnp.dot(
        lhs[:, :72].astype(jnp.bfloat16), weight_ref[...], preferred_element_type=jnp.float32
    )
    for i in range(16):
        part[i // 4, i // 2 % 2, i % 2] = result[i : i + 1]
    ds = [
        rdma(part.at[at_z(k)], got_z.at[k - 1], s.at[4 + k], r.at[4 + k], zn[k]) for k in (1, 2, 3)
    ]
    for d in ds:
        d.start()
    for d in ds:
        d.wait()
    mid[...] = part[z] + got_z[0] + got_z[1] + got_z[2]
    d = rdma(mid.at[1 - x], got_x, s.at[8], r.at[8], xn)
    d.start()
    d.wait()
    near[0] = mid[x] + got_x[...]
    d = rdma(near.at[0], got_c, s.at[9], r.at[9], twin)
    d.start()
    d.wait()
    near[1] = near[0] + got_c[...]
    out_ref[y] = near[1, y]
    d = rdma(near.at[1, 1 - y], out_ref.at[y], s.at[10], r.at[10], yn)
    d.start()
    d.wait()


def image_modulation(cond, weight):
    f32, vm = jnp.float32, pltpu.VMEM
    return pl.pallas_call(
        mod_kernel,
        out_shape=[
            jax.ShapeDtypeStruct((2, 1, 3456), f32),
            jax.ShapeDtypeStruct((16, 128), f32),
        ],
        in_specs=[pl.BlockSpec(memory_space=vm)] * 2,
        out_specs=[pl.BlockSpec(memory_space=vm)] * 2,
        scratch_shapes=[
            vm((4, 2, 2, 16, 128), f32),
            vm((4, 2, 2, 1, 3456), f32),
            vm((3, 2, 2, 1, 3456), f32),
            vm((2, 2, 1, 3456), f32),
            vm((2, 1, 3456), f32),
            vm((2, 2, 1, 3456), f32),
            vm((2, 1, 3456), f32),
            pltpu.SemaphoreType.DMA((11,)),
            pltpu.SemaphoreType.DMA((11,)),
        ],
        compiler_params=pltpu.CompilerParams(collective_id=2, has_side_effects=True),
        name="image_modulation",
    )(cond, weight)


def totals_kernel(mod_ref, bias_ref, mods, sums, got_m, got_b, got_z, s, r):
    z, x, c, y = place()
    xn, yn, twin = (z, 1 - x, c, y), (z, x, c, 1 - y), (z, x, 1 - c, y)
    zn = [None] + [(at_z(k), x, c, y) for k in (1, 2, 3)]
    greet([xn, yn, twin] + zn[1:])
    d = rdma(mod_ref, got_m, s.at[0], r.at[0], twin)
    e = rdma(bias_ref, got_b.at[0], s.at[1], r.at[1], twin)
    d.start()
    e.start()
    d.wait()
    e.wait()
    mods[z, x, y] = (mod_ref[...] + got_m[...]).astype(jnp.bfloat16)
    sums[...] = bias_ref[...] + got_b[0]
    d = rdma(mods.at[z, x, y], mods.at[z, x, y], s.at[2], r.at[2], yn)
    e = rdma(sums, got_b.at[1], s.at[3], r.at[3], yn)
    d.start()
    e.start()
    d.wait()
    e.wait()
    sums[...] = sums[...] + got_b[1]
    d = rdma(mods.at[z, x], mods.at[z, x], s.at[4], r.at[4], xn)
    e = rdma(sums, got_b.at[2], s.at[5], r.at[5], xn)
    d.start()
    e.start()
    d.wait()
    e.wait()
    got_z[0] = sums[...] + got_b[2]
    ds = [rdma(mods.at[z], mods.at[z], s.at[5 + k], r.at[5 + k], zn[k]) for k in (1, 2, 3)]
    ds += [rdma(got_z.at[0], got_z.at[k], s.at[8 + k], r.at[8 + k], zn[k]) for k in (1, 2, 3)]
    for d in ds:
        d.start()
    for d in ds:
        d.wait()
    sums[...] = (got_z[0] + got_z[1]) + (got_z[2] + got_z[3])


def share_totals(mod_grad, bias_grad):
    f32, vm = jnp.float32, pltpu.VMEM
    return pl.pallas_call(
        totals_kernel,
        out_shape=[
            jax.ShapeDtypeStruct((4, 2, 2, 16, 432), jnp.bfloat16),
            jax.ShapeDtypeStruct((72, 128), f32),
        ],
        in_specs=[pl.BlockSpec(memory_space=vm)] * 2,
        out_specs=[pl.BlockSpec(memory_space=vm)] * 2,
        scratch_shapes=[
            vm((16, 432), f32),
            vm((3, 72, 128), f32),
            vm((4, 72, 128), f32),
            pltpu.SemaphoreType.DMA((12,)),
            pltpu.SemaphoreType.DMA((12,)),
        ],
        compiler_params=pltpu.CompilerParams(collective_id=3, has_side_effects=True),
        name="share_totals",
    )(mod_grad, bias_grad)


def norm_kernel(in_ref, out_ref, box, got_z, s, r):
    z, x, c, y = place()
    xn, yn, twin = (z, 1 - x, c, y), (z, x, c, 1 - y), (z, x, 1 - c, y)
    zn = [None] + [(at_z(k), x, c, y) for k in (1, 2, 3)]
    greet([xn, yn, twin] + zn[1:])
    total = in_ref[...]
    for i, to in enumerate((twin, yn, xn)):
        box[2 * i] = total
        d = rdma(box.at[2 * i], box.at[2 * i + 1], s.at[i], r.at[i], to)
        d.start()
        d.wait()
        total = total + box[2 * i + 1]
    got_z[0] = total
    ds = [rdma(got_z.at[0], got_z.at[k], s.at[2 + k], r.at[2 + k], zn[k]) for k in (1, 2, 3)]
    for d in ds:
        d.start()
    for d in ds:
        d.wait()
    out_ref[...] = (got_z[0] + got_z[1]) + (got_z[2] + got_z[3])


def sum_everywhere(value):
    f32, vm = jnp.float32, pltpu.VMEM
    return pl.pallas_call(
        norm_kernel,
        out_shape=jax.ShapeDtypeStruct((8, 128), f32),
        in_specs=[pl.BlockSpec(memory_space=vm)],
        out_specs=pl.BlockSpec(memory_space=vm),
        scratch_shapes=[
            vm((6, 8, 128), f32),
            vm((4, 8, 128), f32),
            pltpu.SemaphoreType.DMA((6,)),
            pltpu.SemaphoreType.DMA((6,)),
        ],
        compiler_params=pltpu.CompilerParams(collective_id=4, has_side_effects=True),
        name="sum_everywhere",
    )(value)


def swap_halves(value):
    return lax.ppermute(value, ("c", "y"), [(0, 0), (1, 2), (2, 1), (3, 3)])


def to_twin(value):
    return lax.ppermute(value, "c", [(0, 1), (1, 0)])


def both_halves(value):
    c = lax.axis_index("c")
    other = to_twin(value)
    return jnp.where(c == 0, jnp.concatenate([value, other]), jnp.concatenate([other, value]))


def sum_halves(value):
    c = lax.axis_index("c")
    half = value.shape[0] // 2
    mine = lax.dynamic_slice_in_dim(value, c * half, half)
    other = to_twin(lax.dynamic_slice_in_dim(value, (1 - c) * half, half).astype(jnp.bfloat16))
    return mine + other.astype(jnp.float32)


def wide(left, weight):
    return jnp.concatenate(
        [jnp.dot(left, weight[i], preferred_element_type=jnp.float32) for i in (0, 1)], axis=1
    )


def wide_back(gradient, weight):
    half = weight.shape[2]
    return sum(
        lax.dot_general(
            gradient[:, i * half : (i + 1) * half],
            weight[i],
            (((1,), (1,)), ((), ())),
            preferred_element_type=jnp.float32,
        )
        for i in (0, 1)
    )


def weight_grad(left, right, name):
    rows, cols, _ = PIECES[name]
    half = right.shape[1] // 2
    return jnp.stack(
        [
            lax.dot_general(
                left,
                right[:, i * half : (i + 1) * half],
                (((0,), (0,)), ((), ())),
                preferred_element_type=jnp.float32,
            ).astype(jnp.bfloat16)
            for i in (0, 1)
        ]
    ).reshape(2, 4, 2, rows, cols)


def core_columns(shard, width):
    rows, cols = shard.shape
    blocks = shard.reshape(rows, cols // (2 * width), 2, width)
    return blocks.transpose(2, 0, 1, 3).reshape(2, rows, cols // 2)


def chip_piece(shard, width):
    c = lax.axis_index("c")
    split = core_columns(shard, width)
    mine = lax.dynamic_index_in_dim(split, c, 0, keepdims=False)
    other = to_twin(lax.dynamic_index_in_dim(split, 1 - c, 0, keepdims=False))
    return jnp.where(c == 0, jnp.concatenate([mine, other]), jnp.concatenate([other, mine]))


def shard_from_pieces(piece, width):
    c = lax.axis_index("c")
    half = piece.shape[0] // 2
    mine = lax.dynamic_slice_in_dim(piece, c * half, half)
    other = to_twin(lax.dynamic_slice_in_dim(piece, (1 - c) * half, half))
    split = jnp.where(c == 0, jnp.stack([mine, other]), jnp.stack([other, mine]))
    cols = piece.shape[1]
    return split.reshape(2, half, cols // width, width).transpose(1, 2, 0, 3).reshape(half, 2 * cols)


def core_bias(piece, width):
    c = lax.axis_index("c")
    blocks = piece.reshape(-1, 2, width)
    return lax.dynamic_index_in_dim(blocks, c, 1, keepdims=False).reshape(-1)


def bias_slot(piece, width):
    c = lax.axis_index("c")
    blocks = piece.reshape(-1, 1, width)
    pick = (jnp.arange(2) == c).astype(jnp.float32)[None, :, None]
    return (blocks * pick).reshape(-1)


def on_device_fast(
    tokens,
    cotangent,
    buckets,
    timesteps,
    labels,
    class_table,
    step_count,
    modulate_master,
    modulate_first,
    modulate_second,
    attend_master,
    attend_first,
    attend_second,
    project_master,
    project_first,
    project_second,
    expand_master,
    expand_first,
    expand_second,
    reduce_master,
    reduce_first,
    reduce_second,
    biases_master,
    biases_first,
    biases_second,
):
    z, x, c, y = place()
    bf16, f32 = jnp.bfloat16, jnp.float32
    block = FF // 16
    own = (
        chip_piece(attend_master.astype(bf16), HEAD_DIM),
        project_master.astype(bf16),
        chip_piece(expand_master.astype(bf16), block),
        reduce_master.astype(bf16),
    )
    weight_q, weight_p, weight_u, weight_d = gather_weights(own)
    weight_q = weight_q.reshape(2, D, 864)
    weight_p = weight_p.reshape(2, 576, 576)
    weight_u = weight_u.reshape(2, D, D)
    weight_d = weight_d.reshape(2, 2304, 576)

    class_row = lax.dynamic_slice_in_dim(class_table, labels[0], 1).astype(f32)
    condition = jax.nn.silu(class_row + time_features(timesteps, D)).astype(bf16).astype(f32)
    cond_tiles = jnp.pad(condition.reshape(16, 72), ((0, 0), (0, 56)))
    bias_low = biases_master.astype(bf16).astype(f32)
    modulation, cond_all = image_modulation(cond_tiles, modulate_master.astype(bf16))
    modulation = modulation.reshape(6 * D) + bias_low[: 6 * D]
    shift_one, scale_one, gating_one, shift_two, scale_two, gating_two = (
        modulation[i * D : (i + 1) * D][None, :] for i in range(6)
    )
    offset_base = 6 * D
    bias_query = core_bias(bias_low[offset_base : offset_base + D], HEAD_DIM)
    bias_value = core_bias(bias_low[offset_base + D : offset_base + 2 * D], HEAD_DIM)
    bias_proj = bias_low[offset_base + 2 * D : offset_base + 3 * D]
    bias_hidden = core_bias(bias_low[offset_base + 3 * D : offset_base + 3 * D + FF], block)
    bias_output = bias_low[offset_base + 3 * D + FF :]

    moved = swap_halves(jnp.stack([tokens, cotangent]))
    tokens, cotangent = moved[0], moved[1]
    bucket = swap_halves(buckets)
    unit_cells = SIDE // 8
    heights = table_pick(bucket, row_units) * unit_cells
    widths = table_pick(bucket, col_units) * unit_cells
    lengths = heights * widths
    half_rows = tokens.shape[0]
    position = c * half_rows + jnp.arange(half_rows, dtype=jnp.int32)
    live_rows = (position < lengths[0]).astype(f32)
    residual_zero = tokens.astype(f32) + grid_features(position, widths, D)

    hidden_attend = both_halves(modulate(residual_zero, shift_one, scale_one).astype(bf16))
    packed = wide(hidden_attend, weight_q)
    queries = (packed[:, :576] + bias_query).astype(bf16)
    key_rows = packed[:, 576:1152].astype(bf16)
    value_rows = (packed[:, 1152:] + bias_value).astype(bf16)
    attention, log_sums = attend(queries, key_rows, value_rows, lengths)
    branch_attend = sum_halves(wide(attention, weight_p)) + bias_proj
    residual_one = residual_zero + gating_one * branch_attend
    hidden_expand = both_halves(modulate(residual_one, shift_two, scale_two).astype(bf16))
    widened = wide(hidden_expand, weight_u) + bias_hidden
    activated = jax.nn.gelu(widened, approximate=True).astype(bf16)
    branch_expand = sum_halves(wide(activated, weight_d)) + bias_output
    output = swap_halves((residual_one + gating_two * branch_expand).astype(bf16))

    outer_grad = cotangent.astype(f32) * live_rows[:, None]
    gating_later = jnp.sum(outer_grad * branch_expand, axis=0)
    closing_grad = (outer_grad * gating_two).astype(bf16)
    closing_all = both_halves(closing_grad)
    active_grad = wide_back(closing_all, weight_d)
    _, gelu_pullback = jax.vjp(lambda inner: jax.nn.gelu(inner, approximate=True), widened)
    widened_grad = gelu_pullback(active_grad)[0].astype(bf16)
    grad_reduce = weight_grad(activated, closing_all, "d")
    grad_expand = weight_grad(hidden_expand, widened_grad, "u")
    hidden_grad = sum_halves(wide_back(widened_grad, weight_u))

    def norm_back(residual, scaling, gradient):
        average = jnp.mean(residual, axis=-1, keepdims=True)
        centred = residual - average
        inverse = lax.rsqrt(jnp.mean(centred * centred, axis=-1, keepdims=True) + 1e-06)
        normed = centred * inverse
        inner = gradient * (1.0 + scaling)
        part = (
            inner
            - jnp.mean(inner, axis=-1, keepdims=True)
            - normed * jnp.mean(inner * normed, axis=-1, keepdims=True)
        ) * inverse
        return part, jnp.sum(gradient, axis=0), jnp.sum(gradient * normed, axis=0)

    residual_part, shift_later, scale_later = norm_back(residual_one, scale_two, hidden_grad)
    middle_grad = outer_grad + residual_part
    gating_early = jnp.sum(middle_grad * branch_attend, axis=0)
    branch_grad = (middle_grad * gating_one).astype(bf16)
    branch_all = both_halves(branch_grad)
    heads_grad = wide_back(branch_all, weight_p).astype(bf16)
    grad_project = weight_grad(attention, branch_all, "p")
    query_grad, keyrow_grad, value_grad = attend_back(
        queries, key_rows, value_rows, heads_grad, log_sums, lengths
    )
    packed_grad = jnp.concatenate([query_grad, keyrow_grad, value_grad], axis=1)
    grad_attend = weight_grad(hidden_attend, packed_grad, "q")
    normed_grad = sum_halves(wide_back(packed_grad, weight_q))
    input_part, shift_early, scale_early = norm_back(residual_zero, scale_one, normed_grad)
    input_grad = swap_halves((middle_grad + input_part).astype(bf16)).astype(f32)

    mod_grad = jnp.concatenate(
        [shift_early, scale_early, gating_early, shift_later, scale_later, gating_later]
    )
    bias_share = jnp.concatenate(
        [
            bias_slot(jnp.sum(query_grad.astype(f32), axis=0), HEAD_DIM),
            bias_slot(jnp.sum(value_grad.astype(f32), axis=0), HEAD_DIM),
            jnp.sum(branch_grad.astype(f32), axis=0),
            bias_slot(jnp.sum(widened_grad.astype(f32), axis=0), block),
            jnp.sum(closing_grad.astype(f32), axis=0),
        ]
    )
    sums_q, sums_p, sums_u, sums_d = scatter_grads(
        (grad_attend, grad_project, grad_expand, grad_reduce)
    )
    mods, bias_sums = share_totals(mod_grad.reshape(16, 432), bias_share.reshape(72, 128))
    mods = mods.reshape(16, 2, 3456)
    grad_mod = lax.dot_general(
        cond_all[:, :72].astype(bf16),
        lax.dynamic_index_in_dim(mods, y, 1, keepdims=False),
        (((0,), (0,)), ((), ())),
        preferred_element_type=f32,
    )
    bias_total = jnp.concatenate([jnp.sum(mods.astype(f32), axis=0).reshape(-1), bias_sums.reshape(-1)])
    grad_attend = shard_from_pieces(sums_q, HEAD_DIM)
    grad_expand = shard_from_pieces(sums_u, block)
    reduced = (grad_mod, grad_attend, sums_p, grad_expand, sums_d)
    local_squares = sum(jnp.sum(gradient * gradient) for gradient in reduced)
    square_total = sum_everywhere(jnp.full((8, 128), local_squares))[0, 0]
    grad_norm = jnp.sqrt(square_total + jnp.sum(bias_total * bias_total))
    clip_factor = jnp.minimum(1.0, 1.0 / (grad_norm + 1e-06))
    correction = 1.0 - jnp.power(0.5, step_count.astype(f32))
    rate = 0.5 * D ** (-0.5)
    states = (
        (modulate_master, modulate_first, modulate_second, grad_mod, rate),
        (attend_master, attend_first, attend_second, grad_attend, rate),
        (project_master, project_first, project_second, sums_p, rate),
        (expand_master, expand_first, expand_second, grad_expand, rate),
        (reduce_master, reduce_first, reduce_second, sums_d, 0.5 * FF ** (-0.5)),
        (biases_master, biases_first, biases_second, bias_total, 0.1),
    )
    updates = []
    for master, first, second, gradient, learn_rate in states:
        updates += adam_update(
            master, first, second, gradient, learn_rate, clip_factor, correction
        )
    return (output, input_grad, grad_norm, *updates)


def fast_solution(mesh):
    return jax.shard_map(
        on_device_fast,
        mesh=mesh,
        in_specs=(
            P(("z", "x", "c", "y"), None),
            P(("z", "x", "c", "y"), None),
            P(("z", "x", "c")),
            P(("z", "x", "c")),
            P(("z", "x", "c")),
            P(),
            P(),
            P(("z", "x", "c"), "y"),
            P(("z", "x", "c"), "y"),
            P(("z", "x", "c"), "y"),
            P(("z", "x", "c"), "y"),
            P(("z", "x", "c"), "y"),
            P(("z", "x", "c"), "y"),
            P(("z", "x", "c"), "y"),
            P(("z", "x", "c"), "y"),
            P(("z", "x", "c"), "y"),
            P(("z", "x", "c"), "y"),
            P(("z", "x", "c"), "y"),
            P(("z", "x", "c"), "y"),
            P(("z", "x", "c"), "y"),
            P(("z", "x", "c"), "y"),
            P(("z", "x", "c"), "y"),
            P(),
            P(),
            P(),
        ),
        out_specs=(
            P(("z", "x", "c", "y"), None),
            P(("z", "x", "c", "y"), None),
            P(),
            P(("z", "x", "c"), "y"),
            P(("z", "x", "c"), "y"),
            P(("z", "x", "c"), "y"),
            P(("z", "x", "c"), "y"),
            P(("z", "x", "c"), "y"),
            P(("z", "x", "c"), "y"),
            P(("z", "x", "c"), "y"),
            P(("z", "x", "c"), "y"),
            P(("z", "x", "c"), "y"),
            P(("z", "x", "c"), "y"),
            P(("z", "x", "c"), "y"),
            P(("z", "x", "c"), "y"),
            P(("z", "x", "c"), "y"),
            P(("z", "x", "c"), "y"),
            P(("z", "x", "c"), "y"),
            P(),
            P(),
            P(),
        ),
        check_vma=False,
    )


def plain_solution(mesh):
    return jax.shard_map(
        on_device,
        mesh=mesh,
        in_specs=(
            P(("seq", "head"), None),
            P(("seq", "head"), None),
            P("seq"),
            P("seq"),
            P("seq"),
            P(),
            P(),
            P("seq", "head"),
            P("seq", "head"),
            P("seq", "head"),
            P("seq", "head"),
            P("seq", "head"),
            P("seq", "head"),
            P("seq", "head"),
            P("seq", "head"),
            P("seq", "head"),
            P("seq", "head"),
            P("seq", "head"),
            P("seq", "head"),
            P("seq", "head"),
            P("seq", "head"),
            P("seq", "head"),
            P(),
            P(),
            P(),
        ),
        out_specs=(
            P(("seq", "head"), None),
            P(("seq", "head"), None),
            P(),
            P("seq", "head"),
            P("seq", "head"),
            P("seq", "head"),
            P("seq", "head"),
            P("seq", "head"),
            P("seq", "head"),
            P("seq", "head"),
            P("seq", "head"),
            P("seq", "head"),
            P("seq", "head"),
            P("seq", "head"),
            P("seq", "head"),
            P("seq", "head"),
            P("seq", "head"),
            P("seq", "head"),
            P(),
            P(),
            P(),
        ),
        check_vma=False,
    )


def solution(mesh):
    if dict(mesh.shape) == {"seq": 16, "head": 2}:
        grid = Mesh(mesh.devices.reshape(4, 2, 2, 2), ("z", "x", "c", "y"))
        return fast_solution(grid)
    return plain_solution(mesh)
```

```python
import functools
import math

import jax
import jax.numpy as jnp
from jax import lax
from jax.experimental import pallas as pl
from jax.experimental.pallas import tpu as pltpu
from jax.sharding import Mesh
from jax.sharding import PartitionSpec as P

D = 1152
HEAD_DIM = 72
FF = 4608
SIDE = 32
LMAX = 1024


highest = lax.Precision.HIGHEST
row_units = (8, 4, 16, 6, 10, 7, 4, 6)
col_units = (8, 16, 4, 10, 6, 9, 8, 6)


def table_pick(indices, entries):
    matches = indices[..., None] == jnp.arange(len(entries), dtype=jnp.int32)
    return jnp.sum(jnp.where(matches, jnp.array(entries, jnp.int32), 0), axis=-1)


def layer_norm(value):
    average = jnp.mean(value, axis=-1, keepdims=True)
    centred = value - average
    spread = jnp.mean(centred * centred, axis=-1, keepdims=True)
    return centred * lax.rsqrt(spread + 1e-06)


def modulate(value, shift, scaling):
    return layer_norm(value) * (1.0 + scaling) + shift


def time_features(moments, width):
    half_width = width // 2
    frequency = jnp.exp(-math.log(10000.0) * jnp.arange(half_width, dtype=jnp.float32) / half_width)
    angles = moments.astype(jnp.float32)[:, None] * frequency[None, :]
    return jnp.concatenate([jnp.cos(angles), jnp.sin(angles)], axis=1)


def grid_features(position, row_wide, width):
    quarter = width // 4
    omegas = jnp.exp(-math.log(10000.0) * jnp.arange(quarter, dtype=jnp.float32) / quarter)
    row_angle = (position // row_wide).astype(jnp.float32)[:, None] * omegas[None, :]
    col_angle = (position % row_wide).astype(jnp.float32)[:, None] * omegas[None, :]
    return jnp.concatenate(
        [jnp.sin(row_angle), jnp.cos(row_angle), jnp.sin(col_angle), jnp.cos(col_angle)], axis=1
    )


def fold_rows(left_side, weight_slab):
    return jnp.dot(
        left_side,
        lax.all_gather(weight_slab, "seq", axis=0, tiled=True),
        preferred_element_type=jnp.float32,
    )


def back_cols(gradient, weight_slab):
    return lax.dot_general(
        gradient,
        lax.all_gather(weight_slab, "seq", axis=0, tiled=True),
        (((1,), (1,)), ((), ())),
        preferred_element_type=jnp.float32,
    )


def rows_seq(left_side, right_side):
    return lax.psum_scatter(
        lax.dot_general(
            left_side, right_side, (((0,), (0,)), ((), ())), preferred_element_type=jnp.float32
        ).astype(jnp.bfloat16),
        "seq",
        scatter_dimension=0,
        tiled=True,
    ).astype(jnp.float32)


def attend(queries, key_rows, value_rows, lengths):
    heads_here = queries.shape[1] // HEAD_DIM
    block_rows = min(512, LMAX)
    score_scale = HEAD_DIM ** (-0.5)
    image_count = lengths.shape[0]

    def per_image(packed):
        query_image, key_image, value_image, length = packed
        key_heads = key_image.reshape(LMAX, heads_here, HEAD_DIM)
        value_heads = value_image.reshape(LMAX, heads_here, HEAD_DIM)
        live_keys = jnp.arange(LMAX, dtype=jnp.int32) < length

        def per_block(query_block):
            scores = (
                jnp.einsum(
                    "qhe,khe->hqk", query_block, key_heads, preferred_element_type=jnp.float32
                )
                * score_scale
            )
            scores = jnp.where(live_keys[None, None, :], scores, -1e30)
            maximum = jnp.max(scores, axis=-1, keepdims=True)
            weights = jnp.exp(scores - maximum)
            totals = jnp.sum(weights, axis=-1, keepdims=True)
            probability = (weights / totals).astype(jnp.bfloat16)
            result = jnp.einsum(
                "hqk,khe->qhe", probability, value_heads, preferred_element_type=jnp.float32
            )
            return (result.astype(jnp.bfloat16), (maximum + jnp.log(totals))[:, :, 0])

        blocks = query_image.reshape(LMAX // block_rows, block_rows, heads_here, HEAD_DIM)
        result, log_sums = lax.map(per_block, blocks)
        return (result.reshape(LMAX, heads_here * HEAD_DIM), log_sums)

    stacked = (
        queries.reshape(image_count, LMAX, -1),
        key_rows.reshape(image_count, LMAX, -1),
        value_rows.reshape(image_count, LMAX, -1),
        lengths,
    )
    result, log_sums = lax.map(per_image, stacked)
    return (result.reshape(image_count * LMAX, -1), log_sums)


def attend_back(queries, key_rows, value_rows, grad_rows, log_sums, lengths):
    heads_here = queries.shape[1] // HEAD_DIM
    block_rows = min(512, LMAX)
    score_scale = HEAD_DIM ** (-0.5)
    image_count = lengths.shape[0]

    def per_image(packed):
        query_image, key_image, value_image, grad_image, logsum_image, length = packed
        key_heads = key_image.reshape(LMAX, heads_here, HEAD_DIM)
        value_heads = value_image.reshape(LMAX, heads_here, HEAD_DIM)
        live_keys = jnp.arange(LMAX, dtype=jnp.int32) < length

        def per_block(running, inputs):
            key_grad, value_grad = running
            query_block, grad_block, logsum_block = inputs
            scores = (
                jnp.einsum(
                    "qhe,khe->hqk", query_block, key_heads, preferred_element_type=jnp.float32
                )
                * score_scale
            )
            scores = jnp.where(live_keys[None, None, :], scores, -1e30)
            probability = jnp.exp(scores - logsum_block[:, :, None])
            grad_prob = jnp.einsum(
                "qhe,khe->hqk", grad_block, value_heads, preferred_element_type=jnp.float32
            )
            inner_sum = jnp.sum(probability * grad_prob, axis=-1, keepdims=True)
            grad_score = (probability * (grad_prob - inner_sum)).astype(jnp.bfloat16)
            query_grad = (
                jnp.einsum(
                    "hqk,khe->qhe", grad_score, key_heads, preferred_element_type=jnp.float32
                )
                * score_scale
            )
            key_grad = (
                key_grad
                + jnp.einsum(
                    "hqk,qhe->khe", grad_score, query_block, preferred_element_type=jnp.float32
                )
                * score_scale
            )
            value_grad = value_grad + jnp.einsum(
                "hqk,qhe->khe",
                probability.astype(jnp.bfloat16),
                grad_block,
                preferred_element_type=jnp.float32,
            )
            return ((key_grad, value_grad), query_grad.astype(jnp.bfloat16))

        initial = (
            jnp.zeros((LMAX, heads_here, HEAD_DIM), jnp.float32),
            jnp.zeros((LMAX, heads_here, HEAD_DIM), jnp.float32),
        )
        blocks = (
            query_image.reshape(LMAX // block_rows, block_rows, heads_here, HEAD_DIM),
            grad_image.reshape(LMAX // block_rows, block_rows, heads_here, HEAD_DIM),
            logsum_image,
        )
        (key_grad, value_grad), query_grad = lax.scan(per_block, initial, blocks)
        return (
            query_grad.reshape(LMAX, -1),
            key_grad.reshape(LMAX, -1).astype(jnp.bfloat16),
            value_grad.reshape(LMAX, -1).astype(jnp.bfloat16),
        )

    stacked = (
        queries.reshape(image_count, LMAX, -1),
        key_rows.reshape(image_count, LMAX, -1),
        value_rows.reshape(image_count, LMAX, -1),
        grad_rows.reshape(image_count, LMAX, -1),
        log_sums,
        lengths,
    )
    query_grad, key_grad, value_grad = lax.map(per_image, stacked)
    return (
        query_grad.reshape(image_count * LMAX, -1),
        key_grad.reshape(image_count * LMAX, -1),
        value_grad.reshape(image_count * LMAX, -1),
    )


def adam_update(master, first_moment, second_moment, gradient, learn_rate, clip_factor, correction):
    clipped = gradient * clip_factor
    first_new = 0.5 * first_moment + 0.5 * clipped
    second_new = 0.5 * second_moment + 0.5 * clipped * clipped
    direction = first_new / correction / (jnp.sqrt(second_new / correction) + 1e-08)
    return (master - learn_rate * (direction + 0.1 * master), first_new, second_new)


def on_device(
    tokens,
    cotangent,
    buckets,
    timesteps,
    labels,
    class_table,
    step_count,
    modulate_master,
    modulate_first,
    modulate_second,
    attend_master,
    attend_first,
    attend_second,
    project_master,
    project_first,
    project_second,
    expand_master,
    expand_first,
    expand_second,
    reduce_master,
    reduce_first,
    reduce_second,
    biases_master,
    biases_first,
    biases_second,
):
    head_index = lax.axis_index("head")
    head_count = lax.axis_size("head")
    tok_rows = tokens.shape[0]
    image_count = buckets.shape[0]
    unit_cells = SIDE // 8
    heights = table_pick(buckets, row_units) * unit_cells
    widths = table_pick(buckets, col_units) * unit_cells
    lengths = heights * widths
    row_index = head_index * tok_rows + jnp.arange(tok_rows, dtype=jnp.int32)
    image_of = row_index // LMAX
    position = row_index % LMAX
    choose = image_of[:, None] == jnp.arange(image_count, dtype=jnp.int32)[None, :]
    pick_rows = choose.astype(jnp.float32)
    row_wide = jnp.sum(jnp.where(choose, widths[None, :], 0), axis=1)
    row_length = jnp.sum(jnp.where(choose, lengths[None, :], 0), axis=1)
    live_rows = (position < row_length).astype(jnp.float32)
    grid_cells = grid_features(position, row_wide, D)
    class_pick = (
        labels[:, None] == jnp.arange(class_table.shape[0], dtype=jnp.int32)[None, :]
    ).astype(jnp.bfloat16)
    class_rows = jnp.dot(class_pick, class_table, preferred_element_type=jnp.float32)
    condition = jax.nn.silu(class_rows + time_features(timesteps, D)).astype(jnp.bfloat16)
    bias_low = biases_master.astype(jnp.bfloat16).astype(jnp.float32)
    offset_base = 6 * D
    bias_query = bias_low[offset_base : offset_base + D]
    bias_value = bias_low[offset_base + D : offset_base + 2 * D]
    bias_proj = bias_low[offset_base + 2 * D : offset_base + 3 * D]
    bias_hidden = bias_low[offset_base + 3 * D : offset_base + 3 * D + FF]
    bias_output = bias_low[offset_base + 3 * D + FF :]
    head_slabs = (
        lax.all_gather(attend_master.astype(jnp.bfloat16), "head", axis=1, tiled=True),
        lax.all_gather(project_master.astype(jnp.bfloat16), "head", axis=1, tiled=True),
        lax.all_gather(expand_master.astype(jnp.bfloat16), "head", axis=1, tiled=True),
        lax.all_gather(reduce_master.astype(jnp.bfloat16), "head", axis=1, tiled=True),
    )
    attend_slab, project_slab, expand_slab, reduce_slab = head_slabs
    mod_width = 6 * D // head_count
    mod_share = fold_rows(condition, modulate_master.astype(jnp.bfloat16))
    mod_share = mod_share + lax.dynamic_slice_in_dim(bias_low, head_index * mod_width, mod_width)
    modulation = lax.all_gather(mod_share, "head", axis=1, tiled=True)
    mod_rows = jnp.dot(pick_rows, modulation, precision=highest)
    shift_one, scale_one, gating_one, shift_two, scale_two, gating_two = jnp.split(
        mod_rows, 6, axis=1
    )
    residual_zero = tokens.astype(jnp.float32) + grid_cells
    hidden_attend = modulate(residual_zero, shift_one, scale_one).astype(jnp.bfloat16)
    packed = fold_rows(hidden_attend, attend_slab)
    queries = (packed[:, :D] + bias_query).astype(jnp.bfloat16)
    key_rows = packed[:, D : 2 * D].astype(jnp.bfloat16)
    value_rows = (packed[:, 2 * D :] + bias_value).astype(jnp.bfloat16)
    query_heads, key_heads, value_heads = (
        lax.all_to_all(queries, "head", split_axis=1, concat_axis=0, tiled=True),
        lax.all_to_all(key_rows, "head", split_axis=1, concat_axis=0, tiled=True),
        lax.all_to_all(value_rows, "head", split_axis=1, concat_axis=0, tiled=True),
    )
    head_out, log_sums = attend(query_heads, key_heads, value_heads, lengths)
    attention = lax.all_to_all(head_out, "head", split_axis=0, concat_axis=1, tiled=True)
    branch_attend = fold_rows(attention, project_slab) + bias_proj
    residual_one = residual_zero + gating_one * branch_attend
    hidden_expand = modulate(residual_one, shift_two, scale_two).astype(jnp.bfloat16)
    widened = fold_rows(hidden_expand, expand_slab) + bias_hidden
    activated = jax.nn.gelu(widened, approximate=True).astype(jnp.bfloat16)
    branch_expand = fold_rows(activated, reduce_slab) + bias_output
    output = (residual_one + gating_two * branch_expand).astype(jnp.bfloat16)
    outer_grad = cotangent.astype(jnp.float32) * live_rows[:, None]
    gating_later = outer_grad * branch_expand
    closing_grad = (outer_grad * gating_two).astype(jnp.bfloat16)
    active_grad = back_cols(closing_grad, reduce_slab)
    gelu_value, gelu_pullback = jax.vjp(lambda inner: jax.nn.gelu(inner, approximate=True), widened)
    widened_grad = gelu_pullback(active_grad)[0].astype(jnp.bfloat16)
    hidden_grad = back_cols(widened_grad, expand_slab)
    later_value, later_pullback = jax.vjp(modulate, residual_one, shift_two, scale_two)
    residual_part, shift_later, scale_later = later_pullback(hidden_grad)
    middle_grad = outer_grad + residual_part
    gating_early = middle_grad * branch_attend
    branch_grad = (middle_grad * gating_one).astype(jnp.bfloat16)
    attend_grad = back_cols(branch_grad, project_slab).astype(jnp.bfloat16)
    heads_grad = lax.all_to_all(attend_grad, "head", split_axis=1, concat_axis=0, tiled=True)
    query_grad, keyrow_grad, value_grad = attend_back(
        query_heads, key_heads, value_heads, heads_grad, log_sums, lengths
    )
    query_back, keys_back, values_back = (
        lax.all_to_all(query_grad, "head", split_axis=0, concat_axis=1, tiled=True),
        lax.all_to_all(keyrow_grad, "head", split_axis=0, concat_axis=1, tiled=True),
        lax.all_to_all(value_grad, "head", split_axis=0, concat_axis=1, tiled=True),
    )
    packed_grad = jnp.concatenate([query_back, keys_back, values_back], axis=1)
    normed_grad = back_cols(packed_grad, attend_slab)
    early_value, early_pullback = jax.vjp(modulate, residual_zero, shift_one, scale_one)
    input_part, shift_early, scale_early = early_pullback(normed_grad)
    input_grad = middle_grad + input_part
    mod_token_grad = jnp.concatenate(
        [shift_early, scale_early, gating_early, shift_later, scale_later, gating_later], axis=1
    )
    mod_grad = lax.dot_general(
        pick_rows, mod_token_grad, (((0,), (0,)), ((), ())), precision=highest
    )
    mod_summed = lax.psum_scatter(mod_grad, "head", scatter_dimension=1, tiled=True)
    mod_rounded = mod_summed.astype(jnp.bfloat16)
    grad_mod = rows_seq(condition, mod_rounded)
    mod_slot = lax.dynamic_update_slice_in_dim(
        jnp.zeros((6 * D,), jnp.float32),
        jnp.sum(mod_rounded.astype(jnp.float32), axis=0),
        head_index * mod_width,
        0,
    )
    bias_share = jnp.concatenate(
        [
            mod_slot,
            jnp.sum(query_back.astype(jnp.float32), axis=0),
            jnp.sum(values_back.astype(jnp.float32), axis=0),
            jnp.sum(branch_grad.astype(jnp.float32), axis=0),
            jnp.sum(widened_grad.astype(jnp.float32), axis=0),
            jnp.sum(closing_grad.astype(jnp.float32), axis=0),
        ]
    )
    operand_pairs = (
        (hidden_attend, packed_grad),
        (attention, branch_grad),
        (hidden_expand, widened_grad),
        (activated, closing_grad),
    )
    term_slabs = tuple((rows_seq(left_side, right_side) for left_side, right_side in operand_pairs))
    reduced = (
        lax.psum_scatter(
            term_slabs[0].astype(jnp.bfloat16), "head", scatter_dimension=1, tiled=True
        ).astype(jnp.float32),
        lax.psum_scatter(
            term_slabs[1].astype(jnp.bfloat16), "head", scatter_dimension=1, tiled=True
        ).astype(jnp.float32),
        lax.psum_scatter(
            term_slabs[2].astype(jnp.bfloat16), "head", scatter_dimension=1, tiled=True
        ).astype(jnp.float32),
        lax.psum_scatter(
            term_slabs[3].astype(jnp.bfloat16), "head", scatter_dimension=1, tiled=True
        ).astype(jnp.float32),
    )
    grad_attend, grad_project, grad_expand, grad_reduce = reduced
    local_squares = jnp.sum(grad_mod * grad_mod) + sum(
        (jnp.sum(gradient * gradient) for gradient in reduced)
    )
    bias_total, square_total = lax.psum((bias_share, local_squares), ("seq", "head"))
    grad_norm = jnp.sqrt(square_total + jnp.sum(bias_total * bias_total))
    clip_factor = jnp.minimum(1.0, 1.0 / (grad_norm + 1e-06))
    correction = 1.0 - jnp.power(0.5, step_count.astype(jnp.float32))
    modulate_new = adam_update(
        modulate_master,
        modulate_first,
        modulate_second,
        grad_mod,
        0.5 * D ** (-0.5),
        clip_factor,
        correction,
    )
    attend_new = adam_update(
        attend_master,
        attend_first,
        attend_second,
        grad_attend,
        0.5 * D ** (-0.5),
        clip_factor,
        correction,
    )
    project_new = adam_update(
        project_master,
        project_first,
        project_second,
        grad_project,
        0.5 * D ** (-0.5),
        clip_factor,
        correction,
    )
    expand_new = adam_update(
        expand_master,
        expand_first,
        expand_second,
        grad_expand,
        0.5 * D ** (-0.5),
        clip_factor,
        correction,
    )
    reduce_new = adam_update(
        reduce_master,
        reduce_first,
        reduce_second,
        grad_reduce,
        0.5 * FF ** (-0.5),
        clip_factor,
        correction,
    )
    biases_new = adam_update(
        biases_master, biases_first, biases_second, bias_total, 0.1, clip_factor, correction
    )
    return (
        output,
        input_grad,
        grad_norm,
        modulate_new[0],
        modulate_new[1],
        modulate_new[2],
        attend_new[0],
        attend_new[1],
        attend_new[2],
        project_new[0],
        project_new[1],
        project_new[2],
        expand_new[0],
        expand_new[1],
        expand_new[2],
        reduce_new[0],
        reduce_new[1],
        reduce_new[2],
        biases_new[0],
        biases_new[1],
        biases_new[2],
    )


ALPHA = HEAD_DIM ** (-0.5) * math.log2(math.e)
GELU_A = math.sqrt(2.0 / math.pi)
GELU_B = 0.044715
BLOCK = FF // 16
BF, F32 = jnp.bfloat16, jnp.float32
ANY, VM = pl.ANY, pltpu.VMEM
PIECES = {"q": (144, 864, 48), "p": (72, 576, None), "u": (144, 1152, 48), "d": (288, 576, 96)}
NAMES = ("q", "p", "u", "d")
MESH = pl.DeviceIdType.MESH


def place():
    return tuple(lax.axis_index(a) for a in ("z", "x", "c", "y"))


def at_z(k):
    z = lax.axis_index("z")
    return (z, z + 1 - 2 * (z % 2), (z + 2) % 4, 3 - z)[k]


def rdma(src, dst, send, recv, to):
    return pltpu.make_async_remote_copy(
        src_ref=src, dst_ref=dst, send_sem=send, recv_sem=recv, device_id=to, device_id_type=MESH
    )


def partners():
    z, x, c, y = place()
    xn, yn, twin = (z, 1 - x, c, y), (z, x, c, 1 - y), (z, x, 1 - c, y)
    return xn, yn, twin, [(at_z(k), x, c, y) for k in range(4)]


def greet(others, swapped=False):
    z, x, c, y = place()
    barrier = pltpu.get_barrier_semaphore()
    for to in others:
        pl.semaphore_signal(barrier, inc=1, device_id=to, device_id_type=MESH)
    if swapped:

        @pl.when(c != y)
        def _():
            pl.semaphore_signal(barrier, inc=1, device_id=(z, x, y, c), device_id_type=MESH)

        pl.semaphore_wait(barrier, len(others) + (c + y) % 2)
    else:
        pl.semaphore_wait(barrier, len(others))


CHUNKS = (
    (0, 0, 80, 32),
    (0, 80, 64, 16),
    (1, 0, 72, None),
    (2, 0, 80, 32),
    (2, 80, 64, 16),
    (3, 0, 144, 48),
    (3, 144, 144, 48),
)


def parts_of(chunk, k):
    _, _, rows, cut = CHUNKS[chunk]
    if cut is None:
        return ((0, rows), None) if k == 0 else (None, (0, rows))
    return (0, cut), (cut, rows - cut)


def piece_at(full, w, y, zk, x, first, count):
    rows = PIECES[NAMES[w]][0]
    if count == 72:
        return full.at[y, zk * 2 + x]
    return full.at[y, pl.ds(pl.multiple_of((zk * 2 + x) * rows + first, 16), count)]


def matmul(left, right):
    return jnp.dot(left, right, preferred_element_type=F32)


def matmul_nt(left, right):
    return lax.dot_general(left, right, (((1,), (1,)), ((), ())), preferred_element_type=F32)


def matmul_tn(left, right):
    return lax.dot_general(left, right, (((0,), (0,)), ((), ())), preferred_element_type=F32)


class Gather:
    def __init__(self, own, full, sems):
        self.own, self.full = own, full
        self.zs, self.zr, self.xs, self.xr, self.ys, self.yr, self.fs, self.fr, self.ps, self.pr = sems
        self.sent = []

    def piece(self, w, flip_y, k, flip_x):
        z, x, c, y = place()
        weight, first, count, _ = CHUNKS[w]
        return piece_at(
            self.full[weight], weight, 1 - y if flip_y else y, at_z(k), 1 - x if flip_x else x, first, count
        )

    def source(self, w):
        weight, first, count, _ = CHUNKS[w]
        return self.own[weight].at[pl.ds(first, count)]

    def send(self, make):
        make().start()
        self.sent.append(make)

    def arrived(self, ref, s, r):
        rdma(ref, ref, s, r, partners()[0]).wait_recv()

    def start(self, w):
        def to_x():
            return rdma(self.source(w), self.piece(w, 0, 0, 0), self.xs.at[w, 0], self.xr.at[w, 0], partners()[0])

        def to_y():
            return rdma(self.source(w), self.piece(w, 0, 0, 0), self.ys.at[w, 0], self.yr.at[w, 0], partners()[1])

        def to_z(k):
            to = partners()[3][k]
            return rdma(self.source(w), self.piece(w, 0, 0, 0), self.zs.at[w, k], self.zr.at[w, k], to)

        self.send(to_x)
        self.send(to_y)
        for k in (1, 2, 3):
            self.send(functools.partial(to_z, k))

    def column(self, w, k):
        self.arrived(self.piece(w, 0, k, 0), self.zs.at[w, k], self.zr.at[w, k])

        def to_x():
            piece = self.piece(w, 0, k, 0)
            return rdma(piece, piece, self.xs.at[w, k], self.xr.at[w, k], partners()[0])

        def to_y():
            piece = self.piece(w, 0, k, 0)
            return rdma(piece, piece, self.ys.at[w, k], self.yr.at[w, k], partners()[1])

        self.send(to_x)
        self.send(to_y)

    def plane(self, w, k):
        spans = parts_of(w, k)

        def pass_on(i):
            part = self.piece(w, i, k, 1 - i).at[pl.ds(*spans[i])]
            return rdma(part, part, self.fs.at[w, k, i], self.fr.at[w, k, i], partners()[1 - i])

        self.arrived(self.piece(w, 0, k, 1), self.xs.at[w, k], self.xr.at[w, k])
        if k in (0, 2) and spans[0] is not None:
            self.send(functools.partial(pass_on, 0))
        self.arrived(self.piece(w, 1, k, 0), self.ys.at[w, k], self.yr.at[w, k])
        if k in (0, 2) and spans[1] is not None:
            self.send(functools.partial(pass_on, 1))

    def corner(self, w, k):
        for i, span in enumerate(parts_of(w, k)):
            if span is not None:
                part = self.piece(w, 1, k, 1).at[pl.ds(*span)]
                self.arrived(part, self.fs.at[w, k, i], self.fr.at[w, k, i])

        def to_pair():
            piece = self.piece(w, 1, k, 1)
            return rdma(piece, piece, self.ps.at[w, k], self.pr.at[w, k], partners()[3][1])

        self.send(to_pair)

    def last(self, w, k):
        self.arrived(self.piece(w, 1, k ^ 1, 1), self.ps.at[w, k], self.pr.at[w, k])

    def finish(self):
        for make in self.sent:
            make().wait_send()

    def steps(self):
        def each(method, chunks, ks):
            return [(method, i, k) for i in chunks for k in ks]

        column, plane, corner, last = self.column, self.plane, self.corner, self.last
        one = (0, 1)
        plan = [(self.start, 0), (self.start, 1), (self.start, 2)]
        plan += each(column, one, (1,)) + each(plane, one, (0,))
        plan += each(column, one, (2,)) + each(column, one, (3,)) + [(self.start, 3)]
        plan += each(corner, one, (0,)) + each(plane, one, (2,))
        plan += each(column, (2,), (1,)) + [(self.start, 4)]
        plan += each(plane, one, (1,)) + each(corner, one, (2,))
        plan += each(plane, (2,), (0,)) + each(column, (2,), (2, 3)) + each(column, (3,), (1,))
        plan += each(plane, one, (3,)) + each(last, one, (0, 2))
        count = len(CHUNKS)
        for t in range(-2, count + 4):
            wave = [(self.start, t + 2)] if t + 2 < count else []
            for lag, make in enumerate(
                (
                    lambda i: each(column, (i,), (1,)),
                    lambda i: each(plane, (i,), (0,)) + each(column, (i,), (2, 3)),
                    lambda i: each(corner, (i,), (0,)) + each(plane, (i,), (2, 1)),
                    lambda i: each(corner, (i,), (2,)) + each(plane, (i,), (3,)),
                    lambda i: each(last, (i,), (0, 2)),
                )
            ):
                if t >= 0 and 0 <= t - lag < count:
                    wave += make(t - lag)
            plan += [step for step in wave if step not in plan]
        return plan


def mod_steps(cond_ref, weight, bias, out_ref, lhs, bufs, s, r):
    conds, part, got_z, mid, got_x, near, got_c = bufs

    def hop(i):
        z, x, c, y = place()
        xn, yn, twin, zn = partners()
        if i == 0:
            pairs = [(conds.at[z, x, c], conds.at[z, x, c], twin)]
        elif i == 1:
            pairs = [(conds.at[z, x], conds.at[z, x], xn)]
        elif i == 2:
            pairs = [(conds.at[z], conds.at[z], zn[k]) for k in (1, 2, 3)]
        elif i == 3:
            pairs = [(part.at[at_z(k)], got_z.at[k - 1], zn[k]) for k in (1, 2, 3)]
        elif i == 4:
            pairs = [(mid.at[1 - x], got_x, xn)]
        elif i == 5:
            pairs = [(near.at[0], got_c, twin)]
        else:
            pairs = [(near.at[1, 1 - y], near.at[2, y], yn)]
        return [
            rdma(src, dst, s.at[i, n], r.at[i, n], to) for n, (src, dst, to) in enumerate(pairs)
        ]

    def go(i):
        for d in hop(i):
            d.start()

    def end(i):
        for d in hop(i):
            d.wait()

    def step(i):
        z, x, c, y = place()
        if i > 0:
            end(i - 1)
        if i == 0:
            conds[z, x, c] = cond_ref[...]
        elif i == 3:
            me = (z * 2 + x) * 2 + c
            for n in range(16):
                lhs[pl.ds(n, 1), :] = conds[n // 4, n // 2 % 2, n % 2, pl.ds(me, 1), :]
            for j in range(3):
                cols = slice(j * D, (j + 1) * D)
                result = matmul(lhs[:, :72].astype(BF), weight[:, cols].astype(BF))
                for n in range(16):
                    part[n // 4, n // 2 % 2, n % 2, :, cols] = result[n : n + 1]
        elif i == 4:
            mid[...] = part[z] + got_z[0] + got_z[1] + got_z[2]
        elif i == 5:
            near[0] = mid[x] + got_x[...]
        elif i == 6:
            near[1] = near[0] + got_c[...]
            near[2, y] = near[1, y]
        if i < 7:
            go(i)
        else:
            for n in range(2):
                out_ref[n] = near[2, n] + bias[:, n * 3456 : (n + 1) * 3456]

    return [functools.partial(step, i) for i in range(8)]


def normed_tile(value):
    average = jnp.mean(value, axis=-1, keepdims=True)
    centred = value - average
    spread = jnp.mean(centred * centred, axis=-1, keepdims=True)
    return centred * lax.rsqrt(spread + 1e-06)


def rounded(value):
    return value.astype(BF).astype(F32)


def pick(bucket, entries):
    return sum(
        jnp.where(bucket == float(i), float(e * (SIDE // 8)), 0.0) for i, e in enumerate(entries)
    )


def start_rows(tok, table, bucket, first, rows):
    wide = pick(bucket, col_units)
    spot = (first + lax.broadcasted_iota(jnp.int32, (rows, 1), 0)).astype(F32)
    lane = lax.broadcasted_iota(jnp.int32, (1, 64), 1).astype(F32)
    grid_row = jnp.where((spot >= lane * wide) & (spot < (lane + 1.0) * wide), 1.0, 0.0)
    left = spot - wide * jnp.sum(grid_row * lane, axis=1, keepdims=True)
    grid_col = jnp.where(left == lane, 1.0, 0.0)
    high = table.astype(BF)
    low = (table - high.astype(F32)).astype(BF)
    parts = [matmul(hot.astype(BF), high) + matmul(hot.astype(BF), low) for hot in (grid_row, grid_col)]
    return tok.astype(F32) + jnp.concatenate(parts, axis=1)


def forward_kernel(*refs):
    (tok, cot, bucket_in, table, att_m, proj_m, exp_m, red_m, mod_w, cond_in, bias_in) = refs[:11]
    gq, gp, gu, gd = full = refs[11:15]
    (mod_out, lhs, x0_out, dy_out, cl_out, h1_out, q_out, k_out, v_out) = refs[15:24]
    (attnt_out, lse_out, ba_out, x1_out, h2_out, act_out, der_out, bb_out, y_out, gred_out) = refs[24:34]
    (oq, op, ou, od, fq, tq, fu, tu) = refs[34:42]
    mod_bufs = refs[42:49]
    (xs, x0, dy, bucket, closing, h1, qa, ka, vt, attnt, attn) = refs[49:60]
    (ps, pr, ds, dr, acc, x1, h2, act, der, ba, bb, yo, gstage) = refs[60:73]
    (b_all, b_q, b_v, b_u) = refs[73:77]
    lsem = refs[77]
    gather_sems = refs[78:88]
    ms, mr, ws, wr, ts, tr, os, outs_sem, gsem = refs[88:97]
    z, x, c, y = place()
    xn, yn, twin, zn = partners()
    half = x0.shape[0]
    mine = pl.multiple_of(c * half, half)
    other = pl.multiple_of((1 - c) * half, half)
    gather = Gather((oq, op, ou, od), full, gather_sems)
    mods = mod_steps(cond_in, mod_w, b_all, mod_out, lhs, mod_bufs, ms, mr)
    greet([xn, yn, twin] + zn[1:], swapped=True)
    mods[0]()

    def split(master, width, f, t, i):
        count = master.shape[1] // (2 * width)
        sides = [
            jnp.concatenate(
                [master[:, (2 * j + p) * width : (2 * j + p + 1) * width] for j in range(count)], axis=1
            )
            for p in (0, 1)
        ]
        t[...] = jnp.where(c == 0, sides[1], sides[0])
        rdma(t, f.at[c], os.at[0, i], os.at[1, i], twin).start()
        f[c] = jnp.where(c == 0, sides[0], sides[1])

    def joined(f, t, i, piece):
        rdma(t, f.at[c], os.at[0, i], os.at[1, i], twin).wait()
        piece[...] = jnp.concatenate([f[0], f[1]], axis=0).astype(BF)

    split(att_m, HEAD_DIM, fq, tq, 0)
    mods[1]()
    split(exp_m, BLOCK, fu, tu, 1)
    mods[2]()
    joined(fq, tq, 0, oq)
    steps = gather.steps()
    done = [2]
    gather.start(0)
    gather.start(1)

    swap_to = (z, x, y, c)
    PART = 128
    moves = [(bucket_in, bucket)]
    for i in range(half // PART):
        moves.append((xs.at[pl.ds(i * PART, PART)], x0.at[pl.ds(i * PART, PART)]))
    for i in range(half // PART):
        moves.append((cot.at[pl.ds(i * PART, PART)], dy.at[pl.ds(i * PART, PART)]))

    def move(i):
        @pl.when(c != y)
        def _():
            rdma(*moves[i], ws.at[i], wr.at[i], swap_to).start()

        @pl.when(c == y)
        def _():
            pltpu.make_async_copy(*moves[i], ws.at[i]).start()

    def moved(i):
        @pl.when(c != y)
        def _():
            rdma(*moves[i], ws.at[i], wr.at[i], swap_to).wait()

        @pl.when(c == y)
        def _():
            pltpu.make_async_copy(*moves[i], ws.at[i]).wait()

    move(0)
    for i in range(half // PART):
        rows = slice(i * PART, (i + 1) * PART)
        xs[rows, :] = start_rows(
            tok[rows, :], table[...], bucket_in[0:1, 0:1], y * half + i * PART, PART
        ).astype(BF)
        move(1 + i)
    mods[3]()
    joined(fu, tu, 1, ou)
    op[...] = proj_m[...].astype(BF)
    od[...] = red_m[...].astype(BF)
    owns = [
        pltpu.make_async_copy(
            gather.own[w], piece_at(full[w], w, y, z, x, 0, PIECES[NAMES[w]][0]), lsem.at[w]
        )
        for w in range(4)
    ]
    for d in owns:
        d.start()
    b_all[...] = rounded(bias_in[...])

    def of_core(base, width, count):
        return jnp.concatenate(
            [
                jnp.where(
                    c == 0,
                    b_all[:, base + 2 * j * width : base + (2 * j + 1) * width],
                    b_all[:, base + (2 * j + 1) * width : base + (2 * j + 2) * width],
                )
                for j in range(count)
            ],
            axis=1,
        )

    b_q[...] = of_core(6 * D, HEAD_DIM, 8)
    b_v[...] = of_core(7 * D, HEAD_DIM, 8)
    b_u[...] = of_core(9 * D, BLOCK, 8)
    b_p = b_all.at[:, pl.ds(8 * D, D)]
    b_d = b_all.at[:, pl.ds(9 * D + FF, D)]

    def tick(n):
        for f, *a in steps[done[0] : done[0] + n]:
            f(*a)
        done[0] = min(done[0] + n, len(steps))

    def tick_until(chunk):
        last = max(i for i, s in enumerate(steps) if s[0] == gather.last and s[1] == chunk)
        tick(max(0, last + 1 - done[0]))

    tick(3)
    mods[4]()
    tick(3)
    mods[5]()
    tick(2)
    mods[6]()
    tick(2)
    mods[7]()
    for i in range(1 + half // PART):
        moved(i)

    def vec(i):
        return mod_out[i // 3, :, (i % 3) * D : (i % 3 + 1) * D]

    TILE, WIDE = 128, 256
    tiles = half // TILE

    def own_tile(ref, t):
        return ref.at[pl.ds(pl.multiple_of(mine + t * TILE, TILE), TILE)]

    def give(ref, t, i):
        part = own_tile(ref, t)
        return rdma(part, part, ts.at[i, t], tr.at[i, t], twin)

    def norm_one(t, _):
        rows = pl.ds(pl.multiple_of(t * TILE, TILE), TILE)
        value = normed_tile(x0[rows, :].astype(F32)) * (1.0 + vec(1)) + vec(0)
        own_tile(h1, t)[...] = value.astype(BF)
        give(h1, t, 0).start()
        return 0

    for t in range(tiles):
        norm_one(t, 0)
        tick(1)
    tick_until(1)
    for i in range(half // PART):
        move(1 + half // PART + i)

    def both_got(ref, i):
        for t in range(tiles):
            give(ref, t, i).wait_send()
            part = ref.at[pl.ds(pl.multiple_of(other + t * TILE, TILE), TILE)]
            rdma(part, part, ts.at[i, t], tr.at[i, t], twin).wait_recv()

    out_copies = []

    def put(src, dst):
        d = pltpu.make_async_copy(src, dst, outs_sem.at[len(out_copies)])
        d.start()
        out_copies.append(d)

    def load(src, dst, i):
        d = pltpu.make_async_copy(src, dst, lsem.at[i])
        d.start()
        d.wait()

    owns[0].wait()
    live = pick(bucket[0:1, 0:1], row_units) * pick(bucket[0:1, 0:1], col_units)
    lane = lax.broadcasted_iota(jnp.int32, (1, 128), 1)

    def qkv(weight):
        load(gq, weight, 4)

        def rows_of(i, _):
            start = pl.multiple_of(i * 256, 256)
            rows = pl.ds(start, 256)
            left = h1[rows, :]
            one = matmul(left, weight[0])
            two = matmul(left, weight[1])
            spot = (start + lax.broadcasted_iota(jnp.int32, (256, 1), 0)).astype(F32)
            mask = jnp.where(lane == HEAD_DIM, jnp.where(spot < live, 0.0, -1e30), 0.0)
            ones = jnp.where(lane == HEAD_DIM, 1.0, 0.0)
            for j in range(8):
                cols = slice(j * HEAD_DIM, (j + 1) * HEAD_DIM)
                query = one[:, cols] + b_q[:, cols]
                key = one[:, 576 + j * 72 : 648 + j * 72] if j < 4 else two[:, j * 72 - 288 : j * 72 - 216]
                value = two[:, 288 + j * 72 : 360 + j * 72] + b_v[:, cols]
                fill = jnp.zeros((256, 56), F32)
                qa[j, rows, :] = (jnp.concatenate([query, fill], axis=1) + ones).astype(BF)
                ka[j, rows, :] = (jnp.concatenate([key, fill], axis=1) + mask).astype(BF)
                vt[j, :, rows] = value.T.astype(BF)
            return 0

        rows_of(2 * c, 0)
        tick(2)
        rows_of(2 * c + 1, 0)
        both_got(h1, 0)
        tick(2)
        rows_of(2 - 2 * c, 0)
        tick(2)
        rows_of(3 - 2 * c, 0)

    pl.run_scoped(qkv, VM((2, D, 864), BF))
    put(h1, h1_out)
    tick(1)
    put(qa, q_out)
    put(ka, k_out)
    put(vt, v_out)

    def head(j, _):
        def queries(i, _):
            rows = pl.ds(pl.multiple_of(i * 256, 256), 256)
            scores = matmul_nt(ka[j], qa[j, rows, :]) * ALPHA
            top = jnp.max(scores, axis=0, keepdims=True)
            prob = jnp.exp2(scores - top)
            total = jnp.sum(prob, axis=0, keepdims=True)
            result = matmul(vt[j], prob.astype(BF)) * (1.0 / total)
            attnt[j, :, rows] = result
            lse_out[j, :, rows] = top + jnp.log2(total)
            return 0

        lax.fori_loop(0, 4, queries, 0)
        return 0

    for j in range(8):
        head(j, 0)
        tick(3)

    for i in range(half // PART):
        moved(1 + half // PART + i)

    def close(t, _):
        rows = pl.ds(pl.multiple_of(t * TILE, TILE), TILE)
        spot = (mine + t * TILE + lax.broadcasted_iota(jnp.int32, (TILE, 1), 0)).astype(F32)
        outer = jnp.where(spot < live, dy[rows, :].astype(F32), 0.0)
        dy[rows, :] = outer.astype(BF)
        own_tile(closing, t)[...] = (outer * vec(5)).astype(BF)
        give(closing, t, 1).start()
        return 0

    lax.fori_loop(0, tiles, close, 0)
    put(attnt, attnt_out)
    tick_until(2)
    owns[1].wait()

    def proj(weight, stage, raw):
        load(gp, raw, 5)
        for i in (0, 1):
            for h in range(8):
                stage[h * 72 : h * 72 + 72, :] = raw[i, h].astype(F32)
            weight[i] = stage[...].astype(BF)

        def attn_rows(i, _):
            rows = pl.ds(pl.multiple_of(i * 256, 256), 256)
            value = jnp.concatenate([attnt[j, :, rows] for j in range(8)], axis=0)
            attn[rows, :] = value.T.astype(BF)
            return 0

        lax.fori_loop(0, 4, attn_rows, 0)

        def for_twin(t, _):
            rows = pl.ds(pl.multiple_of(t * WIDE, WIDE), WIDE)
            left = attn[pl.ds(pl.multiple_of(other + t * WIDE, WIDE), WIDE), :]
            for i in (0, 1):
                ps[rows, i * 576 : (i + 1) * 576] = matmul(left, weight[i]).astype(BF)
            rdma(ps.at[rows], pr.at[rows], ts.at[2, t], tr.at[2, t], twin).start()
            return 0

        for t in range(half // WIDE):
            for_twin(t, 0)
            tick(1)

        def for_me(t, _):
            rows = pl.ds(pl.multiple_of(t * WIDE, WIDE), WIDE)
            left = attn[pl.ds(pl.multiple_of(mine + t * WIDE, WIDE), WIDE), :]
            for i in (0, 1):
                acc[rows, i * 576 : (i + 1) * 576] = matmul(left, weight[i])
            return 0

        for t in range(half // WIDE):
            for_me(t, 0)
            tick(1)

    pl.run_scoped(proj, VM((2, 576, 576), BF), VM((576, 576), F32), VM((2, 8, 72, 576), BF))

    def middle(t, _):
        rows = pl.ds(pl.multiple_of(t * TILE, TILE), TILE)
        branch = acc[rows, :] + pr[rows, :].astype(F32) + b_p[...]
        ba[rows, :] = branch.astype(BF)
        value = x0[rows, :].astype(F32) + vec(2) * branch
        x1[rows, :] = value
        own_tile(h2, t)[...] = (normed_tile(value) * (1.0 + vec(4)) + vec(3)).astype(BF)
        give(h2, t, 3).start()
        return 0

    def half_got(src, dst, i, t):
        rows = pl.ds(t * WIDE, WIDE)
        rdma(src.at[rows], dst.at[rows], ts.at[i, t], tr.at[i, t], twin).wait()

    for t in range(tiles):
        if t % 2 == 0:
            half_got(ps, pr, 2, t // 2)
        middle(t, 0)
    put(ba, ba_out)
    put(x1, x1_out)
    put(x0, x0_out)
    put(dy, dy_out)
    tick_until(4)
    owns[2].wait()
    both_got(h2, 3)
    both_got(closing, 1)
    put(h2, h2_out)
    put(closing, cl_out)

    def up(weight):
        load(gu, weight, 6)

        def rows_of(n, _):
            rows = pl.ds(pl.multiple_of(n * 128, 128), 128)
            left = h2[rows, :]
            for i in (0, 1):
                cols = slice(i * D, (i + 1) * D)
                u = matmul(left, weight[i]) + b_u[:, cols]
                square = u * u
                bent = jnp.tanh(GELU_A * u * (1.0 + GELU_B * square))
                act[rows, cols] = (0.5 * u * (1.0 + bent)).astype(BF)
                slope = (0.5 * GELU_A) * u * (1.0 - bent * bent) * (1.0 + 3.0 * GELU_B * square)
                der[rows, cols] = (0.5 * (1.0 + bent) + slope).astype(BF)
            return 0

        for n in range(8):
            rows_of(n, 0)
            tick(1)

    pl.run_scoped(up, VM((2, D, D), BF))
    put(act, act_out)
    put(der, der_out)

    gouts = []
    for t in range(6):
        slot = t % 2
        if t >= 2:
            gouts[t - 2].wait()
        left = act[:, t * 384 : (t + 1) * 384]
        for i in (0, 1):
            gstage[slot, i] = matmul_tn(left, closing[:, i * 576 : (i + 1) * 576]).astype(BF)
        d = pltpu.make_async_copy(
            gstage.at[slot], gred_out.at[:, pl.ds(t * 384, 384)], gsem.at[slot]
        )
        d.start()
        gouts.append(d)
        tick(2)
    for d in gouts[-2:]:
        d.wait()
    tick(len(steps))
    owns[3].wait()

    def down(weight):
        load(gd, weight, 7)

        def for_twin(t, _):
            rows = pl.ds(pl.multiple_of(t * WIDE, WIDE), WIDE)
            left = act[pl.ds(pl.multiple_of(other + t * WIDE, WIDE), WIDE), :]
            for i in (0, 1):
                ds[rows, i * 576 : (i + 1) * 576] = matmul(left, weight[i]).astype(BF)
            rdma(ds.at[rows], dr.at[rows], ts.at[4, t], tr.at[4, t], twin).start()
            return 0

        for t in range(half // WIDE):
            for_twin(t, 0)
            tick(1)

        def for_me(t, _):
            rows = pl.ds(pl.multiple_of(t * WIDE, WIDE), WIDE)
            left = act[pl.ds(pl.multiple_of(mine + t * WIDE, WIDE), WIDE), :]
            for i in (0, 1):
                acc[rows, i * 576 : (i + 1) * 576] = matmul(left, weight[i])
            return 0

        for t in range(half // WIDE):
            for_me(t, 0)
            tick(1)

    pl.run_scoped(down, VM((2, 2304, 576), BF))

    def finish(t, _):
        rows = pl.ds(pl.multiple_of(t * TILE, TILE), TILE)
        branch = acc[rows, :] + dr[rows, :].astype(F32) + b_d[...]
        bb[rows, :] = branch.astype(BF)
        yo[rows, :] = (x1[rows, :] + vec(5) * branch).astype(BF)
        return 0

    for t in range(tiles):
        if t % 2 == 0:
            half_got(ds, dr, 4, t // 2)
        finish(t, 0)
    put(bb, bb_out)
    put(yo, y_out)
    for d in out_copies:
        d.wait()
    gather.finish()


def forward_block(tokens, cotangent, bucket, table, masters, modulate_master, cond, biases):
    shapes = {
        "gq": (2, D, 864),
        "gp": (2, 8, 72, 576),
        "gu": (2, D, D),
        "gd": (2, 2304, 576),
    }
    half = tokens.shape[0]
    rows = 2 * half
    out_shape, out_specs = [], []

    def out(shape, dtype, space=ANY):
        out_shape.append(jax.ShapeDtypeStruct(shape, dtype))
        out_specs.append(pl.BlockSpec(memory_space=space))

    for s in shapes.values():
        out(s, BF)
    out((2, 1, 3456), F32, VM)
    out((16, 128), F32, VM)
    out((half, D), BF)
    out((half, D), BF)
    out((rows, D), BF)
    out((rows, D), BF)
    out((8, rows, 128), BF)
    out((8, rows, 128), BF)
    out((8, 72, rows), BF)
    out((8, 72, rows), F32)
    out((8, 1, rows), F32, VM)
    out((half, D), BF)
    out((half, D), F32)
    out((rows, D), BF)
    out((rows, 2304), BF)
    out((rows, 2304), BF)
    out((half, D), BF)
    out((half, D), BF)
    out((2, 2304, 576), BF)
    dma = pltpu.SemaphoreType.DMA
    scratch = [
        VM((144, 864), BF),
        VM((72, 576), BF),
        VM((144, D), BF),
        VM((288, 576), BF),
        VM((2, 72, 864), F32),
        VM((72, 864), F32),
        VM((2, 72, D), F32),
        VM((72, D), F32),
        VM((4, 2, 2, 16, 128), F32),
        VM((4, 2, 2, 1, 3456), F32),
        VM((3, 2, 2, 1, 3456), F32),
        VM((2, 2, 1, 3456), F32),
        VM((2, 1, 3456), F32),
        VM((3, 2, 1, 3456), F32),
        VM((2, 1, 3456), F32),
        VM((half, D), BF),
        VM((half, D), BF),
        VM((half, D), BF),
        VM((8, 128), F32),
        VM((rows, D), BF),
        VM((rows, D), BF),
        VM((8, rows, 128), BF),
        VM((8, rows, 128), BF),
        VM((8, 72, rows), BF),
        VM((8, 72, rows), F32),
        VM((rows, 576), BF),
        VM((half, D), BF),
        VM((half, D), BF),
        VM((half, D), BF),
        VM((half, D), BF),
        VM((half, D), F32),
        VM((half, D), F32),
        VM((rows, D), BF),
        VM((rows, 2304), BF),
        VM((rows, 2304), BF),
        VM((half, D), BF),
        VM((half, D), BF),
        VM((half, D), BF),
        VM((2, 2, 384, 576), BF),
        VM((1, 14 * D), F32),
        VM((1, 576), F32),
        VM((1, 576), F32),
        VM((1, 2304), F32),
        dma((8,)),
    ]
    n = len(CHUNKS)
    scratch += [dma((n, 4))] * 6 + [dma((n, 4, 2))] * 2 + [dma((n, 4))] * 2
    scratch += [
        dma((7, 3)),
        dma((7, 3)),
        dma((9,)),
        dma((9,)),
        dma((5, 4)),
        dma((5, 4)),
        dma((2, 2)),
        dma((20,)),
        dma((2,)),
    ]
    vm = pl.BlockSpec(memory_space=VM)
    hbm = pl.BlockSpec(memory_space=ANY)
    return pl.pallas_call(
        forward_kernel,
        out_shape=out_shape,
        in_specs=[vm, hbm] + [vm] * 9,
        out_specs=out_specs,
        scratch_shapes=scratch,
        compiler_params=pltpu.CompilerParams(
            collective_id=0, has_side_effects=True, vmem_limit_bytes=60 * 2**20
        ),
        name="forward_block",
    )(tokens, cotangent, bucket, table, *masters, modulate_master, cond, biases)


OLD_PIECES = {"q": (144, 864, 96), "p": (72, 576, None), "u": (144, 1152, 96), "d": (288, 576, 192)}


def old_parts(rows, cut, k):
    if cut is None:
        return ((0, rows), None) if k % 2 == 0 else (None, (0, rows))
    return (0, cut), (cut, rows - cut)


def scatter_kernel(*refs):
    grads, outs = refs[0:4], refs[4:8]
    held, diag, by_x, by_y, by_z = (refs[8 + 4 * i : 12 + 4 * i] for i in range(5))
    lsem, fs, fr, xs, xr, ys, yr, zs, zr = refs[28:]
    z, x, c, y = place()
    xn, yn = (z, 1 - x, c, y), (z, x, c, 1 - y)
    zn = [None] + [(at_z(k), x, c, y) for k in (1, 2, 3)]
    f32 = jnp.float32
    for w in range(4):
        pltpu.make_async_copy(grads[w], held[w], lsem.at[w]).start()
    greet([xn, yn] + zn[1:])
    pending = []
    order = (3, 2, 1, 0)

    def z_of(k):
        return z if k == 0 else at_z(k)

    for w in range(4):
        rows, _, cut = OLD_PIECES[NAMES[w]]
        pltpu.make_async_copy(grads[w], held[w], lsem.at[w]).wait()
        for k in order:
            spans = old_parts(rows, cut, k)
            for i, (span, to) in enumerate(zip(spans, (yn, xn))):
                if span is not None:
                    d = rdma(
                        held[w].at[1 - y, z_of(k), 1 - x, pl.ds(*span)],
                        diag[w].at[k, pl.ds(*span)],
                        fs.at[w, k, i],
                        fr.at[w, k, i],
                        to,
                    )
                    d.start()
                    pending.append(d)
    for w in range(4):
        rows, _, cut = OLD_PIECES[NAMES[w]]
        for k in order:
            spans = old_parts(rows, cut, k)
            for i, span in enumerate(spans):
                piece = held[w].at[(y, z_of(k), 1 - x) if i == 0 else (1 - y, z_of(k), x)]
                if span is not None:
                    part = diag[w].at[k, pl.ds(*span)]
                    rdma(part, part, fs.at[w, k, i], fr.at[w, k, i], xn).wait_recv()
                    target = piece.at[pl.ds(*span)]
                    target[...] = (target[...].astype(f32) + part[...].astype(f32)).astype(
                        jnp.bfloat16
                    )
                box, to, s, r = ((by_x, xn, xs, xr), (by_y, yn, ys, yr))[i]
                d = rdma(piece, box[w].at[k], s.at[w, k], r.at[w, k], to)
                d.start()
                pending.append(d)
    for w in range(4):
        for k in order:
            for box, s, r in ((by_x, xs, xr), (by_y, ys, yr)):
                part = box[w].at[k]
                rdma(part, part, s.at[w, k], r.at[w, k], xn).wait_recv()
            piece = held[w].at[y, z_of(k), x]
            total = piece[...].astype(f32) + by_x[w][k].astype(f32) + by_y[w][k].astype(f32)
            if k == 0:
                outs[w][...] = total
            else:
                piece[...] = total.astype(jnp.bfloat16)
                d = rdma(piece, by_z[w].at[k - 1], zs.at[w, k - 1], zr.at[w, k - 1], zn[k])
                d.start()
                pending.append(d)
    for w in range(4):
        total = outs[w][...]
        for k in (1, 2, 3):
            part = by_z[w].at[k - 1]
            rdma(part, part, zs.at[w, k - 1], zr.at[w, k - 1], zn[k]).wait_recv()
            total = total + part[...].astype(f32)
        outs[w][...] = total
    for d in pending:
        d.wait_send()


def scatter_grads(grads):
    dma = pltpu.SemaphoreType.DMA
    shapes = [OLD_PIECES[n][:2] for n in NAMES]

    def boxes(*lead):
        return [pltpu.VMEM(lead + s, jnp.bfloat16) for s in shapes]

    return pl.pallas_call(
        scatter_kernel,
        out_shape=[jax.ShapeDtypeStruct(s, jnp.float32) for s in shapes],
        in_specs=[pl.BlockSpec(memory_space=pl.ANY)] * 4,
        out_specs=[pl.BlockSpec(memory_space=pltpu.VMEM)] * 4,
        scratch_shapes=boxes(2, 4, 2)
        + boxes(4)
        + boxes(4)
        + boxes(4)
        + boxes(3)
        + [dma((4,))]
        + [dma((4, 4, 2))] * 2
        + [dma((4, 4))] * 6,
        compiler_params=pltpu.CompilerParams(
            collective_id=1, has_side_effects=True, vmem_limit_bytes=56 * 2**20
        ),
        name="scatter_grads",
    )(*grads)


def totals_kernel(mod_ref, bias_ref, mods, sums, got_m, got_b, got_z, s, r):
    z, x, c, y = place()
    xn, yn, twin = (z, 1 - x, c, y), (z, x, c, 1 - y), (z, x, 1 - c, y)
    zn = [None] + [(at_z(k), x, c, y) for k in (1, 2, 3)]
    greet([xn, yn, twin] + zn[1:])
    d = rdma(mod_ref, got_m, s.at[0], r.at[0], twin)
    e = rdma(bias_ref, got_b.at[0], s.at[1], r.at[1], twin)
    d.start()
    e.start()
    d.wait()
    e.wait()
    mods[z, x, y] = (mod_ref[...] + got_m[...]).astype(jnp.bfloat16)
    sums[...] = bias_ref[...] + got_b[0]
    d = rdma(mods.at[z, x, y], mods.at[z, x, y], s.at[2], r.at[2], yn)
    e = rdma(sums, got_b.at[1], s.at[3], r.at[3], yn)
    d.start()
    e.start()
    d.wait()
    e.wait()
    sums[...] = sums[...] + got_b[1]
    d = rdma(mods.at[z, x], mods.at[z, x], s.at[4], r.at[4], xn)
    e = rdma(sums, got_b.at[2], s.at[5], r.at[5], xn)
    d.start()
    e.start()
    d.wait()
    e.wait()
    got_z[0] = sums[...] + got_b[2]
    ds = [rdma(mods.at[z], mods.at[z], s.at[5 + k], r.at[5 + k], zn[k]) for k in (1, 2, 3)]
    ds += [rdma(got_z.at[0], got_z.at[k], s.at[8 + k], r.at[8 + k], zn[k]) for k in (1, 2, 3)]
    for d in ds:
        d.start()
    for d in ds:
        d.wait()
    sums[...] = (got_z[0] + got_z[1]) + (got_z[2] + got_z[3])


def share_totals(mod_grad, bias_grad):
    f32, vm = jnp.float32, pltpu.VMEM
    return pl.pallas_call(
        totals_kernel,
        out_shape=[
            jax.ShapeDtypeStruct((4, 2, 2, 16, 432), jnp.bfloat16),
            jax.ShapeDtypeStruct((72, 128), f32),
        ],
        in_specs=[pl.BlockSpec(memory_space=vm)] * 2,
        out_specs=[pl.BlockSpec(memory_space=vm)] * 2,
        scratch_shapes=[
            vm((16, 432), f32),
            vm((3, 72, 128), f32),
            vm((4, 72, 128), f32),
            pltpu.SemaphoreType.DMA((12,)),
            pltpu.SemaphoreType.DMA((12,)),
        ],
        compiler_params=pltpu.CompilerParams(collective_id=3, has_side_effects=True),
        name="share_totals",
    )(mod_grad, bias_grad)


def norm_kernel(in_ref, out_ref, box, got_z, s, r):
    z, x, c, y = place()
    xn, yn, twin = (z, 1 - x, c, y), (z, x, c, 1 - y), (z, x, 1 - c, y)
    zn = [None] + [(at_z(k), x, c, y) for k in (1, 2, 3)]
    greet([xn, yn, twin] + zn[1:])
    total = in_ref[...]
    for i, to in enumerate((twin, yn, xn)):
        box[2 * i] = total
        d = rdma(box.at[2 * i], box.at[2 * i + 1], s.at[i], r.at[i], to)
        d.start()
        d.wait()
        total = total + box[2 * i + 1]
    got_z[0] = total
    ds = [rdma(got_z.at[0], got_z.at[k], s.at[2 + k], r.at[2 + k], zn[k]) for k in (1, 2, 3)]
    for d in ds:
        d.start()
    for d in ds:
        d.wait()
    out_ref[...] = (got_z[0] + got_z[1]) + (got_z[2] + got_z[3])


def sum_everywhere(value):
    f32, vm = jnp.float32, pltpu.VMEM
    return pl.pallas_call(
        norm_kernel,
        out_shape=jax.ShapeDtypeStruct((8, 128), f32),
        in_specs=[pl.BlockSpec(memory_space=vm)],
        out_specs=pl.BlockSpec(memory_space=vm),
        scratch_shapes=[
            vm((6, 8, 128), f32),
            vm((4, 8, 128), f32),
            pltpu.SemaphoreType.DMA((6,)),
            pltpu.SemaphoreType.DMA((6,)),
        ],
        compiler_params=pltpu.CompilerParams(collective_id=4, has_side_effects=True),
        name="sum_everywhere",
    )(value)


def swap_halves(value):
    return lax.ppermute(value, ("c", "y"), [(0, 0), (1, 2), (2, 1), (3, 3)])


def to_twin(value):
    return lax.ppermute(value, "c", [(0, 1), (1, 0)])


def both_halves(value):
    c = lax.axis_index("c")
    other = to_twin(value)
    return jnp.where(c == 0, jnp.concatenate([value, other]), jnp.concatenate([other, value]))


def sum_halves(value):
    c = lax.axis_index("c")
    half = value.shape[0] // 2
    mine = lax.dynamic_slice_in_dim(value, c * half, half)
    other = to_twin(lax.dynamic_slice_in_dim(value, (1 - c) * half, half).astype(jnp.bfloat16))
    return mine + other.astype(jnp.float32)


def wide(left, weight):
    return jnp.concatenate(
        [jnp.dot(left, weight[i], preferred_element_type=jnp.float32) for i in (0, 1)], axis=1
    )


def wide_back(gradient, weight):
    half = weight.shape[2]
    return sum(
        lax.dot_general(
            gradient[:, i * half : (i + 1) * half],
            weight[i],
            (((1,), (1,)), ((), ())),
            preferred_element_type=jnp.float32,
        )
        for i in (0, 1)
    )


def weight_grad(left, right, name):
    rows, cols, _ = PIECES[name]
    half = right.shape[1] // 2
    return jnp.stack(
        [
            lax.dot_general(
                left,
                right[:, i * half : (i + 1) * half],
                (((0,), (0,)), ((), ())),
                preferred_element_type=jnp.float32,
            ).astype(jnp.bfloat16)
            for i in (0, 1)
        ]
    ).reshape(2, 4, 2, rows, cols)


def shard_from_pieces(piece, width):
    c = lax.axis_index("c")
    half = piece.shape[0] // 2
    mine = lax.dynamic_slice_in_dim(piece, c * half, half)
    other = to_twin(lax.dynamic_slice_in_dim(piece, (1 - c) * half, half))
    split = jnp.where(c == 0, jnp.stack([mine, other]), jnp.stack([other, mine]))
    cols = piece.shape[1]
    return split.reshape(2, half, cols // width, width).transpose(1, 2, 0, 3).reshape(half, 2 * cols)


def core_bias(piece, width):
    c = lax.axis_index("c")
    blocks = piece.reshape(-1, 2, width)
    return lax.dynamic_index_in_dim(blocks, c, 1, keepdims=False).reshape(-1)


def bias_slot(piece, width):
    c = lax.axis_index("c")
    blocks = piece.reshape(-1, 1, width)
    pick = (jnp.arange(2) == c).astype(jnp.float32)[None, :, None]
    return (blocks * pick).reshape(-1)


def on_device_fast(
    tokens,
    cotangent,
    buckets,
    timesteps,
    labels,
    class_table,
    step_count,
    modulate_master,
    modulate_first,
    modulate_second,
    attend_master,
    attend_first,
    attend_second,
    project_master,
    project_first,
    project_second,
    expand_master,
    expand_first,
    expand_second,
    reduce_master,
    reduce_first,
    reduce_second,
    biases_master,
    biases_first,
    biases_second,
):

    z, x, c, y = place()
    bf16, f32 = jnp.bfloat16, jnp.float32
    block = FF // 16
    class_row = lax.dynamic_slice_in_dim(class_table, labels[0], 1).astype(f32)
    condition = jax.nn.silu(class_row + time_features(timesteps, D)).astype(bf16).astype(f32)
    cond_tiles = jnp.pad(condition.reshape(16, 72), ((0, 0), (0, 56)))
    bucket = jnp.broadcast_to(buckets.astype(f32)[:, None], (8, 128))
    steps = jnp.arange(64, dtype=f32)[:, None]
    omegas = jnp.exp(-math.log(10000.0) * jnp.arange(288, dtype=f32) / 288)[None, :]
    table = jnp.concatenate([jnp.sin(steps * omegas), jnp.cos(steps * omegas)], axis=1)
    (
        weight_q,
        weight_p,
        weight_u,
        weight_d,
        modulation,
        cond_all,
        residual_zero,
        outer_grad,
        closing_all,
        hidden_attend,
        queries,
        key_rows,
        value_rows,
        attn_t,
        log_sums,
        branch_attend,
        residual_one,
        hidden_expand,
        activated,
        slope,
        branch_expand,
        output,
        grad_reduce,
    ) = forward_block(
        tokens,
        cotangent,
        bucket,
        table,
        (attend_master, project_master, expand_master, reduce_master),
        modulate_master,
        cond_tiles,
        biases_master[None, :],
    )

    modulation = modulation.reshape(6 * D)
    shift_one, scale_one, gating_one, shift_two, scale_two, gating_two = (
        modulation[i * D : (i + 1) * D][None, :] for i in range(6)
    )
    chip_bucket = swap_halves(buckets)
    unit = SIDE // 8
    lengths = table_pick(chip_bucket, row_units) * unit * table_pick(chip_bucket, col_units) * unit

    def flat(heads):
        return heads.transpose(1, 0, 2).reshape(1024, 576)

    queries, key_rows = flat(queries[:, :, :72]), flat(key_rows[:, :, :72])
    value_rows = value_rows.reshape(576, 1024).T
    attention = attn_t.reshape(576, 1024).T.astype(bf16)
    log_sums = log_sums.reshape(8, 2, 512).transpose(1, 0, 2)[None] * math.log(2.0)
    weight_p = weight_p.reshape(2, 576, 576)
    output = swap_halves(output)
    residual_zero = residual_zero.astype(f32)
    outer_grad = outer_grad.astype(f32)
    gating_later = jnp.sum(outer_grad * branch_expand, axis=0)
    closing_grad = (outer_grad * gating_two).astype(bf16)
    active_grad = wide_back(closing_all, weight_d)
    widened_grad = (active_grad * slope).astype(bf16)
    grad_reduce = grad_reduce.reshape(2, 4, 2, 288, 576)
    grad_expand = weight_grad(hidden_expand, widened_grad, "u")
    hidden_grad = sum_halves(wide_back(widened_grad, weight_u))
    def norm_back(residual, scaling, gradient):
        average = jnp.mean(residual, axis=-1, keepdims=True)
        centred = residual - average
        inverse = lax.rsqrt(jnp.mean(centred * centred, axis=-1, keepdims=True) + 1e-06)
        normed = centred * inverse
        inner = gradient * (1.0 + scaling)
        part = (
            inner
            - jnp.mean(inner, axis=-1, keepdims=True)
            - normed * jnp.mean(inner * normed, axis=-1, keepdims=True)
        ) * inverse
        return part, jnp.sum(gradient, axis=0), jnp.sum(gradient * normed, axis=0)

    residual_part, shift_later, scale_later = norm_back(residual_one, scale_two, hidden_grad)
    middle_grad = outer_grad + residual_part
    gating_early = jnp.sum(middle_grad * branch_attend, axis=0)
    branch_grad = (middle_grad * gating_one).astype(bf16)
    branch_all = both_halves(branch_grad)
    heads_grad = wide_back(branch_all, weight_p).astype(bf16)
    grad_project = weight_grad(attention, branch_all, "p")
    query_grad, keyrow_grad, value_grad = attend_back(
        queries, key_rows, value_rows, heads_grad, log_sums, lengths
    )
    packed_grad = jnp.concatenate([query_grad, keyrow_grad, value_grad], axis=1)
    grad_attend = weight_grad(hidden_attend, packed_grad, "q")
    normed_grad = sum_halves(wide_back(packed_grad, weight_q))
    input_part, shift_early, scale_early = norm_back(residual_zero, scale_one, normed_grad)
    input_grad = swap_halves((middle_grad + input_part).astype(bf16)).astype(f32)

    mod_grad = jnp.concatenate(
        [shift_early, scale_early, gating_early, shift_later, scale_later, gating_later]
    )
    bias_share = jnp.concatenate(
        [
            bias_slot(jnp.sum(query_grad.astype(f32), axis=0), HEAD_DIM),
            bias_slot(jnp.sum(value_grad.astype(f32), axis=0), HEAD_DIM),
            jnp.sum(branch_grad.astype(f32), axis=0),
            bias_slot(jnp.sum(widened_grad.astype(f32), axis=0), block),
            jnp.sum(closing_grad.astype(f32), axis=0),
        ]
    )
    sums_q, sums_p, sums_u, sums_d = scatter_grads(
        (grad_attend, grad_project, grad_expand, grad_reduce)
    )
    mods, bias_sums = share_totals(mod_grad.reshape(16, 432), bias_share.reshape(72, 128))
    mods = mods.reshape(16, 2, 3456)
    grad_mod = lax.dot_general(
        cond_all[:, :72].astype(bf16),
        lax.dynamic_index_in_dim(mods, y, 1, keepdims=False),
        (((0,), (0,)), ((), ())),
        preferred_element_type=f32,
    )
    bias_total = jnp.concatenate([jnp.sum(mods.astype(f32), axis=0).reshape(-1), bias_sums.reshape(-1)])
    grad_attend = shard_from_pieces(sums_q, HEAD_DIM)
    grad_expand = shard_from_pieces(sums_u, block)
    reduced = (grad_mod, grad_attend, sums_p, grad_expand, sums_d)
    local_squares = sum(jnp.sum(gradient * gradient) for gradient in reduced)
    square_total = sum_everywhere(jnp.full((8, 128), local_squares))[0, 0]
    grad_norm = jnp.sqrt(square_total + jnp.sum(bias_total * bias_total))
    clip_factor = jnp.minimum(1.0, 1.0 / (grad_norm + 1e-06))
    correction = 1.0 - jnp.power(0.5, step_count.astype(f32))
    rate = 0.5 * D ** (-0.5)
    states = (
        (modulate_master, modulate_first, modulate_second, grad_mod, rate),
        (attend_master, attend_first, attend_second, grad_attend, rate),
        (project_master, project_first, project_second, sums_p, rate),
        (expand_master, expand_first, expand_second, grad_expand, rate),
        (reduce_master, reduce_first, reduce_second, sums_d, 0.5 * FF ** (-0.5)),
        (biases_master, biases_first, biases_second, bias_total, 0.1),
    )
    updates = []
    for master, first, second, gradient, learn_rate in states:
        updates += adam_update(
            master, first, second, gradient, learn_rate, clip_factor, correction
        )
    return (output, input_grad, grad_norm, *updates)


def fast_solution(mesh):
    return jax.shard_map(
        on_device_fast,
        mesh=mesh,
        in_specs=(
            P(("z", "x", "c", "y"), None),
            P(("z", "x", "c", "y"), None),
            P(("z", "x", "c")),
            P(("z", "x", "c")),
            P(("z", "x", "c")),
            P(),
            P(),
            P(("z", "x", "c"), "y"),
            P(("z", "x", "c"), "y"),
            P(("z", "x", "c"), "y"),
            P(("z", "x", "c"), "y"),
            P(("z", "x", "c"), "y"),
            P(("z", "x", "c"), "y"),
            P(("z", "x", "c"), "y"),
            P(("z", "x", "c"), "y"),
            P(("z", "x", "c"), "y"),
            P(("z", "x", "c"), "y"),
            P(("z", "x", "c"), "y"),
            P(("z", "x", "c"), "y"),
            P(("z", "x", "c"), "y"),
            P(("z", "x", "c"), "y"),
            P(("z", "x", "c"), "y"),
            P(),
            P(),
            P(),
        ),
        out_specs=(
            P(("z", "x", "c", "y"), None),
            P(("z", "x", "c", "y"), None),
            P(),
            P(("z", "x", "c"), "y"),
            P(("z", "x", "c"), "y"),
            P(("z", "x", "c"), "y"),
            P(("z", "x", "c"), "y"),
            P(("z", "x", "c"), "y"),
            P(("z", "x", "c"), "y"),
            P(("z", "x", "c"), "y"),
            P(("z", "x", "c"), "y"),
            P(("z", "x", "c"), "y"),
            P(("z", "x", "c"), "y"),
            P(("z", "x", "c"), "y"),
            P(("z", "x", "c"), "y"),
            P(("z", "x", "c"), "y"),
            P(("z", "x", "c"), "y"),
            P(("z", "x", "c"), "y"),
            P(),
            P(),
            P(),
        ),
        check_vma=False,
    )


def plain_solution(mesh):
    return jax.shard_map(
        on_device,
        mesh=mesh,
        in_specs=(
            P(("seq", "head"), None),
            P(("seq", "head"), None),
            P("seq"),
            P("seq"),
            P("seq"),
            P(),
            P(),
            P("seq", "head"),
            P("seq", "head"),
            P("seq", "head"),
            P("seq", "head"),
            P("seq", "head"),
            P("seq", "head"),
            P("seq", "head"),
            P("seq", "head"),
            P("seq", "head"),
            P("seq", "head"),
            P("seq", "head"),
            P("seq", "head"),
            P("seq", "head"),
            P("seq", "head"),
            P("seq", "head"),
            P(),
            P(),
            P(),
        ),
        out_specs=(
            P(("seq", "head"), None),
            P(("seq", "head"), None),
            P(),
            P("seq", "head"),
            P("seq", "head"),
            P("seq", "head"),
            P("seq", "head"),
            P("seq", "head"),
            P("seq", "head"),
            P("seq", "head"),
            P("seq", "head"),
            P("seq", "head"),
            P("seq", "head"),
            P("seq", "head"),
            P("seq", "head"),
            P("seq", "head"),
            P("seq", "head"),
            P("seq", "head"),
            P(),
            P(),
            P(),
        ),
        check_vma=False,
    )


def solution(mesh):
    if dict(mesh.shape) == {"seq": 16, "head": 2}:
        grid = Mesh(mesh.devices.reshape(4, 2, 2, 2), ("z", "x", "c", "y"))
        return fast_solution(grid)
    return plain_solution(mesh)
```

```python
import functools
import math

import jax
import jax.numpy as jnp
from jax import lax
from jax.experimental import pallas as pl
from jax.experimental.pallas import tpu as pltpu
from jax.sharding import Mesh
from jax.sharding import PartitionSpec as P

D = 1152
HEAD_DIM = 72
FF = 4608
SIDE = 32
LMAX = 1024


highest = lax.Precision.HIGHEST
row_units = (8, 4, 16, 6, 10, 7, 4, 6)
col_units = (8, 16, 4, 10, 6, 9, 8, 6)


def table_pick(indices, entries):
    matches = indices[..., None] == jnp.arange(len(entries), dtype=jnp.int32)
    return jnp.sum(jnp.where(matches, jnp.array(entries, jnp.int32), 0), axis=-1)


def layer_norm(value):
    average = jnp.mean(value, axis=-1, keepdims=True)
    centred = value - average
    spread = jnp.mean(centred * centred, axis=-1, keepdims=True)
    return centred * lax.rsqrt(spread + 1e-06)


def modulate(value, shift, scaling):
    return layer_norm(value) * (1.0 + scaling) + shift


def time_features(moments, width):
    half_width = width // 2
    frequency = jnp.exp(-math.log(10000.0) * jnp.arange(half_width, dtype=jnp.float32) / half_width)
    angles = moments.astype(jnp.float32)[:, None] * frequency[None, :]
    return jnp.concatenate([jnp.cos(angles), jnp.sin(angles)], axis=1)


def grid_features(position, row_wide, width):
    quarter = width // 4
    omegas = jnp.exp(-math.log(10000.0) * jnp.arange(quarter, dtype=jnp.float32) / quarter)
    row_angle = (position // row_wide).astype(jnp.float32)[:, None] * omegas[None, :]
    col_angle = (position % row_wide).astype(jnp.float32)[:, None] * omegas[None, :]
    return jnp.concatenate(
        [jnp.sin(row_angle), jnp.cos(row_angle), jnp.sin(col_angle), jnp.cos(col_angle)], axis=1
    )


def fold_rows(left_side, weight_slab):
    return jnp.dot(
        left_side,
        lax.all_gather(weight_slab, "seq", axis=0, tiled=True),
        preferred_element_type=jnp.float32,
    )


def back_cols(gradient, weight_slab):
    return lax.dot_general(
        gradient,
        lax.all_gather(weight_slab, "seq", axis=0, tiled=True),
        (((1,), (1,)), ((), ())),
        preferred_element_type=jnp.float32,
    )


def rows_seq(left_side, right_side):
    return lax.psum_scatter(
        lax.dot_general(
            left_side, right_side, (((0,), (0,)), ((), ())), preferred_element_type=jnp.float32
        ).astype(jnp.bfloat16),
        "seq",
        scatter_dimension=0,
        tiled=True,
    ).astype(jnp.float32)


def attend(queries, key_rows, value_rows, lengths):
    heads_here = queries.shape[1] // HEAD_DIM
    block_rows = min(512, LMAX)
    score_scale = HEAD_DIM ** (-0.5)
    image_count = lengths.shape[0]

    def per_image(packed):
        query_image, key_image, value_image, length = packed
        key_heads = key_image.reshape(LMAX, heads_here, HEAD_DIM)
        value_heads = value_image.reshape(LMAX, heads_here, HEAD_DIM)
        live_keys = jnp.arange(LMAX, dtype=jnp.int32) < length

        def per_block(query_block):
            scores = (
                jnp.einsum(
                    "qhe,khe->hqk", query_block, key_heads, preferred_element_type=jnp.float32
                )
                * score_scale
            )
            scores = jnp.where(live_keys[None, None, :], scores, -1e30)
            maximum = jnp.max(scores, axis=-1, keepdims=True)
            weights = jnp.exp(scores - maximum)
            totals = jnp.sum(weights, axis=-1, keepdims=True)
            probability = (weights / totals).astype(jnp.bfloat16)
            result = jnp.einsum(
                "hqk,khe->qhe", probability, value_heads, preferred_element_type=jnp.float32
            )
            return (result.astype(jnp.bfloat16), (maximum + jnp.log(totals))[:, :, 0])

        blocks = query_image.reshape(LMAX // block_rows, block_rows, heads_here, HEAD_DIM)
        result, log_sums = lax.map(per_block, blocks)
        return (result.reshape(LMAX, heads_here * HEAD_DIM), log_sums)

    stacked = (
        queries.reshape(image_count, LMAX, -1),
        key_rows.reshape(image_count, LMAX, -1),
        value_rows.reshape(image_count, LMAX, -1),
        lengths,
    )
    result, log_sums = lax.map(per_image, stacked)
    return (result.reshape(image_count * LMAX, -1), log_sums)


def attend_back(queries, key_rows, value_rows, grad_rows, log_sums, lengths):
    heads_here = queries.shape[1] // HEAD_DIM
    block_rows = min(512, LMAX)
    score_scale = HEAD_DIM ** (-0.5)
    image_count = lengths.shape[0]

    def per_image(packed):
        query_image, key_image, value_image, grad_image, logsum_image, length = packed
        key_heads = key_image.reshape(LMAX, heads_here, HEAD_DIM)
        value_heads = value_image.reshape(LMAX, heads_here, HEAD_DIM)
        live_keys = jnp.arange(LMAX, dtype=jnp.int32) < length

        def per_block(running, inputs):
            key_grad, value_grad = running
            query_block, grad_block, logsum_block = inputs
            scores = (
                jnp.einsum(
                    "qhe,khe->hqk", query_block, key_heads, preferred_element_type=jnp.float32
                )
                * score_scale
            )
            scores = jnp.where(live_keys[None, None, :], scores, -1e30)
            probability = jnp.exp(scores - logsum_block[:, :, None])
            grad_prob = jnp.einsum(
                "qhe,khe->hqk", grad_block, value_heads, preferred_element_type=jnp.float32
            )
            inner_sum = jnp.sum(probability * grad_prob, axis=-1, keepdims=True)
            grad_score = (probability * (grad_prob - inner_sum)).astype(jnp.bfloat16)
            query_grad = (
                jnp.einsum(
                    "hqk,khe->qhe", grad_score, key_heads, preferred_element_type=jnp.float32
                )
                * score_scale
            )
            key_grad = (
                key_grad
                + jnp.einsum(
                    "hqk,qhe->khe", grad_score, query_block, preferred_element_type=jnp.float32
                )
                * score_scale
            )
            value_grad = value_grad + jnp.einsum(
                "hqk,qhe->khe",
                probability.astype(jnp.bfloat16),
                grad_block,
                preferred_element_type=jnp.float32,
            )
            return ((key_grad, value_grad), query_grad.astype(jnp.bfloat16))

        initial = (
            jnp.zeros((LMAX, heads_here, HEAD_DIM), jnp.float32),
            jnp.zeros((LMAX, heads_here, HEAD_DIM), jnp.float32),
        )
        blocks = (
            query_image.reshape(LMAX // block_rows, block_rows, heads_here, HEAD_DIM),
            grad_image.reshape(LMAX // block_rows, block_rows, heads_here, HEAD_DIM),
            logsum_image,
        )
        (key_grad, value_grad), query_grad = lax.scan(per_block, initial, blocks)
        return (
            query_grad.reshape(LMAX, -1),
            key_grad.reshape(LMAX, -1).astype(jnp.bfloat16),
            value_grad.reshape(LMAX, -1).astype(jnp.bfloat16),
        )

    stacked = (
        queries.reshape(image_count, LMAX, -1),
        key_rows.reshape(image_count, LMAX, -1),
        value_rows.reshape(image_count, LMAX, -1),
        grad_rows.reshape(image_count, LMAX, -1),
        log_sums,
        lengths,
    )
    query_grad, key_grad, value_grad = lax.map(per_image, stacked)
    return (
        query_grad.reshape(image_count * LMAX, -1),
        key_grad.reshape(image_count * LMAX, -1),
        value_grad.reshape(image_count * LMAX, -1),
    )


def adam_update(master, first_moment, second_moment, gradient, learn_rate, clip_factor, correction):
    clipped = gradient * clip_factor
    first_new = 0.5 * first_moment + 0.5 * clipped
    second_new = 0.5 * second_moment + 0.5 * clipped * clipped
    direction = first_new / correction / (jnp.sqrt(second_new / correction) + 1e-08)
    return (master - learn_rate * (direction + 0.1 * master), first_new, second_new)


def on_device(
    tokens,
    cotangent,
    buckets,
    timesteps,
    labels,
    class_table,
    step_count,
    modulate_master,
    modulate_first,
    modulate_second,
    attend_master,
    attend_first,
    attend_second,
    project_master,
    project_first,
    project_second,
    expand_master,
    expand_first,
    expand_second,
    reduce_master,
    reduce_first,
    reduce_second,
    biases_master,
    biases_first,
    biases_second,
):
    head_index = lax.axis_index("head")
    head_count = lax.axis_size("head")
    tok_rows = tokens.shape[0]
    image_count = buckets.shape[0]
    unit_cells = SIDE // 8
    heights = table_pick(buckets, row_units) * unit_cells
    widths = table_pick(buckets, col_units) * unit_cells
    lengths = heights * widths
    row_index = head_index * tok_rows + jnp.arange(tok_rows, dtype=jnp.int32)
    image_of = row_index // LMAX
    position = row_index % LMAX
    choose = image_of[:, None] == jnp.arange(image_count, dtype=jnp.int32)[None, :]
    pick_rows = choose.astype(jnp.float32)
    row_wide = jnp.sum(jnp.where(choose, widths[None, :], 0), axis=1)
    row_length = jnp.sum(jnp.where(choose, lengths[None, :], 0), axis=1)
    live_rows = (position < row_length).astype(jnp.float32)
    grid_cells = grid_features(position, row_wide, D)
    class_pick = (
        labels[:, None] == jnp.arange(class_table.shape[0], dtype=jnp.int32)[None, :]
    ).astype(jnp.bfloat16)
    class_rows = jnp.dot(class_pick, class_table, preferred_element_type=jnp.float32)
    condition = jax.nn.silu(class_rows + time_features(timesteps, D)).astype(jnp.bfloat16)
    bias_low = biases_master.astype(jnp.bfloat16).astype(jnp.float32)
    offset_base = 6 * D
    bias_query = bias_low[offset_base : offset_base + D]
    bias_value = bias_low[offset_base + D : offset_base + 2 * D]
    bias_proj = bias_low[offset_base + 2 * D : offset_base + 3 * D]
    bias_hidden = bias_low[offset_base + 3 * D : offset_base + 3 * D + FF]
    bias_output = bias_low[offset_base + 3 * D + FF :]
    head_slabs = (
        lax.all_gather(attend_master.astype(jnp.bfloat16), "head", axis=1, tiled=True),
        lax.all_gather(project_master.astype(jnp.bfloat16), "head", axis=1, tiled=True),
        lax.all_gather(expand_master.astype(jnp.bfloat16), "head", axis=1, tiled=True),
        lax.all_gather(reduce_master.astype(jnp.bfloat16), "head", axis=1, tiled=True),
    )
    attend_slab, project_slab, expand_slab, reduce_slab = head_slabs
    mod_width = 6 * D // head_count
    mod_share = fold_rows(condition, modulate_master.astype(jnp.bfloat16))
    mod_share = mod_share + lax.dynamic_slice_in_dim(bias_low, head_index * mod_width, mod_width)
    modulation = lax.all_gather(mod_share, "head", axis=1, tiled=True)
    mod_rows = jnp.dot(pick_rows, modulation, precision=highest)
    shift_one, scale_one, gating_one, shift_two, scale_two, gating_two = jnp.split(
        mod_rows, 6, axis=1
    )
    residual_zero = tokens.astype(jnp.float32) + grid_cells
    hidden_attend = modulate(residual_zero, shift_one, scale_one).astype(jnp.bfloat16)
    packed = fold_rows(hidden_attend, attend_slab)
    queries = (packed[:, :D] + bias_query).astype(jnp.bfloat16)
    key_rows = packed[:, D : 2 * D].astype(jnp.bfloat16)
    value_rows = (packed[:, 2 * D :] + bias_value).astype(jnp.bfloat16)
    query_heads, key_heads, value_heads = (
        lax.all_to_all(queries, "head", split_axis=1, concat_axis=0, tiled=True),
        lax.all_to_all(key_rows, "head", split_axis=1, concat_axis=0, tiled=True),
        lax.all_to_all(value_rows, "head", split_axis=1, concat_axis=0, tiled=True),
    )
    head_out, log_sums = attend(query_heads, key_heads, value_heads, lengths)
    attention = lax.all_to_all(head_out, "head", split_axis=0, concat_axis=1, tiled=True)
    branch_attend = fold_rows(attention, project_slab) + bias_proj
    residual_one = residual_zero + gating_one * branch_attend
    hidden_expand = modulate(residual_one, shift_two, scale_two).astype(jnp.bfloat16)
    widened = fold_rows(hidden_expand, expand_slab) + bias_hidden
    activated = jax.nn.gelu(widened, approximate=True).astype(jnp.bfloat16)
    branch_expand = fold_rows(activated, reduce_slab) + bias_output
    output = (residual_one + gating_two * branch_expand).astype(jnp.bfloat16)
    outer_grad = cotangent.astype(jnp.float32) * live_rows[:, None]
    gating_later = outer_grad * branch_expand
    closing_grad = (outer_grad * gating_two).astype(jnp.bfloat16)
    active_grad = back_cols(closing_grad, reduce_slab)
    gelu_value, gelu_pullback = jax.vjp(lambda inner: jax.nn.gelu(inner, approximate=True), widened)
    widened_grad = gelu_pullback(active_grad)[0].astype(jnp.bfloat16)
    hidden_grad = back_cols(widened_grad, expand_slab)
    later_value, later_pullback = jax.vjp(modulate, residual_one, shift_two, scale_two)
    residual_part, shift_later, scale_later = later_pullback(hidden_grad)
    middle_grad = outer_grad + residual_part
    gating_early = middle_grad * branch_attend
    branch_grad = (middle_grad * gating_one).astype(jnp.bfloat16)
    attend_grad = back_cols(branch_grad, project_slab).astype(jnp.bfloat16)
    heads_grad = lax.all_to_all(attend_grad, "head", split_axis=1, concat_axis=0, tiled=True)
    query_grad, keyrow_grad, value_grad = attend_back(
        query_heads, key_heads, value_heads, heads_grad, log_sums, lengths
    )
    query_back, keys_back, values_back = (
        lax.all_to_all(query_grad, "head", split_axis=0, concat_axis=1, tiled=True),
        lax.all_to_all(keyrow_grad, "head", split_axis=0, concat_axis=1, tiled=True),
        lax.all_to_all(value_grad, "head", split_axis=0, concat_axis=1, tiled=True),
    )
    packed_grad = jnp.concatenate([query_back, keys_back, values_back], axis=1)
    normed_grad = back_cols(packed_grad, attend_slab)
    early_value, early_pullback = jax.vjp(modulate, residual_zero, shift_one, scale_one)
    input_part, shift_early, scale_early = early_pullback(normed_grad)
    input_grad = middle_grad + input_part
    mod_token_grad = jnp.concatenate(
        [shift_early, scale_early, gating_early, shift_later, scale_later, gating_later], axis=1
    )
    mod_grad = lax.dot_general(
        pick_rows, mod_token_grad, (((0,), (0,)), ((), ())), precision=highest
    )
    mod_summed = lax.psum_scatter(mod_grad, "head", scatter_dimension=1, tiled=True)
    mod_rounded = mod_summed.astype(jnp.bfloat16)
    grad_mod = rows_seq(condition, mod_rounded)
    mod_slot = lax.dynamic_update_slice_in_dim(
        jnp.zeros((6 * D,), jnp.float32),
        jnp.sum(mod_rounded.astype(jnp.float32), axis=0),
        head_index * mod_width,
        0,
    )
    bias_share = jnp.concatenate(
        [
            mod_slot,
            jnp.sum(query_back.astype(jnp.float32), axis=0),
            jnp.sum(values_back.astype(jnp.float32), axis=0),
            jnp.sum(branch_grad.astype(jnp.float32), axis=0),
            jnp.sum(widened_grad.astype(jnp.float32), axis=0),
            jnp.sum(closing_grad.astype(jnp.float32), axis=0),
        ]
    )
    operand_pairs = (
        (hidden_attend, packed_grad),
        (attention, branch_grad),
        (hidden_expand, widened_grad),
        (activated, closing_grad),
    )
    term_slabs = tuple((rows_seq(left_side, right_side) for left_side, right_side in operand_pairs))
    reduced = (
        lax.psum_scatter(
            term_slabs[0].astype(jnp.bfloat16), "head", scatter_dimension=1, tiled=True
        ).astype(jnp.float32),
        lax.psum_scatter(
            term_slabs[1].astype(jnp.bfloat16), "head", scatter_dimension=1, tiled=True
        ).astype(jnp.float32),
        lax.psum_scatter(
            term_slabs[2].astype(jnp.bfloat16), "head", scatter_dimension=1, tiled=True
        ).astype(jnp.float32),
        lax.psum_scatter(
            term_slabs[3].astype(jnp.bfloat16), "head", scatter_dimension=1, tiled=True
        ).astype(jnp.float32),
    )
    grad_attend, grad_project, grad_expand, grad_reduce = reduced
    local_squares = jnp.sum(grad_mod * grad_mod) + sum(
        (jnp.sum(gradient * gradient) for gradient in reduced)
    )
    bias_total, square_total = lax.psum((bias_share, local_squares), ("seq", "head"))
    grad_norm = jnp.sqrt(square_total + jnp.sum(bias_total * bias_total))
    clip_factor = jnp.minimum(1.0, 1.0 / (grad_norm + 1e-06))
    correction = 1.0 - jnp.power(0.5, step_count.astype(jnp.float32))
    modulate_new = adam_update(
        modulate_master,
        modulate_first,
        modulate_second,
        grad_mod,
        0.5 * D ** (-0.5),
        clip_factor,
        correction,
    )
    attend_new = adam_update(
        attend_master,
        attend_first,
        attend_second,
        grad_attend,
        0.5 * D ** (-0.5),
        clip_factor,
        correction,
    )
    project_new = adam_update(
        project_master,
        project_first,
        project_second,
        grad_project,
        0.5 * D ** (-0.5),
        clip_factor,
        correction,
    )
    expand_new = adam_update(
        expand_master,
        expand_first,
        expand_second,
        grad_expand,
        0.5 * D ** (-0.5),
        clip_factor,
        correction,
    )
    reduce_new = adam_update(
        reduce_master,
        reduce_first,
        reduce_second,
        grad_reduce,
        0.5 * FF ** (-0.5),
        clip_factor,
        correction,
    )
    biases_new = adam_update(
        biases_master, biases_first, biases_second, bias_total, 0.1, clip_factor, correction
    )
    return (
        output,
        input_grad,
        grad_norm,
        modulate_new[0],
        modulate_new[1],
        modulate_new[2],
        attend_new[0],
        attend_new[1],
        attend_new[2],
        project_new[0],
        project_new[1],
        project_new[2],
        expand_new[0],
        expand_new[1],
        expand_new[2],
        reduce_new[0],
        reduce_new[1],
        reduce_new[2],
        biases_new[0],
        biases_new[1],
        biases_new[2],
    )


ALPHA = HEAD_DIM ** (-0.5) * math.log2(math.e)
GELU_A = math.sqrt(2.0 / math.pi)
GELU_B = 0.044715
BLOCK = FF // 16
BF, F32 = jnp.bfloat16, jnp.float32
ANY, VM = pl.ANY, pltpu.VMEM
PIECES = {"q": (144, 864, 48), "p": (72, 576, None), "u": (144, 1152, 48), "d": (288, 576, 96)}
NAMES = ("q", "p", "u", "d")
MESH = pl.DeviceIdType.MESH


def place():
    return tuple(lax.axis_index(a) for a in ("z", "x", "c", "y"))


def at_z(k):
    z = lax.axis_index("z")
    return (z, z + 1 - 2 * (z % 2), (z + 2) % 4, 3 - z)[k]


def rdma(src, dst, send, recv, to):
    return pltpu.make_async_remote_copy(
        src_ref=src, dst_ref=dst, send_sem=send, recv_sem=recv, device_id=to, device_id_type=MESH
    )


def partners():
    z, x, c, y = place()
    xn, yn, twin = (z, 1 - x, c, y), (z, x, c, 1 - y), (z, x, 1 - c, y)
    return xn, yn, twin, [(at_z(k), x, c, y) for k in range(4)]


def greet(others, swapped=False):
    z, x, c, y = place()
    barrier = pltpu.get_barrier_semaphore()
    for to in others:
        pl.semaphore_signal(barrier, inc=1, device_id=to, device_id_type=MESH)
    if swapped:

        @pl.when(c != y)
        def _():
            pl.semaphore_signal(barrier, inc=1, device_id=(z, x, y, c), device_id_type=MESH)

        pl.semaphore_wait(barrier, len(others) + (c + y) % 2)
    else:
        pl.semaphore_wait(barrier, len(others))


CHUNKS = (
    (0, 0, 80, 32),
    (0, 80, 64, 16),
    (1, 0, 72, None),
    (2, 0, 80, 32),
    (2, 80, 64, 16),
    (3, 0, 144, 48),
    (3, 144, 144, 48),
)


def parts_of(chunk, k):
    _, _, rows, cut = CHUNKS[chunk]
    if cut is None:
        return ((0, rows), None) if k == 0 else (None, (0, rows))
    return (0, cut), (cut, rows - cut)


def piece_at(full, w, y, zk, x, first, count):
    rows = PIECES[NAMES[w]][0]
    if count == 72:
        return full.at[y, zk * 2 + x]
    return full.at[y, pl.ds(pl.multiple_of((zk * 2 + x) * rows + first, 16), count)]


def matmul(left, right):
    return jnp.dot(left, right, preferred_element_type=F32)


def matmul_nt(left, right):
    return lax.dot_general(left, right, (((1,), (1,)), ((), ())), preferred_element_type=F32)


def matmul_tn(left, right):
    return lax.dot_general(left, right, (((0,), (0,)), ((), ())), preferred_element_type=F32)


class Gather:
    def __init__(self, own, full, sems):
        self.own, self.full = own, full
        self.zs, self.zr, self.xs, self.xr, self.ys, self.yr, self.fs, self.fr, self.ps, self.pr = sems
        self.sent = []

    def piece(self, w, flip_y, k, flip_x):
        z, x, c, y = place()
        weight, first, count, _ = CHUNKS[w]
        return piece_at(
            self.full[weight], weight, 1 - y if flip_y else y, at_z(k), 1 - x if flip_x else x, first, count
        )

    def source(self, w):
        weight, first, count, _ = CHUNKS[w]
        return self.own[weight].at[pl.ds(first, count)]

    def send(self, make):
        make().start()
        self.sent.append(make)

    def arrived(self, ref, s, r):
        rdma(ref, ref, s, r, partners()[0]).wait_recv()

    def start(self, w):
        def to_x():
            return rdma(self.source(w), self.piece(w, 0, 0, 0), self.xs.at[w, 0], self.xr.at[w, 0], partners()[0])

        def to_y():
            return rdma(self.source(w), self.piece(w, 0, 0, 0), self.ys.at[w, 0], self.yr.at[w, 0], partners()[1])

        def to_z(k):
            to = partners()[3][k]
            return rdma(self.source(w), self.piece(w, 0, 0, 0), self.zs.at[w, k], self.zr.at[w, k], to)

        self.send(to_x)
        self.send(to_y)
        for k in (1, 2, 3):
            self.send(functools.partial(to_z, k))

    def column(self, w, k):
        self.arrived(self.piece(w, 0, k, 0), self.zs.at[w, k], self.zr.at[w, k])

        def to_x():
            piece = self.piece(w, 0, k, 0)
            return rdma(piece, piece, self.xs.at[w, k], self.xr.at[w, k], partners()[0])

        def to_y():
            piece = self.piece(w, 0, k, 0)
            return rdma(piece, piece, self.ys.at[w, k], self.yr.at[w, k], partners()[1])

        self.send(to_x)
        self.send(to_y)

    def plane(self, w, k):
        spans = parts_of(w, k)

        def pass_on(i):
            part = self.piece(w, i, k, 1 - i).at[pl.ds(*spans[i])]
            return rdma(part, part, self.fs.at[w, k, i], self.fr.at[w, k, i], partners()[1 - i])

        self.arrived(self.piece(w, 0, k, 1), self.xs.at[w, k], self.xr.at[w, k])
        if k in (0, 2) and spans[0] is not None:
            self.send(functools.partial(pass_on, 0))
        self.arrived(self.piece(w, 1, k, 0), self.ys.at[w, k], self.yr.at[w, k])
        if k in (0, 2) and spans[1] is not None:
            self.send(functools.partial(pass_on, 1))

    def corner(self, w, k):
        for i, span in enumerate(parts_of(w, k)):
            if span is not None:
                part = self.piece(w, 1, k, 1).at[pl.ds(*span)]
                self.arrived(part, self.fs.at[w, k, i], self.fr.at[w, k, i])

        def to_pair():
            piece = self.piece(w, 1, k, 1)
            return rdma(piece, piece, self.ps.at[w, k], self.pr.at[w, k], partners()[3][1])

        self.send(to_pair)

    def last(self, w, k):
        self.arrived(self.piece(w, 1, k ^ 1, 1), self.ps.at[w, k], self.pr.at[w, k])

    def finish(self):
        for make in self.sent:
            make().wait_send()

    def steps(self):
        def each(method, chunks, ks):
            return [(method, i, k) for i in chunks for k in ks]

        column, plane, corner, last = self.column, self.plane, self.corner, self.last
        one = (0, 1)
        plan = [(self.start, 0), (self.start, 1), (self.start, 2)]
        plan += each(column, one, (1,)) + each(plane, one, (0,))
        plan += each(column, one, (2,)) + each(column, one, (3,)) + [(self.start, 3)]
        plan += each(corner, one, (0,)) + each(plane, one, (2,))
        plan += each(column, (2,), (1,)) + [(self.start, 4)]
        plan += each(plane, one, (1,)) + each(corner, one, (2,))
        plan += each(plane, (2,), (0,)) + each(column, (2,), (2, 3)) + each(column, (3,), (1,))
        plan += each(plane, one, (3,)) + each(last, one, (0, 2))
        count = len(CHUNKS)
        for t in range(-2, count + 4):
            wave = [(self.start, t + 2)] if t + 2 < count else []
            for lag, make in enumerate(
                (
                    lambda i: each(column, (i,), (1,)),
                    lambda i: each(plane, (i,), (0,)) + each(column, (i,), (2, 3)),
                    lambda i: each(corner, (i,), (0,)) + each(plane, (i,), (2, 1)),
                    lambda i: each(corner, (i,), (2,)) + each(plane, (i,), (3,)),
                    lambda i: each(last, (i,), (0, 2)),
                )
            ):
                if t >= 0 and 0 <= t - lag < count:
                    wave += make(t - lag)
            plan += [step for step in wave if step not in plan]
        return plan


def mod_steps(cond_ref, weight, bias, out_ref, lhs, bufs, s, r):
    conds, part, got_z, mid, got_x, near, got_c = bufs

    def hop(i):
        z, x, c, y = place()
        xn, yn, twin, zn = partners()
        if i == 0:
            pairs = [(conds.at[z, x, c], conds.at[z, x, c], twin)]
        elif i == 1:
            pairs = [(conds.at[z, x], conds.at[z, x], xn)]
        elif i == 2:
            pairs = [(conds.at[z], conds.at[z], zn[k]) for k in (1, 2, 3)]
        elif i == 3:
            pairs = [(part.at[at_z(k)], got_z.at[k - 1], zn[k]) for k in (1, 2, 3)]
        elif i == 4:
            pairs = [(mid.at[1 - x], got_x, xn)]
        elif i == 5:
            pairs = [(near.at[0], got_c, twin)]
        else:
            pairs = [(near.at[1, 1 - y], near.at[2, y], yn)]
        return [
            rdma(src, dst, s.at[i, n], r.at[i, n], to) for n, (src, dst, to) in enumerate(pairs)
        ]

    def go(i):
        for d in hop(i):
            d.start()

    def end(i):
        for d in hop(i):
            d.wait()

    def step(i):
        z, x, c, y = place()
        if i > 0:
            end(i - 1)
        if i == 0:
            conds[z, x, c] = cond_ref[...]
        elif i == 3:
            me = (z * 2 + x) * 2 + c
            for n in range(16):
                lhs[pl.ds(n, 1), :] = conds[n // 4, n // 2 % 2, n % 2, pl.ds(me, 1), :]
            for j in range(3):
                cols = slice(j * D, (j + 1) * D)
                result = matmul(lhs[:, :72].astype(BF), weight[:, cols].astype(BF))
                for n in range(16):
                    part[n // 4, n // 2 % 2, n % 2, :, cols] = result[n : n + 1]
        elif i == 4:
            mid[...] = part[z] + got_z[0] + got_z[1] + got_z[2]
        elif i == 5:
            near[0] = mid[x] + got_x[...]
        elif i == 6:
            near[1] = near[0] + got_c[...]
            near[2, y] = near[1, y]
        if i < 7:
            go(i)
        else:
            for n in range(2):
                out_ref[n] = near[2, n] + bias[:, n * 3456 : (n + 1) * 3456]

    return [functools.partial(step, i) for i in range(8)]


def normed_tile(value):
    average = jnp.mean(value, axis=-1, keepdims=True)
    centred = value - average
    spread = jnp.mean(centred * centred, axis=-1, keepdims=True)
    return centred * lax.rsqrt(spread + 1e-06)


def rounded(value):
    return value.astype(BF).astype(F32)


def pick(bucket, entries):
    return sum(
        jnp.where(bucket == float(i), float(e * (SIDE // 8)), 0.0) for i, e in enumerate(entries)
    )


def start_rows(tok, table, bucket, first, rows):
    wide = pick(bucket, col_units)
    spot = (first + lax.broadcasted_iota(jnp.int32, (rows, 1), 0)).astype(F32)
    lane = lax.broadcasted_iota(jnp.int32, (1, 64), 1).astype(F32)
    grid_row = jnp.where((spot >= lane * wide) & (spot < (lane + 1.0) * wide), 1.0, 0.0)
    left = spot - wide * jnp.sum(grid_row * lane, axis=1, keepdims=True)
    grid_col = jnp.where(left == lane, 1.0, 0.0)
    high = table.astype(BF)
    low = (table - high.astype(F32)).astype(BF)
    parts = [matmul(hot.astype(BF), high) + matmul(hot.astype(BF), low) for hot in (grid_row, grid_col)]
    return tok.astype(F32) + jnp.concatenate(parts, axis=1)


def forward_kernel(*refs):
    (tok, cot, bucket_in, table, att_m, proj_m, exp_m, red_m, mod_w, cond_in, bias_in) = refs[:11]
    gq, gp, gu, gd = full = refs[11:15]
    (mod_out, lhs, x0_out, dy_out, cl_out, h1_out, q_out, k_out, v_out) = refs[15:24]
    (attnt_out, lse_out, ba_out, x1_out, h2_out, der_out, bb_out, y_out, gred_out) = refs[24:33]
    (oq, op, ou, od, fq, tq, fu, tu) = refs[33:41]
    mod_bufs = refs[41:48]
    (xs, x0, dy, bucket, closing, h1, qa, ka, vt, attnt, attn) = refs[48:59]
    (ps, pr, ds, dr, acc, x1, h2, act, der, ba, bb, yo, gstage) = refs[59:72]
    (b_all, b_q, b_v, b_u) = refs[72:76]
    lsem = refs[76]
    gather_sems = refs[77:87]
    ms, mr, ws, wr, ts, tr, os, outs_sem, gsem = refs[87:96]
    z, x, c, y = place()
    xn, yn, twin, zn = partners()
    half = x0.shape[0]
    mine = pl.multiple_of(c * half, half)
    other = pl.multiple_of((1 - c) * half, half)
    gather = Gather((oq, op, ou, od), full, gather_sems)
    mods = mod_steps(cond_in, mod_w, b_all, mod_out, lhs, mod_bufs, ms, mr)
    greet([xn, yn, twin] + zn[1:], swapped=True)
    mods[0]()

    def split(master, width, f, t, i):
        count = master.shape[1] // (2 * width)
        sides = [
            jnp.concatenate(
                [master[:, (2 * j + p) * width : (2 * j + p + 1) * width] for j in range(count)], axis=1
            )
            for p in (0, 1)
        ]
        t[...] = jnp.where(c == 0, sides[1], sides[0])
        rdma(t, f.at[c], os.at[0, i], os.at[1, i], twin).start()
        f[c] = jnp.where(c == 0, sides[0], sides[1])

    def joined(f, t, i, piece):
        rdma(t, f.at[c], os.at[0, i], os.at[1, i], twin).wait()
        piece[...] = jnp.concatenate([f[0], f[1]], axis=0).astype(BF)

    split(att_m, HEAD_DIM, fq, tq, 0)
    mods[1]()
    split(exp_m, BLOCK, fu, tu, 1)
    mods[2]()
    joined(fq, tq, 0, oq)
    steps = gather.steps()
    done = [2]
    gather.start(0)
    gather.start(1)

    swap_to = (z, x, y, c)
    PART = 128
    moves = [(bucket_in, bucket)]
    for i in range(half // PART):
        moves.append((xs.at[pl.ds(i * PART, PART)], x0.at[pl.ds(i * PART, PART)]))
    for i in range(half // PART):
        moves.append((cot.at[pl.ds(i * PART, PART)], dy.at[pl.ds(i * PART, PART)]))

    def move(i):
        @pl.when(c != y)
        def _():
            rdma(*moves[i], ws.at[i], wr.at[i], swap_to).start()

        @pl.when(c == y)
        def _():
            pltpu.make_async_copy(*moves[i], ws.at[i]).start()

    def moved(i):
        @pl.when(c != y)
        def _():
            rdma(*moves[i], ws.at[i], wr.at[i], swap_to).wait()

        @pl.when(c == y)
        def _():
            pltpu.make_async_copy(*moves[i], ws.at[i]).wait()

    move(0)
    for i in range(half // PART):
        rows = slice(i * PART, (i + 1) * PART)
        xs[rows, :] = start_rows(
            tok[rows, :], table[...], bucket_in[0:1, 0:1], y * half + i * PART, PART
        ).astype(BF)
        move(1 + i)
    mods[3]()
    joined(fu, tu, 1, ou)
    op[...] = proj_m[...].astype(BF)
    od[...] = red_m[...].astype(BF)
    owns = [
        pltpu.make_async_copy(
            gather.own[w], piece_at(full[w], w, y, z, x, 0, PIECES[NAMES[w]][0]), lsem.at[w]
        )
        for w in range(4)
    ]
    for d in owns:
        d.start()
    b_all[...] = rounded(bias_in[...])

    def of_core(base, width, count):
        return jnp.concatenate(
            [
                jnp.where(
                    c == 0,
                    b_all[:, base + 2 * j * width : base + (2 * j + 1) * width],
                    b_all[:, base + (2 * j + 1) * width : base + (2 * j + 2) * width],
                )
                for j in range(count)
            ],
            axis=1,
        )

    b_q[...] = of_core(6 * D, HEAD_DIM, 8)
    b_v[...] = of_core(7 * D, HEAD_DIM, 8)
    b_u[...] = of_core(9 * D, BLOCK, 8)
    b_p = b_all.at[:, pl.ds(8 * D, D)]
    b_d = b_all.at[:, pl.ds(9 * D + FF, D)]

    def tick(n):
        for f, *a in steps[done[0] : done[0] + n]:
            f(*a)
        done[0] = min(done[0] + n, len(steps))

    def tick_until(chunk):
        last = max(i for i, s in enumerate(steps) if s[0] == gather.last and s[1] == chunk)
        tick(max(0, last + 1 - done[0]))

    tick(3)
    mods[4]()
    tick(3)
    mods[5]()
    tick(2)
    mods[6]()
    tick(2)
    mods[7]()
    for i in range(1 + half // PART):
        moved(i)

    def vec(i):
        return mod_out[i // 3, :, (i % 3) * D : (i % 3 + 1) * D]

    TILE, WIDE = 128, 256
    tiles = half // TILE

    def own_tile(ref, t):
        return ref.at[pl.ds(pl.multiple_of(mine + t * TILE, TILE), TILE)]

    def give(ref, t, i):
        part = own_tile(ref, t)
        return rdma(part, part, ts.at[i, t], tr.at[i, t], twin)

    def norm_one(t, _):
        rows = pl.ds(pl.multiple_of(t * TILE, TILE), TILE)
        value = normed_tile(x0[rows, :].astype(F32)) * (1.0 + vec(1)) + vec(0)
        own_tile(h1, t)[...] = value.astype(BF)
        give(h1, t, 0).start()
        return 0

    for t in range(tiles):
        norm_one(t, 0)
        tick(1)
    tick_until(1)
    for i in range(half // PART):
        move(1 + half // PART + i)

    def both_got(ref, i):
        for t in range(tiles):
            give(ref, t, i).wait_send()
            part = ref.at[pl.ds(pl.multiple_of(other + t * TILE, TILE), TILE)]
            rdma(part, part, ts.at[i, t], tr.at[i, t], twin).wait_recv()

    out_copies = []

    def put(src, dst):
        d = pltpu.make_async_copy(src, dst, outs_sem.at[len(out_copies)])
        d.start()
        out_copies.append(d)

    def load(src, dst, i):
        d = pltpu.make_async_copy(src, dst, lsem.at[i])
        d.start()
        d.wait()

    owns[0].wait()
    live = pick(bucket[0:1, 0:1], row_units) * pick(bucket[0:1, 0:1], col_units)
    lane = lax.broadcasted_iota(jnp.int32, (1, 128), 1)

    def qkv(weight):
        load(gq, weight, 4)

        def rows_of(i, _):
            start = pl.multiple_of(i * 256, 256)
            rows = pl.ds(start, 256)
            left = h1[rows, :]
            one = matmul(left, weight[0])
            two = matmul(left, weight[1])
            spot = (start + lax.broadcasted_iota(jnp.int32, (256, 1), 0)).astype(F32)
            mask = jnp.where(lane == HEAD_DIM, jnp.where(spot < live, 0.0, -1e30), 0.0)
            ones = jnp.where(lane == HEAD_DIM, 1.0, 0.0)
            for j in range(8):
                cols = slice(j * HEAD_DIM, (j + 1) * HEAD_DIM)
                query = one[:, cols] + b_q[:, cols]
                key = one[:, 576 + j * 72 : 648 + j * 72] if j < 4 else two[:, j * 72 - 288 : j * 72 - 216]
                value = two[:, 288 + j * 72 : 360 + j * 72] + b_v[:, cols]
                fill = jnp.zeros((256, 56), F32)
                qa[j, rows, :] = (jnp.concatenate([query, fill], axis=1) + ones).astype(BF)
                ka[j, rows, :] = (jnp.concatenate([key, fill], axis=1) + mask).astype(BF)
                vt[j, :, rows] = value.T.astype(BF)
            return 0

        rows_of(2 * c, 0)
        tick(2)
        rows_of(2 * c + 1, 0)
        both_got(h1, 0)
        tick(2)
        rows_of(2 - 2 * c, 0)
        tick(2)
        rows_of(3 - 2 * c, 0)

    pl.run_scoped(qkv, VM((2, D, 864), BF))
    put(h1, h1_out)
    tick(1)
    put(qa, q_out)
    put(ka, k_out)
    put(vt, v_out)

    def head(j, _):
        def queries(i, _):
            rows = pl.ds(pl.multiple_of(i * 256, 256), 256)
            scores = matmul_nt(ka[j], qa[j, rows, :]) * ALPHA
            top = jnp.max(scores, axis=0, keepdims=True)
            prob = jnp.exp2(scores - top)
            total = jnp.sum(prob, axis=0, keepdims=True)
            result = matmul(vt[j], prob.astype(BF)) * (1.0 / total)
            attnt[j, :, rows] = result
            lse_out[j, :, rows] = top + jnp.log2(total)
            return 0

        lax.fori_loop(0, 4, queries, 0)
        return 0

    for j in range(8):
        head(j, 0)
        tick(3)

    for i in range(half // PART):
        moved(1 + half // PART + i)

    def close(t, _):
        rows = pl.ds(pl.multiple_of(t * TILE, TILE), TILE)
        spot = (mine + t * TILE + lax.broadcasted_iota(jnp.int32, (TILE, 1), 0)).astype(F32)
        outer = jnp.where(spot < live, dy[rows, :].astype(F32), 0.0)
        dy[rows, :] = outer.astype(BF)
        own_tile(closing, t)[...] = (outer * vec(5)).astype(BF)
        give(closing, t, 1).start()
        return 0

    lax.fori_loop(0, tiles, close, 0)
    put(attnt, attnt_out)
    tick_until(2)
    owns[1].wait()

    def proj(weight, stage, raw):
        load(gp, raw, 5)
        for i in (0, 1):
            for h in range(8):
                stage[h * 72 : h * 72 + 72, :] = raw[i, h].astype(F32)
            weight[i] = stage[...].astype(BF)

        def attn_rows(i, _):
            rows = pl.ds(pl.multiple_of(i * 256, 256), 256)
            value = jnp.concatenate([attnt[j, :, rows] for j in range(8)], axis=0)
            attn[rows, :] = value.T.astype(BF)
            return 0

        lax.fori_loop(0, 4, attn_rows, 0)

        def for_twin(t, _):
            rows = pl.ds(pl.multiple_of(t * WIDE, WIDE), WIDE)
            left = attn[pl.ds(pl.multiple_of(other + t * WIDE, WIDE), WIDE), :]
            for i in (0, 1):
                ps[rows, i * 576 : (i + 1) * 576] = matmul(left, weight[i]).astype(BF)
            rdma(ps.at[rows], pr.at[rows], ts.at[2, t], tr.at[2, t], twin).start()
            return 0

        for t in range(half // WIDE):
            for_twin(t, 0)
            tick(1)

        def for_me(t, _):
            rows = pl.ds(pl.multiple_of(t * WIDE, WIDE), WIDE)
            left = attn[pl.ds(pl.multiple_of(mine + t * WIDE, WIDE), WIDE), :]
            for i in (0, 1):
                acc[rows, i * 576 : (i + 1) * 576] = matmul(left, weight[i])
            return 0

        for t in range(half // WIDE):
            for_me(t, 0)
            tick(1)

    pl.run_scoped(proj, VM((2, 576, 576), BF), VM((576, 576), F32), VM((2, 8, 72, 576), BF))

    def middle(t, _):
        rows = pl.ds(pl.multiple_of(t * TILE, TILE), TILE)
        branch = acc[rows, :] + pr[rows, :].astype(F32) + b_p[...]
        ba[rows, :] = branch.astype(BF)
        value = x0[rows, :].astype(F32) + vec(2) * branch
        x1[rows, :] = value
        own_tile(h2, t)[...] = (normed_tile(value) * (1.0 + vec(4)) + vec(3)).astype(BF)
        give(h2, t, 3).start()
        return 0

    def half_got(src, dst, i, t):
        rows = pl.ds(t * WIDE, WIDE)
        rdma(src.at[rows], dst.at[rows], ts.at[i, t], tr.at[i, t], twin).wait()

    for t in range(tiles):
        if t % 2 == 0:
            half_got(ps, pr, 2, t // 2)
        middle(t, 0)
    put(ba, ba_out)
    put(x1, x1_out)
    put(x0, x0_out)
    put(dy, dy_out)
    tick_until(4)
    owns[2].wait()
    both_got(h2, 3)
    both_got(closing, 1)
    put(h2, h2_out)
    put(closing, cl_out)

    def up(weight):
        load(gu, weight, 6)

        def rows_of(n, _):
            rows = pl.ds(pl.multiple_of(n * 128, 128), 128)
            left = h2[rows, :]
            for i in (0, 1):
                cols = slice(i * D, (i + 1) * D)
                u = matmul(left, weight[i]) + b_u[:, cols]
                square = u * u
                bent = jnp.tanh(GELU_A * u * (1.0 + GELU_B * square))
                act[rows, cols] = (0.5 * u * (1.0 + bent)).astype(BF)
                slope = (0.5 * GELU_A) * u * (1.0 - bent * bent) * (1.0 + 3.0 * GELU_B * square)
                der[rows, cols] = (0.5 * (1.0 + bent) + slope).astype(BF)
            return 0

        for n in range(8):
            rows_of(n, 0)
            tick(1)

    pl.run_scoped(up, VM((2, D, D), BF))
    put(der, der_out)

    gouts = []
    for t in range(6):
        slot = t % 2
        if t >= 2:
            gouts[t - 2].wait()
        left = act[:, t * 384 : (t + 1) * 384]
        for i in (0, 1):
            gstage[slot, i] = matmul_tn(left, closing[:, i * 576 : (i + 1) * 576]).astype(BF)
        d = pltpu.make_async_copy(
            gstage.at[slot], gred_out.at[:, pl.ds(t * 384, 384)], gsem.at[slot]
        )
        d.start()
        gouts.append(d)
        tick(2)
    for d in gouts[-2:]:
        d.wait()
    tick(len(steps))
    owns[3].wait()

    def down(weight):
        load(gd, weight, 7)

        def for_twin(t, _):
            rows = pl.ds(pl.multiple_of(t * WIDE, WIDE), WIDE)
            left = act[pl.ds(pl.multiple_of(other + t * WIDE, WIDE), WIDE), :]
            for i in (0, 1):
                ds[rows, i * 576 : (i + 1) * 576] = matmul(left, weight[i]).astype(BF)
            rdma(ds.at[rows], dr.at[rows], ts.at[4, t], tr.at[4, t], twin).start()
            return 0

        for t in range(half // WIDE):
            for_twin(t, 0)
            tick(1)

        def for_me(t, _):
            rows = pl.ds(pl.multiple_of(t * WIDE, WIDE), WIDE)
            left = act[pl.ds(pl.multiple_of(mine + t * WIDE, WIDE), WIDE), :]
            for i in (0, 1):
                acc[rows, i * 576 : (i + 1) * 576] = matmul(left, weight[i])
            return 0

        for t in range(half // WIDE):
            for_me(t, 0)
            tick(1)

    pl.run_scoped(down, VM((2, 2304, 576), BF))

    def finish(t, _):
        rows = pl.ds(pl.multiple_of(t * TILE, TILE), TILE)
        branch = acc[rows, :] + dr[rows, :].astype(F32) + b_d[...]
        bb[rows, :] = branch.astype(BF)
        yo[rows, :] = (x1[rows, :] + vec(5) * branch).astype(BF)
        return 0

    for t in range(tiles):
        if t % 2 == 0:
            half_got(ds, dr, 4, t // 2)
        finish(t, 0)
    put(bb, bb_out)
    put(yo, y_out)
    for d in out_copies:
        d.wait()
    gather.finish()


def forward_block(tokens, cotangent, bucket, table, masters, modulate_master, cond, biases):
    shapes = {
        "gq": (2, D, 864),
        "gp": (2, 8, 72, 576),
        "gu": (2, D, D),
        "gd": (2, 2304, 576),
    }
    half = tokens.shape[0]
    rows = 2 * half
    out_shape, out_specs = [], []

    def out(shape, dtype, space=ANY):
        out_shape.append(jax.ShapeDtypeStruct(shape, dtype))
        out_specs.append(pl.BlockSpec(memory_space=space))

    for s in shapes.values():
        out(s, BF)
    out((2, 1, 3456), F32, VM)
    out((16, 128), F32, VM)
    out((half, D), BF)
    out((half, D), BF)
    out((rows, D), BF)
    out((rows, D), BF)
    out((8, rows, 128), BF)
    out((8, rows, 128), BF)
    out((8, 72, rows), BF)
    out((8, 72, rows), F32)
    out((8, 1, rows), F32, VM)
    out((half, D), BF)
    out((half, D), F32)
    out((rows, D), BF)
    out((rows, 2304), BF)
    out((half, D), BF)
    out((half, D), BF)
    out((2, 2304, 576), BF)
    dma = pltpu.SemaphoreType.DMA
    scratch = [
        VM((144, 864), BF),
        VM((72, 576), BF),
        VM((144, D), BF),
        VM((288, 576), BF),
        VM((2, 72, 864), F32),
        VM((72, 864), F32),
        VM((2, 72, D), F32),
        VM((72, D), F32),
        VM((4, 2, 2, 16, 128), F32),
        VM((4, 2, 2, 1, 3456), F32),
        VM((3, 2, 2, 1, 3456), F32),
        VM((2, 2, 1, 3456), F32),
        VM((2, 1, 3456), F32),
        VM((3, 2, 1, 3456), F32),
        VM((2, 1, 3456), F32),
        VM((half, D), BF),
        VM((half, D), BF),
        VM((half, D), BF),
        VM((8, 128), F32),
        VM((rows, D), BF),
        VM((rows, D), BF),
        VM((8, rows, 128), BF),
        VM((8, rows, 128), BF),
        VM((8, 72, rows), BF),
        VM((8, 72, rows), F32),
        VM((rows, 576), BF),
        VM((half, D), BF),
        VM((half, D), BF),
        VM((half, D), BF),
        VM((half, D), BF),
        VM((half, D), F32),
        VM((half, D), F32),
        VM((rows, D), BF),
        VM((rows, 2304), BF),
        VM((rows, 2304), BF),
        VM((half, D), BF),
        VM((half, D), BF),
        VM((half, D), BF),
        VM((2, 2, 384, 576), BF),
        VM((1, 14 * D), F32),
        VM((1, 576), F32),
        VM((1, 576), F32),
        VM((1, 2304), F32),
        dma((8,)),
    ]
    n = len(CHUNKS)
    scratch += [dma((n, 4))] * 6 + [dma((n, 4, 2))] * 2 + [dma((n, 4))] * 2
    scratch += [
        dma((7, 3)),
        dma((7, 3)),
        dma((9,)),
        dma((9,)),
        dma((5, 4)),
        dma((5, 4)),
        dma((2, 2)),
        dma((20,)),
        dma((2,)),
    ]
    vm = pl.BlockSpec(memory_space=VM)
    hbm = pl.BlockSpec(memory_space=ANY)
    return pl.pallas_call(
        forward_kernel,
        out_shape=out_shape,
        in_specs=[vm, hbm] + [vm] * 9,
        out_specs=out_specs,
        scratch_shapes=scratch,
        compiler_params=pltpu.CompilerParams(
            collective_id=0, has_side_effects=True, vmem_limit_bytes=60 * 2**20
        ),
        name="forward_block",
    )(tokens, cotangent, bucket, table, *masters, modulate_master, cond, biases)


class Scatter:
    def __init__(self, grads, boxes, outs, sems):
        self.grads, self.outs = grads, outs
        self.pair_box, self.diag_box, self.x_box, self.y_box, self.z_box = boxes
        self.ps, self.pr, self.fs, self.fr, self.xs, self.xr, self.ys, self.yr, self.zs, self.zr = sems
        self.sent = []

    def piece(self, i, flip_y, k, flip_x):
        z, x, c, y = place()
        weight, first, count, _ = CHUNKS[i]
        return piece_at(
            self.grads[weight], weight, 1 - y if flip_y else y, at_z(k), 1 - x if flip_x else x, first, count
        )

    def box(self, boxes, i, n):
        weight, first, count, _ = CHUNKS[i]
        return boxes[weight].at[n, pl.ds(first, count)]

    def send(self, make):
        make().start()
        self.sent.append(make)

    def arrived(self, ref, s, r):
        rdma(ref, ref, s, r, partners()[0]).wait_recv()

    def add(self, target, *others):
        rows = target.shape[0]
        step = 16 if rows % 16 == 0 else rows

        def some(n, _):
            at = pl.ds(pl.multiple_of(n * step, step), step) if rows != step else slice(None)
            total = target[at, :].astype(F32)
            for o in others:
                total = total + o[at, :].astype(F32)
            target[at, :] = total.astype(BF)
            return 0

        if rows == step:
            some(0, 0)
        else:
            lax.fori_loop(0, rows // step, some, 0)

    def across(self, i, k, by_y):
        if by_y:
            return rdma(
                self.piece(i, 1, k, 0), self.box(self.y_box, i, k), self.ys.at[i, k], self.yr.at[i, k], partners()[1]
            )
        return rdma(
            self.piece(i, 0, k, 1), self.box(self.x_box, i, k), self.xs.at[i, k], self.xr.at[i, k], partners()[0]
        )

    def start(self, i):
        def to_pair(k):
            return rdma(
                self.piece(i, 1, k ^ 1, 1),
                self.box(self.pair_box, i, k // 2),
                self.ps.at[i, k],
                self.pr.at[i, k],
                partners()[3][1],
            )

        for k in (0, 2):
            self.send(functools.partial(to_pair, k))
        for k in (1, 3):
            for by_y in (0, 1):
                self.send(functools.partial(self.across, i, k, by_y))

    def corner(self, i, k):
        box = self.box(self.pair_box, i, k // 2)
        self.arrived(box, self.ps.at[i, k], self.pr.at[i, k])
        self.add(self.piece(i, 1, k, 1), box)
        spans = parts_of(i, k)

        def part(n):
            return rdma(
                self.piece(i, 1, k, 1).at[pl.ds(*spans[n])],
                self.box(self.diag_box, i, k // 2).at[pl.ds(*spans[n])],
                self.fs.at[i, k, n],
                self.fr.at[i, k, n],
                partners()[1 - n],
            )

        for n in (0, 1):
            if spans[n] is not None:
                self.send(functools.partial(part, n))

    def plane(self, i, k):
        spans = parts_of(i, k)
        for n in (0, 1):
            if spans[n] is not None:
                part = self.box(self.diag_box, i, k // 2).at[pl.ds(*spans[n])]
                self.arrived(part, self.fs.at[i, k, n], self.fr.at[i, k, n])
                self.add(self.piece(i, n, k, 1 - n).at[pl.ds(*spans[n])], part)
            self.send(functools.partial(self.across, i, k, n))

    def both(self, i, k):
        boxes = []
        for boxes_of, s, r in ((self.x_box, self.xs, self.xr), (self.y_box, self.ys, self.yr)):
            box = self.box(boxes_of, i, k)
            self.arrived(box, s.at[i, k], r.at[i, k])
            boxes.append(box)
        return boxes

    def column(self, i, k):
        self.add(self.piece(i, 0, k, 0), *self.both(i, k))

        def along():
            return rdma(
                self.piece(i, 0, k, 0),
                self.box(self.z_box, i, k - 1),
                self.zs.at[i, k],
                self.zr.at[i, k],
                partners()[3][k],
            )

        self.send(along)

    def last(self, i):
        weight, first, count, _ = CHUNKS[i]
        boxes = self.both(i, 0)
        for k in (1, 2, 3):
            box = self.box(self.z_box, i, k - 1)
            self.arrived(box, self.zs.at[i, k], self.zr.at[i, k])
            boxes.append(box)
        total = self.piece(i, 0, 0, 0)[...].astype(F32)
        for box in boxes:
            total = total + box[...].astype(F32)
        self.outs[weight][first : first + count, :] = total

    def finish(self):
        for make in self.sent:
            make().wait_send()

    def steps(self, i):
        return (
            [(self.start, i), (self.corner, i, 0), (self.corner, i, 2)],
            [(self.plane, i, 0), (self.plane, i, 2), (self.column, i, 1)],
            [(self.column, i, 3), (self.column, i, 2)],
            [(self.last, i)],
        )


def total_steps(dm, bs, lhs, mods, bufs, gmod, bias_out, s, r):
    dmt, got_m, got_b, sb, got_z, near = bufs

    def hop(i):
        z, x, c, y = place()
        xn, yn, twin, zn = partners()
        if i == 0:
            pairs = [(dm, got_m, twin), (bs, got_b.at[0], twin)]
        elif i == 1:
            pairs = [(dmt.at[1 - y], mods.at[z, x, y], yn), (sb.at[0], got_b.at[1], yn)]
        elif i == 2:
            pairs = [(mods.at[z, x], mods.at[z, x], xn), (sb.at[1], got_b.at[2], xn)]
        elif i == 3:
            pairs = [(mods.at[z], mods.at[z], zn[k]) for k in (1, 2, 3)]
            pairs += [(sb.at[2], got_z.at[k - 1], zn[k]) for k in (1, 2, 3)]
        else:
            pairs = [(near.at[0], near.at[1], yn)]
        return [
            rdma(src, dst, s.at[i, n], r.at[i, n], to) for n, (src, dst, to) in enumerate(pairs)
        ]

    def step(i):
        z, x, c, y = place()
        if i > 0:
            for d in hop(i - 1):
                d.wait()
        if i == 1:
            dmt[...] = rounded(dm[...] + got_m[...])
            mods[z, x, y] = dmt[y]
            sb[0] = bs[...] + got_b[0]
        elif i == 2:
            sb[1] = sb[0] + got_b[1]
        elif i == 3:
            sb[2] = sb[1] + got_b[2]
        elif i == 4:
            rows = [mods[n // 4, n // 2 % 2, n % 2] for n in range(16)]
            total = rows[0]
            for row in rows[1:]:
                total = total + row
            near[0] = total
            bias_out[:, 6 * D :] = (sb[2] + got_z[0]) + (got_z[1] + got_z[2])
            left = lhs[:, :72].astype(BF)
            right = jnp.concatenate(rows, axis=0).astype(BF)
            for j in range(3):
                cols = slice(j * D, (j + 1) * D)
                gmod[:, cols] = matmul_tn(left, right[:, cols])
        elif i == 5:
            for n in (0, 1):
                bias_out[:, n * 3456 : (n + 1) * 3456] = jnp.where(y == n, near[0], near[1])
        if i < 5:
            for d in hop(i):
                d.start()

    return [functools.partial(step, i) for i in range(6)]


def backward_kernel(*refs):
    gq, gp, gu, gd, mod, lhs = refs[:6]
    (x0_in, dy_in, cl_in, h1_in, q_in, k_in, v_in, at_in, lse) = refs[6:15]
    (ba_in, x1_in, h2_in, der_in, bb_in, y_in, gred) = refs[15:22]
    (out, ig_out, s_att, s_proj, s_exp, s_red, gmod, bias_out, norm_out) = refs[22:31]
    grads = refs[31:35]
    boxes = [refs[35 + 4 * i : 39 + 4 * i] for i in range(5)]
    fq, fu, gotq, gotu = refs[55:59]
    dba, dx1, ps, pr, dm, bs, mods = refs[59:66]
    total_bufs = refs[66:72]
    sq = refs[72]
    lsem = refs[73]
    scatter_sems = refs[74:84]
    ts, tr, ws, wr, hs, hr, ns, nr = refs[84:92]
    z, x, c, y = place()
    xn, yn, twin, zn = partners()
    half = dx1.shape[0]
    mine = pl.multiple_of(c * half, half)
    other = pl.multiple_of((1 - c) * half, half)
    scatter = Scatter(grads, boxes, (fq, s_proj, fu, s_red), scatter_sems)
    hops = total_steps(dm, bs, lhs, mods, total_bufs, gmod, bias_out, hs, hr)
    pltpu.make_async_copy(gred, grads[3], lsem.at[0]).start()
    greet([xn, yn, twin] + zn[1:], swapped=True)
    dm[...] = jnp.zeros_like(dm)
    bs[...] = jnp.zeros_like(bs)
    TILE, WIDE = 128, 256
    swap_to = (z, x, y, c)

    def vec(i):
        return mod[i // 3, :, (i % 3) * D : (i % 3 + 1) * D]

    def add_mod(i, value):
        cols = slice((i % 3) * D, (i % 3 + 1) * D)
        dm[i // 3, :, cols] = dm[i // 3, :, cols] + jnp.sum(value, axis=0, keepdims=True)

    def add_bias(at, value):
        cols = slice(at, at + value.shape[1])
        bs[:, cols] = bs[:, cols] + value

    def load(src, dst, i):
        d = pltpu.make_async_copy(src, dst, lsem.at[i])
        d.start()
        return d

    queue = []

    def tick(n):
        for _ in range(min(n, len(queue))):
            f, *a = queue.pop(0)
            f(*a)

    def moves(i):
        if i == 0:
            return y_in, out
        rows = pl.ds((i - 1) * TILE, TILE)
        return dba.at[rows], ig_out.at[rows]

    def move(i):
        @pl.when(c != y)
        def _():
            rdma(*moves(i), ws.at[i], wr.at[i], swap_to).start()

        @pl.when(c == y)
        def _():
            pltpu.make_async_copy(*moves(i), ws.at[i]).start()

    def moved(i):
        @pl.when(c != y)
        def _():
            rdma(*moves(i), ws.at[i], wr.at[i], swap_to).wait()

        @pl.when(c == y)
        def _():
            pltpu.make_async_copy(*moves(i), ws.at[i]).wait()

    load_d = pltpu.make_async_copy(gred, grads[3], lsem.at[0])
    load_d.wait()
    scatter.start(5)
    scatter.start(6)
    five, six = scatter.steps(5), scatter.steps(6)
    queue += five[0][1:] + six[0][1:] + five[1] + six[1] + five[2] + six[2] + five[3] + six[3]

    def own_tile(ref, t):
        return ref.at[pl.ds(pl.multiple_of(mine + t * TILE, TILE), TILE)]

    def widen(du):
        def through(weight, closing, der):
            loads = [load(gd, weight, 1), load(cl_in, closing, 2)]
            ders = [load(der_in.at[pl.ds(0, TILE)], der.at[0], 3)]
            for d in loads:
                d.wait()
            sums = jnp.zeros((1, 2304), F32)
            for n in range(8):
                rows = slice(n * TILE, (n + 1) * TILE)
                if n < 7:
                    ders.append(load(der_in.at[pl.ds((n + 1) * TILE, TILE)], der.at[(n + 1) % 2], 3 + (n + 1) % 2))
                left = closing[rows, :]
                value = matmul_nt(left[:, :576], weight[0]) + matmul_nt(left[:, 576:], weight[1])
                ders[n].wait()
                value = (value * der[n % 2].astype(F32)).astype(BF)
                du[rows, :] = value
                sums = sums + jnp.sum(value.astype(F32), axis=0, keepdims=True)
                tick(1)
            for j in range(8):
                block = sums[:, j * BLOCK : (j + 1) * BLOCK]
                for p in (0, 1):
                    add_bias(3 * D + (2 * j + p) * BLOCK, jnp.where(c == p, block, 0.0))

        pl.run_scoped(through, VM((2, 2304, 576), BF), VM((2 * half, D), BF), VM((2, TILE, 2304), BF))

        def expand_grad(h2):
            load(h2_in, h2, 2).wait()
            for t in range(3):
                left = h2[:, t * 384 : (t + 1) * 384]
                for i in (0, 1):
                    grads[2][i, t * 384 : (t + 1) * 384, :] = matmul_tn(
                        left, du[:, i * D : (i + 1) * D]
                    ).astype(BF)
                    tick(1)

        pl.run_scoped(expand_grad, VM((2 * half, D), BF))
        scatter.start(3)
        scatter.start(4)
        three, four = scatter.steps(3), scatter.steps(4)
        queue.extend(three[0][1:] + four[0][1:] + three[1] + four[1] + three[2] + four[2] + three[3] + four[3])
        move(0)

        def back(weight):
            load(gu, weight, 1).wait()

            def product(start):
                left = du[pl.ds(start, WIDE), :]
                return matmul_nt(left[:, :D], weight[0]) + matmul_nt(left[:, D:], weight[1])

            for t in range(half // WIDE):
                rows = pl.ds(t * WIDE, WIDE)
                ps[rows, :] = product(pl.multiple_of(other + t * WIDE, WIDE)).astype(BF)
                rdma(ps.at[rows], pr.at[rows], ts.at[0, t], tr.at[0, t], twin).start()
                tick(1)
            for t in range(half // WIDE):
                dx1[pl.ds(t * WIDE, WIDE), :] = product(pl.multiple_of(mine + t * WIDE, WIDE))
                tick(1)

        pl.run_scoped(back, VM((2, D, D), BF))

    pl.run_scoped(widen, VM((2 * half, 2304), BF))

    def half_got(i, t):
        rows = pl.ds(t * WIDE, WIDE)
        rdma(ps.at[rows], pr.at[rows], ts.at[i, t], tr.at[i, t], twin).wait()

    def norm_back(value, scaling, gradient):
        average = jnp.mean(value, axis=-1, keepdims=True)
        centred = value - average
        inverse = lax.rsqrt(jnp.mean(centred * centred, axis=-1, keepdims=True) + 1e-06)
        normed = centred * inverse
        inner = gradient * (1.0 + scaling)
        part = inner - jnp.mean(inner, axis=-1, keepdims=True)
        part = part - normed * jnp.mean(inner * normed, axis=-1, keepdims=True)
        return part * inverse, normed

    def middle(x1, dy, ba, bb):
        loads = [load(x1_in, x1, 1), load(dy_in, dy, 2), load(ba_in, ba, 3), load(bb_in, bb, 4)]
        for d in loads:
            d.wait()
        for t in range(half // TILE):
            if t % 2 == 0:
                half_got(0, t // 2)
            rows = slice(t * TILE, (t + 1) * TILE)
            gradient = dx1[rows, :] + pr[rows, :].astype(F32)
            part, normed = norm_back(x1[rows, :], vec(4), gradient)
            add_mod(3, gradient)
            add_mod(4, gradient * normed)
            outer = dy[rows, :].astype(F32)
            add_mod(5, outer * bb[rows, :].astype(F32))
            add_bias(9216 - D, jnp.sum(rounded(outer * vec(5)), axis=0, keepdims=True))
            total = outer + part
            dx1[rows, :] = total
            add_mod(2, total * ba[rows, :].astype(F32))
            branch = (total * vec(2)).astype(BF)
            own_tile(dba, t)[...] = branch
            tile = own_tile(dba, t)
            rdma(tile, tile, ts.at[1, t], tr.at[1, t], twin).start()
            add_bias(2 * D, jnp.sum(branch.astype(F32), axis=0, keepdims=True))
            tick(1)

    pl.run_scoped(middle, VM((half, D), F32), VM((half, D), BF), VM((half, D), BF), VM((half, D), BF))

    def attention(dot, dqkv):
        def project(weight, stage, raw, attnt, attn):
            loads = [load(gp, raw, 1), load(at_in, attnt, 2)]
            for d in loads:
                d.wait()
            for i in (0, 1):
                for h in range(8):
                    stage[h * 72 : h * 72 + 72, :] = raw[i, h].astype(F32)
                weight[i] = stage[...].astype(BF)
            attn[...] = jnp.concatenate([attnt[h] for h in range(8)], axis=0).astype(BF)
            for t in range(half // TILE):
                tile = own_tile(dba, t)
                rdma(tile, tile, ts.at[1, t], tr.at[1, t], twin).wait_send()
                part = dba.at[pl.ds(pl.multiple_of(other + t * TILE, TILE), TILE)]
                rdma(part, part, ts.at[1, t], tr.at[1, t], twin).wait_recv()
            for n in range(4):
                rows = slice(n * WIDE, (n + 1) * WIDE)
                right = dba[rows, :]
                value = matmul_nt(weight[0], right[:, :576]) + matmul_nt(weight[1], right[:, 576:])
                for h in range(8):
                    dot[h, :, rows] = value[h * 72 : h * 72 + 72, :].astype(BF)
                tick(1)
            for i in (0, 1):
                stage[...] = matmul(attn[...], dba[:, i * 576 : (i + 1) * 576])
                for h in range(8):
                    grads[1][i, h] = stage[h * 72 : h * 72 + 72, :].astype(BF)

        pl.run_scoped(
            project,
            VM((2, 576, 576), BF),
            VM((576, 576), F32),
            VM((2, 8, 72, 576), BF),
            VM((8, 72, 2 * half), F32),
            VM((576, 2 * half), BF),
        )
        scatter.start(2)
        two = scatter.steps(2)
        queue.extend(two[0][1:] + two[1] + two[2] + two[3])

        def heads(qa, ka, vt, at, dk, dv, dq):
            def fetch(h):
                n = h % 2
                return [
                    load(src.at[h], dst.at[n], 1 + 4 * n + m)
                    for m, (src, dst) in enumerate(((q_in, qa), (k_in, ka), (v_in, vt), (at_in, at)))
                ]

            coming = fetch(0)
            for h in range(8):
                n = h % 2
                for d in coming:
                    d.wait()
                if h < 7:
                    coming = fetch(h + 1)
                value = vt[n].T
                key_t = ka[n, :, :72].T
                inner = jnp.sum(at[n] * dot[h].astype(F32), axis=0, keepdims=True)
                dk[...] = jnp.zeros_like(dk)
                dv[...] = jnp.zeros_like(dv)
                for i in range(4):
                    rows = slice(i * 256, (i + 1) * 256)
                    query = qa[n, rows, :]
                    grad = dot[h, :, rows]
                    scores = matmul_nt(ka[n], query)
                    prob = jnp.exp2(scores * ALPHA - lse[h, :, rows])
                    change = matmul(value, grad) - inner[:, rows]
                    dscore = (prob * change).astype(BF)
                    dv[...] += matmul_nt(grad, prob.astype(BF))
                    dk[...] += matmul_nt(query[:, :72].T, dscore)
                    dq[:, rows] = matmul(key_t, dscore)
                    if i % 2 == 1:
                        tick(1)
                scale = HEAD_DIM ** (-0.5)
                dqkv[0, :, h * 72 : h * 72 + 72] = (dq[...] * scale).T.astype(BF)
                key_grad = (dk[...] * scale).T.astype(BF)
                if h < 4:
                    dqkv[0, :, 576 + h * 72 : 648 + h * 72] = key_grad
                else:
                    dqkv[1, :, h * 72 - 288 : h * 72 - 216] = key_grad
                dqkv[1, :, 288 + h * 72 : 360 + h * 72] = dv[...].T.astype(BF)

        pl.run_scoped(
            heads,
            VM((2, 2 * half, 128), BF),
            VM((2, 2 * half, 128), BF),
            VM((2, 72, 2 * half), BF),
            VM((2, 72, 2 * half), F32),
            VM((72, 2 * half), F32),
            VM((72, 2 * half), F32),
            VM((72, 2 * half), F32),
        )

        def attend_grad(h1):
            load(h1_in, h1, 1).wait()
            for t in range(3):
                left = h1[:, t * 384 : (t + 1) * 384]
                for i in (0, 1):
                    grads[0][i, t * 384 : (t + 1) * 384, :] = matmul_tn(left, dqkv[i]).astype(BF)
                    tick(1)

        pl.run_scoped(attend_grad, VM((2 * half, D), BF))
        scatter.start(0)
        scatter.start(1)
        zero, one = scatter.steps(0), scatter.steps(1)
        queue.extend(zero[0][1:] + one[0][1:] + zero[1] + one[1] + zero[2] + one[2] + zero[3] + one[3])

        def back(weight, x0):
            loads = [load(gq, weight, 1), load(x0_in, x0, 2)]
            for d in loads:
                d.wait()

            def product(start):
                rows = pl.ds(start, WIDE)
                return matmul_nt(dqkv[0, rows, :], weight[0]) + matmul_nt(dqkv[1, rows, :], weight[1])

            for t in range(half // WIDE):
                rows = pl.ds(t * WIDE, WIDE)
                ps[rows, :] = product(pl.multiple_of(other + t * WIDE, WIDE)).astype(BF)
                rdma(ps.at[rows], pr.at[rows], ts.at[2, t], tr.at[2, t], twin).start()
                tick(1)
            for t in range(half // WIDE):
                value = product(pl.multiple_of(mine + t * WIDE, WIDE))
                half_got(2, t)
                tick(1)
                for n in range(WIDE // TILE):
                    rows = slice(t * WIDE + n * TILE, t * WIDE + (n + 1) * TILE)
                    gradient = value[n * TILE : (n + 1) * TILE, :] + pr[rows, :].astype(F32)
                    part, normed = norm_back(x0[rows, :].astype(F32), vec(1), gradient)
                    add_mod(0, gradient)
                    add_mod(1, gradient * normed)
                    dba[rows, :] = (dx1[rows, :] + part).astype(BF)
                    move(1 + t * (WIDE // TILE) + n)

        pl.run_scoped(back, VM((2, D, 864), BF), VM((half, D), BF))
        for i in (0, 1):
            sums = jnp.sum(dqkv[i].astype(F32), axis=0, keepdims=True)
            for j in range(8):
                block = sums[:, i * 288 + j * 72 : i * 288 + j * 72 + 72]
                for p in (0, 1):
                    add_bias(i * D + (2 * j + p) * 72, jnp.where(c == p, block, 0.0))

    pl.run_scoped(attention, VM((8, 72, 2 * half), BF), VM((2, 2 * half, 864), BF))
    for hop in hops:
        hop()
        tick(3)
    tick(len(queue))

    last_half = 72
    def give(f, got, i):
        return rdma(f.at[pl.ds(pl.multiple_of((1 - c) * 72, 8), 72)], got, ts.at[3, i], tr.at[3, i], twin)

    give(fq, gotq, 0).start()
    give(fu, gotu, 1).start()

    def squares(value):
        return jnp.sum(jnp.sum(value * value, axis=0, keepdims=True), axis=1, keepdims=True)

    bias_squares = squares(bias_out[...])
    total = squares(fq[...]) + squares(fu[...]) + squares(s_proj[...]) + squares(s_red[...]) + squares(gmod[...])
    total = jnp.broadcast_to(total, (8, 128))
    for i, to in enumerate((twin, yn, xn)):
        sq[2 * i] = total
        d = rdma(sq.at[2 * i], sq.at[2 * i + 1], ns.at[i], nr.at[i], to)
        d.start()
        d.wait()
        total = total + sq[2 * i + 1]
    sq[6] = total
    last = [rdma(sq.at[6], sq.at[6 + k], ns.at[2 + k], nr.at[2 + k], zn[k]) for k in (1, 2, 3)]
    for d in last:
        d.start()

    def interleave(f, got, shard, width, i):
        give(f, got, i).wait()
        own = jnp.where(c == 0, f[:72, :], f[72:, :])
        sides = (jnp.where(c == 0, own, got[...]), jnp.where(c == 0, got[...], own))
        count = own.shape[1] // width
        shard[...] = jnp.concatenate(
            [sides[p][:, j * width : (j + 1) * width] for j in range(count) for p in (0, 1)], axis=1
        )

    interleave(fq, gotq, s_att, HEAD_DIM, 0)
    interleave(fu, gotu, s_exp, BLOCK, 1)
    for d in last:
        d.wait()
    norm_out[...] = (sq[6] + sq[7]) + (sq[8] + sq[9]) + bias_squares
    for i in range(1 + half // TILE):
        moved(i)
    scatter.finish()


def backward_block(kept):
    half = kept[6].shape[0]
    rows = 2 * half
    sd = jax.ShapeDtypeStruct
    vm = pl.BlockSpec(memory_space=VM)
    hbm = pl.BlockSpec(memory_space=ANY)
    sizes = ((D, 864), (72, 576), (D, D), (2304, 576))
    pieces = [PIECES[n][:2] for n in NAMES]
    dma = pltpu.SemaphoreType.DMA
    n = len(CHUNKS)
    scratch = [
        VM((2, D, 864), BF),
        VM((2, 8, 72, 576), BF),
        VM((2, D, D), BF),
        VM((2, 2304, 576), BF),
    ]
    for count in (2, 2, 4, 4, 3):
        scratch += [VM((count,) + p, BF) for p in pieces]
    scratch += [
        VM((144, 864), F32),
        VM((144, D), F32),
        VM((72, 864), F32),
        VM((72, D), F32),
        VM((rows, D), BF),
        VM((half, D), F32),
        VM((half, D), BF),
        VM((half, D), BF),
        VM((2, 1, 3456), F32),
        VM((1, 9216), F32),
        VM((4, 2, 2, 1, 3456), F32),
        VM((2, 1, 3456), F32),
        VM((2, 1, 3456), F32),
        VM((3, 1, 9216), F32),
        VM((3, 1, 9216), F32),
        VM((3, 1, 9216), F32),
        VM((2, 1, 3456), F32),
        VM((10, 8, 128), F32),
        dma((9,)),
    ]
    scratch += [dma((n, 4))] * 2 + [dma((n, 4, 2))] * 2 + [dma((n, 4))] * 6
    scratch += [dma((4, 4))] * 2 + [dma((5,))] * 2 + [dma((5, 6))] * 2 + [dma((6,))] * 2
    places = [hbm] * 4 + [vm, vm] + [hbm] * 8 + [vm] + [hbm] * 7
    return pl.pallas_call(
        backward_kernel,
        out_shape=[
            sd((half, D), BF),
            sd((half, D), BF),
            sd((72, 1728), F32),
            sd((72, 576), F32),
            sd((72, 2304), F32),
            sd((288, 576), F32),
            sd((72, 3456), F32),
            sd((1, 14 * D), F32),
            sd((8, 128), F32),
        ],
        in_specs=places,
        out_specs=[hbm, hbm] + [vm] * 7,
        scratch_shapes=scratch,
        compiler_params=pltpu.CompilerParams(
            collective_id=1, has_side_effects=True, vmem_limit_bytes=62 * 2**20
        ),
        name="backward_block",
    )(*kept)


def on_device_fast(
    tokens,
    cotangent,
    buckets,
    timesteps,
    labels,
    class_table,
    step_count,
    modulate_master,
    modulate_first,
    modulate_second,
    attend_master,
    attend_first,
    attend_second,
    project_master,
    project_first,
    project_second,
    expand_master,
    expand_first,
    expand_second,
    reduce_master,
    reduce_first,
    reduce_second,
    biases_master,
    biases_first,
    biases_second,
):

    z, x, c, y = place()
    bf16, f32 = jnp.bfloat16, jnp.float32
    block = FF // 16
    class_row = lax.dynamic_slice_in_dim(class_table, labels[0], 1).astype(f32)
    condition = jax.nn.silu(class_row + time_features(timesteps, D)).astype(bf16).astype(f32)
    cond_tiles = jnp.pad(condition.reshape(16, 72), ((0, 0), (0, 56)))
    bucket = jnp.broadcast_to(buckets.astype(f32)[:, None], (8, 128))
    steps = jnp.arange(64, dtype=f32)[:, None]
    omegas = jnp.exp(-math.log(10000.0) * jnp.arange(288, dtype=f32) / 288)[None, :]
    table = jnp.concatenate([jnp.sin(steps * omegas), jnp.cos(steps * omegas)], axis=1)
    kept = forward_block(
        tokens,
        cotangent,
        bucket,
        table,
        (attend_master, project_master, expand_master, reduce_master),
        modulate_master,
        cond_tiles,
        biases_master[None, :],
    )
    (output, input_grad, grad_attend, grad_project, grad_expand, grad_reduce, grad_mod, bias_total, squares) = (
        backward_block(kept)
    )
    grad_norm = jnp.sqrt(squares[0, 0])
    bias_total = bias_total[0]
    clip_factor = jnp.minimum(1.0, 1.0 / (grad_norm + 1e-06))
    correction = 1.0 - jnp.power(0.5, step_count.astype(f32))
    rate = 0.5 * D ** (-0.5)
    states = (
        (modulate_master, modulate_first, modulate_second, grad_mod, rate),
        (attend_master, attend_first, attend_second, grad_attend, rate),
        (project_master, project_first, project_second, grad_project, rate),
        (expand_master, expand_first, expand_second, grad_expand, rate),
        (reduce_master, reduce_first, reduce_second, grad_reduce, 0.5 * FF ** (-0.5)),
        (biases_master, biases_first, biases_second, bias_total, 0.1),
    )
    updates = []
    for master, first, second, gradient, learn_rate in states:
        updates += adam_update(
            master, first, second, gradient, learn_rate, clip_factor, correction
        )
    return (output, input_grad.astype(f32), grad_norm, *updates)


def fast_solution(mesh):
    return jax.shard_map(
        on_device_fast,
        mesh=mesh,
        in_specs=(
            P(("z", "x", "c", "y"), None),
            P(("z", "x", "c", "y"), None),
            P(("z", "x", "c")),
            P(("z", "x", "c")),
            P(("z", "x", "c")),
            P(),
            P(),
            P(("z", "x", "c"), "y"),
            P(("z", "x", "c"), "y"),
            P(("z", "x", "c"), "y"),
            P(("z", "x", "c"), "y"),
            P(("z", "x", "c"), "y"),
            P(("z", "x", "c"), "y"),
            P(("z", "x", "c"), "y"),
            P(("z", "x", "c"), "y"),
            P(("z", "x", "c"), "y"),
            P(("z", "x", "c"), "y"),
            P(("z", "x", "c"), "y"),
            P(("z", "x", "c"), "y"),
            P(("z", "x", "c"), "y"),
            P(("z", "x", "c"), "y"),
            P(("z", "x", "c"), "y"),
            P(),
            P(),
            P(),
        ),
        out_specs=(
            P(("z", "x", "c", "y"), None),
            P(("z", "x", "c", "y"), None),
            P(),
            P(("z", "x", "c"), "y"),
            P(("z", "x", "c"), "y"),
            P(("z", "x", "c"), "y"),
            P(("z", "x", "c"), "y"),
            P(("z", "x", "c"), "y"),
            P(("z", "x", "c"), "y"),
            P(("z", "x", "c"), "y"),
            P(("z", "x", "c"), "y"),
            P(("z", "x", "c"), "y"),
            P(("z", "x", "c"), "y"),
            P(("z", "x", "c"), "y"),
            P(("z", "x", "c"), "y"),
            P(("z", "x", "c"), "y"),
            P(("z", "x", "c"), "y"),
            P(("z", "x", "c"), "y"),
            P(),
            P(),
            P(),
        ),
        check_vma=False,
    )


def plain_solution(mesh):
    return jax.shard_map(
        on_device,
        mesh=mesh,
        in_specs=(
            P(("seq", "head"), None),
            P(("seq", "head"), None),
            P("seq"),
            P("seq"),
            P("seq"),
            P(),
            P(),
            P("seq", "head"),
            P("seq", "head"),
            P("seq", "head"),
            P("seq", "head"),
            P("seq", "head"),
            P("seq", "head"),
            P("seq", "head"),
            P("seq", "head"),
            P("seq", "head"),
            P("seq", "head"),
            P("seq", "head"),
            P("seq", "head"),
            P("seq", "head"),
            P("seq", "head"),
            P("seq", "head"),
            P(),
            P(),
            P(),
        ),
        out_specs=(
            P(("seq", "head"), None),
            P(("seq", "head"), None),
            P(),
            P("seq", "head"),
            P("seq", "head"),
            P("seq", "head"),
            P("seq", "head"),
            P("seq", "head"),
            P("seq", "head"),
            P("seq", "head"),
            P("seq", "head"),
            P("seq", "head"),
            P("seq", "head"),
            P("seq", "head"),
            P("seq", "head"),
            P("seq", "head"),
            P("seq", "head"),
            P("seq", "head"),
            P(),
            P(),
            P(),
        ),
        check_vma=False,
    )


def solution(mesh):
    if dict(mesh.shape) == {"seq": 16, "head": 2}:
        grid = Mesh(mesh.devices.reshape(4, 2, 2, 2), ("z", "x", "c", "y"))
        return fast_solution(grid)
    return plain_solution(mesh)
```

```python
import functools
import math

import jax
import jax.numpy as jnp
from jax import lax
from jax.experimental import pallas as pl
from jax.experimental.pallas import tpu as pltpu
from jax.sharding import Mesh
from jax.sharding import PartitionSpec as P

D = 1152
HEAD_DIM = 72
FF = 4608
SIDE = 32
LMAX = 1024


highest = lax.Precision.HIGHEST
row_units = (8, 4, 16, 6, 10, 7, 4, 6)
col_units = (8, 16, 4, 10, 6, 9, 8, 6)


def table_pick(indices, entries):
    matches = indices[..., None] == jnp.arange(len(entries), dtype=jnp.int32)
    return jnp.sum(jnp.where(matches, jnp.array(entries, jnp.int32), 0), axis=-1)


def layer_norm(value):
    average = jnp.mean(value, axis=-1, keepdims=True)
    centred = value - average
    spread = jnp.mean(centred * centred, axis=-1, keepdims=True)
    return centred * lax.rsqrt(spread + 1e-06)


def modulate(value, shift, scaling):
    return layer_norm(value) * (1.0 + scaling) + shift


def time_features(moments, width):
    half_width = width // 2
    frequency = jnp.exp(-math.log(10000.0) * jnp.arange(half_width, dtype=jnp.float32) / half_width)
    angles = moments.astype(jnp.float32)[:, None] * frequency[None, :]
    return jnp.concatenate([jnp.cos(angles), jnp.sin(angles)], axis=1)


def grid_features(position, row_wide, width):
    quarter = width // 4
    omegas = jnp.exp(-math.log(10000.0) * jnp.arange(quarter, dtype=jnp.float32) / quarter)
    row_angle = (position // row_wide).astype(jnp.float32)[:, None] * omegas[None, :]
    col_angle = (position % row_wide).astype(jnp.float32)[:, None] * omegas[None, :]
    return jnp.concatenate(
        [jnp.sin(row_angle), jnp.cos(row_angle), jnp.sin(col_angle), jnp.cos(col_angle)], axis=1
    )


def fold_rows(left_side, weight_slab):
    return jnp.dot(
        left_side,
        lax.all_gather(weight_slab, "seq", axis=0, tiled=True),
        preferred_element_type=jnp.float32,
    )


def back_cols(gradient, weight_slab):
    return lax.dot_general(
        gradient,
        lax.all_gather(weight_slab, "seq", axis=0, tiled=True),
        (((1,), (1,)), ((), ())),
        preferred_element_type=jnp.float32,
    )


def rows_seq(left_side, right_side):
    return lax.psum_scatter(
        lax.dot_general(
            left_side, right_side, (((0,), (0,)), ((), ())), preferred_element_type=jnp.float32
        ).astype(jnp.bfloat16),
        "seq",
        scatter_dimension=0,
        tiled=True,
    ).astype(jnp.float32)


def attend(queries, key_rows, value_rows, lengths):
    heads_here = queries.shape[1] // HEAD_DIM
    block_rows = min(512, LMAX)
    score_scale = HEAD_DIM ** (-0.5)
    image_count = lengths.shape[0]

    def per_image(packed):
        query_image, key_image, value_image, length = packed
        key_heads = key_image.reshape(LMAX, heads_here, HEAD_DIM)
        value_heads = value_image.reshape(LMAX, heads_here, HEAD_DIM)
        live_keys = jnp.arange(LMAX, dtype=jnp.int32) < length

        def per_block(query_block):
            scores = (
                jnp.einsum(
                    "qhe,khe->hqk", query_block, key_heads, preferred_element_type=jnp.float32
                )
                * score_scale
            )
            scores = jnp.where(live_keys[None, None, :], scores, -1e30)
            maximum = jnp.max(scores, axis=-1, keepdims=True)
            weights = jnp.exp(scores - maximum)
            totals = jnp.sum(weights, axis=-1, keepdims=True)
            probability = (weights / totals).astype(jnp.bfloat16)
            result = jnp.einsum(
                "hqk,khe->qhe", probability, value_heads, preferred_element_type=jnp.float32
            )
            return (result.astype(jnp.bfloat16), (maximum + jnp.log(totals))[:, :, 0])

        blocks = query_image.reshape(LMAX // block_rows, block_rows, heads_here, HEAD_DIM)
        result, log_sums = lax.map(per_block, blocks)
        return (result.reshape(LMAX, heads_here * HEAD_DIM), log_sums)

    stacked = (
        queries.reshape(image_count, LMAX, -1),
        key_rows.reshape(image_count, LMAX, -1),
        value_rows.reshape(image_count, LMAX, -1),
        lengths,
    )
    result, log_sums = lax.map(per_image, stacked)
    return (result.reshape(image_count * LMAX, -1), log_sums)


def attend_back(queries, key_rows, value_rows, grad_rows, log_sums, lengths):
    heads_here = queries.shape[1] // HEAD_DIM
    block_rows = min(512, LMAX)
    score_scale = HEAD_DIM ** (-0.5)
    image_count = lengths.shape[0]

    def per_image(packed):
        query_image, key_image, value_image, grad_image, logsum_image, length = packed
        key_heads = key_image.reshape(LMAX, heads_here, HEAD_DIM)
        value_heads = value_image.reshape(LMAX, heads_here, HEAD_DIM)
        live_keys = jnp.arange(LMAX, dtype=jnp.int32) < length

        def per_block(running, inputs):
            key_grad, value_grad = running
            query_block, grad_block, logsum_block = inputs
            scores = (
                jnp.einsum(
                    "qhe,khe->hqk", query_block, key_heads, preferred_element_type=jnp.float32
                )
                * score_scale
            )
            scores = jnp.where(live_keys[None, None, :], scores, -1e30)
            probability = jnp.exp(scores - logsum_block[:, :, None])
            grad_prob = jnp.einsum(
                "qhe,khe->hqk", grad_block, value_heads, preferred_element_type=jnp.float32
            )
            inner_sum = jnp.sum(probability * grad_prob, axis=-1, keepdims=True)
            grad_score = (probability * (grad_prob - inner_sum)).astype(jnp.bfloat16)
            query_grad = (
                jnp.einsum(
                    "hqk,khe->qhe", grad_score, key_heads, preferred_element_type=jnp.float32
                )
                * score_scale
            )
            key_grad = (
                key_grad
                + jnp.einsum(
                    "hqk,qhe->khe", grad_score, query_block, preferred_element_type=jnp.float32
                )
                * score_scale
            )
            value_grad = value_grad + jnp.einsum(
                "hqk,qhe->khe",
                probability.astype(jnp.bfloat16),
                grad_block,
                preferred_element_type=jnp.float32,
            )
            return ((key_grad, value_grad), query_grad.astype(jnp.bfloat16))

        initial = (
            jnp.zeros((LMAX, heads_here, HEAD_DIM), jnp.float32),
            jnp.zeros((LMAX, heads_here, HEAD_DIM), jnp.float32),
        )
        blocks = (
            query_image.reshape(LMAX // block_rows, block_rows, heads_here, HEAD_DIM),
            grad_image.reshape(LMAX // block_rows, block_rows, heads_here, HEAD_DIM),
            logsum_image,
        )
        (key_grad, value_grad), query_grad = lax.scan(per_block, initial, blocks)
        return (
            query_grad.reshape(LMAX, -1),
            key_grad.reshape(LMAX, -1).astype(jnp.bfloat16),
            value_grad.reshape(LMAX, -1).astype(jnp.bfloat16),
        )

    stacked = (
        queries.reshape(image_count, LMAX, -1),
        key_rows.reshape(image_count, LMAX, -1),
        value_rows.reshape(image_count, LMAX, -1),
        grad_rows.reshape(image_count, LMAX, -1),
        log_sums,
        lengths,
    )
    query_grad, key_grad, value_grad = lax.map(per_image, stacked)
    return (
        query_grad.reshape(image_count * LMAX, -1),
        key_grad.reshape(image_count * LMAX, -1),
        value_grad.reshape(image_count * LMAX, -1),
    )


def adam_update(master, first_moment, second_moment, gradient, learn_rate, clip_factor, correction):
    clipped = gradient * clip_factor
    first_new = 0.5 * first_moment + 0.5 * clipped
    second_new = 0.5 * second_moment + 0.5 * clipped * clipped
    direction = first_new / correction / (jnp.sqrt(second_new / correction) + 1e-08)
    return (master - learn_rate * (direction + 0.1 * master), first_new, second_new)


def on_device(
    tokens,
    cotangent,
    buckets,
    timesteps,
    labels,
    class_table,
    step_count,
    modulate_master,
    modulate_first,
    modulate_second,
    attend_master,
    attend_first,
    attend_second,
    project_master,
    project_first,
    project_second,
    expand_master,
    expand_first,
    expand_second,
    reduce_master,
    reduce_first,
    reduce_second,
    biases_master,
    biases_first,
    biases_second,
):
    head_index = lax.axis_index("head")
    head_count = lax.axis_size("head")
    tok_rows = tokens.shape[0]
    image_count = buckets.shape[0]
    unit_cells = SIDE // 8
    heights = table_pick(buckets, row_units) * unit_cells
    widths = table_pick(buckets, col_units) * unit_cells
    lengths = heights * widths
    row_index = head_index * tok_rows + jnp.arange(tok_rows, dtype=jnp.int32)
    image_of = row_index // LMAX
    position = row_index % LMAX
    choose = image_of[:, None] == jnp.arange(image_count, dtype=jnp.int32)[None, :]
    pick_rows = choose.astype(jnp.float32)
    row_wide = jnp.sum(jnp.where(choose, widths[None, :], 0), axis=1)
    row_length = jnp.sum(jnp.where(choose, lengths[None, :], 0), axis=1)
    live_rows = (position < row_length).astype(jnp.float32)
    grid_cells = grid_features(position, row_wide, D)
    class_pick = (
        labels[:, None] == jnp.arange(class_table.shape[0], dtype=jnp.int32)[None, :]
    ).astype(jnp.bfloat16)
    class_rows = jnp.dot(class_pick, class_table, preferred_element_type=jnp.float32)
    condition = jax.nn.silu(class_rows + time_features(timesteps, D)).astype(jnp.bfloat16)
    bias_low = biases_master.astype(jnp.bfloat16).astype(jnp.float32)
    offset_base = 6 * D
    bias_query = bias_low[offset_base : offset_base + D]
    bias_value = bias_low[offset_base + D : offset_base + 2 * D]
    bias_proj = bias_low[offset_base + 2 * D : offset_base + 3 * D]
    bias_hidden = bias_low[offset_base + 3 * D : offset_base + 3 * D + FF]
    bias_output = bias_low[offset_base + 3 * D + FF :]
    head_slabs = (
        lax.all_gather(attend_master.astype(jnp.bfloat16), "head", axis=1, tiled=True),
        lax.all_gather(project_master.astype(jnp.bfloat16), "head", axis=1, tiled=True),
        lax.all_gather(expand_master.astype(jnp.bfloat16), "head", axis=1, tiled=True),
        lax.all_gather(reduce_master.astype(jnp.bfloat16), "head", axis=1, tiled=True),
    )
    attend_slab, project_slab, expand_slab, reduce_slab = head_slabs
    mod_width = 6 * D // head_count
    mod_share = fold_rows(condition, modulate_master.astype(jnp.bfloat16))
    mod_share = mod_share + lax.dynamic_slice_in_dim(bias_low, head_index * mod_width, mod_width)
    modulation = lax.all_gather(mod_share, "head", axis=1, tiled=True)
    mod_rows = jnp.dot(pick_rows, modulation, precision=highest)
    shift_one, scale_one, gating_one, shift_two, scale_two, gating_two = jnp.split(
        mod_rows, 6, axis=1
    )
    residual_zero = tokens.astype(jnp.float32) + grid_cells
    hidden_attend = modulate(residual_zero, shift_one, scale_one).astype(jnp.bfloat16)
    packed = fold_rows(hidden_attend, attend_slab)
    queries = (packed[:, :D] + bias_query).astype(jnp.bfloat16)
    key_rows = packed[:, D : 2 * D].astype(jnp.bfloat16)
    value_rows = (packed[:, 2 * D :] + bias_value).astype(jnp.bfloat16)
    query_heads, key_heads, value_heads = (
        lax.all_to_all(queries, "head", split_axis=1, concat_axis=0, tiled=True),
        lax.all_to_all(key_rows, "head", split_axis=1, concat_axis=0, tiled=True),
        lax.all_to_all(value_rows, "head", split_axis=1, concat_axis=0, tiled=True),
    )
    head_out, log_sums = attend(query_heads, key_heads, value_heads, lengths)
    attention = lax.all_to_all(head_out, "head", split_axis=0, concat_axis=1, tiled=True)
    branch_attend = fold_rows(attention, project_slab) + bias_proj
    residual_one = residual_zero + gating_one * branch_attend
    hidden_expand = modulate(residual_one, shift_two, scale_two).astype(jnp.bfloat16)
    widened = fold_rows(hidden_expand, expand_slab) + bias_hidden
    activated = jax.nn.gelu(widened, approximate=True).astype(jnp.bfloat16)
    branch_expand = fold_rows(activated, reduce_slab) + bias_output
    output = (residual_one + gating_two * branch_expand).astype(jnp.bfloat16)
    outer_grad = cotangent.astype(jnp.float32) * live_rows[:, None]
    gating_later = outer_grad * branch_expand
    closing_grad = (outer_grad * gating_two).astype(jnp.bfloat16)
    active_grad = back_cols(closing_grad, reduce_slab)
    gelu_value, gelu_pullback = jax.vjp(lambda inner: jax.nn.gelu(inner, approximate=True), widened)
    widened_grad = gelu_pullback(active_grad)[0].astype(jnp.bfloat16)
    hidden_grad = back_cols(widened_grad, expand_slab)
    later_value, later_pullback = jax.vjp(modulate, residual_one, shift_two, scale_two)
    residual_part, shift_later, scale_later = later_pullback(hidden_grad)
    middle_grad = outer_grad + residual_part
    gating_early = middle_grad * branch_attend
    branch_grad = (middle_grad * gating_one).astype(jnp.bfloat16)
    attend_grad = back_cols(branch_grad, project_slab).astype(jnp.bfloat16)
    heads_grad = lax.all_to_all(attend_grad, "head", split_axis=1, concat_axis=0, tiled=True)
    query_grad, keyrow_grad, value_grad = attend_back(
        query_heads, key_heads, value_heads, heads_grad, log_sums, lengths
    )
    query_back, keys_back, values_back = (
        lax.all_to_all(query_grad, "head", split_axis=0, concat_axis=1, tiled=True),
        lax.all_to_all(keyrow_grad, "head", split_axis=0, concat_axis=1, tiled=True),
        lax.all_to_all(value_grad, "head", split_axis=0, concat_axis=1, tiled=True),
    )
    packed_grad = jnp.concatenate([query_back, keys_back, values_back], axis=1)
    normed_grad = back_cols(packed_grad, attend_slab)
    early_value, early_pullback = jax.vjp(modulate, residual_zero, shift_one, scale_one)
    input_part, shift_early, scale_early = early_pullback(normed_grad)
    input_grad = middle_grad + input_part
    mod_token_grad = jnp.concatenate(
        [shift_early, scale_early, gating_early, shift_later, scale_later, gating_later], axis=1
    )
    mod_grad = lax.dot_general(
        pick_rows, mod_token_grad, (((0,), (0,)), ((), ())), precision=highest
    )
    mod_summed = lax.psum_scatter(mod_grad, "head", scatter_dimension=1, tiled=True)
    mod_rounded = mod_summed.astype(jnp.bfloat16)
    grad_mod = rows_seq(condition, mod_rounded)
    mod_slot = lax.dynamic_update_slice_in_dim(
        jnp.zeros((6 * D,), jnp.float32),
        jnp.sum(mod_rounded.astype(jnp.float32), axis=0),
        head_index * mod_width,
        0,
    )
    bias_share = jnp.concatenate(
        [
            mod_slot,
            jnp.sum(query_back.astype(jnp.float32), axis=0),
            jnp.sum(values_back.astype(jnp.float32), axis=0),
            jnp.sum(branch_grad.astype(jnp.float32), axis=0),
            jnp.sum(widened_grad.astype(jnp.float32), axis=0),
            jnp.sum(closing_grad.astype(jnp.float32), axis=0),
        ]
    )
    operand_pairs = (
        (hidden_attend, packed_grad),
        (attention, branch_grad),
        (hidden_expand, widened_grad),
        (activated, closing_grad),
    )
    term_slabs = tuple((rows_seq(left_side, right_side) for left_side, right_side in operand_pairs))
    reduced = (
        lax.psum_scatter(
            term_slabs[0].astype(jnp.bfloat16), "head", scatter_dimension=1, tiled=True
        ).astype(jnp.float32),
        lax.psum_scatter(
            term_slabs[1].astype(jnp.bfloat16), "head", scatter_dimension=1, tiled=True
        ).astype(jnp.float32),
        lax.psum_scatter(
            term_slabs[2].astype(jnp.bfloat16), "head", scatter_dimension=1, tiled=True
        ).astype(jnp.float32),
        lax.psum_scatter(
            term_slabs[3].astype(jnp.bfloat16), "head", scatter_dimension=1, tiled=True
        ).astype(jnp.float32),
    )
    grad_attend, grad_project, grad_expand, grad_reduce = reduced
    local_squares = jnp.sum(grad_mod * grad_mod) + sum(
        (jnp.sum(gradient * gradient) for gradient in reduced)
    )
    bias_total, square_total = lax.psum((bias_share, local_squares), ("seq", "head"))
    grad_norm = jnp.sqrt(square_total + jnp.sum(bias_total * bias_total))
    clip_factor = jnp.minimum(1.0, 1.0 / (grad_norm + 1e-06))
    correction = 1.0 - jnp.power(0.5, step_count.astype(jnp.float32))
    modulate_new = adam_update(
        modulate_master,
        modulate_first,
        modulate_second,
        grad_mod,
        0.5 * D ** (-0.5),
        clip_factor,
        correction,
    )
    attend_new = adam_update(
        attend_master,
        attend_first,
        attend_second,
        grad_attend,
        0.5 * D ** (-0.5),
        clip_factor,
        correction,
    )
    project_new = adam_update(
        project_master,
        project_first,
        project_second,
        grad_project,
        0.5 * D ** (-0.5),
        clip_factor,
        correction,
    )
    expand_new = adam_update(
        expand_master,
        expand_first,
        expand_second,
        grad_expand,
        0.5 * D ** (-0.5),
        clip_factor,
        correction,
    )
    reduce_new = adam_update(
        reduce_master,
        reduce_first,
        reduce_second,
        grad_reduce,
        0.5 * FF ** (-0.5),
        clip_factor,
        correction,
    )
    biases_new = adam_update(
        biases_master, biases_first, biases_second, bias_total, 0.1, clip_factor, correction
    )
    return (
        output,
        input_grad,
        grad_norm,
        modulate_new[0],
        modulate_new[1],
        modulate_new[2],
        attend_new[0],
        attend_new[1],
        attend_new[2],
        project_new[0],
        project_new[1],
        project_new[2],
        expand_new[0],
        expand_new[1],
        expand_new[2],
        reduce_new[0],
        reduce_new[1],
        reduce_new[2],
        biases_new[0],
        biases_new[1],
        biases_new[2],
    )


ALPHA = HEAD_DIM ** (-0.5) * math.log2(math.e)
GELU_A = math.sqrt(2.0 / math.pi)
GELU_B = 0.044715
BLOCK = FF // 16
BF, F32 = jnp.bfloat16, jnp.float32
ANY, VM = pl.ANY, pltpu.VMEM
PIECES = {"q": (144, 864, 48), "p": (72, 576, None), "u": (144, 1152, 48), "d": (288, 576, 96)}
NAMES = ("q", "p", "u", "d")
MESH = pl.DeviceIdType.MESH


def place():
    return tuple(lax.axis_index(a) for a in ("z", "x", "c", "y"))


def at_z(k):
    z = lax.axis_index("z")
    return (z, z + 1 - 2 * (z % 2), (z + 2) % 4, 3 - z)[k]


def rdma(src, dst, send, recv, to):
    return pltpu.make_async_remote_copy(
        src_ref=src, dst_ref=dst, send_sem=send, recv_sem=recv, device_id=to, device_id_type=MESH
    )


def partners():
    z, x, c, y = place()
    xn, yn, twin = (z, 1 - x, c, y), (z, x, c, 1 - y), (z, x, 1 - c, y)
    return xn, yn, twin, [(at_z(k), x, c, y) for k in range(4)]


def greet(others, swapped=False):
    z, x, c, y = place()
    barrier = pltpu.get_barrier_semaphore()
    for to in others:
        pl.semaphore_signal(barrier, inc=1, device_id=to, device_id_type=MESH)
    if swapped:

        @pl.when(c != y)
        def _():
            pl.semaphore_signal(barrier, inc=1, device_id=(z, x, y, c), device_id_type=MESH)

        pl.semaphore_wait(barrier, len(others) + (c + y) % 2)
    else:
        pl.semaphore_wait(barrier, len(others))


CHUNKS = (
    (0, 0, 80, 32),
    (0, 80, 64, 16),
    (1, 0, 72, None),
    (2, 0, 80, 32),
    (2, 80, 64, 16),
    (3, 0, 144, 48),
    (3, 144, 144, 48),
)


def parts_of(chunk, k):
    _, _, rows, cut = CHUNKS[chunk]
    if cut is None:
        return ((0, rows), None) if k == 0 else (None, (0, rows))
    return (0, cut), (cut, rows - cut)


def piece_at(full, w, y, zk, x, first, count):
    rows = PIECES[NAMES[w]][0]
    if count == 72:
        return full.at[y, zk * 2 + x]
    return full.at[y, pl.ds(pl.multiple_of((zk * 2 + x) * rows + first, 16), count)]


def matmul(left, right):
    return jnp.dot(left, right, preferred_element_type=F32)


def matmul_nt(left, right):
    return lax.dot_general(left, right, (((1,), (1,)), ((), ())), preferred_element_type=F32)


def matmul_tn(left, right):
    return lax.dot_general(left, right, (((0,), (0,)), ((), ())), preferred_element_type=F32)


class Gather:
    def __init__(self, own, full, sems):
        self.own, self.full = own, full
        self.zs, self.zr, self.xs, self.xr, self.ys, self.yr, self.fs, self.fr, self.ps, self.pr = sems
        self.sent = []

    def piece(self, w, flip_y, k, flip_x):
        z, x, c, y = place()
        weight, first, count, _ = CHUNKS[w]
        return piece_at(
            self.full[weight], weight, 1 - y if flip_y else y, at_z(k), 1 - x if flip_x else x, first, count
        )

    def source(self, w):
        weight, first, count, _ = CHUNKS[w]
        return self.own[weight].at[pl.ds(first, count)]

    def send(self, make):
        make().start()
        self.sent.append(make)

    def arrived(self, ref, s, r):
        rdma(ref, ref, s, r, partners()[0]).wait_recv()

    def start(self, w):
        def to_x():
            return rdma(self.source(w), self.piece(w, 0, 0, 0), self.xs.at[w, 0], self.xr.at[w, 0], partners()[0])

        def to_y():
            return rdma(self.source(w), self.piece(w, 0, 0, 0), self.ys.at[w, 0], self.yr.at[w, 0], partners()[1])

        def to_z(k):
            to = partners()[3][k]
            return rdma(self.source(w), self.piece(w, 0, 0, 0), self.zs.at[w, k], self.zr.at[w, k], to)

        self.send(to_x)
        self.send(to_y)
        for k in (1, 2, 3):
            self.send(functools.partial(to_z, k))

    def column(self, w, k):
        self.arrived(self.piece(w, 0, k, 0), self.zs.at[w, k], self.zr.at[w, k])

        def to_x():
            piece = self.piece(w, 0, k, 0)
            return rdma(piece, piece, self.xs.at[w, k], self.xr.at[w, k], partners()[0])

        def to_y():
            piece = self.piece(w, 0, k, 0)
            return rdma(piece, piece, self.ys.at[w, k], self.yr.at[w, k], partners()[1])

        self.send(to_x)
        self.send(to_y)

    def plane(self, w, k):
        spans = parts_of(w, k)

        def pass_on(i):
            part = self.piece(w, i, k, 1 - i).at[pl.ds(*spans[i])]
            return rdma(part, part, self.fs.at[w, k, i], self.fr.at[w, k, i], partners()[1 - i])

        self.arrived(self.piece(w, 0, k, 1), self.xs.at[w, k], self.xr.at[w, k])
        if k in (0, 2) and spans[0] is not None:
            self.send(functools.partial(pass_on, 0))
        self.arrived(self.piece(w, 1, k, 0), self.ys.at[w, k], self.yr.at[w, k])
        if k in (0, 2) and spans[1] is not None:
            self.send(functools.partial(pass_on, 1))

    def corner(self, w, k):
        for i, span in enumerate(parts_of(w, k)):
            if span is not None:
                part = self.piece(w, 1, k, 1).at[pl.ds(*span)]
                self.arrived(part, self.fs.at[w, k, i], self.fr.at[w, k, i])

        def to_pair():
            piece = self.piece(w, 1, k, 1)
            return rdma(piece, piece, self.ps.at[w, k], self.pr.at[w, k], partners()[3][1])

        self.send(to_pair)

    def last(self, w, k):
        self.arrived(self.piece(w, 1, k ^ 1, 1), self.ps.at[w, k], self.pr.at[w, k])

    def finish(self):
        for make in self.sent:
            make().wait_send()

    def steps(self):
        def each(method, chunks, ks):
            return [(method, i, k) for i in chunks for k in ks]

        column, plane, corner, last = self.column, self.plane, self.corner, self.last
        one = (0, 1)
        plan = [(self.start, 0), (self.start, 1), (self.start, 2)]
        plan += each(column, one, (1,)) + each(plane, one, (0,))
        plan += each(column, one, (2,)) + each(column, one, (3,)) + [(self.start, 3)]
        plan += each(corner, one, (0,)) + each(plane, one, (2,))
        plan += each(column, (2,), (1,)) + [(self.start, 4)]
        plan += each(plane, one, (1,)) + each(corner, one, (2,))
        plan += each(plane, (2,), (0,)) + each(column, (2,), (2, 3)) + each(column, (3,), (1,))
        plan += each(plane, one, (3,)) + each(last, one, (0, 2))
        count = len(CHUNKS)
        for t in range(-2, count + 4):
            wave = [(self.start, t + 2)] if t + 2 < count else []
            if 0 <= t - 4 < count:
                wave += each(last, (t - 4,), (0, 2))
            for lag, make in enumerate(
                (
                    lambda i: each(column, (i,), (1,)),
                    lambda i: each(plane, (i,), (0,)) + each(column, (i,), (2, 3)),
                    lambda i: each(corner, (i,), (0,)) + each(plane, (i,), (2, 1)),
                    lambda i: each(corner, (i,), (2,)) + each(plane, (i,), (3,)),
                )
            ):
                if t >= 0 and 0 <= t - lag < count:
                    wave += make(t - lag)
            plan += [step for step in wave if step not in plan]
        return plan


def mod_steps(cond_ref, weight, bias, out_ref, lhs, bufs, s, r):
    conds, part, got_z, mid, got_x, near, got_c = bufs

    def hop(i):
        z, x, c, y = place()
        xn, yn, twin, zn = partners()
        if i == 0:
            pairs = [(conds.at[z, x, c], conds.at[z, x, c], twin)]
        elif i == 1:
            pairs = [(conds.at[z, x], conds.at[z, x], xn)]
        elif i == 2:
            pairs = [(conds.at[z], conds.at[z], zn[k]) for k in (1, 2, 3)]
        elif i == 3:
            pairs = [(part.at[at_z(k)], got_z.at[k - 1], zn[k]) for k in (1, 2, 3)]
        elif i == 4:
            pairs = [(mid.at[1 - x], got_x, xn)]
        elif i == 5:
            pairs = [(near.at[0], got_c, twin)]
        else:
            pairs = [(near.at[1, 1 - y], near.at[2, y], yn)]
        return [
            rdma(src, dst, s.at[i, n], r.at[i, n], to) for n, (src, dst, to) in enumerate(pairs)
        ]

    def go(i):
        for d in hop(i):
            d.start()

    def end(i):
        for d in hop(i):
            d.wait()

    def step(i):
        z, x, c, y = place()
        if i > 0:
            end(i - 1)
        if i == 0:
            conds[z, x, c] = cond_ref[...]
        elif i == 3:
            me = (z * 2 + x) * 2 + c
            for n in range(16):
                lhs[pl.ds(n, 1), :] = conds[n // 4, n // 2 % 2, n % 2, pl.ds(me, 1), :]
            for j in range(3):
                cols = slice(j * D, (j + 1) * D)
                result = matmul(lhs[:, :72].astype(BF), weight[:, cols].astype(BF))
                for n in range(16):
                    part[n // 4, n // 2 % 2, n % 2, :, cols] = result[n : n + 1]
        elif i == 4:
            mid[...] = part[z] + got_z[0] + got_z[1] + got_z[2]
        elif i == 5:
            near[0] = mid[x] + got_x[...]
        elif i == 6:
            near[1] = near[0] + got_c[...]
            near[2, y] = near[1, y]
        if i < 7:
            go(i)
        else:
            for n in range(2):
                out_ref[n] = near[2, n] + bias[:, n * 3456 : (n + 1) * 3456]

    return [functools.partial(step, i) for i in range(8)]


def normed_tile(value):
    average = jnp.mean(value, axis=-1, keepdims=True)
    centred = value - average
    spread = jnp.mean(centred * centred, axis=-1, keepdims=True)
    return centred * lax.rsqrt(spread + 1e-06)


SPACE = (6, 6, 6, 6)


def rounded(value):
    return value.astype(BF).astype(F32)


def pick(bucket, entries):
    return sum(
        jnp.where(bucket == float(i), float(e * (SIDE // 8)), 0.0) for i, e in enumerate(entries)
    )


def start_rows(tok, table, bucket, first, rows):
    wide = pick(bucket, col_units)
    spot = (first + lax.broadcasted_iota(jnp.int32, (rows, 1), 0)).astype(F32)
    lane = lax.broadcasted_iota(jnp.int32, (1, 64), 1).astype(F32)
    grid_row = jnp.where((spot >= lane * wide) & (spot < (lane + 1.0) * wide), 1.0, 0.0)
    left = spot - wide * jnp.sum(grid_row * lane, axis=1, keepdims=True)
    grid_col = jnp.where(left == lane, 1.0, 0.0)
    high = table.astype(BF)
    low = (table - high.astype(F32)).astype(BF)
    parts = [matmul(hot.astype(BF), high) + matmul(hot.astype(BF), low) for hot in (grid_row, grid_col)]
    return tok.astype(F32) + jnp.concatenate(parts, axis=1)


def forward_kernel(*refs):
    (tok, cot, bucket_in, table, att_m, proj_m, exp_m, red_m, mod_w, cond_in, bias_in) = refs[:11]
    gq, gp, gu, gd = full = refs[11:15]
    (mod_out, lhs, x0_out, dy_out, cl_out, h1_out, q_out, k_out, v_out) = refs[15:24]
    (attnt_out, lse_out, ba_out, x1_out, h2_out, der_out, bb_out, y_out, gred_out) = refs[24:33]
    (oq, op, ou, od, fq, tq, fu, tu) = refs[33:41]
    mod_bufs = refs[41:48]
    (xs, x0, dy, bucket, closing, h1, qa, ka, vt, attnt, attn) = refs[48:59]
    (ps, pr, ds, dr, acc, x1, h2, act, der, ba, bb, yo, gstage) = refs[59:72]
    (b_all, b_q, b_v, b_u) = refs[72:76]
    lsem = refs[76]
    gather_sems = refs[77:87]
    ms, mr, ws, wr, ts, tr, os, outs_sem, gsem = refs[87:96]
    z, x, c, y = place()
    xn, yn, twin, zn = partners()
    half = x0.shape[0]
    mine = pl.multiple_of(c * half, half)
    other = pl.multiple_of((1 - c) * half, half)
    gather = Gather((oq, op, ou, od), full, gather_sems)
    mods = mod_steps(cond_in, mod_w, b_all, mod_out, lhs, mod_bufs, ms, mr)
    greet([xn, yn, twin] + zn[1:], swapped=True)
    mods[0]()

    def split(master, width, f, t, i):
        count = master.shape[1] // (2 * width)
        sides = [
            jnp.concatenate(
                [master[:, (2 * j + p) * width : (2 * j + p + 1) * width] for j in range(count)], axis=1
            )
            for p in (0, 1)
        ]
        t[...] = jnp.where(c == 0, sides[1], sides[0])
        rdma(t, f.at[c], os.at[0, i], os.at[1, i], twin).start()
        f[c] = jnp.where(c == 0, sides[0], sides[1])

    def joined(f, t, i, piece):
        rdma(t, f.at[c], os.at[0, i], os.at[1, i], twin).wait()
        piece[...] = jnp.concatenate([f[0], f[1]], axis=0).astype(BF)

    steps = [step for step in gather.steps() if step[0] != gather.start or step[1] > 2]
    done = [0]

    def tick(n):
        for f, *a in steps[done[0] : done[0] + n]:
            f(*a)
        done[0] = min(done[0] + n, len(steps))

    def tick_until(chunk):
        last = max(i for i, s in enumerate(steps) if s[0] == gather.last and s[1] == chunk)
        tick(max(0, last + 1 - done[0]))

    swap_to = (z, x, y, c)
    PART = 128
    moves = [(bucket_in, bucket)]
    for i in range(half // PART):
        moves.append((xs.at[pl.ds(i * PART, PART)], x0.at[pl.ds(i * PART, PART)]))
    for i in range(half // PART):
        moves.append((cot.at[pl.ds(i * PART, PART)], dy.at[pl.ds(i * PART, PART)]))

    def move(i):
        @pl.when(c != y)
        def _():
            rdma(*moves[i], ws.at[i], wr.at[i], swap_to).start()

        @pl.when(c == y)
        def _():
            pltpu.make_async_copy(*moves[i], ws.at[i]).start()

    def moved(i):
        @pl.when(c != y)
        def _():
            rdma(*moves[i], ws.at[i], wr.at[i], swap_to).wait()

        @pl.when(c == y)
        def _():
            pltpu.make_async_copy(*moves[i], ws.at[i]).wait()

    def first_rows(i):
        rows = slice(i * PART, (i + 1) * PART)
        xs[rows, :] = start_rows(
            tok[rows, :], table[...], bucket_in[0:1, 0:1], y * half + i * PART, PART
        ).astype(BF)
        move(1 + i)

    move(0)
    split(att_m, HEAD_DIM, fq, tq, 0)
    mods[1]()
    op[...] = proj_m[...].astype(BF)
    gather.start(2)
    first_rows(0)
    first_rows(1)
    joined(fq, tq, 0, oq)
    gather.start(0)
    gather.start(1)
    mods[2]()
    split(exp_m, BLOCK, fu, tu, 1)
    first_rows(2)
    first_rows(3)
    tick(2)
    joined(fu, tu, 1, ou)
    tick(4)
    mods[3]()
    od[...] = red_m[...].astype(BF)
    owns = [
        pltpu.make_async_copy(
            gather.own[w], piece_at(full[w], w, y, z, x, 0, PIECES[NAMES[w]][0]), lsem.at[w]
        )
        for w in range(4)
    ]
    for d in owns:
        d.start()
    tick(SPACE[0])
    mods[4]()
    b_all[...] = rounded(bias_in[...])
    tick(SPACE[1])
    mods[5]()
    tick(SPACE[2])
    mods[6]()
    tick(SPACE[3])
    mods[7]()

    def of_core(base, width, count):
        return jnp.concatenate(
            [
                jnp.where(
                    c == 0,
                    b_all[:, base + 2 * j * width : base + (2 * j + 1) * width],
                    b_all[:, base + (2 * j + 1) * width : base + (2 * j + 2) * width],
                )
                for j in range(count)
            ],
            axis=1,
        )

    b_p = b_all.at[:, pl.ds(8 * D, D)]
    b_d = b_all.at[:, pl.ds(9 * D + FF, D)]
    for i in range(1 + half // PART):
        moved(i)

    def vec(i):
        return mod_out[i // 3, :, (i % 3) * D : (i % 3 + 1) * D]

    TILE, WIDE = 128, 256
    tiles = half // TILE

    def own_tile(ref, t):
        return ref.at[pl.ds(pl.multiple_of(mine + t * TILE, TILE), TILE)]

    def give(ref, t, i):
        part = own_tile(ref, t)
        return rdma(part, part, ts.at[i, t], tr.at[i, t], twin)

    def norm_one(t, _):
        rows = pl.ds(pl.multiple_of(t * TILE, TILE), TILE)
        value = normed_tile(x0[rows, :].astype(F32)) * (1.0 + vec(1)) + vec(0)
        own_tile(h1, t)[...] = value.astype(BF)
        give(h1, t, 0).start()
        return 0

    for t in range(tiles):
        norm_one(t, 0)
        tick(1)
    tick_until(1)
    for i in range(half // PART):
        move(1 + half // PART + i)

    def both_got(ref, i):
        for t in range(tiles):
            give(ref, t, i).wait_send()
            part = ref.at[pl.ds(pl.multiple_of(other + t * TILE, TILE), TILE)]
            rdma(part, part, ts.at[i, t], tr.at[i, t], twin).wait_recv()

    out_copies = []

    def put(src, dst):
        d = pltpu.make_async_copy(src, dst, outs_sem.at[len(out_copies)])
        d.start()
        out_copies.append(d)

    def load(src, dst, i):
        d = pltpu.make_async_copy(src, dst, lsem.at[i])
        d.start()
        d.wait()

    owns[0].wait()
    live = pick(bucket[0:1, 0:1], row_units) * pick(bucket[0:1, 0:1], col_units)
    lane = lax.broadcasted_iota(jnp.int32, (1, 128), 1)

    b_q[...] = of_core(6 * D, HEAD_DIM, 8)
    b_v[...] = of_core(7 * D, HEAD_DIM, 8)
    b_u[...] = of_core(9 * D, BLOCK, 8)

    def qkv(weight):
        load(gq, weight, 4)

        def rows_of(start):
            rows = pl.ds(start, half)
            left = h1[rows, :]
            spot = (start + lax.broadcasted_iota(jnp.int32, (half, 1), 0)).astype(F32)
            mask = jnp.where(lane == HEAD_DIM, jnp.where(spot < live, 0.0, -1e30), 0.0)
            ones = jnp.where(lane == HEAD_DIM, 1.0, 0.0)
            fill = jnp.zeros((half, 56), F32)

            def put_key(j, key):
                ka[j, rows, :] = (jnp.concatenate([key, fill], axis=1) + mask).astype(BF)

            one = matmul(left, weight[0])
            for j in range(8):
                cols = slice(j * HEAD_DIM, (j + 1) * HEAD_DIM)
                query = (one[:, cols] + b_q[:, cols]) * ALPHA
                qa[j, rows, :] = (jnp.concatenate([query, fill], axis=1) + ones).astype(BF)
            for j in range(4):
                put_key(j, one[:, 576 + j * 72 : 648 + j * 72])
            tick(2)
            two = matmul(left, weight[1])
            for j in range(4):
                put_key(4 + j, two[:, j * 72 : j * 72 + 72])
            for j in range(8):
                cols = slice(j * HEAD_DIM, (j + 1) * HEAD_DIM)
                value = two[:, 288 + j * 72 : 360 + j * 72] + b_v[:, cols]
                vt[j, :, rows] = value.T.astype(BF)
            tick(2)

        rows_of(mine)
        both_got(h1, 0)
        rows_of(other)

    pl.run_scoped(qkv, VM((2, D, 864), BF))
    put(h1, h1_out)
    tick(1)
    put(qa, q_out)
    put(ka, k_out)
    put(vt, v_out)

    def head(j, _):
        def queries(i, _):
            rows = pl.ds(pl.multiple_of(i * 512, 512), 512)
            scores = matmul_nt(ka[j], qa[j, rows, :])
            top = jnp.max(scores, axis=0, keepdims=True)
            prob = jnp.exp2(scores - top)
            total = jnp.sum(prob, axis=0, keepdims=True)
            result = matmul(vt[j], prob.astype(BF)) * (1.0 / total)
            attnt[j, :, rows] = result
            lse_out[j, :, rows] = top + jnp.log2(total)
            return 0

        lax.fori_loop(0, 2, queries, 0)
        return 0

    for j in range(8):
        head(j, 0)
        tick(3)

    for i in range(half // PART):
        moved(1 + half // PART + i)

    def close(t, _):
        rows = pl.ds(pl.multiple_of(t * TILE, TILE), TILE)
        spot = (mine + t * TILE + lax.broadcasted_iota(jnp.int32, (TILE, 1), 0)).astype(F32)
        outer = jnp.where(spot < live, dy[rows, :].astype(F32), 0.0)
        dy[rows, :] = outer.astype(BF)
        own_tile(closing, t)[...] = (outer * vec(5)).astype(BF)
        give(closing, t, 1).start()
        return 0

    lax.fori_loop(0, tiles, close, 0)
    put(attnt, attnt_out)
    tick_until(2)
    owns[1].wait()

    def proj(weight, stage, raw):
        load(gp, raw, 5)
        for i in (0, 1):
            for h in range(8):
                stage[h * 72 : h * 72 + 72, :] = raw[i, h].astype(F32)
            weight[i] = stage[...].astype(BF)

        def attn_rows(i, _):
            rows = pl.ds(pl.multiple_of(i * 256, 256), 256)
            value = jnp.concatenate([attnt[j, :, rows] for j in range(8)], axis=0)
            attn[rows, :] = value.T.astype(BF)
            return 0

        lax.fori_loop(0, 4, attn_rows, 0)

        def for_twin(t, _):
            rows = pl.ds(pl.multiple_of(t * WIDE, WIDE), WIDE)
            left = attn[pl.ds(pl.multiple_of(other + t * WIDE, WIDE), WIDE), :]
            for i in (0, 1):
                ps[rows, i * 576 : (i + 1) * 576] = matmul(left, weight[i]).astype(BF)
            rdma(ps.at[rows], pr.at[rows], ts.at[2, t], tr.at[2, t], twin).start()
            return 0

        for t in range(half // WIDE):
            for_twin(t, 0)
            tick(1)

        def for_me(t, _):
            rows = pl.ds(pl.multiple_of(t * WIDE, WIDE), WIDE)
            left = attn[pl.ds(pl.multiple_of(mine + t * WIDE, WIDE), WIDE), :]
            for i in (0, 1):
                acc[rows, i * 576 : (i + 1) * 576] = matmul(left, weight[i])
            return 0

        for t in range(half // WIDE):
            for_me(t, 0)
            tick(1)

    pl.run_scoped(proj, VM((2, 576, 576), BF), VM((576, 576), F32), VM((2, 8, 72, 576), BF))

    def middle(t, _):
        rows = pl.ds(pl.multiple_of(t * TILE, TILE), TILE)
        branch = acc[rows, :] + pr[rows, :].astype(F32) + b_p[...]
        ba[rows, :] = branch.astype(BF)
        value = x0[rows, :].astype(F32) + vec(2) * branch
        x1[rows, :] = value
        own_tile(h2, t)[...] = (normed_tile(value) * (1.0 + vec(4)) + vec(3)).astype(BF)
        give(h2, t, 3).start()
        return 0

    def half_got(src, dst, i, t):
        rows = pl.ds(t * WIDE, WIDE)
        rdma(src.at[rows], dst.at[rows], ts.at[i, t], tr.at[i, t], twin).wait()

    for t in range(tiles):
        if t % 2 == 0:
            half_got(ps, pr, 2, t // 2)
        middle(t, 0)
    put(ba, ba_out)
    put(x1, x1_out)
    put(x0, x0_out)
    put(dy, dy_out)
    tick_until(4)
    owns[2].wait()
    both_got(h2, 3)
    both_got(closing, 1)
    put(h2, h2_out)
    put(closing, cl_out)

    def up(weight):
        load(gu, weight, 6)

        def block_of(start, i, n):
            rows = pl.ds(start, half)
            part = slice(n * 384, (n + 1) * 384)
            cols = slice(i * D + n * 384, i * D + (n + 1) * 384)
            u = matmul(h2[rows, :], weight[i, :, part]) + b_u[:, cols]
            square = u * u
            inner = u * (GELU_A + GELU_A * GELU_B * square)
            bent = jnp.tanh(inner)
            half_up = 0.5 + 0.5 * bent
            act[rows, cols] = (u * half_up).astype(BF)
            slope = u * (GELU_A + 3.0 * GELU_A * GELU_B * square)
            der[rows, cols] = (half_up + slope * (half_up * (1.0 - bent))).astype(BF)

        for start in (mine, other):
            for i in (0, 1):
                for n in range(3):
                    block_of(start, i, n)
                    tick(n % 2)

    pl.run_scoped(up, VM((2, D, D), BF))
    put(der, der_out)

    gouts = []
    for t in range(6):
        slot = t % 2
        if t >= 2:
            gouts[t - 2].wait()
        value = matmul(act[:, t * 384 : (t + 1) * 384].T, closing[...])
        for i in (0, 1):
            gstage[slot, i] = value[:, i * 576 : (i + 1) * 576].astype(BF)
        d = pltpu.make_async_copy(
            gstage.at[slot], gred_out.at[:, pl.ds(t * 384, 384)], gsem.at[slot]
        )
        d.start()
        gouts.append(d)
        tick(1)
    for d in gouts[-2:]:
        d.wait()
    tick(len(steps))
    owns[3].wait()

    def down(weight):
        load(gd, weight, 7)

        for i in (0, 1):
            cols = slice(i * 576, (i + 1) * 576)
            ds[:, cols] = matmul(act[pl.ds(other, half), :], weight[i]).astype(BF)
        rdma(ds, dr, ts.at[4, 0], tr.at[4, 0], twin).start()
        for i in (0, 1):
            cols = slice(i * 576, (i + 1) * 576)
            acc[:, cols] = matmul(act[pl.ds(mine, half), :], weight[i])
        rdma(ds, dr, ts.at[4, 0], tr.at[4, 0], twin).wait()

    pl.run_scoped(down, VM((2, 2304, 576), BF))

    def finish(t, _):
        rows = pl.ds(pl.multiple_of(t * TILE, TILE), TILE)
        branch = acc[rows, :] + dr[rows, :].astype(F32) + b_d[...]
        bb[rows, :] = branch.astype(BF)
        yo[rows, :] = (x1[rows, :] + vec(5) * branch).astype(BF)
        return 0

    for t in range(tiles):
        finish(t, 0)
    put(bb, bb_out)
    put(yo, y_out)
    for d in out_copies:
        d.wait()
    gather.finish()


def forward_block(tokens, cotangent, bucket, table, masters, modulate_master, cond, biases):
    shapes = {
        "gq": (2, D, 864),
        "gp": (2, 8, 72, 576),
        "gu": (2, D, D),
        "gd": (2, 2304, 576),
    }
    half = tokens.shape[0]
    rows = 2 * half
    out_shape, out_specs = [], []

    def out(shape, dtype, space=ANY):
        out_shape.append(jax.ShapeDtypeStruct(shape, dtype))
        out_specs.append(pl.BlockSpec(memory_space=space))

    for s in shapes.values():
        out(s, BF)
    out((2, 1, 3456), F32, VM)
    out((16, 128), F32, VM)
    out((half, D), BF)
    out((half, D), BF)
    out((rows, D), BF)
    out((rows, D), BF)
    out((8, rows, 128), BF)
    out((8, rows, 128), BF)
    out((8, 72, rows), BF)
    out((8, 72, rows), F32)
    out((8, 1, rows), F32, VM)
    out((half, D), BF)
    out((half, D), F32)
    out((rows, D), BF)
    out((rows, 2304), BF)
    out((half, D), BF)
    out((half, D), BF)
    out((2, 2304, 576), BF)
    dma = pltpu.SemaphoreType.DMA
    scratch = [
        VM((144, 864), BF),
        VM((72, 576), BF),
        VM((144, D), BF),
        VM((288, 576), BF),
        VM((2, 72, 864), F32),
        VM((72, 864), F32),
        VM((2, 72, D), F32),
        VM((72, D), F32),
        VM((4, 2, 2, 16, 128), F32),
        VM((4, 2, 2, 1, 3456), F32),
        VM((3, 2, 2, 1, 3456), F32),
        VM((2, 2, 1, 3456), F32),
        VM((2, 1, 3456), F32),
        VM((3, 2, 1, 3456), F32),
        VM((2, 1, 3456), F32),
        VM((half, D), BF),
        VM((half, D), BF),
        VM((half, D), BF),
        VM((8, 128), F32),
        VM((rows, D), BF),
        VM((rows, D), BF),
        VM((8, rows, 128), BF),
        VM((8, rows, 128), BF),
        VM((8, 72, rows), BF),
        VM((8, 72, rows), F32),
        VM((rows, 576), BF),
        VM((half, D), BF),
        VM((half, D), BF),
        VM((half, D), BF),
        VM((half, D), BF),
        VM((half, D), F32),
        VM((half, D), F32),
        VM((rows, D), BF),
        VM((rows, 2304), BF),
        VM((rows, 2304), BF),
        VM((half, D), BF),
        VM((half, D), BF),
        VM((half, D), BF),
        VM((2, 2, 384, 576), BF),
        VM((1, 14 * D), F32),
        VM((1, 576), F32),
        VM((1, 576), F32),
        VM((1, 2304), F32),
        dma((8,)),
    ]
    n = len(CHUNKS)
    scratch += [dma((n, 4))] * 6 + [dma((n, 4, 2))] * 2 + [dma((n, 4))] * 2
    scratch += [
        dma((7, 3)),
        dma((7, 3)),
        dma((9,)),
        dma((9,)),
        dma((5, 4)),
        dma((5, 4)),
        dma((2, 2)),
        dma((20,)),
        dma((2,)),
    ]
    vm = pl.BlockSpec(memory_space=VM)
    hbm = pl.BlockSpec(memory_space=ANY)
    return pl.pallas_call(
        forward_kernel,
        out_shape=out_shape,
        in_specs=[vm, hbm] + [vm] * 9,
        out_specs=out_specs,
        scratch_shapes=scratch,
        compiler_params=pltpu.CompilerParams(
            collective_id=0, has_side_effects=True, vmem_limit_bytes=60 * 2**20
        ),
        name="forward_block",
    )(tokens, cotangent, bucket, table, *masters, modulate_master, cond, biases)


class Scatter:
    def __init__(self, grads, boxes, outs, sems):
        self.grads, self.outs = grads, outs
        self.pair_box, self.diag_box, self.x_box, self.y_box, self.z_box = boxes
        self.ps, self.pr, self.fs, self.fr, self.xs, self.xr, self.ys, self.yr, self.zs, self.zr = sems
        self.sent = []

    def piece(self, i, flip_y, k, flip_x):
        z, x, c, y = place()
        weight, first, count, _ = CHUNKS[i]
        return piece_at(
            self.grads[weight], weight, 1 - y if flip_y else y, at_z(k), 1 - x if flip_x else x, first, count
        )

    def box(self, boxes, i, n):
        weight, first, count, _ = CHUNKS[i]
        return boxes[weight].at[n, pl.ds(first, count)]

    def send(self, make):
        make().start()
        self.sent.append(make)

    def arrived(self, ref, s, r):
        rdma(ref, ref, s, r, partners()[0]).wait_recv()

    def add(self, target, *others):
        rows = target.shape[0]
        step = 16 if rows % 16 == 0 else rows

        def some(n, _):
            at = pl.ds(pl.multiple_of(n * step, step), step) if rows != step else slice(None)
            total = target[at, :].astype(F32)
            for o in others:
                total = total + o[at, :].astype(F32)
            target[at, :] = total.astype(BF)
            return 0

        if rows == step:
            some(0, 0)
        else:
            lax.fori_loop(0, rows // step, some, 0)

    def across(self, i, k, by_y):
        if by_y:
            return rdma(
                self.piece(i, 1, k, 0), self.box(self.y_box, i, k), self.ys.at[i, k], self.yr.at[i, k], partners()[1]
            )
        return rdma(
            self.piece(i, 0, k, 1), self.box(self.x_box, i, k), self.xs.at[i, k], self.xr.at[i, k], partners()[0]
        )

    def start(self, i):
        def to_pair(k):
            return rdma(
                self.piece(i, 1, k ^ 1, 1),
                self.box(self.pair_box, i, k // 2),
                self.ps.at[i, k],
                self.pr.at[i, k],
                partners()[3][1],
            )

        for k in (0, 2):
            self.send(functools.partial(to_pair, k))
        for k in (1, 3):
            for by_y in (0, 1):
                self.send(functools.partial(self.across, i, k, by_y))

    def corner(self, i, k):
        box = self.box(self.pair_box, i, k // 2)
        self.arrived(box, self.ps.at[i, k], self.pr.at[i, k])
        self.add(self.piece(i, 1, k, 1), box)
        spans = parts_of(i, k)

        def part(n):
            return rdma(
                self.piece(i, 1, k, 1).at[pl.ds(*spans[n])],
                self.box(self.diag_box, i, k // 2).at[pl.ds(*spans[n])],
                self.fs.at[i, k, n],
                self.fr.at[i, k, n],
                partners()[1 - n],
            )

        for n in (0, 1):
            if spans[n] is not None:
                self.send(functools.partial(part, n))

    def plane(self, i, k):
        spans = parts_of(i, k)
        for n in (0, 1):
            if spans[n] is not None:
                part = self.box(self.diag_box, i, k // 2).at[pl.ds(*spans[n])]
                self.arrived(part, self.fs.at[i, k, n], self.fr.at[i, k, n])
                self.add(self.piece(i, n, k, 1 - n).at[pl.ds(*spans[n])], part)
            self.send(functools.partial(self.across, i, k, n))

    def both(self, i, k):
        boxes = []
        for boxes_of, s, r in ((self.x_box, self.xs, self.xr), (self.y_box, self.ys, self.yr)):
            box = self.box(boxes_of, i, k)
            self.arrived(box, s.at[i, k], r.at[i, k])
            boxes.append(box)
        return boxes

    def column(self, i, k):
        self.add(self.piece(i, 0, k, 0), *self.both(i, k))

        def along():
            return rdma(
                self.piece(i, 0, k, 0),
                self.box(self.z_box, i, k - 1),
                self.zs.at[i, k],
                self.zr.at[i, k],
                partners()[3][k],
            )

        self.send(along)

    def last(self, i):
        weight, first, count, _ = CHUNKS[i]
        boxes = self.both(i, 0)
        for k in (1, 2, 3):
            box = self.box(self.z_box, i, k - 1)
            self.arrived(box, self.zs.at[i, k], self.zr.at[i, k])
            boxes.append(box)
        total = self.piece(i, 0, 0, 0)[...].astype(F32)
        for box in boxes:
            total = total + box[...].astype(F32)
        self.outs[weight][first : first + count, :] = total

    def finish(self):
        for make in self.sent:
            make().wait_send()

    def steps(self, i):
        return (
            [(self.start, i), (self.corner, i, 0), (self.corner, i, 2)],
            [(self.plane, i, 0), (self.plane, i, 2), (self.column, i, 1)],
            [(self.column, i, 3), (self.column, i, 2)],
            [(self.last, i)],
        )


def total_steps(dm, bs, lhs, mods, bufs, gmod, bias_out, s, r):
    dmt, got_m, got_b, sb, got_z, near = bufs

    def hop(i):
        z, x, c, y = place()
        xn, yn, twin, zn = partners()
        if i == 0:
            pairs = [(dm, got_m, twin), (bs, got_b.at[0], twin)]
        elif i == 1:
            pairs = [(dmt.at[1 - y], mods.at[z, x, y], yn), (sb.at[0], got_b.at[1], yn)]
        elif i == 2:
            pairs = [(mods.at[z, x], mods.at[z, x], xn), (sb.at[1], got_b.at[2], xn)]
        elif i == 3:
            pairs = [(mods.at[z], mods.at[z], zn[k]) for k in (1, 2, 3)]
            pairs += [(sb.at[2], got_z.at[k - 1], zn[k]) for k in (1, 2, 3)]
        else:
            pairs = [(near.at[0], near.at[1], yn)]
        return [
            rdma(src, dst, s.at[i, n], r.at[i, n], to) for n, (src, dst, to) in enumerate(pairs)
        ]

    def step(i):
        z, x, c, y = place()
        if i > 0:
            for d in hop(i - 1):
                d.wait()
        if i == 1:
            dmt[...] = rounded(dm[...] + got_m[...])
            mods[z, x, y] = dmt[y]
            sb[0] = bs[...] + got_b[0]
        elif i == 2:
            sb[1] = sb[0] + got_b[1]
        elif i == 3:
            sb[2] = sb[1] + got_b[2]
        elif i == 4:
            rows = [mods[n // 4, n // 2 % 2, n % 2] for n in range(16)]
            total = rows[0]
            for row in rows[1:]:
                total = total + row
            near[0] = total
            bias_out[:, 6 * D :] = (sb[2] + got_z[0]) + (got_z[1] + got_z[2])
            left = lhs[:, :72].astype(BF)
            right = jnp.concatenate(rows, axis=0).astype(BF)
            for j in range(3):
                cols = slice(j * D, (j + 1) * D)
                gmod[:, cols] = matmul_tn(left, right[:, cols])
        elif i == 5:
            for n in (0, 1):
                bias_out[:, n * 3456 : (n + 1) * 3456] = jnp.where(y == n, near[0], near[1])
        if i < 5:
            for d in hop(i):
                d.start()

    return [functools.partial(step, i) for i in range(6)]


BEATS = {
    "down": "010101",
    "expand": "010101",
    "up": "010101",
    "middle": "1010",
    "project": "1010",
    "heads": "0001",
    "attend": "010101",
    "back": "111111",
    "input": "1111",
    "hops": "111111",
}


def backward_kernel(*refs):
    gq, gp, gu, gd, mod, lhs = refs[:6]
    (x0_in, dy_in, cl_in, h1_in, q_in, k_in, v_in, at_in, lse) = refs[6:15]
    (ba_in, x1_in, h2_in, der_in, bb_in, y_in, gred) = refs[15:22]
    (out, ig_out, s_att, s_proj, s_exp, s_red, gmod, bias_out, norm_out) = refs[22:31]
    grads = refs[31:35]
    boxes = [refs[35 + 4 * i : 39 + 4 * i] for i in range(5)]
    fq, fu, gotq, gotu = refs[55:59]
    dba, dx1, ps, pr, dm, bs, mods = refs[59:66]
    total_bufs = refs[66:72]
    sq, here = refs[72:74]
    lsem = refs[74]
    scatter_sems = refs[75:85]
    ts, tr, ws, wr, hs, hr, ns, nr = refs[85:93]
    z, x, c, y = place()
    xn, yn, twin, zn = partners()
    half = dx1.shape[0]
    mine = pl.multiple_of(c * half, half)
    other = pl.multiple_of((1 - c) * half, half)
    scatter = Scatter(grads, boxes, (fq, s_proj, fu, s_red), scatter_sems)
    hops = total_steps(dm, bs, lhs, mods, total_bufs, gmod, bias_out, hs, hr)
    pltpu.make_async_copy(gred, grads[3], lsem.at[0]).start()
    greet([xn, yn, twin] + zn[1:], swapped=True)
    dm[...] = jnp.zeros_like(dm)
    bs[...] = jnp.zeros_like(bs)
    TILE = 128
    swap_to = (z, x, y, c)

    def vec(i):
        return mod[i // 3, :, (i % 3) * D : (i % 3 + 1) * D]

    def add_mod(i, value):
        cols = slice((i % 3) * D, (i % 3 + 1) * D)
        dm[i // 3, :, cols] = dm[i // 3, :, cols] + jnp.sum(value, axis=0, keepdims=True)

    def add_bias(at, value):
        cols = slice(at, at + value.shape[1])
        bs[:, cols] = bs[:, cols] + value

    def load(src, dst, i):
        d = pltpu.make_async_copy(src, dst, lsem.at[i])
        d.start()
        return d

    queue = []

    def tick(n):
        for _ in range(min(n, len(queue))):
            f, *a = queue.pop(0)
            f(*a)

    def beat(where, n):
        tick(int(BEATS[where][n]))

    def moves(i):
        if i == 0:
            return y_in, out
        rows = pl.ds((i - 1) * TILE, TILE)
        return dba.at[rows], ig_out.at[rows]

    def move(i):
        @pl.when(c != y)
        def _():
            rdma(*moves(i), ws.at[i], wr.at[i], swap_to).start()

        @pl.when(c == y)
        def _():
            pltpu.make_async_copy(*moves(i), ws.at[i]).start()

    def moved(i):
        @pl.when(c != y)
        def _():
            rdma(*moves(i), ws.at[i], wr.at[i], swap_to).wait()

        @pl.when(c == y)
        def _():
            pltpu.make_async_copy(*moves(i), ws.at[i]).wait()

    load_d = pltpu.make_async_copy(gred, grads[3], lsem.at[0])
    load_d.wait()
    scatter.start(5)
    scatter.start(6)
    five, six = scatter.steps(5), scatter.steps(6)
    queue += five[0][1:] + six[0][1:] + five[1] + six[1] + five[2] + six[2] + five[3] + six[3]

    def own_tile(ref, t):
        return ref.at[pl.ds(pl.multiple_of(mine + t * TILE, TILE), TILE)]

    def widen(du):
        def through(weight, closing, der):
            loads = [load(gd, weight, 1), load(cl_in, closing, 2)]

            def slopes(n):
                return load(der_in.at[:, pl.ds(n * 384, 384)], der.at[n % 2], 3 + n % 2)

            coming = slopes(0)
            for d in loads:
                d.wait()
            for n in range(6):
                cols = slice(n * 384, (n + 1) * 384)
                coming.wait()
                if n < 5:
                    coming = slopes(n + 1)
                right = jnp.concatenate([weight[0, cols, :], weight[1, cols, :]], axis=1)
                value = (matmul_nt(closing[...], right) * der[n % 2].astype(F32)).astype(BF)
                du[:, cols] = value
                sums = jnp.sum(value.astype(F32), axis=0, keepdims=True)
                here[:, cols] = sums
                beat("down", n)
            for j in range(8):
                block = here[:, j * BLOCK : (j + 1) * BLOCK]
                for p in (0, 1):
                    add_bias(3 * D + (2 * j + p) * BLOCK, jnp.where(c == p, block, 0.0))

        pl.run_scoped(through, VM((2, 2304, 576), BF), VM((2 * half, D), BF), VM((2, 2 * half, 384), BF))

        def expand_grad(h2):
            load(h2_in, h2, 2).wait()
            for t in range(3):
                left = h2[:, t * 384 : (t + 1) * 384].T
                for i in (0, 1):
                    grads[2][i, t * 384 : (t + 1) * 384, :] = matmul(
                        left, du[:, i * D : (i + 1) * D]
                    ).astype(BF)
                    beat("expand", 2 * t + i)

        pl.run_scoped(expand_grad, VM((2 * half, D), BF))
        scatter.start(3)
        scatter.start(4)
        three, four = scatter.steps(3), scatter.steps(4)
        queue.extend(three[0][1:] + four[0][1:] + three[1] + four[1] + three[2] + four[2] + three[3] + four[3])
        move(0)

        def back(weight):
            load(gu, weight, 1).wait()

            def product(start, n):
                rows = pl.ds(start, half)
                part = slice(n * 384, (n + 1) * 384)
                return matmul_nt(du[rows, :D], weight[0, part, :]) + matmul_nt(du[rows, D:], weight[1, part, :])

            for n in range(3):
                ps[:, n * 384 : (n + 1) * 384] = product(other, n).astype(BF)
                beat("up", n)
            rdma(ps, pr, ts.at[0, 0], tr.at[0, 0], twin).start()
            for n in range(3):
                dx1[:, n * 384 : (n + 1) * 384] = product(mine, n)
                beat("up", 3 + n)

        pl.run_scoped(back, VM((2, D, D), BF))

    pl.run_scoped(widen, VM((2 * half, 2304), BF))

    def sums_got(i):
        rdma(ps, pr, ts.at[i, 0], tr.at[i, 0], twin).wait()

    def norm_back(value, scaling, gradient):
        average = jnp.mean(value, axis=-1, keepdims=True)
        centred = value - average
        inverse = lax.rsqrt(jnp.mean(centred * centred, axis=-1, keepdims=True) + 1e-06)
        normed = centred * inverse
        inner = gradient * (1.0 + scaling)
        part = inner - jnp.mean(inner, axis=-1, keepdims=True)
        part = part - normed * jnp.mean(inner * normed, axis=-1, keepdims=True)
        return part * inverse, normed

    def middle(x1, dy, ba, bb):
        loads = [load(x1_in, x1, 1), load(dy_in, dy, 2), load(ba_in, ba, 3), load(bb_in, bb, 4)]
        for d in loads:
            d.wait()
        sums_got(0)
        for t in range(half // TILE):
            rows = slice(t * TILE, (t + 1) * TILE)
            gradient = dx1[rows, :] + pr[rows, :].astype(F32)
            part, normed = norm_back(x1[rows, :], vec(4), gradient)
            add_mod(3, gradient)
            add_mod(4, gradient * normed)
            outer = dy[rows, :].astype(F32)
            add_mod(5, outer * bb[rows, :].astype(F32))
            add_bias(9216 - D, jnp.sum(rounded(outer * vec(5)), axis=0, keepdims=True))
            total = outer + part
            dx1[rows, :] = total
            add_mod(2, total * ba[rows, :].astype(F32))
            branch = (total * vec(2)).astype(BF)
            own_tile(dba, t)[...] = branch
            tile = own_tile(dba, t)
            rdma(tile, tile, ts.at[1, t], tr.at[1, t], twin).start()
            add_bias(2 * D, jnp.sum(branch.astype(F32), axis=0, keepdims=True))
            beat("middle", t)

    pl.run_scoped(middle, VM((half, D), F32), VM((half, D), BF), VM((half, D), BF), VM((half, D), BF))

    def attention(dot, dqkv):
        def project(weight, stage, raw, attnt, attn):
            loads = [load(gp, raw, 1), load(at_in, attnt, 2)]
            for d in loads:
                d.wait()
            for i in (0, 1):
                for h in range(8):
                    stage[h * 72 : h * 72 + 72, :] = raw[i, h].astype(F32)
                weight[i] = stage[...].astype(BF)
            attn[...] = jnp.concatenate([attnt[h] for h in range(8)], axis=0).astype(BF)
            for t in range(half // TILE):
                tile = own_tile(dba, t)
                rdma(tile, tile, ts.at[1, t], tr.at[1, t], twin).wait_send()
                part = dba.at[pl.ds(pl.multiple_of(other + t * TILE, TILE), TILE)]
                rdma(part, part, ts.at[1, t], tr.at[1, t], twin).wait_recv()
            for n in range(4):
                rows = slice(n * 256, (n + 1) * 256)
                right = dba[rows, :]
                value = matmul_nt(weight[0], right[:, :576]) + matmul_nt(weight[1], right[:, 576:])
                for h in range(8):
                    dot[h, :, rows] = value[h * 72 : h * 72 + 72, :].astype(BF)
                beat("project", n)
            for i in (0, 1):
                stage[...] = matmul(attn[...], dba[:, i * 576 : (i + 1) * 576])
                for h in range(8):
                    grads[1][i, h] = stage[h * 72 : h * 72 + 72, :].astype(BF)

        pl.run_scoped(
            project,
            VM((2, 576, 576), BF),
            VM((576, 576), F32),
            VM((2, 8, 72, 576), BF),
            VM((8, 72, 2 * half), F32),
            VM((576, 2 * half), BF),
        )
        scatter.start(2)
        two = scatter.steps(2)
        queue.extend(two[0][1:] + two[1] + two[2] + two[3])

        def heads(qa, ka, vt, at, dk, dv, dq):
            def fetch(h):
                n = h % 2
                return [
                    load(src.at[h], dst.at[n], 1 + 4 * n + m)
                    for m, (src, dst) in enumerate(((q_in, qa), (k_in, ka), (v_in, vt), (at_in, at)))
                ]

            coming = fetch(0)
            for h in range(8):
                n = h % 2
                for d in coming:
                    d.wait()
                if h < 7:
                    coming = fetch(h + 1)
                value = vt[n].T
                key_t = ka[n, :, :72].T
                inner = jnp.sum(at[n] * dot[h].astype(F32), axis=0, keepdims=True)
                dk[...] = jnp.zeros_like(dk)
                dv[...] = jnp.zeros_like(dv)
                for i in range(4):
                    rows = slice(i * 256, (i + 1) * 256)
                    query = qa[n, rows, :]
                    grad = dot[h, :, rows]
                    scores = matmul_nt(ka[n], query)
                    prob = jnp.exp2(scores - lse[h, :, rows])
                    change = matmul(value, grad) - inner[:, rows]
                    dscore = (prob * change).astype(BF)
                    dv[...] += matmul_nt(grad, prob.astype(BF))
                    dk[...] += matmul_nt(query[:, :72].T, dscore)
                    dq[:, rows] = matmul(key_t, dscore)
                    beat("heads", i)
                scale = HEAD_DIM ** (-0.5)
                dqkv[0, :, h * 72 : h * 72 + 72] = (dq[...] * scale).T.astype(BF)
                key_grad = (dk[...] * math.log(2.0)).T.astype(BF)
                if h < 4:
                    dqkv[0, :, 576 + h * 72 : 648 + h * 72] = key_grad
                else:
                    dqkv[1, :, h * 72 - 288 : h * 72 - 216] = key_grad
                dqkv[1, :, 288 + h * 72 : 360 + h * 72] = dv[...].T.astype(BF)

        pl.run_scoped(
            heads,
            VM((2, 2 * half, 128), BF),
            VM((2, 2 * half, 128), BF),
            VM((2, 72, 2 * half), BF),
            VM((2, 72, 2 * half), F32),
            VM((72, 2 * half), F32),
            VM((72, 2 * half), F32),
            VM((72, 2 * half), F32),
        )

        def attend_grad(h1):
            load(h1_in, h1, 1).wait()
            for t in range(3):
                left = h1[:, t * 384 : (t + 1) * 384].T
                for i in (0, 1):
                    grads[0][i, t * 384 : (t + 1) * 384, :] = matmul(left, dqkv[i]).astype(BF)
                    beat("attend", 2 * t + i)

        pl.run_scoped(attend_grad, VM((2 * half, D), BF))
        scatter.start(0)
        scatter.start(1)
        zero, one = scatter.steps(0), scatter.steps(1)
        queue.extend(zero[0][1:] + one[0][1:] + zero[1] + one[1] + zero[2] + one[2] + zero[3] + one[3])

        def back(weight, x0, acc):
            loads = [load(gq, weight, 1), load(x0_in, x0, 2)]
            for d in loads:
                d.wait()

            def product(start, n):
                rows = pl.ds(start, half)
                part = slice(n * 384, (n + 1) * 384)
                return matmul_nt(dqkv[0, rows, :], weight[0, part, :]) + matmul_nt(
                    dqkv[1, rows, :], weight[1, part, :]
                )

            for n in range(3):
                ps[:, n * 384 : (n + 1) * 384] = product(other, n).astype(BF)
                beat("back", n)
            rdma(ps, pr, ts.at[2, 0], tr.at[2, 0], twin).start()
            for n in range(3):
                acc[:, n * 384 : (n + 1) * 384] = product(mine, n)
                beat("back", 3 + n)
            sums_got(2)
            for t in range(half // TILE):
                rows = slice(t * TILE, (t + 1) * TILE)
                gradient = acc[rows, :] + pr[rows, :].astype(F32)
                part, normed = norm_back(x0[rows, :].astype(F32), vec(1), gradient)
                add_mod(0, gradient)
                add_mod(1, gradient * normed)
                dba[rows, :] = (dx1[rows, :] + part).astype(BF)
                move(1 + t)
                beat("input", t)

        pl.run_scoped(back, VM((2, D, 864), BF), VM((half, D), BF), VM((half, D), F32))
        for i in (0, 1):
            sums = jnp.sum(dqkv[i].astype(F32), axis=0, keepdims=True)
            for j in range(8):
                block = sums[:, i * 288 + j * 72 : i * 288 + j * 72 + 72]
                for p in (0, 1):
                    add_bias(i * D + (2 * j + p) * 72, jnp.where(c == p, block, 0.0))

    pl.run_scoped(attention, VM((8, 72, 2 * half), BF), VM((2, 2 * half, 864), BF))
    for n, hop in enumerate(hops):
        hop()
        beat("hops", n)
    tick(len(queue))

    last_half = 72
    def give(f, got, i):
        return rdma(f.at[pl.ds(pl.multiple_of((1 - c) * 72, 8), 72)], got, ts.at[3, i], tr.at[3, i], twin)

    give(fq, gotq, 0).start()
    give(fu, gotu, 1).start()

    def squares(value):
        return jnp.sum(jnp.sum(value * value, axis=0, keepdims=True), axis=1, keepdims=True)

    bias_squares = squares(bias_out[...])
    total = squares(fq[...]) + squares(fu[...]) + squares(s_proj[...]) + squares(s_red[...]) + squares(gmod[...])
    total = jnp.broadcast_to(total, (8, 128))
    for i, to in enumerate((twin, yn, xn)):
        sq[2 * i] = total
        d = rdma(sq.at[2 * i], sq.at[2 * i + 1], ns.at[i], nr.at[i], to)
        d.start()
        d.wait()
        total = total + sq[2 * i + 1]
    sq[6] = total
    last = [rdma(sq.at[6], sq.at[6 + k], ns.at[2 + k], nr.at[2 + k], zn[k]) for k in (1, 2, 3)]
    for d in last:
        d.start()

    def interleave(f, got, shard, width, i):
        give(f, got, i).wait()
        own = jnp.where(c == 0, f[:72, :], f[72:, :])
        sides = (jnp.where(c == 0, own, got[...]), jnp.where(c == 0, got[...], own))
        count = own.shape[1] // width
        shard[...] = jnp.concatenate(
            [sides[p][:, j * width : (j + 1) * width] for j in range(count) for p in (0, 1)], axis=1
        )

    interleave(fq, gotq, s_att, HEAD_DIM, 0)
    interleave(fu, gotu, s_exp, BLOCK, 1)
    for d in last:
        d.wait()
    norm_out[...] = (sq[6] + sq[7]) + (sq[8] + sq[9]) + bias_squares
    for i in range(1 + half // TILE):
        moved(i)
    scatter.finish()


def backward_block(kept):
    half = kept[6].shape[0]
    rows = 2 * half
    sd = jax.ShapeDtypeStruct
    vm = pl.BlockSpec(memory_space=VM)
    hbm = pl.BlockSpec(memory_space=ANY)
    sizes = ((D, 864), (72, 576), (D, D), (2304, 576))
    pieces = [PIECES[n][:2] for n in NAMES]
    dma = pltpu.SemaphoreType.DMA
    n = len(CHUNKS)
    scratch = [
        VM((2, D, 864), BF),
        VM((2, 8, 72, 576), BF),
        VM((2, D, D), BF),
        VM((2, 2304, 576), BF),
    ]
    for count in (2, 2, 4, 4, 3):
        scratch += [VM((count,) + p, BF) for p in pieces]
    scratch += [
        VM((144, 864), F32),
        VM((144, D), F32),
        VM((72, 864), F32),
        VM((72, D), F32),
        VM((rows, D), BF),
        VM((half, D), F32),
        VM((half, D), BF),
        VM((half, D), BF),
        VM((2, 1, 3456), F32),
        VM((1, 9216), F32),
        VM((4, 2, 2, 1, 3456), F32),
        VM((2, 1, 3456), F32),
        VM((2, 1, 3456), F32),
        VM((3, 1, 9216), F32),
        VM((3, 1, 9216), F32),
        VM((3, 1, 9216), F32),
        VM((2, 1, 3456), F32),
        VM((10, 8, 128), F32),
        VM((1, 2304), F32),
        dma((9,)),
    ]
    scratch += [dma((n, 4))] * 2 + [dma((n, 4, 2))] * 2 + [dma((n, 4))] * 6
    scratch += [dma((4, 4))] * 2 + [dma((5,))] * 2 + [dma((5, 6))] * 2 + [dma((6,))] * 2
    places = [hbm] * 4 + [vm, vm] + [hbm] * 8 + [vm] + [hbm] * 7
    return pl.pallas_call(
        backward_kernel,
        out_shape=[
            sd((half, D), BF),
            sd((half, D), BF),
            sd((72, 1728), F32),
            sd((72, 576), F32),
            sd((72, 2304), F32),
            sd((288, 576), F32),
            sd((72, 3456), F32),
            sd((1, 14 * D), F32),
            sd((8, 128), F32),
        ],
        in_specs=places,
        out_specs=[hbm, hbm] + [vm] * 7,
        scratch_shapes=scratch,
        compiler_params=pltpu.CompilerParams(
            collective_id=1, has_side_effects=True, vmem_limit_bytes=62 * 2**20
        ),
        name="backward_block",
    )(*kept)


def step_kernel(squares, correction, *refs):
    count = len(RATES)
    norm = jnp.sqrt(squares[0:1, 0:1])
    clip = jnp.minimum(1.0, 1.0 / (norm + 1e-06))
    fix = correction[0:1, 0:1]
    for i, rate in enumerate(RATES):
        master, first, second, gradient = (refs[4 * i + j][...] for j in range(4))
        new = adam_update(master, first, second, gradient, rate, clip, fix)
        for j in range(3):
            refs[4 * count + 3 * i + j][...] = new[j]


RATES = (0.5 * D ** (-0.5),) * 4 + (0.5 * FF ** (-0.5),)


def step_weights(squares, correction, states):
    grid = 9

    def spec(shape):
        return pl.BlockSpec((shape[0] // grid, shape[1]), lambda i: (i, 0))

    whole = pl.BlockSpec((8, 128), lambda i: (0, 0))
    flat = [value for state in states for value in state]
    new = [value for state in states for value in state[:3]]
    return pl.pallas_call(
        step_kernel,
        grid=(grid,),
        out_shape=[jax.ShapeDtypeStruct(v.shape, v.dtype) for v in new],
        in_specs=[whole, whole] + [spec(v.shape) for v in flat],
        out_specs=[spec(v.shape) for v in new],
        compiler_params=pltpu.CompilerParams(vmem_limit_bytes=62 * 2**20),
        name="step_weights",
    )(squares, correction, *flat)


def on_device_fast(
    tokens,
    cotangent,
    buckets,
    timesteps,
    labels,
    class_table,
    step_count,
    modulate_master,
    modulate_first,
    modulate_second,
    attend_master,
    attend_first,
    attend_second,
    project_master,
    project_first,
    project_second,
    expand_master,
    expand_first,
    expand_second,
    reduce_master,
    reduce_first,
    reduce_second,
    biases_master,
    biases_first,
    biases_second,
):

    z, x, c, y = place()
    bf16, f32 = jnp.bfloat16, jnp.float32
    block = FF // 16
    class_row = lax.dynamic_slice_in_dim(class_table, labels[0], 1).astype(f32)
    condition = jax.nn.silu(class_row + time_features(timesteps, D)).astype(bf16).astype(f32)
    cond_tiles = jnp.pad(condition.reshape(16, 72), ((0, 0), (0, 56)))
    bucket = jnp.broadcast_to(buckets.astype(f32)[:, None], (8, 128))
    steps = jnp.arange(64, dtype=f32)[:, None]
    omegas = jnp.exp(-math.log(10000.0) * jnp.arange(288, dtype=f32) / 288)[None, :]
    table = jnp.concatenate([jnp.sin(steps * omegas), jnp.cos(steps * omegas)], axis=1)
    kept = forward_block(
        tokens,
        cotangent,
        bucket,
        table,
        (attend_master, project_master, expand_master, reduce_master),
        modulate_master,
        cond_tiles,
        biases_master[None, :],
    )
    (output, input_grad, grad_attend, grad_project, grad_expand, grad_reduce, grad_mod, bias_total, squares) = (
        backward_block(kept)
    )
    correction = 1.0 - jnp.power(0.5, step_count.astype(f32))
    states = (
        (modulate_master, modulate_first, modulate_second, grad_mod),
        (attend_master, attend_first, attend_second, grad_attend),
        (project_master, project_first, project_second, grad_project),
        (expand_master, expand_first, expand_second, grad_expand),
        (reduce_master, reduce_first, reduce_second, grad_reduce),
    )
    updates = list(step_weights(squares, jnp.full((8, 128), correction), states))
    grad_norm = jnp.sqrt(squares[0, 0])
    clip_factor = jnp.minimum(1.0, 1.0 / (grad_norm + 1e-06))
    updates += adam_update(
        biases_master, biases_first, biases_second, bias_total[0], 0.1, clip_factor, correction
    )
    return (output, input_grad.astype(f32), grad_norm, *updates)


def fast_solution(mesh):
    return jax.shard_map(
        on_device_fast,
        mesh=mesh,
        in_specs=(
            P(("z", "x", "c", "y"), None),
            P(("z", "x", "c", "y"), None),
            P(("z", "x", "c")),
            P(("z", "x", "c")),
            P(("z", "x", "c")),
            P(),
            P(),
            P(("z", "x", "c"), "y"),
            P(("z", "x", "c"), "y"),
            P(("z", "x", "c"), "y"),
            P(("z", "x", "c"), "y"),
            P(("z", "x", "c"), "y"),
            P(("z", "x", "c"), "y"),
            P(("z", "x", "c"), "y"),
            P(("z", "x", "c"), "y"),
            P(("z", "x", "c"), "y"),
            P(("z", "x", "c"), "y"),
            P(("z", "x", "c"), "y"),
            P(("z", "x", "c"), "y"),
            P(("z", "x", "c"), "y"),
            P(("z", "x", "c"), "y"),
            P(("z", "x", "c"), "y"),
            P(),
            P(),
            P(),
        ),
        out_specs=(
            P(("z", "x", "c", "y"), None),
            P(("z", "x", "c", "y"), None),
            P(),
            P(("z", "x", "c"), "y"),
            P(("z", "x", "c"), "y"),
            P(("z", "x", "c"), "y"),
            P(("z", "x", "c"), "y"),
            P(("z", "x", "c"), "y"),
            P(("z", "x", "c"), "y"),
            P(("z", "x", "c"), "y"),
            P(("z", "x", "c"), "y"),
            P(("z", "x", "c"), "y"),
            P(("z", "x", "c"), "y"),
            P(("z", "x", "c"), "y"),
            P(("z", "x", "c"), "y"),
            P(("z", "x", "c"), "y"),
            P(("z", "x", "c"), "y"),
            P(("z", "x", "c"), "y"),
            P(),
            P(),
            P(),
        ),
        check_vma=False,
    )


def plain_solution(mesh):
    return jax.shard_map(
        on_device,
        mesh=mesh,
        in_specs=(
            P(("seq", "head"), None),
            P(("seq", "head"), None),
            P("seq"),
            P("seq"),
            P("seq"),
            P(),
            P(),
            P("seq", "head"),
            P("seq", "head"),
            P("seq", "head"),
            P("seq", "head"),
            P("seq", "head"),
            P("seq", "head"),
            P("seq", "head"),
            P("seq", "head"),
            P("seq", "head"),
            P("seq", "head"),
            P("seq", "head"),
            P("seq", "head"),
            P("seq", "head"),
            P("seq", "head"),
            P("seq", "head"),
            P(),
            P(),
            P(),
        ),
        out_specs=(
            P(("seq", "head"), None),
            P(("seq", "head"), None),
            P(),
            P("seq", "head"),
            P("seq", "head"),
            P("seq", "head"),
            P("seq", "head"),
            P("seq", "head"),
            P("seq", "head"),
            P("seq", "head"),
            P("seq", "head"),
            P("seq", "head"),
            P("seq", "head"),
            P("seq", "head"),
            P("seq", "head"),
            P("seq", "head"),
            P("seq", "head"),
            P("seq", "head"),
            P(),
            P(),
            P(),
        ),
        check_vma=False,
    )


def solution(mesh):
    if dict(mesh.shape) == {"seq": 16, "head": 2}:
        grid = Mesh(mesh.devices.reshape(4, 2, 2, 2), ("z", "x", "c", "y"))
        return fast_solution(grid)
    return plain_solution(mesh)
```

```python
import functools
import math

import jax
import jax.numpy as jnp
from jax import lax
from jax.experimental import pallas as pl
from jax.experimental.pallas import tpu as pltpu
from jax.sharding import Mesh
from jax.sharding import PartitionSpec as P

D = 1152
HEAD_DIM = 72
FF = 4608
SIDE = 32
LMAX = 1024


highest = lax.Precision.HIGHEST
row_units = (8, 4, 16, 6, 10, 7, 4, 6)
col_units = (8, 16, 4, 10, 6, 9, 8, 6)


def table_pick(indices, entries):
    matches = indices[..., None] == jnp.arange(len(entries), dtype=jnp.int32)
    return jnp.sum(jnp.where(matches, jnp.array(entries, jnp.int32), 0), axis=-1)


def layer_norm(value):
    average = jnp.mean(value, axis=-1, keepdims=True)
    centred = value - average
    spread = jnp.mean(centred * centred, axis=-1, keepdims=True)
    return centred * lax.rsqrt(spread + 1e-06)


def modulate(value, shift, scaling):
    return layer_norm(value) * (1.0 + scaling) + shift


def time_features(moments, width):
    half_width = width // 2
    frequency = jnp.exp(-math.log(10000.0) * jnp.arange(half_width, dtype=jnp.float32) / half_width)
    angles = moments.astype(jnp.float32)[:, None] * frequency[None, :]
    return jnp.concatenate([jnp.cos(angles), jnp.sin(angles)], axis=1)


def grid_features(position, row_wide, width):
    quarter = width // 4
    omegas = jnp.exp(-math.log(10000.0) * jnp.arange(quarter, dtype=jnp.float32) / quarter)
    row_angle = (position // row_wide).astype(jnp.float32)[:, None] * omegas[None, :]
    col_angle = (position % row_wide).astype(jnp.float32)[:, None] * omegas[None, :]
    return jnp.concatenate(
        [jnp.sin(row_angle), jnp.cos(row_angle), jnp.sin(col_angle), jnp.cos(col_angle)], axis=1
    )


def fold_rows(left_side, weight_slab):
    return jnp.dot(
        left_side,
        lax.all_gather(weight_slab, "seq", axis=0, tiled=True),
        preferred_element_type=jnp.float32,
    )


def back_cols(gradient, weight_slab):
    return lax.dot_general(
        gradient,
        lax.all_gather(weight_slab, "seq", axis=0, tiled=True),
        (((1,), (1,)), ((), ())),
        preferred_element_type=jnp.float32,
    )


def rows_seq(left_side, right_side):
    return lax.psum_scatter(
        lax.dot_general(
            left_side, right_side, (((0,), (0,)), ((), ())), preferred_element_type=jnp.float32
        ).astype(jnp.bfloat16),
        "seq",
        scatter_dimension=0,
        tiled=True,
    ).astype(jnp.float32)


def attend(queries, key_rows, value_rows, lengths):
    heads_here = queries.shape[1] // HEAD_DIM
    block_rows = min(512, LMAX)
    score_scale = HEAD_DIM ** (-0.5)
    image_count = lengths.shape[0]

    def per_image(packed):
        query_image, key_image, value_image, length = packed
        key_heads = key_image.reshape(LMAX, heads_here, HEAD_DIM)
        value_heads = value_image.reshape(LMAX, heads_here, HEAD_DIM)
        live_keys = jnp.arange(LMAX, dtype=jnp.int32) < length

        def per_block(query_block):
            scores = (
                jnp.einsum(
                    "qhe,khe->hqk", query_block, key_heads, preferred_element_type=jnp.float32
                )
                * score_scale
            )
            scores = jnp.where(live_keys[None, None, :], scores, -1e30)
            maximum = jnp.max(scores, axis=-1, keepdims=True)
            weights = jnp.exp(scores - maximum)
            totals = jnp.sum(weights, axis=-1, keepdims=True)
            probability = (weights / totals).astype(jnp.bfloat16)
            result = jnp.einsum(
                "hqk,khe->qhe", probability, value_heads, preferred_element_type=jnp.float32
            )
            return (result.astype(jnp.bfloat16), (maximum + jnp.log(totals))[:, :, 0])

        blocks = query_image.reshape(LMAX // block_rows, block_rows, heads_here, HEAD_DIM)
        result, log_sums = lax.map(per_block, blocks)
        return (result.reshape(LMAX, heads_here * HEAD_DIM), log_sums)

    stacked = (
        queries.reshape(image_count, LMAX, -1),
        key_rows.reshape(image_count, LMAX, -1),
        value_rows.reshape(image_count, LMAX, -1),
        lengths,
    )
    result, log_sums = lax.map(per_image, stacked)
    return (result.reshape(image_count * LMAX, -1), log_sums)


def attend_back(queries, key_rows, value_rows, grad_rows, log_sums, lengths):
    heads_here = queries.shape[1] // HEAD_DIM
    block_rows = min(512, LMAX)
    score_scale = HEAD_DIM ** (-0.5)
    image_count = lengths.shape[0]

    def per_image(packed):
        query_image, key_image, value_image, grad_image, logsum_image, length = packed
        key_heads = key_image.reshape(LMAX, heads_here, HEAD_DIM)
        value_heads = value_image.reshape(LMAX, heads_here, HEAD_DIM)
        live_keys = jnp.arange(LMAX, dtype=jnp.int32) < length

        def per_block(running, inputs):
            key_grad, value_grad = running
            query_block, grad_block, logsum_block = inputs
            scores = (
                jnp.einsum(
                    "qhe,khe->hqk", query_block, key_heads, preferred_element_type=jnp.float32
                )
                * score_scale
            )
            scores = jnp.where(live_keys[None, None, :], scores, -1e30)
            probability = jnp.exp(scores - logsum_block[:, :, None])
            grad_prob = jnp.einsum(
                "qhe,khe->hqk", grad_block, value_heads, preferred_element_type=jnp.float32
            )
            inner_sum = jnp.sum(probability * grad_prob, axis=-1, keepdims=True)
            grad_score = (probability * (grad_prob - inner_sum)).astype(jnp.bfloat16)
            query_grad = (
                jnp.einsum(
                    "hqk,khe->qhe", grad_score, key_heads, preferred_element_type=jnp.float32
                )
                * score_scale
            )
            key_grad = (
                key_grad
                + jnp.einsum(
                    "hqk,qhe->khe", grad_score, query_block, preferred_element_type=jnp.float32
                )
                * score_scale
            )
            value_grad = value_grad + jnp.einsum(
                "hqk,qhe->khe",
                probability.astype(jnp.bfloat16),
                grad_block,
                preferred_element_type=jnp.float32,
            )
            return ((key_grad, value_grad), query_grad.astype(jnp.bfloat16))

        initial = (
            jnp.zeros((LMAX, heads_here, HEAD_DIM), jnp.float32),
            jnp.zeros((LMAX, heads_here, HEAD_DIM), jnp.float32),
        )
        blocks = (
            query_image.reshape(LMAX // block_rows, block_rows, heads_here, HEAD_DIM),
            grad_image.reshape(LMAX // block_rows, block_rows, heads_here, HEAD_DIM),
            logsum_image,
        )
        (key_grad, value_grad), query_grad = lax.scan(per_block, initial, blocks)
        return (
            query_grad.reshape(LMAX, -1),
            key_grad.reshape(LMAX, -1).astype(jnp.bfloat16),
            value_grad.reshape(LMAX, -1).astype(jnp.bfloat16),
        )

    stacked = (
        queries.reshape(image_count, LMAX, -1),
        key_rows.reshape(image_count, LMAX, -1),
        value_rows.reshape(image_count, LMAX, -1),
        grad_rows.reshape(image_count, LMAX, -1),
        log_sums,
        lengths,
    )
    query_grad, key_grad, value_grad = lax.map(per_image, stacked)
    return (
        query_grad.reshape(image_count * LMAX, -1),
        key_grad.reshape(image_count * LMAX, -1),
        value_grad.reshape(image_count * LMAX, -1),
    )


def adam_update(master, first_moment, second_moment, gradient, learn_rate, clip_factor, correction):
    clipped = gradient * clip_factor
    first_new = 0.5 * first_moment + 0.5 * clipped
    second_new = 0.5 * second_moment + 0.5 * clipped * clipped
    direction = first_new / correction / (jnp.sqrt(second_new / correction) + 1e-08)
    return (master - learn_rate * (direction + 0.1 * master), first_new, second_new)


def on_device(
    tokens,
    cotangent,
    buckets,
    timesteps,
    labels,
    class_table,
    step_count,
    modulate_master,
    modulate_first,
    modulate_second,
    attend_master,
    attend_first,
    attend_second,
    project_master,
    project_first,
    project_second,
    expand_master,
    expand_first,
    expand_second,
    reduce_master,
    reduce_first,
    reduce_second,
    biases_master,
    biases_first,
    biases_second,
):
    head_index = lax.axis_index("head")
    head_count = lax.axis_size("head")
    tok_rows = tokens.shape[0]
    image_count = buckets.shape[0]
    unit_cells = SIDE // 8
    heights = table_pick(buckets, row_units) * unit_cells
    widths = table_pick(buckets, col_units) * unit_cells
    lengths = heights * widths
    row_index = head_index * tok_rows + jnp.arange(tok_rows, dtype=jnp.int32)
    image_of = row_index // LMAX
    position = row_index % LMAX
    choose = image_of[:, None] == jnp.arange(image_count, dtype=jnp.int32)[None, :]
    pick_rows = choose.astype(jnp.float32)
    row_wide = jnp.sum(jnp.where(choose, widths[None, :], 0), axis=1)
    row_length = jnp.sum(jnp.where(choose, lengths[None, :], 0), axis=1)
    live_rows = (position < row_length).astype(jnp.float32)
    grid_cells = grid_features(position, row_wide, D)
    class_pick = (
        labels[:, None] == jnp.arange(class_table.shape[0], dtype=jnp.int32)[None, :]
    ).astype(jnp.bfloat16)
    class_rows = jnp.dot(class_pick, class_table, preferred_element_type=jnp.float32)
    condition = jax.nn.silu(class_rows + time_features(timesteps, D)).astype(jnp.bfloat16)
    bias_low = biases_master.astype(jnp.bfloat16).astype(jnp.float32)
    offset_base = 6 * D
    bias_query = bias_low[offset_base : offset_base + D]
    bias_value = bias_low[offset_base + D : offset_base + 2 * D]
    bias_proj = bias_low[offset_base + 2 * D : offset_base + 3 * D]
    bias_hidden = bias_low[offset_base + 3 * D : offset_base + 3 * D + FF]
    bias_output = bias_low[offset_base + 3 * D + FF :]
    head_slabs = (
        lax.all_gather(attend_master.astype(jnp.bfloat16), "head", axis=1, tiled=True),
        lax.all_gather(project_master.astype(jnp.bfloat16), "head", axis=1, tiled=True),
        lax.all_gather(expand_master.astype(jnp.bfloat16), "head", axis=1, tiled=True),
        lax.all_gather(reduce_master.astype(jnp.bfloat16), "head", axis=1, tiled=True),
    )
    attend_slab, project_slab, expand_slab, reduce_slab = head_slabs
    mod_width = 6 * D // head_count
    mod_share = fold_rows(condition, modulate_master.astype(jnp.bfloat16))
    mod_share = mod_share + lax.dynamic_slice_in_dim(bias_low, head_index * mod_width, mod_width)
    modulation = lax.all_gather(mod_share, "head", axis=1, tiled=True)
    mod_rows = jnp.dot(pick_rows, modulation, precision=highest)
    shift_one, scale_one, gating_one, shift_two, scale_two, gating_two = jnp.split(
        mod_rows, 6, axis=1
    )
    residual_zero = tokens.astype(jnp.float32) + grid_cells
    hidden_attend = modulate(residual_zero, shift_one, scale_one).astype(jnp.bfloat16)
    packed = fold_rows(hidden_attend, attend_slab)
    queries = (packed[:, :D] + bias_query).astype(jnp.bfloat16)
    key_rows = packed[:, D : 2 * D].astype(jnp.bfloat16)
    value_rows = (packed[:, 2 * D :] + bias_value).astype(jnp.bfloat16)
    query_heads, key_heads, value_heads = (
        lax.all_to_all(queries, "head", split_axis=1, concat_axis=0, tiled=True),
        lax.all_to_all(key_rows, "head", split_axis=1, concat_axis=0, tiled=True),
        lax.all_to_all(value_rows, "head", split_axis=1, concat_axis=0, tiled=True),
    )
    head_out, log_sums = attend(query_heads, key_heads, value_heads, lengths)
    attention = lax.all_to_all(head_out, "head", split_axis=0, concat_axis=1, tiled=True)
    branch_attend = fold_rows(attention, project_slab) + bias_proj
    residual_one = residual_zero + gating_one * branch_attend
    hidden_expand = modulate(residual_one, shift_two, scale_two).astype(jnp.bfloat16)
    widened = fold_rows(hidden_expand, expand_slab) + bias_hidden
    activated = jax.nn.gelu(widened, approximate=True).astype(jnp.bfloat16)
    branch_expand = fold_rows(activated, reduce_slab) + bias_output
    output = (residual_one + gating_two * branch_expand).astype(jnp.bfloat16)
    outer_grad = cotangent.astype(jnp.float32) * live_rows[:, None]
    gating_later = outer_grad * branch_expand
    closing_grad = (outer_grad * gating_two).astype(jnp.bfloat16)
    active_grad = back_cols(closing_grad, reduce_slab)
    gelu_value, gelu_pullback = jax.vjp(lambda inner: jax.nn.gelu(inner, approximate=True), widened)
    widened_grad = gelu_pullback(active_grad)[0].astype(jnp.bfloat16)
    hidden_grad = back_cols(widened_grad, expand_slab)
    later_value, later_pullback = jax.vjp(modulate, residual_one, shift_two, scale_two)
    residual_part, shift_later, scale_later = later_pullback(hidden_grad)
    middle_grad = outer_grad + residual_part
    gating_early = middle_grad * branch_attend
    branch_grad = (middle_grad * gating_one).astype(jnp.bfloat16)
    attend_grad = back_cols(branch_grad, project_slab).astype(jnp.bfloat16)
    heads_grad = lax.all_to_all(attend_grad, "head", split_axis=1, concat_axis=0, tiled=True)
    query_grad, keyrow_grad, value_grad = attend_back(
        query_heads, key_heads, value_heads, heads_grad, log_sums, lengths
    )
    query_back, keys_back, values_back = (
        lax.all_to_all(query_grad, "head", split_axis=0, concat_axis=1, tiled=True),
        lax.all_to_all(keyrow_grad, "head", split_axis=0, concat_axis=1, tiled=True),
        lax.all_to_all(value_grad, "head", split_axis=0, concat_axis=1, tiled=True),
    )
    packed_grad = jnp.concatenate([query_back, keys_back, values_back], axis=1)
    normed_grad = back_cols(packed_grad, attend_slab)
    early_value, early_pullback = jax.vjp(modulate, residual_zero, shift_one, scale_one)
    input_part, shift_early, scale_early = early_pullback(normed_grad)
    input_grad = middle_grad + input_part
    mod_token_grad = jnp.concatenate(
        [shift_early, scale_early, gating_early, shift_later, scale_later, gating_later], axis=1
    )
    mod_grad = lax.dot_general(
        pick_rows, mod_token_grad, (((0,), (0,)), ((), ())), precision=highest
    )
    mod_summed = lax.psum_scatter(mod_grad, "head", scatter_dimension=1, tiled=True)
    mod_rounded = mod_summed.astype(jnp.bfloat16)
    grad_mod = rows_seq(condition, mod_rounded)
    mod_slot = lax.dynamic_update_slice_in_dim(
        jnp.zeros((6 * D,), jnp.float32),
        jnp.sum(mod_rounded.astype(jnp.float32), axis=0),
        head_index * mod_width,
        0,
    )
    bias_share = jnp.concatenate(
        [
            mod_slot,
            jnp.sum(query_back.astype(jnp.float32), axis=0),
            jnp.sum(values_back.astype(jnp.float32), axis=0),
            jnp.sum(branch_grad.astype(jnp.float32), axis=0),
            jnp.sum(widened_grad.astype(jnp.float32), axis=0),
            jnp.sum(closing_grad.astype(jnp.float32), axis=0),
        ]
    )
    operand_pairs = (
        (hidden_attend, packed_grad),
        (attention, branch_grad),
        (hidden_expand, widened_grad),
        (activated, closing_grad),
    )
    term_slabs = tuple((rows_seq(left_side, right_side) for left_side, right_side in operand_pairs))
    reduced = (
        lax.psum_scatter(
            term_slabs[0].astype(jnp.bfloat16), "head", scatter_dimension=1, tiled=True
        ).astype(jnp.float32),
        lax.psum_scatter(
            term_slabs[1].astype(jnp.bfloat16), "head", scatter_dimension=1, tiled=True
        ).astype(jnp.float32),
        lax.psum_scatter(
            term_slabs[2].astype(jnp.bfloat16), "head", scatter_dimension=1, tiled=True
        ).astype(jnp.float32),
        lax.psum_scatter(
            term_slabs[3].astype(jnp.bfloat16), "head", scatter_dimension=1, tiled=True
        ).astype(jnp.float32),
    )
    grad_attend, grad_project, grad_expand, grad_reduce = reduced
    local_squares = jnp.sum(grad_mod * grad_mod) + sum(
        (jnp.sum(gradient * gradient) for gradient in reduced)
    )
    bias_total, square_total = lax.psum((bias_share, local_squares), ("seq", "head"))
    grad_norm = jnp.sqrt(square_total + jnp.sum(bias_total * bias_total))
    clip_factor = jnp.minimum(1.0, 1.0 / (grad_norm + 1e-06))
    correction = 1.0 - jnp.power(0.5, step_count.astype(jnp.float32))
    modulate_new = adam_update(
        modulate_master,
        modulate_first,
        modulate_second,
        grad_mod,
        0.5 * D ** (-0.5),
        clip_factor,
        correction,
    )
    attend_new = adam_update(
        attend_master,
        attend_first,
        attend_second,
        grad_attend,
        0.5 * D ** (-0.5),
        clip_factor,
        correction,
    )
    project_new = adam_update(
        project_master,
        project_first,
        project_second,
        grad_project,
        0.5 * D ** (-0.5),
        clip_factor,
        correction,
    )
    expand_new = adam_update(
        expand_master,
        expand_first,
        expand_second,
        grad_expand,
        0.5 * D ** (-0.5),
        clip_factor,
        correction,
    )
    reduce_new = adam_update(
        reduce_master,
        reduce_first,
        reduce_second,
        grad_reduce,
        0.5 * FF ** (-0.5),
        clip_factor,
        correction,
    )
    biases_new = adam_update(
        biases_master, biases_first, biases_second, bias_total, 0.1, clip_factor, correction
    )
    return (
        output,
        input_grad,
        grad_norm,
        modulate_new[0],
        modulate_new[1],
        modulate_new[2],
        attend_new[0],
        attend_new[1],
        attend_new[2],
        project_new[0],
        project_new[1],
        project_new[2],
        expand_new[0],
        expand_new[1],
        expand_new[2],
        reduce_new[0],
        reduce_new[1],
        reduce_new[2],
        biases_new[0],
        biases_new[1],
        biases_new[2],
    )


ALPHA = HEAD_DIM ** (-0.5) * math.log2(math.e)
GELU_A = math.sqrt(2.0 / math.pi)
GELU_B = 0.044715
BLOCK = FF // 16
BF, F32 = jnp.bfloat16, jnp.float32
ANY, VM = pl.ANY, pltpu.VMEM
PIECES = {"q": (144, 864, 48), "p": (72, 576, None), "u": (144, 1152, 48), "d": (288, 576, 96)}
NAMES = ("q", "p", "u", "d")
MESH = pl.DeviceIdType.MESH


def place():
    return tuple(lax.axis_index(a) for a in ("z", "x", "c", "y"))


def at_z(k):
    z = lax.axis_index("z")
    return (z, z + 1 - 2 * (z % 2), (z + 2) % 4, 3 - z)[k]


def rdma(src, dst, send, recv, to):
    return pltpu.make_async_remote_copy(
        src_ref=src, dst_ref=dst, send_sem=send, recv_sem=recv, device_id=to, device_id_type=MESH
    )


def partners():
    z, x, c, y = place()
    xn, yn, twin = (z, 1 - x, c, y), (z, x, c, 1 - y), (z, x, 1 - c, y)
    return xn, yn, twin, [(at_z(k), x, c, y) for k in range(4)]


def flipped(f):
    z, x, c, y = place()
    return (z, 1 - x if f & 1 else x, 1 - c if f & 2 else c, 1 - y if f & 4 else y)


def greet():
    barrier = pltpu.get_barrier_semaphore()
    for to in [flipped(f) for f in range(1, 8)] + partners()[3][1:]:
        pl.semaphore_signal(barrier, inc=1, device_id=to, device_id_type=MESH)
    pl.semaphore_wait(barrier, 10)


CHUNKS = (
    (0, 0, 80, 16),
    (0, 80, 64, 16),
    (1, 0, 72, None),
    (2, 0, 80, 16),
    (2, 80, 64, 16),
    (3, 0, 144, 32),
    (3, 144, 144, 32),
)


def parts_of(chunk, k):
    _, _, rows, cut = CHUNKS[chunk]
    if cut is None:
        return ((0, rows), None) if k == 0 else (None, (0, rows))
    return (0, cut), (cut, rows - cut)


def piece_at(full, w, y, zk, x, first, count):
    rows = PIECES[NAMES[w]][0]
    if count == 72:
        return full.at[y, zk * 2 + x]
    return full.at[y, pl.ds(pl.multiple_of((zk * 2 + x) * rows + first, 16), count)]


def matmul(left, right):
    return jnp.dot(left, right, preferred_element_type=F32)


def matmul_nt(left, right):
    return lax.dot_general(left, right, (((1,), (1,)), ((), ())), preferred_element_type=F32)


def matmul_tn(left, right):
    return lax.dot_general(left, right, (((0,), (0,)), ((), ())), preferred_element_type=F32)


class Gather:
    def __init__(self, own, full, sems):
        self.own, self.full = own, full
        self.zs, self.zr, self.xs, self.xr, self.ys, self.yr, self.fs, self.fr, self.ps, self.pr = sems
        self.sent = []

    def piece(self, w, flip_y, k, flip_x):
        z, x, c, y = place()
        weight, first, count, _ = CHUNKS[w]
        return piece_at(
            self.full[weight], weight, 1 - y if flip_y else y, at_z(k), 1 - x if flip_x else x, first, count
        )

    def source(self, w):
        weight, first, count, _ = CHUNKS[w]
        return self.own[weight].at[pl.ds(first, count)]

    def send(self, make):
        make().start()
        self.sent.append(make)

    def arrived(self, ref, s, r):
        rdma(ref, ref, s, r, partners()[0]).wait_recv()

    def start(self, w):
        def to_x():
            return rdma(self.source(w), self.piece(w, 0, 0, 0), self.xs.at[w, 0], self.xr.at[w, 0], partners()[0])

        def to_y():
            return rdma(self.source(w), self.piece(w, 0, 0, 0), self.ys.at[w, 0], self.yr.at[w, 0], partners()[1])

        def to_z(k):
            to = partners()[3][k]
            return rdma(self.source(w), self.piece(w, 0, 0, 0), self.zs.at[w, k], self.zr.at[w, k], to)

        self.send(to_x)
        self.send(to_y)
        for k in (1, 2, 3):
            self.send(functools.partial(to_z, k))

    def column(self, w, k):
        self.arrived(self.piece(w, 0, k, 0), self.zs.at[w, k], self.zr.at[w, k])

        def to_x():
            piece = self.piece(w, 0, k, 0)
            return rdma(piece, piece, self.xs.at[w, k], self.xr.at[w, k], partners()[0])

        def to_y():
            piece = self.piece(w, 0, k, 0)
            return rdma(piece, piece, self.ys.at[w, k], self.yr.at[w, k], partners()[1])

        self.send(to_x)
        self.send(to_y)

    def plane(self, w, k):
        spans = parts_of(w, k)

        def pass_on(i):
            part = self.piece(w, i, k, 1 - i).at[pl.ds(*spans[i])]
            return rdma(part, part, self.fs.at[w, k, i], self.fr.at[w, k, i], partners()[1 - i])

        self.arrived(self.piece(w, 0, k, 1), self.xs.at[w, k], self.xr.at[w, k])
        if k in (0, 2) and spans[0] is not None:
            self.send(functools.partial(pass_on, 0))
        self.arrived(self.piece(w, 1, k, 0), self.ys.at[w, k], self.yr.at[w, k])
        if k in (0, 2) and spans[1] is not None:
            self.send(functools.partial(pass_on, 1))

    def corner(self, w, k):
        for i, span in enumerate(parts_of(w, k)):
            if span is not None:
                part = self.piece(w, 1, k, 1).at[pl.ds(*span)]
                self.arrived(part, self.fs.at[w, k, i], self.fr.at[w, k, i])

        def to_pair():
            piece = self.piece(w, 1, k, 1)
            return rdma(piece, piece, self.ps.at[w, k], self.pr.at[w, k], partners()[3][1])

        self.send(to_pair)

    def last(self, w, k):
        self.arrived(self.piece(w, 1, k ^ 1, 1), self.ps.at[w, k], self.pr.at[w, k])

    def finish(self):
        for make in self.sent:
            make().wait_send()

    def steps(self):
        def each(method, chunks, ks):
            return [(method, i, k) for i in chunks for k in ks]

        column, plane, corner, last = self.column, self.plane, self.corner, self.last
        one = (0, 1)
        plan = [(self.start, 0), (self.start, 1), (self.start, 2)]
        plan += each(column, one, (1,)) + each(plane, one, (0,))
        plan += each(column, one, (2,)) + each(column, one, (3,)) + [(self.start, 3)]
        plan += each(corner, one, (0,)) + each(plane, one, (2,))
        plan += each(column, (2,), (1,)) + [(self.start, 4)]
        plan += each(plane, one, (1,)) + each(corner, one, (2,))
        plan += each(plane, (2,), (0,)) + each(column, (2,), (2, 3)) + each(column, (3,), (1,))
        plan += each(plane, one, (3,)) + each(last, one, (0, 2))
        count = len(CHUNKS)
        for t in range(-2, count + 4):
            wave = [(self.start, t + 2)] if t + 2 < count else []
            if 0 <= t - 4 < count:
                wave += each(last, (t - 4,), (0, 2))
            for lag, make in enumerate(
                (
                    lambda i: each(column, (i,), (1,)),
                    lambda i: each(plane, (i,), (0,)) + each(column, (i,), (2, 3)),
                    lambda i: each(corner, (i,), (0,)) + each(plane, (i,), (2, 1)),
                    lambda i: each(corner, (i,), (2,)) + each(plane, (i,), (3,)),
                )
            ):
                if t >= 0 and 0 <= t - lag < count:
                    wave += make(t - lag)
            plan += [step for step in wave if step not in plan]
        return plan


def mod_steps(cond_ref, weight, bias, out_ref, lhs, bufs, s, r):
    conds, part, got_z, mid, box = bufs

    def hop(i):
        z, x, c, y = place()
        zn = partners()[3]
        if i == 0:
            pairs = [(conds.at[z, x, c], conds.at[z, x, c], flipped(f)) for f in (1, 2, 3)]
        elif i == 1:
            pairs = [(conds.at[z], conds.at[z], zn[k]) for k in (1, 2, 3)]
        elif i == 2:
            pairs = [(part.at[at_z(k)], got_z.at[k - 1], zn[k]) for k in (1, 2, 3)]
        else:
            pairs = []
            for f in range(1, 8):
                to = flipped(f)
                pairs.append((mid.at[to[1], to[3]], box.at[x, c, y], to))
        return [
            rdma(src, dst, s.at[i, n], r.at[i, n], to) for n, (src, dst, to) in enumerate(pairs)
        ]

    def step(i):
        z, x, c, y = place()
        if i > 0:
            for d in hop(i - 1):
                d.wait()
        if i == 0:
            conds[z, x, c] = cond_ref[...]
        elif i == 2:
            me = (z * 2 + x) * 2 + c
            for n in range(16):
                lhs[pl.ds(n, 1), :] = conds[n // 4, n // 2 % 2, n % 2, pl.ds(me, 1), :]
            for j in range(3):
                cols = slice(j * D, (j + 1) * D)
                result = matmul(lhs[:, :72].astype(BF), weight[:, cols].astype(BF))
                for n in range(16):
                    part[n // 4, n // 2 % 2, n % 2, :, cols] = result[n : n + 1]
        elif i == 3:
            mid[...] = part[z] + got_z[0] + got_z[1] + got_z[2]
            box[x, c, y] = mid[x, y]
        elif i == 4:
            for n in range(2):
                total = (box[0, 0, n] + box[0, 1, n]) + (box[1, 0, n] + box[1, 1, n])
                out_ref[n] = total + bias[:, n * 3456 : (n + 1) * 3456]
        if i < 4:
            for d in hop(i):
                d.start()

    return [functools.partial(step, i) for i in range(5)]


def normed_tile(value):
    average = jnp.mean(value, axis=-1, keepdims=True)
    centred = value - average
    spread = jnp.mean(centred * centred, axis=-1, keepdims=True)
    return centred * lax.rsqrt(spread + 1e-06)


SPACE = (8, 12)


def rounded(value):
    return value.astype(BF).astype(F32)


def pick(bucket, entries):
    return sum(
        jnp.where(bucket == float(i), float(e * (SIDE // 8)), 0.0) for i, e in enumerate(entries)
    )


def start_rows(tok, table, bucket, first, rows):
    wide = pick(bucket, col_units)
    spot = (first + lax.broadcasted_iota(jnp.int32, (rows, 1), 0)).astype(F32)
    lane = lax.broadcasted_iota(jnp.int32, (1, 64), 1).astype(F32)
    grid_row = jnp.where((spot >= lane * wide) & (spot < (lane + 1.0) * wide), 1.0, 0.0)
    left = spot - wide * jnp.sum(grid_row * lane, axis=1, keepdims=True)
    grid_col = jnp.where(left == lane, 1.0, 0.0)
    high = table.astype(BF)
    low = (table - high.astype(F32)).astype(BF)
    parts = [matmul(hot.astype(BF), high) + matmul(hot.astype(BF), low) for hot in (grid_row, grid_col)]
    return tok.astype(F32) + jnp.concatenate(parts, axis=1)


def forward_kernel(*refs):
    (tok, cot, bucket_in, table, att_m, proj_m, exp_m, red_m, mod_w, cond_in, bias_in) = refs[:11]
    gq, gp, gu, gd = full = refs[11:15]
    (mod_out, lhs, x0_out, dy_out, cl_out, h1_out, q_out, k_out, v_out) = refs[15:24]
    (attnt_out, lse_out, ba_out, x1_out, h2_out, der_out, bb_out, y_out, gred_out) = refs[24:33]
    (oq, op, ou, od, fq, tq, fu, tu) = refs[33:41]
    mod_bufs = refs[41:46]
    (xs, x0, dy, bucket, closing, h1, qa, ka, vt, attnt, attn) = refs[46:57]
    (ps, pr, ds, dr, acc, x1, h2, act, der, ba, bb, yo, gstage) = refs[57:70]
    (b_all, b_q, b_v, b_u) = refs[70:74]
    lsem = refs[74]
    gather_sems = refs[75:85]
    ms, mr, ws, wr, ts, tr, os, outs_sem, gsem = refs[85:94]
    z, x, c, y = place()
    xn, yn, twin, zn = partners()
    half = x0.shape[0]
    mine = pl.multiple_of(c * half, half)
    other = pl.multiple_of((1 - c) * half, half)
    gather = Gather((oq, op, ou, od), full, gather_sems)
    mods = mod_steps(cond_in, mod_w, b_all, mod_out, lhs, mod_bufs, ms, mr)
    greet()
    mods[0]()

    def split(master, width, f, t, i):
        count = master.shape[1] // (2 * width)
        sides = [
            jnp.concatenate(
                [master[:, (2 * j + p) * width : (2 * j + p + 1) * width] for j in range(count)], axis=1
            )
            for p in (0, 1)
        ]
        t[...] = jnp.where(c == 0, sides[1], sides[0])
        rdma(t, f.at[c], os.at[0, i], os.at[1, i], twin).start()
        f[c] = jnp.where(c == 0, sides[0], sides[1])

    def joined(f, t, i, piece):
        rdma(t, f.at[c], os.at[0, i], os.at[1, i], twin).wait()
        piece[...] = jnp.concatenate([f[0], f[1]], axis=0).astype(BF)

    steps = [step for step in gather.steps() if step[0] != gather.start or step[1] > 2]
    done = [0]

    def tick(n):
        for f, *a in steps[done[0] : done[0] + n]:
            f(*a)
        done[0] = min(done[0] + n, len(steps))

    def tick_until(chunk):
        last = max(i for i, s in enumerate(steps) if s[0] == gather.last and s[1] == chunk)
        tick(max(0, last + 1 - done[0]))

    swap_to = (z, x, y, c)
    PART = 128
    moves = [(bucket_in, bucket)]
    for i in range(half // PART):
        moves.append((xs.at[pl.ds(i * PART, PART)], x0.at[pl.ds(i * PART, PART)]))
    for i in range(half // PART):
        moves.append((cot.at[pl.ds(i * PART, PART)], dy.at[pl.ds(i * PART, PART)]))

    def move(i):
        @pl.when(c != y)
        def _():
            rdma(*moves[i], ws.at[i], wr.at[i], swap_to).start()

        @pl.when(c == y)
        def _():
            pltpu.make_async_copy(*moves[i], ws.at[i]).start()

    def moved(i):
        @pl.when(c != y)
        def _():
            rdma(*moves[i], ws.at[i], wr.at[i], swap_to).wait()

        @pl.when(c == y)
        def _():
            pltpu.make_async_copy(*moves[i], ws.at[i]).wait()

    def first_rows(i):
        rows = slice(i * PART, (i + 1) * PART)
        xs[rows, :] = start_rows(
            tok[rows, :], table[...], bucket_in[0:1, 0:1], y * half + i * PART, PART
        ).astype(BF)
        move(1 + i)

    move(0)
    split(att_m, HEAD_DIM, fq, tq, 0)
    mods[1]()
    op[...] = proj_m[...].astype(BF)
    gather.start(2)
    first_rows(0)
    joined(fq, tq, 0, oq)
    gather.start(0)
    gather.start(1)
    mods[2]()
    first_rows(1)
    split(exp_m, BLOCK, fu, tu, 1)
    first_rows(2)
    tick(2)
    first_rows(3)
    tick(2)
    joined(fu, tu, 1, ou)
    tick(3)
    mods[3]()
    od[...] = red_m[...].astype(BF)
    owns = [
        pltpu.make_async_copy(
            gather.own[w], piece_at(full[w], w, y, z, x, 0, PIECES[NAMES[w]][0]), lsem.at[w]
        )
        for w in range(4)
    ]
    for d in owns:
        d.start()
    b_all[...] = rounded(bias_in[...])
    tick(SPACE[0])
    mods[4]()
    tick(SPACE[1])

    def of_core(base, width, count):
        return jnp.concatenate(
            [
                jnp.where(
                    c == 0,
                    b_all[:, base + 2 * j * width : base + (2 * j + 1) * width],
                    b_all[:, base + (2 * j + 1) * width : base + (2 * j + 2) * width],
                )
                for j in range(count)
            ],
            axis=1,
        )

    b_p = b_all.at[:, pl.ds(8 * D, D)]
    b_d = b_all.at[:, pl.ds(9 * D + FF, D)]
    for i in range(1 + half // PART):
        moved(i)

    def vec(i):
        return mod_out[i // 3, :, (i % 3) * D : (i % 3 + 1) * D]

    TILE, WIDE = 128, 256
    tiles = half // TILE

    def own_tile(ref, t):
        return ref.at[pl.ds(pl.multiple_of(mine + t * TILE, TILE), TILE)]

    def give(ref, t, i):
        part = own_tile(ref, t)
        return rdma(part, part, ts.at[i, t], tr.at[i, t], twin)

    def norm_one(t, _):
        rows = pl.ds(pl.multiple_of(t * TILE, TILE), TILE)
        value = normed_tile(x0[rows, :].astype(F32)) * (1.0 + vec(1)) + vec(0)
        own_tile(h1, t)[...] = value.astype(BF)
        give(h1, t, 0).start()
        return 0

    for t in range(tiles):
        norm_one(t, 0)
        tick(1)
    tick_until(1)
    for i in range(half // PART):
        move(1 + half // PART + i)

    def both_got(ref, i):
        for t in range(tiles):
            give(ref, t, i).wait_send()
            part = ref.at[pl.ds(pl.multiple_of(other + t * TILE, TILE), TILE)]
            rdma(part, part, ts.at[i, t], tr.at[i, t], twin).wait_recv()

    out_copies = []

    def put(src, dst):
        d = pltpu.make_async_copy(src, dst, outs_sem.at[len(out_copies)])
        d.start()
        out_copies.append(d)

    def load(src, dst, i):
        d = pltpu.make_async_copy(src, dst, lsem.at[i])
        d.start()
        d.wait()

    owns[0].wait()
    live = pick(bucket[0:1, 0:1], row_units) * pick(bucket[0:1, 0:1], col_units)
    lane = lax.broadcasted_iota(jnp.int32, (1, 128), 1)

    b_q[...] = of_core(6 * D, HEAD_DIM, 8)
    b_v[...] = of_core(7 * D, HEAD_DIM, 8)
    b_u[...] = of_core(9 * D, BLOCK, 8)

    def qkv(weight):
        load(gq, weight, 4)

        def rows_of(start):
            rows = pl.ds(start, half)
            left = h1[rows, :]
            spot = (start + lax.broadcasted_iota(jnp.int32, (half, 1), 0)).astype(F32)
            mask = jnp.where(lane == HEAD_DIM, jnp.where(spot < live, 0.0, -1e30), 0.0)
            ones = jnp.where(lane == HEAD_DIM, 1.0, 0.0)
            fill = jnp.zeros((half, 56), F32)

            def put_key(j, key):
                ka[j, rows, :] = (jnp.concatenate([key, fill], axis=1) + mask).astype(BF)

            one = matmul(left, weight[0])
            for j in range(8):
                cols = slice(j * HEAD_DIM, (j + 1) * HEAD_DIM)
                query = (one[:, cols] + b_q[:, cols]) * ALPHA
                qa[j, rows, :] = (jnp.concatenate([query, fill], axis=1) + ones).astype(BF)
            for j in range(4):
                put_key(j, one[:, 576 + j * 72 : 648 + j * 72])
            tick(2)
            two = matmul(left, weight[1])
            for j in range(4):
                put_key(4 + j, two[:, j * 72 : j * 72 + 72])
            for j in range(8):
                cols = slice(j * HEAD_DIM, (j + 1) * HEAD_DIM)
                value = two[:, 288 + j * 72 : 360 + j * 72] + b_v[:, cols]
                vt[j, :, rows] = value.T.astype(BF)
            tick(2)

        rows_of(mine)
        both_got(h1, 0)
        rows_of(other)

    pl.run_scoped(qkv, VM((2, D, 864), BF))
    put(h1, h1_out)
    tick(1)
    put(qa, q_out)
    put(ka, k_out)
    put(vt, v_out)

    def head(j, _):
        def queries(i, _):
            rows = pl.ds(pl.multiple_of(i * 512, 512), 512)
            scores = matmul_nt(ka[j], qa[j, rows, :])
            top = jnp.max(scores, axis=0, keepdims=True)
            prob = jnp.exp2(scores - top)
            total = jnp.sum(prob, axis=0, keepdims=True)
            result = matmul(vt[j], prob.astype(BF)) * (1.0 / total)
            attnt[j, :, rows] = result
            lse_out[j, :, rows] = top + jnp.log2(total)
            return 0

        lax.fori_loop(0, 2, queries, 0)
        return 0

    for j in range(8):
        head(j, 0)
        tick(3)

    for i in range(half // PART):
        moved(1 + half // PART + i)

    def close(t, _):
        rows = pl.ds(pl.multiple_of(t * TILE, TILE), TILE)
        spot = (mine + t * TILE + lax.broadcasted_iota(jnp.int32, (TILE, 1), 0)).astype(F32)
        outer = jnp.where(spot < live, dy[rows, :].astype(F32), 0.0)
        dy[rows, :] = outer.astype(BF)
        own_tile(closing, t)[...] = (outer * vec(5)).astype(BF)
        give(closing, t, 1).start()
        return 0

    lax.fori_loop(0, tiles, close, 0)
    put(attnt, attnt_out)
    tick_until(2)
    owns[1].wait()

    def proj(weight, stage, raw):
        load(gp, raw, 5)
        for i in (0, 1):
            for h in range(8):
                stage[h * 72 : h * 72 + 72, :] = raw[i, h].astype(F32)
            weight[i] = stage[...].astype(BF)

        def attn_rows(i, _):
            rows = pl.ds(pl.multiple_of(i * 256, 256), 256)
            value = jnp.concatenate([attnt[j, :, rows] for j in range(8)], axis=0)
            attn[rows, :] = value.T.astype(BF)
            return 0

        lax.fori_loop(0, 4, attn_rows, 0)

        def for_twin(t, _):
            rows = pl.ds(pl.multiple_of(t * WIDE, WIDE), WIDE)
            left = attn[pl.ds(pl.multiple_of(other + t * WIDE, WIDE), WIDE), :]
            for i in (0, 1):
                ps[rows, i * 576 : (i + 1) * 576] = matmul(left, weight[i]).astype(BF)
            rdma(ps.at[rows], pr.at[rows], ts.at[2, t], tr.at[2, t], twin).start()
            return 0

        for t in range(half // WIDE):
            for_twin(t, 0)
            tick(1)

        def for_me(t, _):
            rows = pl.ds(pl.multiple_of(t * WIDE, WIDE), WIDE)
            left = attn[pl.ds(pl.multiple_of(mine + t * WIDE, WIDE), WIDE), :]
            for i in (0, 1):
                acc[rows, i * 576 : (i + 1) * 576] = matmul(left, weight[i])
            return 0

        for t in range(half // WIDE):
            for_me(t, 0)
            tick(1)

    pl.run_scoped(proj, VM((2, 576, 576), BF), VM((576, 576), F32), VM((2, 8, 72, 576), BF))

    def middle(t, _):
        rows = pl.ds(pl.multiple_of(t * TILE, TILE), TILE)
        branch = acc[rows, :] + pr[rows, :].astype(F32) + b_p[...]
        ba[rows, :] = branch.astype(BF)
        value = x0[rows, :].astype(F32) + vec(2) * branch
        x1[rows, :] = value
        own_tile(h2, t)[...] = (normed_tile(value) * (1.0 + vec(4)) + vec(3)).astype(BF)
        give(h2, t, 3).start()
        return 0

    def half_got(src, dst, i, t):
        rows = pl.ds(t * WIDE, WIDE)
        rdma(src.at[rows], dst.at[rows], ts.at[i, t], tr.at[i, t], twin).wait()

    for t in range(tiles):
        if t % 2 == 0:
            half_got(ps, pr, 2, t // 2)
        middle(t, 0)
    put(ba, ba_out)
    put(x1, x1_out)
    put(x0, x0_out)
    put(dy, dy_out)
    tick_until(4)
    owns[2].wait()
    both_got(h2, 3)
    both_got(closing, 1)
    put(h2, h2_out)
    put(closing, cl_out)

    def up(weight):
        load(gu, weight, 6)

        def block_of(start, i, n):
            rows = pl.ds(start, half)
            part = slice(n * 384, (n + 1) * 384)
            cols = slice(i * D + n * 384, i * D + (n + 1) * 384)
            u = matmul(h2[rows, :], weight[i, :, part]) + b_u[:, cols]
            square = u * u
            inner = u * (GELU_A + GELU_A * GELU_B * square)
            bent = jnp.tanh(inner)
            half_up = 0.5 + 0.5 * bent
            act[rows, cols] = (u * half_up).astype(BF)
            slope = u * (GELU_A + 3.0 * GELU_A * GELU_B * square)
            der[rows, cols] = (half_up + slope * (half_up * (1.0 - bent))).astype(BF)

        for start in (mine, other):
            for i in (0, 1):
                for n in range(3):
                    block_of(start, i, n)
                    tick(n % 2)

    pl.run_scoped(up, VM((2, D, D), BF))
    put(der, der_out)

    gouts = []
    for t in range(6):
        slot = t % 2
        if t >= 2:
            gouts[t - 2].wait()
        value = matmul(act[:, t * 384 : (t + 1) * 384].T, closing[...])
        for i in (0, 1):
            gstage[slot, i] = value[:, i * 576 : (i + 1) * 576].astype(BF)
        d = pltpu.make_async_copy(
            gstage.at[slot], gred_out.at[:, pl.ds(t * 384, 384)], gsem.at[slot]
        )
        d.start()
        gouts.append(d)
        tick(1)
    for d in gouts[-2:]:
        d.wait()
    tick(len(steps))
    owns[3].wait()

    def down(weight):
        load(gd, weight, 7)

        for i in (0, 1):
            cols = slice(i * 576, (i + 1) * 576)
            ds[:, cols] = matmul(act[pl.ds(other, half), :], weight[i]).astype(BF)
        rdma(ds, dr, ts.at[4, 0], tr.at[4, 0], twin).start()
        for i in (0, 1):
            cols = slice(i * 576, (i + 1) * 576)
            acc[:, cols] = matmul(act[pl.ds(mine, half), :], weight[i])
        rdma(ds, dr, ts.at[4, 0], tr.at[4, 0], twin).wait()

    pl.run_scoped(down, VM((2, 2304, 576), BF))

    def finish(t, _):
        rows = pl.ds(pl.multiple_of(t * TILE, TILE), TILE)
        branch = acc[rows, :] + dr[rows, :].astype(F32) + b_d[...]
        bb[rows, :] = branch.astype(BF)
        yo[rows, :] = (x1[rows, :] + vec(5) * branch).astype(BF)
        return 0

    for t in range(tiles):
        finish(t, 0)
    put(bb, bb_out)
    put(yo, y_out)
    for d in out_copies:
        d.wait()
    gather.finish()


def forward_block(tokens, cotangent, bucket, table, masters, modulate_master, cond, biases):
    shapes = {
        "gq": (2, D, 864),
        "gp": (2, 8, 72, 576),
        "gu": (2, D, D),
        "gd": (2, 2304, 576),
    }
    half = tokens.shape[0]
    rows = 2 * half
    out_shape, out_specs = [], []

    def out(shape, dtype, space=ANY):
        out_shape.append(jax.ShapeDtypeStruct(shape, dtype))
        out_specs.append(pl.BlockSpec(memory_space=space))

    for s in shapes.values():
        out(s, BF)
    out((2, 1, 3456), F32, VM)
    out((16, 128), F32, VM)
    out((half, D), BF)
    out((half, D), BF)
    out((rows, D), BF)
    out((rows, D), BF)
    out((8, rows, 128), BF)
    out((8, rows, 128), BF)
    out((8, 72, rows), BF)
    out((8, 72, rows), F32)
    out((8, 1, rows), F32, VM)
    out((half, D), BF)
    out((half, D), F32)
    out((rows, D), BF)
    out((rows, 2304), BF)
    out((half, D), BF)
    out((half, D), BF)
    out((2, 2304, 576), BF)
    dma = pltpu.SemaphoreType.DMA
    scratch = [
        VM((144, 864), BF),
        VM((72, 576), BF),
        VM((144, D), BF),
        VM((288, 576), BF),
        VM((2, 72, 864), F32),
        VM((72, 864), F32),
        VM((2, 72, D), F32),
        VM((72, D), F32),
        VM((4, 2, 2, 16, 128), F32),
        VM((4, 2, 2, 1, 3456), F32),
        VM((3, 2, 2, 1, 3456), F32),
        VM((2, 2, 1, 3456), F32),
        VM((2, 2, 2, 1, 3456), F32),
        VM((half, D), BF),
        VM((half, D), BF),
        VM((half, D), BF),
        VM((8, 128), F32),
        VM((rows, D), BF),
        VM((rows, D), BF),
        VM((8, rows, 128), BF),
        VM((8, rows, 128), BF),
        VM((8, 72, rows), BF),
        VM((8, 72, rows), F32),
        VM((rows, 576), BF),
        VM((half, D), BF),
        VM((half, D), BF),
        VM((half, D), BF),
        VM((half, D), BF),
        VM((half, D), F32),
        VM((half, D), F32),
        VM((rows, D), BF),
        VM((rows, 2304), BF),
        VM((rows, 2304), BF),
        VM((half, D), BF),
        VM((half, D), BF),
        VM((half, D), BF),
        VM((2, 2, 384, 576), BF),
        VM((1, 14 * D), F32),
        VM((1, 576), F32),
        VM((1, 576), F32),
        VM((1, 2304), F32),
        dma((8,)),
    ]
    n = len(CHUNKS)
    scratch += [dma((n, 4))] * 6 + [dma((n, 4, 2))] * 2 + [dma((n, 4))] * 2
    scratch += [
        dma((4, 7)),
        dma((4, 7)),
        dma((9,)),
        dma((9,)),
        dma((5, 4)),
        dma((5, 4)),
        dma((2, 2)),
        dma((20,)),
        dma((2,)),
    ]
    vm = pl.BlockSpec(memory_space=VM)
    hbm = pl.BlockSpec(memory_space=ANY)
    return pl.pallas_call(
        forward_kernel,
        out_shape=out_shape,
        in_specs=[vm, hbm] + [vm] * 9,
        out_specs=out_specs,
        scratch_shapes=scratch,
        compiler_params=pltpu.CompilerParams(
            collective_id=0, has_side_effects=True, vmem_limit_bytes=60 * 2**20
        ),
        name="forward_block",
    )(tokens, cotangent, bucket, table, *masters, modulate_master, cond, biases)


class Scatter:
    def __init__(self, grads, boxes, outs, sems):
        self.grads, self.outs = grads, outs
        self.pair_box, self.diag_box, self.x_box, self.y_box, self.z_box = boxes
        self.ps, self.pr, self.fs, self.fr, self.xs, self.xr, self.ys, self.yr, self.zs, self.zr = sems
        self.sent = []

    def piece(self, i, flip_y, k, flip_x):
        z, x, c, y = place()
        weight, first, count, _ = CHUNKS[i]
        return piece_at(
            self.grads[weight], weight, 1 - y if flip_y else y, at_z(k), 1 - x if flip_x else x, first, count
        )

    def box(self, boxes, i, n):
        weight, first, count, _ = CHUNKS[i]
        return boxes[weight].at[n, pl.ds(first, count)]

    def send(self, make):
        make().start()
        self.sent.append(make)

    def arrived(self, ref, s, r):
        rdma(ref, ref, s, r, partners()[0]).wait_recv()

    def add(self, target, *others):
        total = target[...]
        for o in others:
            total = total + o[...]
        target[...] = total

    def across(self, i, k, by_y):
        if by_y:
            return rdma(
                self.piece(i, 1, k, 0), self.box(self.y_box, i, k), self.ys.at[i, k], self.yr.at[i, k], partners()[1]
            )
        return rdma(
            self.piece(i, 0, k, 1), self.box(self.x_box, i, k), self.xs.at[i, k], self.xr.at[i, k], partners()[0]
        )

    def start(self, i):
        def to_pair(k):
            return rdma(
                self.piece(i, 1, k ^ 1, 1),
                self.box(self.pair_box, i, k // 2),
                self.ps.at[i, k],
                self.pr.at[i, k],
                partners()[3][1],
            )

        for k in (0, 2):
            self.send(functools.partial(to_pair, k))
        for k in (1, 3):
            for by_y in (0, 1):
                self.send(functools.partial(self.across, i, k, by_y))

    def corner(self, i, k):
        box = self.box(self.pair_box, i, k // 2)
        self.arrived(box, self.ps.at[i, k], self.pr.at[i, k])
        self.add(self.piece(i, 1, k, 1), box)
        spans = parts_of(i, k)

        def part(n):
            return rdma(
                self.piece(i, 1, k, 1).at[pl.ds(*spans[n])],
                self.box(self.diag_box, i, k // 2).at[pl.ds(*spans[n])],
                self.fs.at[i, k, n],
                self.fr.at[i, k, n],
                partners()[1 - n],
            )

        for n in (0, 1):
            if spans[n] is not None:
                self.send(functools.partial(part, n))

    def plane(self, i, k):
        spans = parts_of(i, k)
        for n in (0, 1):
            if spans[n] is not None:
                part = self.box(self.diag_box, i, k // 2).at[pl.ds(*spans[n])]
                self.arrived(part, self.fs.at[i, k, n], self.fr.at[i, k, n])
                self.add(self.piece(i, n, k, 1 - n).at[pl.ds(*spans[n])], part)
            self.send(functools.partial(self.across, i, k, n))

    def both(self, i, k):
        boxes = []
        for boxes_of, s, r in ((self.x_box, self.xs, self.xr), (self.y_box, self.ys, self.yr)):
            box = self.box(boxes_of, i, k)
            self.arrived(box, s.at[i, k], r.at[i, k])
            boxes.append(box)
        return boxes

    def column(self, i, k):
        self.add(self.piece(i, 0, k, 0), *self.both(i, k))

        def along():
            return rdma(
                self.piece(i, 0, k, 0),
                self.box(self.z_box, i, k - 1),
                self.zs.at[i, k],
                self.zr.at[i, k],
                partners()[3][k],
            )

        self.send(along)

    def last(self, i):
        weight, first, count, _ = CHUNKS[i]
        boxes = self.both(i, 0)
        for k in (1, 2, 3):
            box = self.box(self.z_box, i, k - 1)
            self.arrived(box, self.zs.at[i, k], self.zr.at[i, k])
            boxes.append(box)
        total = self.piece(i, 0, 0, 0)[...].astype(F32)
        for box in boxes:
            total = total + box[...].astype(F32)
        self.outs[weight][first : first + count, :] = total

    def finish(self):
        for make in self.sent:
            make().wait_send()

    def steps(self, i):
        return (
            [(self.start, i), (self.corner, i, 0), (self.corner, i, 2)],
            [(self.plane, i, 0), (self.plane, i, 2), (self.column, i, 1)],
            [(self.column, i, 3), (self.column, i, 2)],
            [(self.last, i)],
        )


def total_steps(dm, bs, lhs, mods, bufs, gmod, bias_out, s, r):
    got_m, got_b, sb, got_z, near = bufs

    def hop(i):
        z, x, c, y = place()
        zn = partners()[3]
        pairs = []
        if i == 0:
            for f in range(1, 8):
                to = flipped(f)
                pairs.append((dm.at[to[3]], got_m.at[x, c, y], to))
                pairs.append((bs, got_b.at[f - 1], to))
        elif i == 1:
            for k in (1, 2, 3):
                pairs.append((mods.at[z], mods.at[z], zn[k]))
                pairs.append((sb, got_z.at[k - 1], zn[k]))
        else:
            pairs.append((near.at[0], near.at[1], flipped(4)))
        return [
            rdma(src, dst, s.at[i, n], r.at[i, n], to) for n, (src, dst, to) in enumerate(pairs)
        ]

    def step(i):
        z, x, c, y = place()
        if i > 0:
            for d in hop(i - 1):
                d.wait()
        if i == 0:
            got_m[x, c, y] = dm[y]
        elif i == 1:
            for n in range(4):
                mods[z, n // 2, n % 2] = rounded(got_m[n // 2, 0, n % 2] + got_m[n // 2, 1, n % 2])
            sb[...] = ((bs[...] + got_b[0]) + (got_b[1] + got_b[2])) + (
                (got_b[3] + got_b[4]) + (got_b[5] + got_b[6])
            )
        elif i == 2:
            rows = [mods[n // 4, n // 2 % 2, n % 2] for n in range(16)]
            total = rows[0]
            for row in rows[1:]:
                total = total + row
            near[0] = total
        elif i == 3:
            for n in (0, 1):
                bias_out[:, n * 3456 : (n + 1) * 3456] = jnp.where(y == n, near[0], near[1])
        if i < 3:
            for d in hop(i):
                d.start()
        if i == 2:
            bias_out[:, 6 * D :] = (sb[...] + got_z[0]) + (got_z[1] + got_z[2])
            left = lhs[:, :72].astype(BF)
            right = jnp.concatenate(rows, axis=0).astype(BF)
            for j in range(3):
                cols = slice(j * D, (j + 1) * D)
                gmod[:, cols] = matmul_tn(left, right[:, cols])

    return [functools.partial(step, i) for i in range(4)]


BEATS = {
    "down": "010101",
    "expand": "010101",
    "up": "010101",
    "middle": "1010",
    "project": "1010",
    "heads": "0001",
    "attend": "010101",
    "back": "000111",
    "input": "1111",
    "hops": "111111",
}


def backward_kernel(*refs):
    gq, gp, gu, gd, mod, lhs = refs[:6]
    (x0_in, dy_in, cl_in, h1_in, q_in, k_in, v_in, at_in, lse) = refs[6:15]
    (ba_in, x1_in, h2_in, der_in, bb_in, y_in, gred) = refs[15:22]
    (out, ig_out, s_att, s_proj, s_exp, s_red, gmod, bias_out, norm_out) = refs[22:31]
    grads = refs[31:35]
    boxes = [refs[35 + 4 * i : 39 + 4 * i] for i in range(5)]
    fq, fu, gotq, gotu = refs[55:59]
    dba, dx1, ps, pr, dm, bs, mods = refs[59:66]
    total_bufs = refs[66:71]
    sq, here = refs[71:73]
    lsem = refs[73]
    scatter_sems = refs[74:84]
    ts, tr, ws, wr, hs, hr, ns, nr = refs[84:92]
    z, x, c, y = place()
    xn, yn, twin, zn = partners()
    half = dx1.shape[0]
    mine = pl.multiple_of(c * half, half)
    other = pl.multiple_of((1 - c) * half, half)
    scatter = Scatter(grads, boxes, (fq, s_proj, fu, s_red), scatter_sems)
    hops = total_steps(dm, bs, lhs, mods, total_bufs, gmod, bias_out, hs, hr)
    pltpu.make_async_copy(gred, grads[3], lsem.at[0]).start()
    greet()
    dm[...] = jnp.zeros_like(dm)
    bs[...] = jnp.zeros_like(bs)
    TILE = 128
    swap_to = (z, x, y, c)

    def vec(i):
        return mod[i // 3, :, (i % 3) * D : (i % 3 + 1) * D]

    def add_mod(i, value):
        cols = slice((i % 3) * D, (i % 3 + 1) * D)
        dm[i // 3, :, cols] = dm[i // 3, :, cols] + jnp.sum(value, axis=0, keepdims=True)

    def add_bias(at, value):
        cols = slice(at, at + value.shape[1])
        bs[:, cols] = bs[:, cols] + value

    def load(src, dst, i):
        d = pltpu.make_async_copy(src, dst, lsem.at[i])
        d.start()
        return d

    queue = []

    def tick(n):
        for _ in range(min(n, len(queue))):
            f, *a = queue.pop(0)
            f(*a)

    def beat(where, n):
        tick(int(BEATS[where][n]))

    def moves(i):
        if i == 0:
            return y_in, out
        rows = pl.ds((i - 1) * TILE, TILE)
        return dba.at[rows], ig_out.at[rows]

    def move(i):
        @pl.when(c != y)
        def _():
            rdma(*moves(i), ws.at[i], wr.at[i], swap_to).start()

        @pl.when(c == y)
        def _():
            pltpu.make_async_copy(*moves(i), ws.at[i]).start()

    def moved(i):
        @pl.when(c != y)
        def _():
            rdma(*moves(i), ws.at[i], wr.at[i], swap_to).wait()

        @pl.when(c == y)
        def _():
            pltpu.make_async_copy(*moves(i), ws.at[i]).wait()

    load_d = pltpu.make_async_copy(gred, grads[3], lsem.at[0])
    load_d.wait()
    scatter.start(5)
    scatter.start(6)
    five, six = scatter.steps(5), scatter.steps(6)
    queue += five[0][1:] + six[0][1:] + five[1] + six[1] + five[2] + six[2] + five[3] + six[3]

    def own_tile(ref, t):
        return ref.at[pl.ds(pl.multiple_of(mine + t * TILE, TILE), TILE)]

    def widen(du):
        def through(weight, closing, der):
            loads = [load(gd, weight, 1), load(cl_in, closing, 2)]

            def slopes(n):
                return load(der_in.at[:, pl.ds(n * 384, 384)], der.at[n % 2], 3 + n % 2)

            coming = slopes(0)
            for d in loads:
                d.wait()
            for n in range(6):
                cols = slice(n * 384, (n + 1) * 384)
                coming.wait()
                if n < 5:
                    coming = slopes(n + 1)
                right = jnp.concatenate([weight[0, cols, :], weight[1, cols, :]], axis=1)
                value = (matmul_nt(closing[...], right) * der[n % 2].astype(F32)).astype(BF)
                du[:, cols] = value
                sums = jnp.sum(value.astype(F32), axis=0, keepdims=True)
                here[:, cols] = sums
                beat("down", n)
            for j in range(8):
                block = here[:, j * BLOCK : (j + 1) * BLOCK]
                for p in (0, 1):
                    add_bias(3 * D + (2 * j + p) * BLOCK, jnp.where(c == p, block, 0.0))

        pl.run_scoped(through, VM((2, 2304, 576), BF), VM((2 * half, D), BF), VM((2, 2 * half, 384), BF))

        def expand_grad(h2):
            load(h2_in, h2, 2).wait()
            for t in range(3):
                left = h2[:, t * 384 : (t + 1) * 384].T
                for i in (0, 1):
                    grads[2][i, t * 384 : (t + 1) * 384, :] = matmul(
                        left, du[:, i * D : (i + 1) * D]
                    ).astype(BF)
                    beat("expand", 2 * t + i)

        pl.run_scoped(expand_grad, VM((2 * half, D), BF))
        scatter.start(3)
        scatter.start(4)
        three, four = scatter.steps(3), scatter.steps(4)
        queue.extend(three[0][1:] + four[0][1:] + three[1] + four[1] + three[2] + four[2] + three[3] + four[3])
        move(0)

        def back(weight):
            load(gu, weight, 1).wait()

            def product(start, n):
                rows = pl.ds(start, half)
                part = slice(n * 384, (n + 1) * 384)
                return matmul_nt(du[rows, :D], weight[0, part, :]) + matmul_nt(du[rows, D:], weight[1, part, :])

            for n in range(3):
                ps[:, n * 384 : (n + 1) * 384] = product(other, n).astype(BF)
                beat("up", n)
            rdma(ps, pr, ts.at[0, 0], tr.at[0, 0], twin).start()
            for n in range(3):
                dx1[:, n * 384 : (n + 1) * 384] = product(mine, n)
                beat("up", 3 + n)

        pl.run_scoped(back, VM((2, D, D), BF))

    pl.run_scoped(widen, VM((2 * half, 2304), BF))

    def sums_got(i):
        rdma(ps, pr, ts.at[i, 0], tr.at[i, 0], twin).wait()

    def norm_back(value, scaling, gradient):
        average = jnp.mean(value, axis=-1, keepdims=True)
        centred = value - average
        inverse = lax.rsqrt(jnp.mean(centred * centred, axis=-1, keepdims=True) + 1e-06)
        normed = centred * inverse
        inner = gradient * (1.0 + scaling)
        part = inner - jnp.mean(inner, axis=-1, keepdims=True)
        part = part - normed * jnp.mean(inner * normed, axis=-1, keepdims=True)
        return part * inverse, normed

    def middle(x1, dy, ba, bb):
        loads = [load(x1_in, x1, 1), load(dy_in, dy, 2), load(ba_in, ba, 3), load(bb_in, bb, 4)]
        for d in loads:
            d.wait()
        sums_got(0)
        for t in range(half // TILE):
            rows = slice(t * TILE, (t + 1) * TILE)
            gradient = dx1[rows, :] + pr[rows, :].astype(F32)
            part, normed = norm_back(x1[rows, :], vec(4), gradient)
            add_mod(3, gradient)
            add_mod(4, gradient * normed)
            outer = dy[rows, :].astype(F32)
            add_mod(5, outer * bb[rows, :].astype(F32))
            add_bias(9216 - D, jnp.sum(rounded(outer * vec(5)), axis=0, keepdims=True))
            total = outer + part
            dx1[rows, :] = total
            add_mod(2, total * ba[rows, :].astype(F32))
            branch = (total * vec(2)).astype(BF)
            own_tile(dba, t)[...] = branch
            tile = own_tile(dba, t)
            rdma(tile, tile, ts.at[1, t], tr.at[1, t], twin).start()
            add_bias(2 * D, jnp.sum(branch.astype(F32), axis=0, keepdims=True))
            beat("middle", t)

    pl.run_scoped(middle, VM((half, D), F32), VM((half, D), BF), VM((half, D), BF), VM((half, D), BF))

    def attention(dot, dqkv):
        def project(weight, stage, raw, attnt, attn):
            loads = [load(gp, raw, 1), load(at_in, attnt, 2)]
            for d in loads:
                d.wait()
            for i in (0, 1):
                for h in range(8):
                    stage[h * 72 : h * 72 + 72, :] = raw[i, h].astype(F32)
                weight[i] = stage[...].astype(BF)
            attn[...] = jnp.concatenate([attnt[h] for h in range(8)], axis=0).astype(BF)
            for t in range(half // TILE):
                tile = own_tile(dba, t)
                rdma(tile, tile, ts.at[1, t], tr.at[1, t], twin).wait_send()
                part = dba.at[pl.ds(pl.multiple_of(other + t * TILE, TILE), TILE)]
                rdma(part, part, ts.at[1, t], tr.at[1, t], twin).wait_recv()
            for n in range(4):
                rows = slice(n * 256, (n + 1) * 256)
                right = dba[rows, :]
                value = matmul_nt(weight[0], right[:, :576]) + matmul_nt(weight[1], right[:, 576:])
                for h in range(8):
                    dot[h, :, rows] = value[h * 72 : h * 72 + 72, :].astype(BF)
                beat("project", n)
            for i in (0, 1):
                stage[...] = matmul(attn[...], dba[:, i * 576 : (i + 1) * 576])
                for h in range(8):
                    grads[1][i, h] = stage[h * 72 : h * 72 + 72, :].astype(BF)

        pl.run_scoped(
            project,
            VM((2, 576, 576), BF),
            VM((576, 576), F32),
            VM((2, 8, 72, 576), BF),
            VM((8, 72, 2 * half), F32),
            VM((576, 2 * half), BF),
        )
        scatter.start(2)
        two = scatter.steps(2)
        queue.extend(two[0][1:] + two[1] + two[2] + two[3])

        def heads(qa, ka, vt, at, dk, dv, dq):
            def fetch(h):
                n = h % 2
                return [
                    load(src.at[h], dst.at[n], 1 + 4 * n + m)
                    for m, (src, dst) in enumerate(((q_in, qa), (k_in, ka), (v_in, vt), (at_in, at)))
                ]

            coming = fetch(0)
            for h in range(8):
                n = h % 2
                for d in coming:
                    d.wait()
                if h < 7:
                    coming = fetch(h + 1)
                value = vt[n].T
                key_t = ka[n, :, :72].T
                inner = jnp.sum(at[n] * dot[h].astype(F32), axis=0, keepdims=True)
                dk[...] = jnp.zeros_like(dk)
                dv[...] = jnp.zeros_like(dv)
                for i in range(4):
                    rows = slice(i * 256, (i + 1) * 256)
                    query = qa[n, rows, :]
                    grad = dot[h, :, rows]
                    scores = matmul_nt(ka[n], query)
                    prob = jnp.exp2(scores - lse[h, :, rows])
                    change = matmul(value, grad) - inner[:, rows]
                    dscore = (prob * change).astype(BF)
                    dv[...] += matmul_nt(grad, prob.astype(BF))
                    dk[...] += matmul_nt(query[:, :72].T, dscore)
                    dq[:, rows] = matmul(key_t, dscore)
                    beat("heads", i)
                scale = HEAD_DIM ** (-0.5)
                dqkv[0, :, h * 72 : h * 72 + 72] = (dq[...] * scale).T.astype(BF)
                key_grad = (dk[...] * math.log(2.0)).T.astype(BF)
                if h < 4:
                    dqkv[0, :, 576 + h * 72 : 648 + h * 72] = key_grad
                else:
                    dqkv[1, :, h * 72 - 288 : h * 72 - 216] = key_grad
                dqkv[1, :, 288 + h * 72 : 360 + h * 72] = dv[...].T.astype(BF)

        pl.run_scoped(
            heads,
            VM((2, 2 * half, 128), BF),
            VM((2, 2 * half, 128), BF),
            VM((2, 72, 2 * half), BF),
            VM((2, 72, 2 * half), F32),
            VM((72, 2 * half), F32),
            VM((72, 2 * half), F32),
            VM((72, 2 * half), F32),
        )

        def attend_grad(h1):
            load(h1_in, h1, 1).wait()
            for t in range(3):
                left = h1[:, t * 384 : (t + 1) * 384].T
                for i in (0, 1):
                    grads[0][i, t * 384 : (t + 1) * 384, :] = matmul(left, dqkv[i]).astype(BF)
                    beat("attend", 2 * t + i)

        pl.run_scoped(attend_grad, VM((2 * half, D), BF))
        scatter.start(0)
        scatter.start(1)
        zero, one = scatter.steps(0), scatter.steps(1)
        queue.extend(zero[0][1:] + one[0][1:] + zero[1] + one[1] + zero[2] + one[2] + zero[3] + one[3])

        def back(weight, x0, acc):
            loads = [load(gq, weight, 1), load(x0_in, x0, 2)]
            for d in loads:
                d.wait()

            def product(start, n):
                rows = pl.ds(start, half)
                part = slice(n * 384, (n + 1) * 384)
                return matmul_nt(dqkv[0, rows, :], weight[0, part, :]) + matmul_nt(
                    dqkv[1, rows, :], weight[1, part, :]
                )

            for n in range(3):
                ps[:, n * 384 : (n + 1) * 384] = product(other, n).astype(BF)
                beat("back", n)
            rdma(ps, pr, ts.at[2, 0], tr.at[2, 0], twin).start()
            for n in range(3):
                acc[:, n * 384 : (n + 1) * 384] = product(mine, n)
                beat("back", 3 + n)
            sums_got(2)
            for t in range(half // TILE):
                rows = slice(t * TILE, (t + 1) * TILE)
                gradient = acc[rows, :] + pr[rows, :].astype(F32)
                part, normed = norm_back(x0[rows, :].astype(F32), vec(1), gradient)
                add_mod(0, gradient)
                add_mod(1, gradient * normed)
                dba[rows, :] = (dx1[rows, :] + part).astype(BF)
                move(1 + t)
                beat("input", t)

        pl.run_scoped(back, VM((2, D, 864), BF), VM((half, D), BF), VM((half, D), F32))
        for i in (0, 1):
            sums = jnp.sum(dqkv[i].astype(F32), axis=0, keepdims=True)
            for j in range(8):
                block = sums[:, i * 288 + j * 72 : i * 288 + j * 72 + 72]
                for p in (0, 1):
                    add_bias(i * D + (2 * j + p) * 72, jnp.where(c == p, block, 0.0))

    pl.run_scoped(attention, VM((8, 72, 2 * half), BF), VM((2, 2 * half, 864), BF))
    for n, hop in enumerate(hops):
        hop()
        beat("hops", n)
    tick(len(queue))

    last_half = 72
    def give(f, got, i):
        return rdma(f.at[pl.ds(pl.multiple_of((1 - c) * 72, 8), 72)], got, ts.at[3, i], tr.at[3, i], twin)

    give(fq, gotq, 0).start()
    give(fu, gotu, 1).start()

    def squares(value):
        return jnp.sum(jnp.sum(value * value, axis=0, keepdims=True), axis=1, keepdims=True)

    bias_squares = squares(bias_out[...])
    total = squares(fq[...]) + squares(fu[...]) + squares(s_proj[...]) + squares(s_red[...]) + squares(gmod[...])
    total = jnp.broadcast_to(total, (8, 128))
    sq[0] = total
    near = [
        rdma(sq.at[0], sq.at[f], ns.at[f - 1], nr.at[f - 1], flipped(f)) for f in range(1, 8)
    ]
    for d in near:
        d.start()
    for d in near:
        d.wait()
    sq[8] = ((sq[0] + sq[1]) + (sq[2] + sq[3])) + ((sq[4] + sq[5]) + (sq[6] + sq[7]))
    last = [rdma(sq.at[8], sq.at[8 + k], ns.at[6 + k], nr.at[6 + k], zn[k]) for k in (1, 2, 3)]
    for d in last:
        d.start()

    def interleave(f, got, shard, width, i):
        give(f, got, i).wait()
        own = jnp.where(c == 0, f[:72, :], f[72:, :])
        sides = (jnp.where(c == 0, own, got[...]), jnp.where(c == 0, got[...], own))
        count = own.shape[1] // width
        shard[...] = jnp.concatenate(
            [sides[p][:, j * width : (j + 1) * width] for j in range(count) for p in (0, 1)], axis=1
        )

    interleave(fq, gotq, s_att, HEAD_DIM, 0)
    interleave(fu, gotu, s_exp, BLOCK, 1)
    for d in last:
        d.wait()
    norm_out[...] = (sq[8] + sq[9]) + (sq[10] + sq[11]) + bias_squares
    for i in range(1 + half // TILE):
        moved(i)
    scatter.finish()


def backward_block(kept):
    half = kept[6].shape[0]
    rows = 2 * half
    sd = jax.ShapeDtypeStruct
    vm = pl.BlockSpec(memory_space=VM)
    hbm = pl.BlockSpec(memory_space=ANY)
    sizes = ((D, 864), (72, 576), (D, D), (2304, 576))
    pieces = [PIECES[n][:2] for n in NAMES]
    dma = pltpu.SemaphoreType.DMA
    n = len(CHUNKS)
    scratch = [
        VM((2, D, 864), BF),
        VM((2, 8, 72, 576), BF),
        VM((2, D, D), BF),
        VM((2, 2304, 576), BF),
    ]
    for count in (2, 2, 4, 4, 3):
        scratch += [VM((count,) + p, BF) for p in pieces]
    scratch += [
        VM((144, 864), F32),
        VM((144, D), F32),
        VM((72, 864), F32),
        VM((72, D), F32),
        VM((rows, D), BF),
        VM((half, D), F32),
        VM((half, D), BF),
        VM((half, D), BF),
        VM((2, 1, 3456), F32),
        VM((1, 9216), F32),
        VM((4, 2, 2, 1, 3456), F32),
        VM((2, 2, 2, 1, 3456), F32),
        VM((7, 1, 9216), F32),
        VM((1, 9216), F32),
        VM((3, 1, 9216), F32),
        VM((2, 1, 3456), F32),
        VM((12, 8, 128), F32),
        VM((1, 2304), F32),
        dma((9,)),
    ]
    scratch += [dma((n, 4))] * 2 + [dma((n, 4, 2))] * 2 + [dma((n, 4))] * 6
    scratch += [dma((4, 4))] * 2 + [dma((5,))] * 2 + [dma((3, 14))] * 2 + [dma((10,))] * 2
    places = [hbm] * 4 + [vm, vm] + [hbm] * 8 + [vm] + [hbm] * 7
    return pl.pallas_call(
        backward_kernel,
        out_shape=[
            sd((half, D), BF),
            sd((half, D), BF),
            sd((72, 1728), F32),
            sd((72, 576), F32),
            sd((72, 2304), F32),
            sd((288, 576), F32),
            sd((72, 3456), F32),
            sd((1, 14 * D), F32),
            sd((8, 128), F32),
        ],
        in_specs=places,
        out_specs=[hbm, hbm] + [vm] * 7,
        scratch_shapes=scratch,
        compiler_params=pltpu.CompilerParams(
            collective_id=1, has_side_effects=True, vmem_limit_bytes=62 * 2**20
        ),
        name="backward_block",
    )(*kept)


def step_kernel(squares, correction, *refs):
    count = len(RATES)
    norm = jnp.sqrt(squares[0:1, 0:1])
    clip = jnp.minimum(1.0, 1.0 / (norm + 1e-06))
    fix = correction[0:1, 0:1]
    for i, rate in enumerate(RATES):
        master, first, second, gradient = (refs[4 * i + j][...] for j in range(4))
        new = adam_update(master, first, second, gradient, rate, clip, fix)
        for j in range(3):
            refs[4 * count + 3 * i + j][...] = new[j]


RATES = (0.5 * D ** (-0.5),) * 4 + (0.5 * FF ** (-0.5),)


def step_weights(squares, correction, states):
    grid = 3

    def spec(shape):
        return pl.BlockSpec((shape[0] // grid, shape[1]), lambda i: (i, 0))

    whole = pl.BlockSpec((8, 128), lambda i: (0, 0))
    flat = [value for state in states for value in state]
    new = [value for state in states for value in state[:3]]
    return pl.pallas_call(
        step_kernel,
        grid=(grid,),
        out_shape=[jax.ShapeDtypeStruct(v.shape, v.dtype) for v in new],
        in_specs=[whole, whole] + [spec(v.shape) for v in flat],
        out_specs=[spec(v.shape) for v in new],
        compiler_params=pltpu.CompilerParams(vmem_limit_bytes=62 * 2**20),
        name="step_weights",
    )(squares, correction, *flat)


def on_device_fast(
    tokens,
    cotangent,
    buckets,
    timesteps,
    labels,
    class_table,
    step_count,
    modulate_master,
    modulate_first,
    modulate_second,
    attend_master,
    attend_first,
    attend_second,
    project_master,
    project_first,
    project_second,
    expand_master,
    expand_first,
    expand_second,
    reduce_master,
    reduce_first,
    reduce_second,
    biases_master,
    biases_first,
    biases_second,
):

    z, x, c, y = place()
    bf16, f32 = jnp.bfloat16, jnp.float32
    block = FF // 16
    class_row = lax.dynamic_slice_in_dim(class_table, labels[0], 1).astype(f32)
    condition = jax.nn.silu(class_row + time_features(timesteps, D)).astype(bf16).astype(f32)
    cond_tiles = jnp.pad(condition.reshape(16, 72), ((0, 0), (0, 56)))
    bucket = jnp.broadcast_to(buckets.astype(f32)[:, None], (8, 128))
    steps = jnp.arange(64, dtype=f32)[:, None]
    omegas = jnp.exp(-math.log(10000.0) * jnp.arange(288, dtype=f32) / 288)[None, :]
    table = jnp.concatenate([jnp.sin(steps * omegas), jnp.cos(steps * omegas)], axis=1)
    kept = forward_block(
        tokens,
        cotangent,
        bucket,
        table,
        (attend_master, project_master, expand_master, reduce_master),
        modulate_master,
        cond_tiles,
        biases_master[None, :],
    )
    (output, input_grad, grad_attend, grad_project, grad_expand, grad_reduce, grad_mod, bias_total, squares) = (
        backward_block(kept)
    )
    correction = 1.0 - jnp.power(0.5, step_count.astype(f32))
    states = (
        (modulate_master, modulate_first, modulate_second, grad_mod),
        (attend_master, attend_first, attend_second, grad_attend),
        (project_master, project_first, project_second, grad_project),
        (expand_master, expand_first, expand_second, grad_expand),
        (reduce_master, reduce_first, reduce_second, grad_reduce),
    )
    updates = list(step_weights(squares, jnp.full((8, 128), correction), states))
    grad_norm = jnp.sqrt(squares[0, 0])
    clip_factor = jnp.minimum(1.0, 1.0 / (grad_norm + 1e-06))
    updates += adam_update(
        biases_master, biases_first, biases_second, bias_total[0], 0.1, clip_factor, correction
    )
    return (output, input_grad.astype(f32), grad_norm, *updates)


def fast_solution(mesh):
    return jax.shard_map(
        on_device_fast,
        mesh=mesh,
        in_specs=(
            P(("z", "x", "c", "y"), None),
            P(("z", "x", "c", "y"), None),
            P(("z", "x", "c")),
            P(("z", "x", "c")),
            P(("z", "x", "c")),
            P(),
            P(),
            P(("z", "x", "c"), "y"),
            P(("z", "x", "c"), "y"),
            P(("z", "x", "c"), "y"),
            P(("z", "x", "c"), "y"),
            P(("z", "x", "c"), "y"),
            P(("z", "x", "c"), "y"),
            P(("z", "x", "c"), "y"),
            P(("z", "x", "c"), "y"),
            P(("z", "x", "c"), "y"),
            P(("z", "x", "c"), "y"),
            P(("z", "x", "c"), "y"),
            P(("z", "x", "c"), "y"),
            P(("z", "x", "c"), "y"),
            P(("z", "x", "c"), "y"),
            P(("z", "x", "c"), "y"),
            P(),
            P(),
            P(),
        ),
        out_specs=(
            P(("z", "x", "c", "y"), None),
            P(("z", "x", "c", "y"), None),
            P(),
            P(("z", "x", "c"), "y"),
            P(("z", "x", "c"), "y"),
            P(("z", "x", "c"), "y"),
            P(("z", "x", "c"), "y"),
            P(("z", "x", "c"), "y"),
            P(("z", "x", "c"), "y"),
            P(("z", "x", "c"), "y"),
            P(("z", "x", "c"), "y"),
            P(("z", "x", "c"), "y"),
            P(("z", "x", "c"), "y"),
            P(("z", "x", "c"), "y"),
            P(("z", "x", "c"), "y"),
            P(("z", "x", "c"), "y"),
            P(("z", "x", "c"), "y"),
            P(("z", "x", "c"), "y"),
            P(),
            P(),
            P(),
        ),
        check_vma=False,
    )


def plain_solution(mesh):
    return jax.shard_map(
        on_device,
        mesh=mesh,
        in_specs=(
            P(("seq", "head"), None),
            P(("seq", "head"), None),
            P("seq"),
            P("seq"),
            P("seq"),
            P(),
            P(),
            P("seq", "head"),
            P("seq", "head"),
            P("seq", "head"),
            P("seq", "head"),
            P("seq", "head"),
            P("seq", "head"),
            P("seq", "head"),
            P("seq", "head"),
            P("seq", "head"),
            P("seq", "head"),
            P("seq", "head"),
            P("seq", "head"),
            P("seq", "head"),
            P("seq", "head"),
            P("seq", "head"),
            P(),
            P(),
            P(),
        ),
        out_specs=(
            P(("seq", "head"), None),
            P(("seq", "head"), None),
            P(),
            P("seq", "head"),
            P("seq", "head"),
            P("seq", "head"),
            P("seq", "head"),
            P("seq", "head"),
            P("seq", "head"),
            P("seq", "head"),
            P("seq", "head"),
            P("seq", "head"),
            P("seq", "head"),
            P("seq", "head"),
            P("seq", "head"),
            P("seq", "head"),
            P("seq", "head"),
            P("seq", "head"),
            P(),
            P(),
            P(),
        ),
        check_vma=False,
    )


def solution(mesh):
    if dict(mesh.shape) == {"seq": 16, "head": 2}:
        grid = Mesh(mesh.devices.reshape(4, 2, 2, 2), ("z", "x", "c", "y"))
        return fast_solution(grid)
    return plain_solution(mesh)
```

```python
import functools
import math

import jax
import jax.numpy as jnp
from jax import lax
from jax.experimental import pallas as pl
from jax.experimental.pallas import tpu as pltpu
from jax.sharding import Mesh
from jax.sharding import PartitionSpec as P

D = 1152
HEAD_DIM = 72
FF = 4608
SIDE = 32
LMAX = 1024


highest = lax.Precision.HIGHEST
row_units = (8, 4, 16, 6, 10, 7, 4, 6)
col_units = (8, 16, 4, 10, 6, 9, 8, 6)


def table_pick(indices, entries):
    matches = indices[..., None] == jnp.arange(len(entries), dtype=jnp.int32)
    return jnp.sum(jnp.where(matches, jnp.array(entries, jnp.int32), 0), axis=-1)


def layer_norm(value):
    average = jnp.mean(value, axis=-1, keepdims=True)
    centred = value - average
    spread = jnp.mean(centred * centred, axis=-1, keepdims=True)
    return centred * lax.rsqrt(spread + 1e-06)


def modulate(value, shift, scaling):
    return layer_norm(value) * (1.0 + scaling) + shift


def time_features(moments, width):
    half_width = width // 2
    frequency = jnp.exp(-math.log(10000.0) * jnp.arange(half_width, dtype=jnp.float32) / half_width)
    angles = moments.astype(jnp.float32)[:, None] * frequency[None, :]
    return jnp.concatenate([jnp.cos(angles), jnp.sin(angles)], axis=1)


def grid_features(position, row_wide, width):
    quarter = width // 4
    omegas = jnp.exp(-math.log(10000.0) * jnp.arange(quarter, dtype=jnp.float32) / quarter)
    row_angle = (position // row_wide).astype(jnp.float32)[:, None] * omegas[None, :]
    col_angle = (position % row_wide).astype(jnp.float32)[:, None] * omegas[None, :]
    return jnp.concatenate(
        [jnp.sin(row_angle), jnp.cos(row_angle), jnp.sin(col_angle), jnp.cos(col_angle)], axis=1
    )


def fold_rows(left_side, weight_slab):
    return jnp.dot(
        left_side,
        lax.all_gather(weight_slab, "seq", axis=0, tiled=True),
        preferred_element_type=jnp.float32,
    )


def back_cols(gradient, weight_slab):
    return lax.dot_general(
        gradient,
        lax.all_gather(weight_slab, "seq", axis=0, tiled=True),
        (((1,), (1,)), ((), ())),
        preferred_element_type=jnp.float32,
    )


def rows_seq(left_side, right_side):
    return lax.psum_scatter(
        lax.dot_general(
            left_side, right_side, (((0,), (0,)), ((), ())), preferred_element_type=jnp.float32
        ).astype(jnp.bfloat16),
        "seq",
        scatter_dimension=0,
        tiled=True,
    ).astype(jnp.float32)


def attend(queries, key_rows, value_rows, lengths):
    heads_here = queries.shape[1] // HEAD_DIM
    block_rows = min(512, LMAX)
    score_scale = HEAD_DIM ** (-0.5)
    image_count = lengths.shape[0]

    def per_image(packed):
        query_image, key_image, value_image, length = packed
        key_heads = key_image.reshape(LMAX, heads_here, HEAD_DIM)
        value_heads = value_image.reshape(LMAX, heads_here, HEAD_DIM)
        live_keys = jnp.arange(LMAX, dtype=jnp.int32) < length

        def per_block(query_block):
            scores = (
                jnp.einsum(
                    "qhe,khe->hqk", query_block, key_heads, preferred_element_type=jnp.float32
                )
                * score_scale
            )
            scores = jnp.where(live_keys[None, None, :], scores, -1e30)
            maximum = jnp.max(scores, axis=-1, keepdims=True)
            weights = jnp.exp(scores - maximum)
            totals = jnp.sum(weights, axis=-1, keepdims=True)
            probability = (weights / totals).astype(jnp.bfloat16)
            result = jnp.einsum(
                "hqk,khe->qhe", probability, value_heads, preferred_element_type=jnp.float32
            )
            return (result.astype(jnp.bfloat16), (maximum + jnp.log(totals))[:, :, 0])

        blocks = query_image.reshape(LMAX // block_rows, block_rows, heads_here, HEAD_DIM)
        result, log_sums = lax.map(per_block, blocks)
        return (result.reshape(LMAX, heads_here * HEAD_DIM), log_sums)

    stacked = (
        queries.reshape(image_count, LMAX, -1),
        key_rows.reshape(image_count, LMAX, -1),
        value_rows.reshape(image_count, LMAX, -1),
        lengths,
    )
    result, log_sums = lax.map(per_image, stacked)
    return (result.reshape(image_count * LMAX, -1), log_sums)


def attend_back(queries, key_rows, value_rows, grad_rows, log_sums, lengths):
    heads_here = queries.shape[1] // HEAD_DIM
    block_rows = min(512, LMAX)
    score_scale = HEAD_DIM ** (-0.5)
    image_count = lengths.shape[0]

    def per_image(packed):
        query_image, key_image, value_image, grad_image, logsum_image, length = packed
        key_heads = key_image.reshape(LMAX, heads_here, HEAD_DIM)
        value_heads = value_image.reshape(LMAX, heads_here, HEAD_DIM)
        live_keys = jnp.arange(LMAX, dtype=jnp.int32) < length

        def per_block(running, inputs):
            key_grad, value_grad = running
            query_block, grad_block, logsum_block = inputs
            scores = (
                jnp.einsum(
                    "qhe,khe->hqk", query_block, key_heads, preferred_element_type=jnp.float32
                )
                * score_scale
            )
            scores = jnp.where(live_keys[None, None, :], scores, -1e30)
            probability = jnp.exp(scores - logsum_block[:, :, None])
            grad_prob = jnp.einsum(
                "qhe,khe->hqk", grad_block, value_heads, preferred_element_type=jnp.float32
            )
            inner_sum = jnp.sum(probability * grad_prob, axis=-1, keepdims=True)
            grad_score = (probability * (grad_prob - inner_sum)).astype(jnp.bfloat16)
            query_grad = (
                jnp.einsum(
                    "hqk,khe->qhe", grad_score, key_heads, preferred_element_type=jnp.float32
                )
                * score_scale
            )
            key_grad = (
                key_grad
                + jnp.einsum(
                    "hqk,qhe->khe", grad_score, query_block, preferred_element_type=jnp.float32
                )
                * score_scale
            )
            value_grad = value_grad + jnp.einsum(
                "hqk,qhe->khe",
                probability.astype(jnp.bfloat16),
                grad_block,
                preferred_element_type=jnp.float32,
            )
            return ((key_grad, value_grad), query_grad.astype(jnp.bfloat16))

        initial = (
            jnp.zeros((LMAX, heads_here, HEAD_DIM), jnp.float32),
            jnp.zeros((LMAX, heads_here, HEAD_DIM), jnp.float32),
        )
        blocks = (
            query_image.reshape(LMAX // block_rows, block_rows, heads_here, HEAD_DIM),
            grad_image.reshape(LMAX // block_rows, block_rows, heads_here, HEAD_DIM),
            logsum_image,
        )
        (key_grad, value_grad), query_grad = lax.scan(per_block, initial, blocks)
        return (
            query_grad.reshape(LMAX, -1),
            key_grad.reshape(LMAX, -1).astype(jnp.bfloat16),
            value_grad.reshape(LMAX, -1).astype(jnp.bfloat16),
        )

    stacked = (
        queries.reshape(image_count, LMAX, -1),
        key_rows.reshape(image_count, LMAX, -1),
        value_rows.reshape(image_count, LMAX, -1),
        grad_rows.reshape(image_count, LMAX, -1),
        log_sums,
        lengths,
    )
    query_grad, key_grad, value_grad = lax.map(per_image, stacked)
    return (
        query_grad.reshape(image_count * LMAX, -1),
        key_grad.reshape(image_count * LMAX, -1),
        value_grad.reshape(image_count * LMAX, -1),
    )


def adam_update(master, first_moment, second_moment, gradient, learn_rate, clip_factor, correction):
    clipped = gradient * clip_factor
    first_new = 0.5 * first_moment + 0.5 * clipped
    second_new = 0.5 * second_moment + 0.5 * clipped * clipped
    direction = first_new / correction / (jnp.sqrt(second_new / correction) + 1e-08)
    return (master - learn_rate * (direction + 0.1 * master), first_new, second_new)


def on_device(
    tokens,
    cotangent,
    buckets,
    timesteps,
    labels,
    class_table,
    step_count,
    modulate_master,
    modulate_first,
    modulate_second,
    attend_master,
    attend_first,
    attend_second,
    project_master,
    project_first,
    project_second,
    expand_master,
    expand_first,
    expand_second,
    reduce_master,
    reduce_first,
    reduce_second,
    biases_master,
    biases_first,
    biases_second,
):
    head_index = lax.axis_index("head")
    head_count = lax.axis_size("head")
    tok_rows = tokens.shape[0]
    image_count = buckets.shape[0]
    unit_cells = SIDE // 8
    heights = table_pick(buckets, row_units) * unit_cells
    widths = table_pick(buckets, col_units) * unit_cells
    lengths = heights * widths
    row_index = head_index * tok_rows + jnp.arange(tok_rows, dtype=jnp.int32)
    image_of = row_index // LMAX
    position = row_index % LMAX
    choose = image_of[:, None] == jnp.arange(image_count, dtype=jnp.int32)[None, :]
    pick_rows = choose.astype(jnp.float32)
    row_wide = jnp.sum(jnp.where(choose, widths[None, :], 0), axis=1)
    row_length = jnp.sum(jnp.where(choose, lengths[None, :], 0), axis=1)
    live_rows = (position < row_length).astype(jnp.float32)
    grid_cells = grid_features(position, row_wide, D)
    class_pick = (
        labels[:, None] == jnp.arange(class_table.shape[0], dtype=jnp.int32)[None, :]
    ).astype(jnp.bfloat16)
    class_rows = jnp.dot(class_pick, class_table, preferred_element_type=jnp.float32)
    condition = jax.nn.silu(class_rows + time_features(timesteps, D)).astype(jnp.bfloat16)
    bias_low = biases_master.astype(jnp.bfloat16).astype(jnp.float32)
    offset_base = 6 * D
    bias_query = bias_low[offset_base : offset_base + D]
    bias_value = bias_low[offset_base + D : offset_base + 2 * D]
    bias_proj = bias_low[offset_base + 2 * D : offset_base + 3 * D]
    bias_hidden = bias_low[offset_base + 3 * D : offset_base + 3 * D + FF]
    bias_output = bias_low[offset_base + 3 * D + FF :]
    head_slabs = (
        lax.all_gather(attend_master.astype(jnp.bfloat16), "head", axis=1, tiled=True),
        lax.all_gather(project_master.astype(jnp.bfloat16), "head", axis=1, tiled=True),
        lax.all_gather(expand_master.astype(jnp.bfloat16), "head", axis=1, tiled=True),
        lax.all_gather(reduce_master.astype(jnp.bfloat16), "head", axis=1, tiled=True),
    )
    attend_slab, project_slab, expand_slab, reduce_slab = head_slabs
    mod_width = 6 * D // head_count
    mod_share = fold_rows(condition, modulate_master.astype(jnp.bfloat16))
    mod_share = mod_share + lax.dynamic_slice_in_dim(bias_low, head_index * mod_width, mod_width)
    modulation = lax.all_gather(mod_share, "head", axis=1, tiled=True)
    mod_rows = jnp.dot(pick_rows, modulation, precision=highest)
    shift_one, scale_one, gating_one, shift_two, scale_two, gating_two = jnp.split(
        mod_rows, 6, axis=1
    )
    residual_zero = tokens.astype(jnp.float32) + grid_cells
    hidden_attend = modulate(residual_zero, shift_one, scale_one).astype(jnp.bfloat16)
    packed = fold_rows(hidden_attend, attend_slab)
    queries = (packed[:, :D] + bias_query).astype(jnp.bfloat16)
    key_rows = packed[:, D : 2 * D].astype(jnp.bfloat16)
    value_rows = (packed[:, 2 * D :] + bias_value).astype(jnp.bfloat16)
    query_heads, key_heads, value_heads = (
        lax.all_to_all(queries, "head", split_axis=1, concat_axis=0, tiled=True),
        lax.all_to_all(key_rows, "head", split_axis=1, concat_axis=0, tiled=True),
        lax.all_to_all(value_rows, "head", split_axis=1, concat_axis=0, tiled=True),
    )
    head_out, log_sums = attend(query_heads, key_heads, value_heads, lengths)
    attention = lax.all_to_all(head_out, "head", split_axis=0, concat_axis=1, tiled=True)
    branch_attend = fold_rows(attention, project_slab) + bias_proj
    residual_one = residual_zero + gating_one * branch_attend
    hidden_expand = modulate(residual_one, shift_two, scale_two).astype(jnp.bfloat16)
    widened = fold_rows(hidden_expand, expand_slab) + bias_hidden
    activated = jax.nn.gelu(widened, approximate=True).astype(jnp.bfloat16)
    branch_expand = fold_rows(activated, reduce_slab) + bias_output
    output = (residual_one + gating_two * branch_expand).astype(jnp.bfloat16)
    outer_grad = cotangent.astype(jnp.float32) * live_rows[:, None]
    gating_later = outer_grad * branch_expand
    closing_grad = (outer_grad * gating_two).astype(jnp.bfloat16)
    active_grad = back_cols(closing_grad, reduce_slab)
    gelu_value, gelu_pullback = jax.vjp(lambda inner: jax.nn.gelu(inner, approximate=True), widened)
    widened_grad = gelu_pullback(active_grad)[0].astype(jnp.bfloat16)
    hidden_grad = back_cols(widened_grad, expand_slab)
    later_value, later_pullback = jax.vjp(modulate, residual_one, shift_two, scale_two)
    residual_part, shift_later, scale_later = later_pullback(hidden_grad)
    middle_grad = outer_grad + residual_part
    gating_early = middle_grad * branch_attend
    branch_grad = (middle_grad * gating_one).astype(jnp.bfloat16)
    attend_grad = back_cols(branch_grad, project_slab).astype(jnp.bfloat16)
    heads_grad = lax.all_to_all(attend_grad, "head", split_axis=1, concat_axis=0, tiled=True)
    query_grad, keyrow_grad, value_grad = attend_back(
        query_heads, key_heads, value_heads, heads_grad, log_sums, lengths
    )
    query_back, keys_back, values_back = (
        lax.all_to_all(query_grad, "head", split_axis=0, concat_axis=1, tiled=True),
        lax.all_to_all(keyrow_grad, "head", split_axis=0, concat_axis=1, tiled=True),
        lax.all_to_all(value_grad, "head", split_axis=0, concat_axis=1, tiled=True),
    )
    packed_grad = jnp.concatenate([query_back, keys_back, values_back], axis=1)
    normed_grad = back_cols(packed_grad, attend_slab)
    early_value, early_pullback = jax.vjp(modulate, residual_zero, shift_one, scale_one)
    input_part, shift_early, scale_early = early_pullback(normed_grad)
    input_grad = middle_grad + input_part
    mod_token_grad = jnp.concatenate(
        [shift_early, scale_early, gating_early, shift_later, scale_later, gating_later], axis=1
    )
    mod_grad = lax.dot_general(
        pick_rows, mod_token_grad, (((0,), (0,)), ((), ())), precision=highest
    )
    mod_summed = lax.psum_scatter(mod_grad, "head", scatter_dimension=1, tiled=True)
    mod_rounded = mod_summed.astype(jnp.bfloat16)
    grad_mod = rows_seq(condition, mod_rounded)
    mod_slot = lax.dynamic_update_slice_in_dim(
        jnp.zeros((6 * D,), jnp.float32),
        jnp.sum(mod_rounded.astype(jnp.float32), axis=0),
        head_index * mod_width,
        0,
    )
    bias_share = jnp.concatenate(
        [
            mod_slot,
            jnp.sum(query_back.astype(jnp.float32), axis=0),
            jnp.sum(values_back.astype(jnp.float32), axis=0),
            jnp.sum(branch_grad.astype(jnp.float32), axis=0),
            jnp.sum(widened_grad.astype(jnp.float32), axis=0),
            jnp.sum(closing_grad.astype(jnp.float32), axis=0),
        ]
    )
    operand_pairs = (
        (hidden_attend, packed_grad),
        (attention, branch_grad),
        (hidden_expand, widened_grad),
        (activated, closing_grad),
    )
    term_slabs = tuple((rows_seq(left_side, right_side) for left_side, right_side in operand_pairs))
    reduced = (
        lax.psum_scatter(
            term_slabs[0].astype(jnp.bfloat16), "head", scatter_dimension=1, tiled=True
        ).astype(jnp.float32),
        lax.psum_scatter(
            term_slabs[1].astype(jnp.bfloat16), "head", scatter_dimension=1, tiled=True
        ).astype(jnp.float32),
        lax.psum_scatter(
            term_slabs[2].astype(jnp.bfloat16), "head", scatter_dimension=1, tiled=True
        ).astype(jnp.float32),
        lax.psum_scatter(
            term_slabs[3].astype(jnp.bfloat16), "head", scatter_dimension=1, tiled=True
        ).astype(jnp.float32),
    )
    grad_attend, grad_project, grad_expand, grad_reduce = reduced
    local_squares = jnp.sum(grad_mod * grad_mod) + sum(
        (jnp.sum(gradient * gradient) for gradient in reduced)
    )
    bias_total, square_total = lax.psum((bias_share, local_squares), ("seq", "head"))
    grad_norm = jnp.sqrt(square_total + jnp.sum(bias_total * bias_total))
    clip_factor = jnp.minimum(1.0, 1.0 / (grad_norm + 1e-06))
    correction = 1.0 - jnp.power(0.5, step_count.astype(jnp.float32))
    modulate_new = adam_update(
        modulate_master,
        modulate_first,
        modulate_second,
        grad_mod,
        0.5 * D ** (-0.5),
        clip_factor,
        correction,
    )
    attend_new = adam_update(
        attend_master,
        attend_first,
        attend_second,
        grad_attend,
        0.5 * D ** (-0.5),
        clip_factor,
        correction,
    )
    project_new = adam_update(
        project_master,
        project_first,
        project_second,
        grad_project,
        0.5 * D ** (-0.5),
        clip_factor,
        correction,
    )
    expand_new = adam_update(
        expand_master,
        expand_first,
        expand_second,
        grad_expand,
        0.5 * D ** (-0.5),
        clip_factor,
        correction,
    )
    reduce_new = adam_update(
        reduce_master,
        reduce_first,
        reduce_second,
        grad_reduce,
        0.5 * FF ** (-0.5),
        clip_factor,
        correction,
    )
    biases_new = adam_update(
        biases_master, biases_first, biases_second, bias_total, 0.1, clip_factor, correction
    )
    return (
        output,
        input_grad,
        grad_norm,
        modulate_new[0],
        modulate_new[1],
        modulate_new[2],
        attend_new[0],
        attend_new[1],
        attend_new[2],
        project_new[0],
        project_new[1],
        project_new[2],
        expand_new[0],
        expand_new[1],
        expand_new[2],
        reduce_new[0],
        reduce_new[1],
        reduce_new[2],
        biases_new[0],
        biases_new[1],
        biases_new[2],
    )


ALPHA = HEAD_DIM ** (-0.5) * math.log2(math.e)
GELU_A = math.sqrt(2.0 / math.pi)
GELU_B = 0.044715
BLOCK = FF // 16
BF, F32 = jnp.bfloat16, jnp.float32
ANY, VM = pl.ANY, pltpu.VMEM
PIECES = {"q": (144, 864, 48), "p": (72, 576, None), "u": (144, 1152, 48), "d": (288, 576, 96)}
NAMES = ("q", "p", "u", "d")
MESH = pl.DeviceIdType.MESH


def place():
    return tuple(lax.axis_index(a) for a in ("z", "x", "c", "y"))


def at_z(k):
    z = lax.axis_index("z")
    return (z, z + 1 - 2 * (z % 2), (z + 2) % 4, 3 - z)[k]


def rdma(src, dst, send, recv, to):
    return pltpu.make_async_remote_copy(
        src_ref=src, dst_ref=dst, send_sem=send, recv_sem=recv, device_id=to, device_id_type=MESH
    )


def partners():
    z, x, c, y = place()
    xn, yn, twin = (z, 1 - x, c, y), (z, x, c, 1 - y), (z, x, 1 - c, y)
    return xn, yn, twin, [(at_z(k), x, c, y) for k in range(4)]


def flipped(f):
    z, x, c, y = place()
    return (z, 1 - x if f & 1 else x, 1 - c if f & 2 else c, 1 - y if f & 4 else y)


def greet():
    barrier = pltpu.get_barrier_semaphore()
    for to in [flipped(f) for f in range(1, 8)] + partners()[3][1:]:
        pl.semaphore_signal(barrier, inc=1, device_id=to, device_id_type=MESH)
    pl.semaphore_wait(barrier, 10)


CHUNKS = (
    (0, 0, 80, 16),
    (0, 80, 64, 16),
    (1, 0, 72, None),
    (2, 0, 80, 16),
    (2, 80, 64, 16),
    (3, 0, 144, 32),
    (3, 144, 144, 32),
)


def parts_of(chunk, k):
    _, _, rows, cut = CHUNKS[chunk]
    if cut is None:
        return ((0, rows), None) if k == 0 else (None, (0, rows))
    return (0, cut), (cut, rows - cut)


def piece_at(full, w, y, zk, x, first, count):
    rows = PIECES[NAMES[w]][0]
    if count == 72:
        return full.at[y, zk * 2 + x]
    return full.at[y, pl.ds(pl.multiple_of((zk * 2 + x) * rows + first, 16), count)]


def matmul(left, right):
    return jnp.dot(left, right, preferred_element_type=F32)


def matmul_nt(left, right):
    return lax.dot_general(left, right, (((1,), (1,)), ((), ())), preferred_element_type=F32)


def matmul_tn(left, right):
    return lax.dot_general(left, right, (((0,), (0,)), ((), ())), preferred_element_type=F32)


class Gather:
    def __init__(self, own, full, sems):
        self.own, self.full = own, full
        self.zs, self.zr, self.xs, self.xr, self.ys, self.yr, self.fs, self.fr, self.ps, self.pr = sems
        self.sent = []

    def piece(self, w, flip_y, k, flip_x):
        z, x, c, y = place()
        weight, first, count, _ = CHUNKS[w]
        return piece_at(
            self.full[weight], weight, 1 - y if flip_y else y, at_z(k), 1 - x if flip_x else x, first, count
        )

    def source(self, w):
        weight, first, count, _ = CHUNKS[w]
        return self.own[weight].at[pl.ds(first, count)]

    def send(self, make):
        make().start()
        self.sent.append(make)

    def arrived(self, ref, s, r):
        rdma(ref, ref, s, r, partners()[0]).wait_recv()

    def start(self, w):
        def to_x():
            return rdma(self.source(w), self.piece(w, 0, 0, 0), self.xs.at[w, 0], self.xr.at[w, 0], partners()[0])

        def to_y():
            return rdma(self.source(w), self.piece(w, 0, 0, 0), self.ys.at[w, 0], self.yr.at[w, 0], partners()[1])

        def to_z(k):
            to = partners()[3][k]
            return rdma(self.source(w), self.piece(w, 0, 0, 0), self.zs.at[w, k], self.zr.at[w, k], to)

        self.send(to_x)
        self.send(to_y)
        for k in (1, 2, 3):
            self.send(functools.partial(to_z, k))

    def column(self, w, k):
        self.arrived(self.piece(w, 0, k, 0), self.zs.at[w, k], self.zr.at[w, k])

        def to_x():
            piece = self.piece(w, 0, k, 0)
            return rdma(piece, piece, self.xs.at[w, k], self.xr.at[w, k], partners()[0])

        def to_y():
            piece = self.piece(w, 0, k, 0)
            return rdma(piece, piece, self.ys.at[w, k], self.yr.at[w, k], partners()[1])

        self.send(to_x)
        self.send(to_y)

    def plane(self, w, k):
        spans = parts_of(w, k)

        def pass_on(i):
            part = self.piece(w, i, k, 1 - i).at[pl.ds(*spans[i])]
            return rdma(part, part, self.fs.at[w, k, i], self.fr.at[w, k, i], partners()[1 - i])

        self.arrived(self.piece(w, 0, k, 1), self.xs.at[w, k], self.xr.at[w, k])
        if k in (0, 2) and spans[0] is not None:
            self.send(functools.partial(pass_on, 0))
        self.arrived(self.piece(w, 1, k, 0), self.ys.at[w, k], self.yr.at[w, k])
        if k in (0, 2) and spans[1] is not None:
            self.send(functools.partial(pass_on, 1))

    def corner(self, w, k):
        for i, span in enumerate(parts_of(w, k)):
            if span is not None:
                part = self.piece(w, 1, k, 1).at[pl.ds(*span)]
                self.arrived(part, self.fs.at[w, k, i], self.fr.at[w, k, i])

        def to_pair():
            piece = self.piece(w, 1, k, 1)
            return rdma(piece, piece, self.ps.at[w, k], self.pr.at[w, k], partners()[3][1])

        self.send(to_pair)

    def last(self, w, k):
        self.arrived(self.piece(w, 1, k ^ 1, 1), self.ps.at[w, k], self.pr.at[w, k])

    def finish(self):
        for make in self.sent:
            make().wait_send()

    def steps(self):
        def each(method, chunks, ks):
            return [(method, i, k) for i in chunks for k in ks]

        column, plane, corner, last = self.column, self.plane, self.corner, self.last
        one = (0, 1)
        plan = [(self.start, 0), (self.start, 1), (self.start, 2)]
        plan += each(column, one, (1,)) + each(plane, one, (0,))
        plan += each(column, one, (2,)) + each(column, one, (3,)) + [(self.start, 3)]
        plan += each(corner, one, (0,)) + each(plane, one, (2,))
        plan += each(column, (2,), (1,)) + [(self.start, 4)]
        plan += each(plane, one, (1,)) + each(corner, one, (2,))
        plan += each(plane, (2,), (0,)) + each(column, (2,), (2, 3)) + each(column, (3,), (1,))
        plan += each(plane, one, (3,)) + each(last, one, (0, 2))
        count = len(CHUNKS)
        for t in range(-2, count + 4):
            wave = [(self.start, t + 2)] if t + 2 < count else []
            if 0 <= t - 4 < count:
                wave += each(last, (t - 4,), (0, 2))
            for lag, make in enumerate(
                (
                    lambda i: each(column, (i,), (1,)),
                    lambda i: each(plane, (i,), (0,)) + each(column, (i,), (2, 3)),
                    lambda i: each(corner, (i,), (0,)) + each(plane, (i,), (2, 1)),
                    lambda i: each(corner, (i,), (2,)) + each(plane, (i,), (3,)),
                )
            ):
                if t >= 0 and 0 <= t - lag < count:
                    wave += make(t - lag)
            plan += [step for step in wave if step not in plan]
        return plan


def mod_steps(cond_ref, weight, bias, out_ref, lhs, bufs, s, r):
    conds, part, got_z, mid, box = bufs

    def hop(i):
        z, x, c, y = place()
        zn = partners()[3]
        if i == 0:
            pairs = [(conds.at[z, x, c], conds.at[z, x, c], flipped(f)) for f in (1, 2, 3)]
        elif i == 1:
            pairs = [(conds.at[z], conds.at[z], zn[k]) for k in (1, 2, 3)]
        elif i == 2:
            pairs = [(part.at[at_z(k)], got_z.at[k - 1], zn[k]) for k in (1, 2, 3)]
        else:
            pairs = []
            for f in range(1, 8):
                to = flipped(f)
                pairs.append((mid.at[to[1], to[3]], box.at[x, c, y], to))
        return [
            rdma(src, dst, s.at[i, n], r.at[i, n], to) for n, (src, dst, to) in enumerate(pairs)
        ]

    def step(i):
        z, x, c, y = place()
        if i > 0:
            for d in hop(i - 1):
                d.wait()
        if i == 0:
            conds[z, x, c] = cond_ref[...]
        elif i == 2:
            me = (z * 2 + x) * 2 + c
            for n in range(16):
                lhs[pl.ds(n, 1), :] = conds[n // 4, n // 2 % 2, n % 2, pl.ds(me, 1), :]
            for j in range(3):
                cols = slice(j * D, (j + 1) * D)
                result = matmul(lhs[:, :72].astype(BF), weight[:, cols].astype(BF))
                for n in range(16):
                    part[n // 4, n // 2 % 2, n % 2, :, cols] = result[n : n + 1]
        elif i == 3:
            mid[...] = part[z] + got_z[0] + got_z[1] + got_z[2]
            box[x, c, y] = mid[x, y]
        elif i == 4:
            for n in range(2):
                total = (box[0, 0, n] + box[0, 1, n]) + (box[1, 0, n] + box[1, 1, n])
                out_ref[n] = total + bias[:, n * 3456 : (n + 1) * 3456]
        if i < 4:
            for d in hop(i):
                d.start()

    return [functools.partial(step, i) for i in range(5)]


def normed_tile(value):
    average = jnp.mean(value, axis=-1, keepdims=True)
    centred = value - average
    spread = jnp.mean(centred * centred, axis=-1, keepdims=True)
    return centred * lax.rsqrt(spread + 1e-06)


SPACE = (8, 12)


def rounded(value):
    return value.astype(BF).astype(F32)


def pick(bucket, entries):
    return sum(
        jnp.where(bucket == float(i), float(e * (SIDE // 8)), 0.0) for i, e in enumerate(entries)
    )


def start_rows(tok, table, bucket, first, rows):
    wide = pick(bucket, col_units)
    spot = (first + lax.broadcasted_iota(jnp.int32, (rows, 1), 0)).astype(F32)
    lane = lax.broadcasted_iota(jnp.int32, (1, 64), 1).astype(F32)
    grid_row = jnp.where((spot >= lane * wide) & (spot < (lane + 1.0) * wide), 1.0, 0.0)
    left = spot - wide * jnp.sum(grid_row * lane, axis=1, keepdims=True)
    grid_col = jnp.where(left == lane, 1.0, 0.0)
    high = table.astype(BF)
    low = (table - high.astype(F32)).astype(BF)
    parts = [matmul(hot.astype(BF), high) + matmul(hot.astype(BF), low) for hot in (grid_row, grid_col)]
    return tok.astype(F32) + jnp.concatenate(parts, axis=1)


def forward_kernel(*refs):
    (tok, cot, bucket_in, table, att_m, proj_m, exp_m, red_m, mod_w, cond_in, bias_in) = refs[:11]
    gq, gp, gu, gd = full = refs[11:15]
    (mod_out, lhs, x0_out, dy_out, cl_out, h1_out, q_out, k_out, v_out) = refs[15:24]
    (attnt_out, lse_out, ba_out, x1_out, h2_out, der_out, bb_out, y_out, gred_out) = refs[24:33]
    (oq, op, ou, od, fq, tq, fu, tu) = refs[33:41]
    mod_bufs = refs[41:46]
    (xs, x0, dy, bucket, closing, h1, qa, ka, vt, attnt, attn) = refs[46:57]
    (ps, pr, ds, dr, acc, x1, h2, act, der, ba, bb, yo, gstage) = refs[57:70]
    (b_all, b_q, b_v, b_u) = refs[70:74]
    lsem = refs[74]
    gather_sems = refs[75:85]
    ms, mr, ws, wr, ts, tr, os, outs_sem, gsem = refs[85:94]
    z, x, c, y = place()
    xn, yn, twin, zn = partners()
    half = x0.shape[0]
    mine = pl.multiple_of(c * half, half)
    other = pl.multiple_of((1 - c) * half, half)
    gather = Gather((oq, op, ou, od), full, gather_sems)
    mods = mod_steps(cond_in, mod_w, b_all, mod_out, lhs, mod_bufs, ms, mr)
    greet()
    mods[0]()

    def split(master, width, f, t, i):
        count = master.shape[1] // (2 * width)
        sides = [
            jnp.concatenate(
                [master[:, (2 * j + p) * width : (2 * j + p + 1) * width] for j in range(count)], axis=1
            )
            for p in (0, 1)
        ]
        t[...] = jnp.where(c == 0, sides[1], sides[0])
        rdma(t, f.at[c], os.at[0, i], os.at[1, i], twin).start()
        f[c] = jnp.where(c == 0, sides[0], sides[1])

    def joined(f, t, i, piece):
        rdma(t, f.at[c], os.at[0, i], os.at[1, i], twin).wait()
        piece[...] = jnp.concatenate([f[0], f[1]], axis=0).astype(BF)

    steps = [step for step in gather.steps() if step[0] != gather.start or step[1] > 2]
    done = [0]

    def tick(n):
        for f, *a in steps[done[0] : done[0] + n]:
            f(*a)
        done[0] = min(done[0] + n, len(steps))

    def tick_until(chunk):
        last = max(i for i, s in enumerate(steps) if s[0] == gather.last and s[1] == chunk)
        tick(max(0, last + 1 - done[0]))

    swap_to = (z, x, y, c)
    PART = 128
    moves = [(bucket_in, bucket)]
    for i in range(half // PART):
        moves.append((xs.at[pl.ds(i * PART, PART)], x0.at[pl.ds(i * PART, PART)]))
    for i in range(half // PART):
        moves.append((cot.at[pl.ds(i * PART, PART)], dy.at[pl.ds(i * PART, PART)]))

    def move(i):
        @pl.when(c != y)
        def _():
            rdma(*moves[i], ws.at[i], wr.at[i], swap_to).start()

        @pl.when(c == y)
        def _():
            pltpu.make_async_copy(*moves[i], ws.at[i]).start()

    def moved(i):
        @pl.when(c != y)
        def _():
            rdma(*moves[i], ws.at[i], wr.at[i], swap_to).wait()

        @pl.when(c == y)
        def _():
            pltpu.make_async_copy(*moves[i], ws.at[i]).wait()

    def first_rows(i):
        rows = slice(i * PART, (i + 1) * PART)
        xs[rows, :] = start_rows(
            tok[rows, :], table[...], bucket_in[0:1, 0:1], y * half + i * PART, PART
        ).astype(BF)
        move(1 + i)

    move(0)
    split(att_m, HEAD_DIM, fq, tq, 0)
    mods[1]()
    op[...] = proj_m[...].astype(BF)
    gather.start(2)
    first_rows(0)
    joined(fq, tq, 0, oq)
    gather.start(0)
    gather.start(1)
    mods[2]()
    first_rows(1)
    split(exp_m, BLOCK, fu, tu, 1)
    first_rows(2)
    tick(2)
    first_rows(3)
    tick(2)
    joined(fu, tu, 1, ou)
    tick(3)
    mods[3]()
    od[...] = red_m[...].astype(BF)
    owns = [
        pltpu.make_async_copy(
            gather.own[w], piece_at(full[w], w, y, z, x, 0, PIECES[NAMES[w]][0]), lsem.at[w]
        )
        for w in range(4)
    ]
    for d in owns:
        d.start()
    b_all[...] = rounded(bias_in[...]).reshape(1, 14 * D)
    tick(SPACE[0])
    mods[4]()
    tick(SPACE[1])

    def of_core(base, width, count):
        return jnp.concatenate(
            [
                jnp.where(
                    c == 0,
                    b_all[:, base + 2 * j * width : base + (2 * j + 1) * width],
                    b_all[:, base + (2 * j + 1) * width : base + (2 * j + 2) * width],
                )
                for j in range(count)
            ],
            axis=1,
        )

    b_p = b_all.at[:, pl.ds(8 * D, D)]
    b_d = b_all.at[:, pl.ds(9 * D + FF, D)]
    for i in range(1 + half // PART):
        moved(i)

    def vec(i):
        return mod_out[i // 3, :, (i % 3) * D : (i % 3 + 1) * D]

    TILE, WIDE = 128, 256
    tiles = half // TILE

    def own_tile(ref, t):
        return ref.at[pl.ds(pl.multiple_of(mine + t * TILE, TILE), TILE)]

    def give(ref, t, i):
        part = own_tile(ref, t)
        return rdma(part, part, ts.at[i, t], tr.at[i, t], twin)

    def norm_one(t, _):
        rows = pl.ds(pl.multiple_of(t * TILE, TILE), TILE)
        value = normed_tile(x0[rows, :].astype(F32)) * (1.0 + vec(1)) + vec(0)
        own_tile(h1, t)[...] = value.astype(BF)
        give(h1, t, 0).start()
        return 0

    for t in range(tiles):
        norm_one(t, 0)
        tick(1)
    tick_until(1)
    for i in range(half // PART):
        move(1 + half // PART + i)

    def both_got(ref, i):
        for t in range(tiles):
            give(ref, t, i).wait_send()
            part = ref.at[pl.ds(pl.multiple_of(other + t * TILE, TILE), TILE)]
            rdma(part, part, ts.at[i, t], tr.at[i, t], twin).wait_recv()

    out_copies = []

    def put(src, dst):
        d = pltpu.make_async_copy(src, dst, outs_sem.at[len(out_copies)])
        d.start()
        out_copies.append(d)

    def load(src, dst, i):
        d = pltpu.make_async_copy(src, dst, lsem.at[i])
        d.start()
        d.wait()

    owns[0].wait()
    live = pick(bucket[0:1, 0:1], row_units) * pick(bucket[0:1, 0:1], col_units)
    lane = lax.broadcasted_iota(jnp.int32, (1, 128), 1)

    b_q[...] = of_core(6 * D, HEAD_DIM, 8)
    b_v[...] = of_core(7 * D, HEAD_DIM, 8)
    b_u[...] = of_core(9 * D, BLOCK, 8)

    def qkv(weight):
        load(gq, weight, 4)

        def rows_of(start):
            rows = pl.ds(start, half)
            left = h1[rows, :]
            spot = (start + lax.broadcasted_iota(jnp.int32, (half, 1), 0)).astype(F32)
            mask = jnp.where(lane == HEAD_DIM, jnp.where(spot < live, 0.0, -1e30), 0.0)
            ones = jnp.where(lane == HEAD_DIM, 1.0, 0.0)
            fill = jnp.zeros((half, 56), F32)

            def put_key(j, key):
                ka[j, rows, :] = (jnp.concatenate([key, fill], axis=1) + mask).astype(BF)

            one = matmul(left, weight[0])
            for j in range(8):
                cols = slice(j * HEAD_DIM, (j + 1) * HEAD_DIM)
                query = (one[:, cols] + b_q[:, cols]) * ALPHA
                qa[j, rows, :] = (jnp.concatenate([query, fill], axis=1) + ones).astype(BF)
            for j in range(4):
                put_key(j, one[:, 576 + j * 72 : 648 + j * 72])
            tick(2)
            two = matmul(left, weight[1])
            for j in range(4):
                put_key(4 + j, two[:, j * 72 : j * 72 + 72])
            for j in range(8):
                cols = slice(j * HEAD_DIM, (j + 1) * HEAD_DIM)
                value = two[:, 288 + j * 72 : 360 + j * 72] + b_v[:, cols]
                vt[j, :, rows] = value.T.astype(BF)
            tick(2)

        rows_of(mine)
        both_got(h1, 0)
        rows_of(other)

    pl.run_scoped(qkv, VM((2, D, 864), BF))
    put(h1, h1_out)
    tick(1)
    put(qa, q_out)
    put(ka, k_out)
    put(vt, v_out)

    def head(j, _):
        def queries(i, _):
            rows = pl.ds(pl.multiple_of(i * 512, 512), 512)
            scores = matmul_nt(ka[j], qa[j, rows, :])
            top = jnp.max(scores, axis=0, keepdims=True)
            prob = jnp.exp2(scores - top)
            total = jnp.sum(prob, axis=0, keepdims=True)
            result = matmul(vt[j], prob.astype(BF)) * (1.0 / total)
            attnt[j, :, rows] = result
            lse_out[j, :, rows] = top + jnp.log2(total)
            return 0

        lax.fori_loop(0, 2, queries, 0)
        return 0

    for j in range(8):
        head(j, 0)
        tick(3)

    for i in range(half // PART):
        moved(1 + half // PART + i)

    def close(t, _):
        rows = pl.ds(pl.multiple_of(t * TILE, TILE), TILE)
        spot = (mine + t * TILE + lax.broadcasted_iota(jnp.int32, (TILE, 1), 0)).astype(F32)
        outer = jnp.where(spot < live, dy[rows, :].astype(F32), 0.0)
        dy[rows, :] = outer.astype(BF)
        own_tile(closing, t)[...] = (outer * vec(5)).astype(BF)
        give(closing, t, 1).start()
        return 0

    lax.fori_loop(0, tiles, close, 0)
    put(attnt, attnt_out)
    tick_until(2)
    owns[1].wait()

    def proj(weight, stage, raw):
        load(gp, raw, 5)
        for i in (0, 1):
            for h in range(8):
                stage[h * 72 : h * 72 + 72, :] = raw[i, h].astype(F32)
            weight[i] = stage[...].astype(BF)

        def attn_rows(i, _):
            rows = pl.ds(pl.multiple_of(i * 256, 256), 256)
            value = jnp.concatenate([attnt[j, :, rows] for j in range(8)], axis=0)
            attn[rows, :] = value.T.astype(BF)
            return 0

        lax.fori_loop(0, 4, attn_rows, 0)

        def for_twin(t, _):
            rows = pl.ds(pl.multiple_of(t * WIDE, WIDE), WIDE)
            left = attn[pl.ds(pl.multiple_of(other + t * WIDE, WIDE), WIDE), :]
            for i in (0, 1):
                ps[rows, i * 576 : (i + 1) * 576] = matmul(left, weight[i]).astype(BF)
            rdma(ps.at[rows], pr.at[rows], ts.at[2, t], tr.at[2, t], twin).start()
            return 0

        for t in range(half // WIDE):
            for_twin(t, 0)
            tick(1)

        def for_me(t, _):
            rows = pl.ds(pl.multiple_of(t * WIDE, WIDE), WIDE)
            left = attn[pl.ds(pl.multiple_of(mine + t * WIDE, WIDE), WIDE), :]
            for i in (0, 1):
                acc[rows, i * 576 : (i + 1) * 576] = matmul(left, weight[i])
            return 0

        for t in range(half // WIDE):
            for_me(t, 0)
            tick(1)

    pl.run_scoped(proj, VM((2, 576, 576), BF), VM((576, 576), F32), VM((2, 8, 72, 576), BF))

    def middle(t, _):
        rows = pl.ds(pl.multiple_of(t * TILE, TILE), TILE)
        branch = acc[rows, :] + pr[rows, :].astype(F32) + b_p[...]
        ba[rows, :] = branch.astype(BF)
        value = x0[rows, :].astype(F32) + vec(2) * branch
        x1[rows, :] = value
        own_tile(h2, t)[...] = (normed_tile(value) * (1.0 + vec(4)) + vec(3)).astype(BF)
        give(h2, t, 3).start()
        return 0

    def half_got(src, dst, i, t):
        rows = pl.ds(t * WIDE, WIDE)
        rdma(src.at[rows], dst.at[rows], ts.at[i, t], tr.at[i, t], twin).wait()

    for t in range(tiles):
        if t % 2 == 0:
            half_got(ps, pr, 2, t // 2)
        middle(t, 0)
    put(ba, ba_out)
    put(x1, x1_out)
    put(x0, x0_out)
    put(dy, dy_out)
    tick_until(4)
    owns[2].wait()
    both_got(h2, 3)
    both_got(closing, 1)
    put(h2, h2_out)
    put(closing, cl_out)

    def up(weight):
        load(gu, weight, 6)

        def block_of(start, i, n):
            rows = pl.ds(start, half)
            part = slice(n * 384, (n + 1) * 384)
            cols = slice(i * D + n * 384, i * D + (n + 1) * 384)
            u = matmul(h2[rows, :], weight[i, :, part]) + b_u[:, cols]
            square = u * u
            inner = u * (GELU_A + GELU_A * GELU_B * square)
            bent = jnp.tanh(inner)
            half_up = 0.5 + 0.5 * bent
            act[rows, cols] = (u * half_up).astype(BF)
            slope = u * (GELU_A + 3.0 * GELU_A * GELU_B * square)
            der[rows, cols] = (half_up + slope * (half_up * (1.0 - bent))).astype(BF)

        for start in (mine, other):
            for i in (0, 1):
                for n in range(3):
                    block_of(start, i, n)
                    tick(n % 2)

    pl.run_scoped(up, VM((2, D, D), BF))
    put(der, der_out)

    gouts = []
    for t in range(6):
        slot = t % 2
        if t >= 2:
            gouts[t - 2].wait()
        value = matmul(act[:, t * 384 : (t + 1) * 384].T, closing[...])
        for i in (0, 1):
            gstage[slot, i] = value[:, i * 576 : (i + 1) * 576].astype(BF)
        d = pltpu.make_async_copy(
            gstage.at[slot], gred_out.at[:, pl.ds(t * 384, 384)], gsem.at[slot]
        )
        d.start()
        gouts.append(d)
        tick(1)
    for d in gouts[-2:]:
        d.wait()
    tick(len(steps))
    owns[3].wait()

    def down(weight):
        load(gd, weight, 7)

        for i in (0, 1):
            cols = slice(i * 576, (i + 1) * 576)
            ds[:, cols] = matmul(act[pl.ds(other, half), :], weight[i]).astype(BF)
        rdma(ds, dr, ts.at[4, 0], tr.at[4, 0], twin).start()
        for i in (0, 1):
            cols = slice(i * 576, (i + 1) * 576)
            acc[:, cols] = matmul(act[pl.ds(mine, half), :], weight[i])
        rdma(ds, dr, ts.at[4, 0], tr.at[4, 0], twin).wait()

    pl.run_scoped(down, VM((2, 2304, 576), BF))

    def finish(t, _):
        rows = pl.ds(pl.multiple_of(t * TILE, TILE), TILE)
        branch = acc[rows, :] + dr[rows, :].astype(F32) + b_d[...]
        bb[rows, :] = branch.astype(BF)
        yo[rows, :] = (x1[rows, :] + vec(5) * branch).astype(BF)
        return 0

    for t in range(tiles):
        finish(t, 0)
    put(bb, bb_out)
    put(yo, y_out)
    for d in out_copies:
        d.wait()
    gather.finish()


def forward_block(tokens, cotangent, bucket, table, masters, modulate_master, cond, biases):
    shapes = {
        "gq": (2, D, 864),
        "gp": (2, 8, 72, 576),
        "gu": (2, D, D),
        "gd": (2, 2304, 576),
    }
    half = tokens.shape[0]
    rows = 2 * half
    out_shape, out_specs = [], []

    def out(shape, dtype, space=ANY):
        out_shape.append(jax.ShapeDtypeStruct(shape, dtype))
        out_specs.append(pl.BlockSpec(memory_space=space))

    for s in shapes.values():
        out(s, BF)
    out((2, 1, 3456), F32, VM)
    out((16, 128), F32, VM)
    out((half, D), BF)
    out((half, D), BF)
    out((rows, D), BF)
    out((rows, D), BF)
    out((8, rows, 128), BF)
    out((8, rows, 128), BF)
    out((8, 72, rows), BF)
    out((8, 72, rows), F32)
    out((8, 1, rows), F32, VM)
    out((half, D), BF)
    out((half, D), F32)
    out((rows, D), BF)
    out((rows, 2304), BF)
    out((half, D), BF)
    out((half, D), BF)
    out((2, 2304, 576), BF)
    dma = pltpu.SemaphoreType.DMA
    scratch = [
        VM((144, 864), BF),
        VM((72, 576), BF),
        VM((144, D), BF),
        VM((288, 576), BF),
        VM((2, 72, 864), F32),
        VM((72, 864), F32),
        VM((2, 72, D), F32),
        VM((72, D), F32),
        VM((4, 2, 2, 16, 128), F32),
        VM((4, 2, 2, 1, 3456), F32),
        VM((3, 2, 2, 1, 3456), F32),
        VM((2, 2, 1, 3456), F32),
        VM((2, 2, 2, 1, 3456), F32),
        VM((half, D), BF),
        VM((half, D), BF),
        VM((half, D), BF),
        VM((8, 128), F32),
        VM((rows, D), BF),
        VM((rows, D), BF),
        VM((8, rows, 128), BF),
        VM((8, rows, 128), BF),
        VM((8, 72, rows), BF),
        VM((8, 72, rows), F32),
        VM((rows, 576), BF),
        VM((half, D), BF),
        VM((half, D), BF),
        VM((half, D), BF),
        VM((half, D), BF),
        VM((half, D), F32),
        VM((half, D), F32),
        VM((rows, D), BF),
        VM((rows, 2304), BF),
        VM((rows, 2304), BF),
        VM((half, D), BF),
        VM((half, D), BF),
        VM((half, D), BF),
        VM((2, 2, 384, 576), BF),
        VM((1, 14 * D), F32),
        VM((1, 576), F32),
        VM((1, 576), F32),
        VM((1, 2304), F32),
        dma((8,)),
    ]
    n = len(CHUNKS)
    scratch += [dma((n, 4))] * 6 + [dma((n, 4, 2))] * 2 + [dma((n, 4))] * 2
    scratch += [
        dma((4, 7)),
        dma((4, 7)),
        dma((9,)),
        dma((9,)),
        dma((5, 4)),
        dma((5, 4)),
        dma((2, 2)),
        dma((20,)),
        dma((2,)),
    ]
    vm = pl.BlockSpec(memory_space=VM)
    hbm = pl.BlockSpec(memory_space=ANY)
    return pl.pallas_call(
        forward_kernel,
        out_shape=out_shape,
        in_specs=[vm, hbm] + [vm] * 9,
        out_specs=out_specs,
        scratch_shapes=scratch,
        compiler_params=pltpu.CompilerParams(
            collective_id=0, has_side_effects=True, vmem_limit_bytes=60 * 2**20
        ),
        name="forward_block",
    )(tokens, cotangent, bucket, table, *masters, modulate_master, cond, biases)


class Scatter:
    def __init__(self, grads, boxes, outs, sems):
        self.grads, self.outs = grads, outs
        self.pair_box, self.diag_box, self.x_box, self.y_box, self.z_box = boxes
        self.ps, self.pr, self.fs, self.fr, self.xs, self.xr, self.ys, self.yr, self.zs, self.zr = sems
        self.sent = []

    def piece(self, i, flip_y, k, flip_x):
        z, x, c, y = place()
        weight, first, count, _ = CHUNKS[i]
        return piece_at(
            self.grads[weight], weight, 1 - y if flip_y else y, at_z(k), 1 - x if flip_x else x, first, count
        )

    def box(self, boxes, i, n):
        weight, first, count, _ = CHUNKS[i]
        return boxes[weight].at[n, pl.ds(first, count)]

    def send(self, make):
        make().start()
        self.sent.append(make)

    def arrived(self, ref, s, r):
        rdma(ref, ref, s, r, partners()[0]).wait_recv()

    def add(self, target, *others):
        total = target[...]
        for o in others:
            total = total + o[...]
        target[...] = total

    def across(self, i, k, by_y):
        if by_y:
            return rdma(
                self.piece(i, 1, k, 0), self.box(self.y_box, i, k), self.ys.at[i, k], self.yr.at[i, k], partners()[1]
            )
        return rdma(
            self.piece(i, 0, k, 1), self.box(self.x_box, i, k), self.xs.at[i, k], self.xr.at[i, k], partners()[0]
        )

    def start(self, i):
        def to_pair(k):
            return rdma(
                self.piece(i, 1, k ^ 1, 1),
                self.box(self.pair_box, i, k // 2),
                self.ps.at[i, k],
                self.pr.at[i, k],
                partners()[3][1],
            )

        for k in (0, 2):
            self.send(functools.partial(to_pair, k))
        for k in (1, 3):
            for by_y in (0, 1):
                self.send(functools.partial(self.across, i, k, by_y))

    def corner(self, i, k):
        box = self.box(self.pair_box, i, k // 2)
        self.arrived(box, self.ps.at[i, k], self.pr.at[i, k])
        self.add(self.piece(i, 1, k, 1), box)
        spans = parts_of(i, k)

        def part(n):
            return rdma(
                self.piece(i, 1, k, 1).at[pl.ds(*spans[n])],
                self.box(self.diag_box, i, k // 2).at[pl.ds(*spans[n])],
                self.fs.at[i, k, n],
                self.fr.at[i, k, n],
                partners()[1 - n],
            )

        for n in (0, 1):
            if spans[n] is not None:
                self.send(functools.partial(part, n))

    def plane(self, i, k):
        spans = parts_of(i, k)
        for n in (0, 1):
            if spans[n] is not None:
                part = self.box(self.diag_box, i, k // 2).at[pl.ds(*spans[n])]
                self.arrived(part, self.fs.at[i, k, n], self.fr.at[i, k, n])
                self.add(self.piece(i, n, k, 1 - n).at[pl.ds(*spans[n])], part)
            self.send(functools.partial(self.across, i, k, n))

    def both(self, i, k):
        boxes = []
        for boxes_of, s, r in ((self.x_box, self.xs, self.xr), (self.y_box, self.ys, self.yr)):
            box = self.box(boxes_of, i, k)
            self.arrived(box, s.at[i, k], r.at[i, k])
            boxes.append(box)
        return boxes

    def column(self, i, k):
        self.add(self.piece(i, 0, k, 0), *self.both(i, k))

        def along():
            return rdma(
                self.piece(i, 0, k, 0),
                self.box(self.z_box, i, k - 1),
                self.zs.at[i, k],
                self.zr.at[i, k],
                partners()[3][k],
            )

        self.send(along)

    def last(self, i):
        weight, first, count, _ = CHUNKS[i]
        boxes = self.both(i, 0)
        for k in (1, 2, 3):
            box = self.box(self.z_box, i, k - 1)
            self.arrived(box, self.zs.at[i, k], self.zr.at[i, k])
            boxes.append(box)
        total = self.piece(i, 0, 0, 0)[...].astype(F32)
        for box in boxes:
            total = total + box[...].astype(F32)
        self.outs[weight][first : first + count, :] = total

    def finish(self):
        for make in self.sent:
            make().wait_send()

    def steps(self, i):
        return (
            [(self.start, i), (self.corner, i, 0), (self.corner, i, 2)],
            [(self.plane, i, 0), (self.plane, i, 2), (self.column, i, 1)],
            [(self.column, i, 3), (self.column, i, 2)],
            [(self.last, i)],
        )


def total_steps(dm, bs, lhs, mods, bufs, gmod, bias_out, s, r):
    got_m, got_b, sb, got_z, near = bufs

    def hop(i):
        z, x, c, y = place()
        zn = partners()[3]
        pairs = []
        if i == 0:
            for f in range(1, 8):
                to = flipped(f)
                pairs.append((dm.at[to[3]], got_m.at[x, c, y], to))
                pairs.append((bs, got_b.at[f - 1], to))
        elif i == 1:
            for k in (1, 2, 3):
                pairs.append((mods.at[z], mods.at[z], zn[k]))
                pairs.append((sb, got_z.at[k - 1], zn[k]))
        else:
            pairs.append((near.at[0], near.at[1], flipped(4)))
        return [
            rdma(src, dst, s.at[i, n], r.at[i, n], to) for n, (src, dst, to) in enumerate(pairs)
        ]

    def step(i):
        z, x, c, y = place()
        if i > 0:
            for d in hop(i - 1):
                d.wait()
        if i == 0:
            got_m[x, c, y] = dm[y]
        elif i == 1:
            for n in range(4):
                mods[z, n // 2, n % 2] = rounded(got_m[n // 2, 0, n % 2] + got_m[n // 2, 1, n % 2])
            sb[...] = ((bs[...] + got_b[0]) + (got_b[1] + got_b[2])) + (
                (got_b[3] + got_b[4]) + (got_b[5] + got_b[6])
            )
        elif i == 2:
            rows = [mods[n // 4, n // 2 % 2, n % 2] for n in range(16)]
            total = rows[0]
            for row in rows[1:]:
                total = total + row
            near[0] = total
        elif i == 3:
            for n in (0, 1):
                bias_out[:, n * 3456 : (n + 1) * 3456] = jnp.where(y == n, near[0], near[1])
        if i < 3:
            for d in hop(i):
                d.start()
        if i == 2:
            bias_out[:, 6 * D :] = (sb[...] + got_z[0]) + (got_z[1] + got_z[2])
            left = lhs[:, :72].astype(BF)
            right = jnp.concatenate(rows, axis=0).astype(BF)
            for j in range(3):
                cols = slice(j * D, (j + 1) * D)
                gmod[:, cols] = matmul_tn(left, right[:, cols])

    return [functools.partial(step, i) for i in range(4)]


BEATS = {
    "down": "010101",
    "expand": "010101",
    "up": "010101",
    "middle": "1010",
    "project": "1010",
    "heads": "0001",
    "attend": "010101",
    "back": "000111",
    "input": "1111",
    "hops": "111111",
}


def backward_kernel(*refs):
    gq, gp, gu, gd, mod, lhs = refs[:6]
    (x0_in, dy_in, cl_in, h1_in, q_in, k_in, v_in, at_in, lse) = refs[6:15]
    (ba_in, x1_in, h2_in, der_in, bb_in, y_in, gred) = refs[15:22]
    (out, ig_out, s_att, s_proj, s_exp, s_red, gmod, bias_out, norm_out) = refs[22:31]
    grads = refs[31:35]
    boxes = [refs[35 + 4 * i : 39 + 4 * i] for i in range(5)]
    fq, fu, gotq, gotu = refs[55:59]
    dba, dx1, ps, pr, dm, bs, mods = refs[59:66]
    total_bufs = refs[66:71]
    sq, here = refs[71:73]
    lsem = refs[73]
    scatter_sems = refs[74:84]
    ts, tr, ws, wr, hs, hr, ns, nr = refs[84:92]
    z, x, c, y = place()
    xn, yn, twin, zn = partners()
    half = dx1.shape[0]
    mine = pl.multiple_of(c * half, half)
    other = pl.multiple_of((1 - c) * half, half)
    scatter = Scatter(grads, boxes, (fq, s_proj, fu, s_red), scatter_sems)
    hops = total_steps(dm, bs, lhs, mods, total_bufs, gmod, bias_out, hs, hr)
    pltpu.make_async_copy(gred, grads[3], lsem.at[0]).start()
    dm[...] = jnp.zeros_like(dm)
    bs[...] = jnp.zeros_like(bs)
    TILE = 128
    swap_to = (z, x, y, c)

    def vec(i):
        return mod[i // 3, :, (i % 3) * D : (i % 3 + 1) * D]

    def add_mod(i, value):
        cols = slice((i % 3) * D, (i % 3 + 1) * D)
        dm[i // 3, :, cols] = dm[i // 3, :, cols] + jnp.sum(value, axis=0, keepdims=True)

    def add_bias(at, value):
        cols = slice(at, at + value.shape[1])
        bs[:, cols] = bs[:, cols] + value

    def load(src, dst, i):
        d = pltpu.make_async_copy(src, dst, lsem.at[i])
        d.start()
        return d

    queue = []

    def tick(n):
        for _ in range(min(n, len(queue))):
            f, *a = queue.pop(0)
            f(*a)

    def beat(where, n):
        tick(int(BEATS[where][n]))

    def moves(i):
        if i == 0:
            return y_in, out
        rows = pl.ds((i - 1) * TILE, TILE)
        return dba.at[rows], ig_out.at[rows]

    def move(i):
        @pl.when(c != y)
        def _():
            rdma(*moves(i), ws.at[i], wr.at[i], swap_to).start()

        @pl.when(c == y)
        def _():
            pltpu.make_async_copy(*moves(i), ws.at[i]).start()

    def moved(i):
        @pl.when(c != y)
        def _():
            rdma(*moves(i), ws.at[i], wr.at[i], swap_to).wait()

        @pl.when(c == y)
        def _():
            pltpu.make_async_copy(*moves(i), ws.at[i]).wait()

    def begin():
        greet()
        pltpu.make_async_copy(gred, grads[3], lsem.at[0]).wait()
        scatter.start(5)
        scatter.start(6)
        five, six = scatter.steps(5), scatter.steps(6)
        queue.extend(five[0][1:] + six[0][1:] + five[1] + six[1] + five[2] + six[2] + five[3] + six[3])

    def own_tile(ref, t):
        return ref.at[pl.ds(pl.multiple_of(mine + t * TILE, TILE), TILE)]

    def widen(du):
        def through(weight, closing, der):
            loads = [load(gd, weight, 1), load(cl_in, closing, 2)]

            def slopes(n):
                return load(der_in.at[:, pl.ds(n * 384, 384)], der.at[n % 2], 3 + n % 2)

            coming = slopes(0)
            begin()
            for d in loads:
                d.wait()
            for n in range(6):
                cols = slice(n * 384, (n + 1) * 384)
                coming.wait()
                if n < 5:
                    coming = slopes(n + 1)
                right = jnp.concatenate([weight[0, cols, :], weight[1, cols, :]], axis=1)
                value = (matmul_nt(closing[...], right) * der[n % 2].astype(F32)).astype(BF)
                du[:, cols] = value
                sums = jnp.sum(value.astype(F32), axis=0, keepdims=True)
                here[:, cols] = sums
                beat("down", n)
            for j in range(8):
                block = here[:, j * BLOCK : (j + 1) * BLOCK]
                for p in (0, 1):
                    add_bias(3 * D + (2 * j + p) * BLOCK, jnp.where(c == p, block, 0.0))

        pl.run_scoped(through, VM((2, 2304, 576), BF), VM((2 * half, D), BF), VM((2, 2 * half, 384), BF))

        def expand(weight, h2):
            load(h2_in, h2, 2).wait()
            weight_load = load(gu, weight, 1)
            for t in range(3):
                left = h2[:, t * 384 : (t + 1) * 384].T
                for i in (0, 1):
                    grads[2][i, t * 384 : (t + 1) * 384, :] = matmul(
                        left, du[:, i * D : (i + 1) * D]
                    ).astype(BF)
                    beat("expand", 2 * t + i)

            scatter.start(3)
            scatter.start(4)
            three, four = scatter.steps(3), scatter.steps(4)
            queue.extend(
                three[0][1:] + four[0][1:] + three[1] + four[1] + three[2] + four[2] + three[3] + four[3]
            )
            move(0)

            def product(start, n):
                rows = pl.ds(start, half)
                part = slice(n * 384, (n + 1) * 384)
                return matmul_nt(du[rows, :D], weight[0, part, :]) + matmul_nt(du[rows, D:], weight[1, part, :])

            weight_load.wait()

            for n in range(3):
                ps[:, n * 384 : (n + 1) * 384] = product(other, n).astype(BF)
                beat("up", n)
            rdma(ps, pr, ts.at[0, 0], tr.at[0, 0], twin).start()
            for n in range(3):
                dx1[:, n * 384 : (n + 1) * 384] = product(mine, n)
                beat("up", 3 + n)

        pl.run_scoped(expand, VM((2, D, D), BF), VM((2 * half, D), BF))

    pl.run_scoped(widen, VM((2 * half, 2304), BF))

    def sums_got(i):
        rdma(ps, pr, ts.at[i, 0], tr.at[i, 0], twin).wait()

    def norm_back(value, scaling, gradient):
        average = jnp.mean(value, axis=-1, keepdims=True)
        centred = value - average
        inverse = lax.rsqrt(jnp.mean(centred * centred, axis=-1, keepdims=True) + 1e-06)
        normed = centred * inverse
        inner = gradient * (1.0 + scaling)
        part = inner - jnp.mean(inner, axis=-1, keepdims=True)
        part = part - normed * jnp.mean(inner * normed, axis=-1, keepdims=True)
        return part * inverse, normed

    def middle(x1, dy, ba, bb):
        loads = [load(x1_in, x1, 1), load(dy_in, dy, 2), load(ba_in, ba, 3), load(bb_in, bb, 4)]
        for d in loads:
            d.wait()
        sums_got(0)
        for t in range(half // TILE):
            rows = slice(t * TILE, (t + 1) * TILE)
            gradient = dx1[rows, :] + pr[rows, :].astype(F32)
            part, normed = norm_back(x1[rows, :], vec(4), gradient)
            add_mod(3, gradient)
            add_mod(4, gradient * normed)
            outer = dy[rows, :].astype(F32)
            add_mod(5, outer * bb[rows, :].astype(F32))
            add_bias(9216 - D, jnp.sum(rounded(outer * vec(5)), axis=0, keepdims=True))
            total = outer + part
            dx1[rows, :] = total
            add_mod(2, total * ba[rows, :].astype(F32))
            branch = (total * vec(2)).astype(BF)
            own_tile(dba, t)[...] = branch
            tile = own_tile(dba, t)
            rdma(tile, tile, ts.at[1, t], tr.at[1, t], twin).start()
            add_bias(2 * D, jnp.sum(branch.astype(F32), axis=0, keepdims=True))
            beat("middle", t)

    pl.run_scoped(middle, VM((half, D), F32), VM((half, D), BF), VM((half, D), BF), VM((half, D), BF))

    def attention(dot, dqkv):
        def project(weight, stage, raw, attnt, attn):
            loads = [load(gp, raw, 1), load(at_in, attnt, 2)]
            for d in loads:
                d.wait()
            for i in (0, 1):
                for h in range(8):
                    stage[h * 72 : h * 72 + 72, :] = raw[i, h].astype(F32)
                weight[i] = stage[...].astype(BF)
            attn[...] = jnp.concatenate([attnt[h] for h in range(8)], axis=0).astype(BF)
            for t in range(half // TILE):
                tile = own_tile(dba, t)
                rdma(tile, tile, ts.at[1, t], tr.at[1, t], twin).wait_send()
                part = dba.at[pl.ds(pl.multiple_of(other + t * TILE, TILE), TILE)]
                rdma(part, part, ts.at[1, t], tr.at[1, t], twin).wait_recv()
            for n in range(4):
                rows = slice(n * 256, (n + 1) * 256)
                right = dba[rows, :]
                value = matmul_nt(weight[0], right[:, :576]) + matmul_nt(weight[1], right[:, 576:])
                for h in range(8):
                    dot[h, :, rows] = value[h * 72 : h * 72 + 72, :].astype(BF)
                beat("project", n)
            for i in (0, 1):
                stage[...] = matmul(attn[...], dba[:, i * 576 : (i + 1) * 576])
                for h in range(8):
                    grads[1][i, h] = stage[h * 72 : h * 72 + 72, :].astype(BF)

        pl.run_scoped(
            project,
            VM((2, 576, 576), BF),
            VM((576, 576), F32),
            VM((2, 8, 72, 576), BF),
            VM((8, 72, 2 * half), F32),
            VM((576, 2 * half), BF),
        )
        scatter.start(2)
        two = scatter.steps(2)
        queue.extend(two[0][1:] + two[1] + two[2] + two[3])

        def heads(qa, ka, vt, at, dk, dv, dq):
            def fetch(h):
                n = h % 2
                return [
                    load(src.at[h], dst.at[n], 1 + 4 * n + m)
                    for m, (src, dst) in enumerate(((q_in, qa), (k_in, ka), (v_in, vt), (at_in, at)))
                ]

            coming = fetch(0)
            for h in range(8):
                n = h % 2
                for d in coming:
                    d.wait()
                if h < 7:
                    coming = fetch(h + 1)
                value = vt[n].T
                key_t = ka[n, :, :72].T
                inner = jnp.sum(at[n] * dot[h].astype(F32), axis=0, keepdims=True)
                dk[...] = jnp.zeros_like(dk)
                dv[...] = jnp.zeros_like(dv)
                for i in range(4):
                    rows = slice(i * 256, (i + 1) * 256)
                    query = qa[n, rows, :]
                    grad = dot[h, :, rows]
                    scores = matmul_nt(ka[n], query)
                    prob = jnp.exp2(scores - lse[h, :, rows])
                    change = matmul(value, grad) - inner[:, rows]
                    dscore = (prob * change).astype(BF)
                    dv[...] += matmul_nt(grad, prob.astype(BF))
                    dk[...] += matmul_nt(query[:, :72].T, dscore)
                    dq[:, rows] = matmul(key_t, dscore)
                    beat("heads", i)
                scale = HEAD_DIM ** (-0.5)
                dqkv[0, :, h * 72 : h * 72 + 72] = (dq[...] * scale).T.astype(BF)
                key_grad = (dk[...] * math.log(2.0)).T.astype(BF)
                if h < 4:
                    dqkv[0, :, 576 + h * 72 : 648 + h * 72] = key_grad
                else:
                    dqkv[1, :, h * 72 - 288 : h * 72 - 216] = key_grad
                dqkv[1, :, 288 + h * 72 : 360 + h * 72] = dv[...].T.astype(BF)

        pl.run_scoped(
            heads,
            VM((2, 2 * half, 128), BF),
            VM((2, 2 * half, 128), BF),
            VM((2, 72, 2 * half), BF),
            VM((2, 72, 2 * half), F32),
            VM((72, 2 * half), F32),
            VM((72, 2 * half), F32),
            VM((72, 2 * half), F32),
        )

        def attend(weight, x0):
            loads = [load(gq, weight, 2), load(x0_in, x0, 3)]
            pl.run_scoped(attend_grad, VM((2 * half, D), BF))
            scatter.start(0)
            scatter.start(1)
            zero, one = scatter.steps(0), scatter.steps(1)
            queue.extend(
                zero[0][1:] + one[0][1:] + zero[1] + one[1] + zero[2] + one[2] + zero[3] + one[3]
            )
            for d in loads:
                d.wait()
            pl.run_scoped(functools.partial(back, weight, x0), VM((half, D), F32))

        def attend_grad(h1):
            load(h1_in, h1, 1).wait()
            for t in range(3):
                left = h1[:, t * 384 : (t + 1) * 384].T
                for i in (0, 1):
                    grads[0][i, t * 384 : (t + 1) * 384, :] = matmul(left, dqkv[i]).astype(BF)
                    beat("attend", 2 * t + i)

        def back(weight, x0, acc):
            def product(start, n):
                rows = pl.ds(start, half)
                part = slice(n * 384, (n + 1) * 384)
                return matmul_nt(dqkv[0, rows, :], weight[0, part, :]) + matmul_nt(
                    dqkv[1, rows, :], weight[1, part, :]
                )

            for n in range(3):
                ps[:, n * 384 : (n + 1) * 384] = product(other, n).astype(BF)
                beat("back", n)
            rdma(ps, pr, ts.at[2, 0], tr.at[2, 0], twin).start()
            for n in range(3):
                acc[:, n * 384 : (n + 1) * 384] = product(mine, n)
                beat("back", 3 + n)
            sums_got(2)
            for t in range(half // TILE):
                rows = slice(t * TILE, (t + 1) * TILE)
                gradient = acc[rows, :] + pr[rows, :].astype(F32)
                part, normed = norm_back(x0[rows, :].astype(F32), vec(1), gradient)
                add_mod(0, gradient)
                add_mod(1, gradient * normed)
                dba[rows, :] = (dx1[rows, :] + part).astype(BF)
                move(1 + t)
                beat("input", t)

        pl.run_scoped(
            attend,
            VM((2, D, 864), BF),
            VM((half, D), BF),
        )
        for i in (0, 1):
            sums = jnp.sum(dqkv[i].astype(F32), axis=0, keepdims=True)
            for j in range(8):
                block = sums[:, i * 288 + j * 72 : i * 288 + j * 72 + 72]
                for p in (0, 1):
                    add_bias(i * D + (2 * j + p) * 72, jnp.where(c == p, block, 0.0))

    pl.run_scoped(attention, VM((8, 72, 2 * half), BF), VM((2, 2 * half, 864), BF))
    for n, hop in enumerate(hops):
        hop()
        beat("hops", n)
    tick(len(queue))

    last_half = 72
    def give(f, got, i):
        return rdma(f.at[pl.ds(pl.multiple_of((1 - c) * 72, 8), 72)], got, ts.at[3, i], tr.at[3, i], twin)

    give(fq, gotq, 0).start()
    give(fu, gotu, 1).start()

    def squares(value):
        return jnp.sum(jnp.sum(value * value, axis=0, keepdims=True), axis=1, keepdims=True)

    bias_squares = squares(bias_out[...])
    total = squares(fq[...]) + squares(fu[...]) + squares(s_proj[...]) + squares(s_red[...]) + squares(gmod[...])
    total = jnp.broadcast_to(total, (8, 128))
    sq[0] = total
    near = [
        rdma(sq.at[0], sq.at[f], ns.at[f - 1], nr.at[f - 1], flipped(f)) for f in range(1, 8)
    ]
    for d in near:
        d.start()
    for d in near:
        d.wait()
    sq[8] = ((sq[0] + sq[1]) + (sq[2] + sq[3])) + ((sq[4] + sq[5]) + (sq[6] + sq[7]))
    last = [rdma(sq.at[8], sq.at[8 + k], ns.at[6 + k], nr.at[6 + k], zn[k]) for k in (1, 2, 3)]
    for d in last:
        d.start()

    def interleave(f, got, shard, width, i):
        give(f, got, i).wait()
        own = jnp.where(c == 0, f[:72, :], f[72:, :])
        sides = (jnp.where(c == 0, own, got[...]), jnp.where(c == 0, got[...], own))
        count = own.shape[1] // width
        shard[...] = jnp.concatenate(
            [sides[p][:, j * width : (j + 1) * width] for j in range(count) for p in (0, 1)], axis=1
        )

    interleave(fq, gotq, s_att, HEAD_DIM, 0)
    interleave(fu, gotu, s_exp, BLOCK, 1)
    for d in last:
        d.wait()
    norm_out[...] = (sq[8] + sq[9]) + (sq[10] + sq[11]) + bias_squares
    for i in range(1 + half // TILE):
        moved(i)
    scatter.finish()


def backward_block(kept):
    half = kept[6].shape[0]
    rows = 2 * half
    sd = jax.ShapeDtypeStruct
    vm = pl.BlockSpec(memory_space=VM)
    hbm = pl.BlockSpec(memory_space=ANY)
    sizes = ((D, 864), (72, 576), (D, D), (2304, 576))
    pieces = [PIECES[n][:2] for n in NAMES]
    dma = pltpu.SemaphoreType.DMA
    n = len(CHUNKS)
    scratch = [
        VM((2, D, 864), BF),
        VM((2, 8, 72, 576), BF),
        VM((2, D, D), BF),
        VM((2, 2304, 576), BF),
    ]
    for count in (2, 2, 4, 4, 3):
        scratch += [VM((count,) + p, BF) for p in pieces]
    scratch += [
        VM((144, 864), F32),
        VM((144, D), F32),
        VM((72, 864), F32),
        VM((72, D), F32),
        VM((rows, D), BF),
        VM((half, D), F32),
        VM((half, D), BF),
        VM((half, D), BF),
        VM((2, 1, 3456), F32),
        VM((1, 9216), F32),
        VM((4, 2, 2, 1, 3456), F32),
        VM((2, 2, 2, 1, 3456), F32),
        VM((7, 1, 9216), F32),
        VM((1, 9216), F32),
        VM((3, 1, 9216), F32),
        VM((2, 1, 3456), F32),
        VM((12, 8, 128), F32),
        VM((1, 2304), F32),
        dma((9,)),
    ]
    scratch += [dma((n, 4))] * 2 + [dma((n, 4, 2))] * 2 + [dma((n, 4))] * 6
    scratch += [dma((4, 4))] * 2 + [dma((5,))] * 2 + [dma((3, 14))] * 2 + [dma((10,))] * 2
    places = [hbm] * 4 + [vm, vm] + [hbm] * 8 + [vm] + [hbm] * 7
    return pl.pallas_call(
        backward_kernel,
        out_shape=[
            sd((half, D), BF),
            sd((half, D), BF),
            sd((72, 1728), F32),
            sd((72, 576), F32),
            sd((72, 2304), F32),
            sd((288, 576), F32),
            sd((72, 3456), F32),
            sd((1, 14 * D), F32),
            sd((8, 128), F32),
        ],
        in_specs=places,
        out_specs=[hbm, hbm] + [vm] * 7,
        scratch_shapes=scratch,
        compiler_params=pltpu.CompilerParams(
            collective_id=1, has_side_effects=True, vmem_limit_bytes=62 * 2**20
        ),
        name="backward_block",
    )(*kept)


def step_kernel(squares, correction, *refs):
    count = len(RATES)
    norm = jnp.sqrt(squares[0:1, 0:1])
    clip = jnp.minimum(1.0, 1.0 / (norm + 1e-06))
    fix = correction[0:1, 0:1]
    for i, rate in enumerate(RATES):
        master, first, second, gradient = (refs[4 * i + j][...] for j in range(4))
        new = adam_update(master, first, second, gradient, rate, clip, fix)
        for j in range(3):
            refs[4 * count + 3 * i + j][...] = new[j]


RATES = (0.5 * D ** (-0.5),) * 4 + (0.5 * FF ** (-0.5),)


def step_weights(squares, correction, states):
    grid = 3

    def spec(shape):
        return pl.BlockSpec((shape[0] // grid, shape[1]), lambda i: (i, 0))

    whole = pl.BlockSpec((8, 128), lambda i: (0, 0))
    flat = [value for state in states for value in state]
    new = [value for state in states for value in state[:3]]
    return pl.pallas_call(
        step_kernel,
        grid=(grid,),
        out_shape=[jax.ShapeDtypeStruct(v.shape, v.dtype) for v in new],
        in_specs=[whole, whole] + [spec(v.shape) for v in flat],
        out_specs=[spec(v.shape) for v in new],
        compiler_params=pltpu.CompilerParams(vmem_limit_bytes=62 * 2**20),
        name="step_weights",
    )(squares, correction, *flat)


def on_device_fast(
    tokens,
    cotangent,
    buckets,
    timesteps,
    labels,
    class_table,
    step_count,
    modulate_master,
    modulate_first,
    modulate_second,
    attend_master,
    attend_first,
    attend_second,
    project_master,
    project_first,
    project_second,
    expand_master,
    expand_first,
    expand_second,
    reduce_master,
    reduce_first,
    reduce_second,
    biases_master,
    biases_first,
    biases_second,
):

    z, x, c, y = place()
    bf16, f32 = jnp.bfloat16, jnp.float32
    block = FF // 16
    class_row = lax.dynamic_slice_in_dim(class_table, labels[0], 1).astype(f32)
    condition = jax.nn.silu(class_row + time_features(timesteps, D)).astype(bf16).astype(f32)
    cond_tiles = jnp.pad(condition.reshape(16, 72), ((0, 0), (0, 56)))
    bucket = jnp.broadcast_to(buckets.astype(f32)[:, None], (8, 128))
    steps = jnp.arange(64, dtype=f32)[:, None]
    omegas = jnp.exp(-math.log(10000.0) * jnp.arange(288, dtype=f32) / 288)[None, :]
    table = jnp.concatenate([jnp.sin(steps * omegas), jnp.cos(steps * omegas)], axis=1)
    kept = forward_block(
        tokens,
        cotangent,
        bucket,
        table,
        (attend_master, project_master, expand_master, reduce_master),
        modulate_master,
        cond_tiles,
        biases_master,
    )
    (output, input_grad, grad_attend, grad_project, grad_expand, grad_reduce, grad_mod, bias_total, squares) = (
        backward_block(kept)
    )
    correction = 1.0 - jnp.power(0.5, step_count.astype(f32))
    states = (
        (modulate_master, modulate_first, modulate_second, grad_mod),
        (attend_master, attend_first, attend_second, grad_attend),
        (project_master, project_first, project_second, grad_project),
        (expand_master, expand_first, expand_second, grad_expand),
        (reduce_master, reduce_first, reduce_second, grad_reduce),
    )
    updates = list(step_weights(squares, jnp.full((8, 128), correction), states))
    grad_norm = jnp.sqrt(squares[0, 0])
    clip_factor = jnp.minimum(1.0, 1.0 / (grad_norm + 1e-06))
    updates += adam_update(
        biases_master, biases_first, biases_second, bias_total[0], 0.1, clip_factor, correction
    )
    return (output, input_grad.astype(f32), grad_norm, *updates)


def fast_solution(mesh):
    return jax.shard_map(
        on_device_fast,
        mesh=mesh,
        in_specs=(
            P(("z", "x", "c", "y"), None),
            P(("z", "x", "c", "y"), None),
            P(("z", "x", "c")),
            P(("z", "x", "c")),
            P(("z", "x", "c")),
            P(),
            P(),
            P(("z", "x", "c"), "y"),
            P(("z", "x", "c"), "y"),
            P(("z", "x", "c"), "y"),
            P(("z", "x", "c"), "y"),
            P(("z", "x", "c"), "y"),
            P(("z", "x", "c"), "y"),
            P(("z", "x", "c"), "y"),
            P(("z", "x", "c"), "y"),
            P(("z", "x", "c"), "y"),
            P(("z", "x", "c"), "y"),
            P(("z", "x", "c"), "y"),
            P(("z", "x", "c"), "y"),
            P(("z", "x", "c"), "y"),
            P(("z", "x", "c"), "y"),
            P(("z", "x", "c"), "y"),
            P(),
            P(),
            P(),
        ),
        out_specs=(
            P(("z", "x", "c", "y"), None),
            P(("z", "x", "c", "y"), None),
            P(),
            P(("z", "x", "c"), "y"),
            P(("z", "x", "c"), "y"),
            P(("z", "x", "c"), "y"),
            P(("z", "x", "c"), "y"),
            P(("z", "x", "c"), "y"),
            P(("z", "x", "c"), "y"),
            P(("z", "x", "c"), "y"),
            P(("z", "x", "c"), "y"),
            P(("z", "x", "c"), "y"),
            P(("z", "x", "c"), "y"),
            P(("z", "x", "c"), "y"),
            P(("z", "x", "c"), "y"),
            P(("z", "x", "c"), "y"),
            P(("z", "x", "c"), "y"),
            P(("z", "x", "c"), "y"),
            P(),
            P(),
            P(),
        ),
        check_vma=False,
    )


def plain_solution(mesh):
    return jax.shard_map(
        on_device,
        mesh=mesh,
        in_specs=(
            P(("seq", "head"), None),
            P(("seq", "head"), None),
            P("seq"),
            P("seq"),
            P("seq"),
            P(),
            P(),
            P("seq", "head"),
            P("seq", "head"),
            P("seq", "head"),
            P("seq", "head"),
            P("seq", "head"),
            P("seq", "head"),
            P("seq", "head"),
            P("seq", "head"),
            P("seq", "head"),
            P("seq", "head"),
            P("seq", "head"),
            P("seq", "head"),
            P("seq", "head"),
            P("seq", "head"),
            P("seq", "head"),
            P(),
            P(),
            P(),
        ),
        out_specs=(
            P(("seq", "head"), None),
            P(("seq", "head"), None),
            P(),
            P("seq", "head"),
            P("seq", "head"),
            P("seq", "head"),
            P("seq", "head"),
            P("seq", "head"),
            P("seq", "head"),
            P("seq", "head"),
            P("seq", "head"),
            P("seq", "head"),
            P("seq", "head"),
            P("seq", "head"),
            P("seq", "head"),
            P("seq", "head"),
            P("seq", "head"),
            P("seq", "head"),
            P(),
            P(),
            P(),
        ),
        check_vma=False,
    )


def solution(mesh):
    if dict(mesh.shape) == {"seq": 16, "head": 2}:
        grid = Mesh(mesh.devices.reshape(4, 2, 2, 2), ("z", "x", "c", "y"))
        return fast_solution(grid)
    return plain_solution(mesh)
```

```python
import functools
import math

import jax
import jax.numpy as jnp
from jax import lax
from jax.experimental import pallas as pl
from jax.experimental.pallas import tpu as pltpu
from jax.sharding import Mesh
from jax.sharding import PartitionSpec as P

D = 1152
HEAD_DIM = 72
FF = 4608
SIDE = 32
LMAX = 1024


highest = lax.Precision.HIGHEST
row_units = (8, 4, 16, 6, 10, 7, 4, 6)
col_units = (8, 16, 4, 10, 6, 9, 8, 6)


def table_pick(indices, entries):
    matches = indices[..., None] == jnp.arange(len(entries), dtype=jnp.int32)
    return jnp.sum(jnp.where(matches, jnp.array(entries, jnp.int32), 0), axis=-1)


def layer_norm(value):
    average = jnp.mean(value, axis=-1, keepdims=True)
    centred = value - average
    spread = jnp.mean(centred * centred, axis=-1, keepdims=True)
    return centred * lax.rsqrt(spread + 1e-06)


def modulate(value, shift, scaling):
    return layer_norm(value) * (1.0 + scaling) + shift


def time_features(moments, width):
    half_width = width // 2
    frequency = jnp.exp(-math.log(10000.0) * jnp.arange(half_width, dtype=jnp.float32) / half_width)
    angles = moments.astype(jnp.float32)[:, None] * frequency[None, :]
    return jnp.concatenate([jnp.cos(angles), jnp.sin(angles)], axis=1)


def grid_features(position, row_wide, width):
    quarter = width // 4
    omegas = jnp.exp(-math.log(10000.0) * jnp.arange(quarter, dtype=jnp.float32) / quarter)
    row_angle = (position // row_wide).astype(jnp.float32)[:, None] * omegas[None, :]
    col_angle = (position % row_wide).astype(jnp.float32)[:, None] * omegas[None, :]
    return jnp.concatenate(
        [jnp.sin(row_angle), jnp.cos(row_angle), jnp.sin(col_angle), jnp.cos(col_angle)], axis=1
    )


def fold_rows(left_side, weight_slab):
    return jnp.dot(
        left_side,
        lax.all_gather(weight_slab, "seq", axis=0, tiled=True),
        preferred_element_type=jnp.float32,
    )


def back_cols(gradient, weight_slab):
    return lax.dot_general(
        gradient,
        lax.all_gather(weight_slab, "seq", axis=0, tiled=True),
        (((1,), (1,)), ((), ())),
        preferred_element_type=jnp.float32,
    )


def rows_seq(left_side, right_side):
    return lax.psum_scatter(
        lax.dot_general(
            left_side, right_side, (((0,), (0,)), ((), ())), preferred_element_type=jnp.float32
        ).astype(jnp.bfloat16),
        "seq",
        scatter_dimension=0,
        tiled=True,
    ).astype(jnp.float32)


def attend(queries, key_rows, value_rows, lengths):
    heads_here = queries.shape[1] // HEAD_DIM
    block_rows = min(512, LMAX)
    score_scale = HEAD_DIM ** (-0.5)
    image_count = lengths.shape[0]

    def per_image(packed):
        query_image, key_image, value_image, length = packed
        key_heads = key_image.reshape(LMAX, heads_here, HEAD_DIM)
        value_heads = value_image.reshape(LMAX, heads_here, HEAD_DIM)
        live_keys = jnp.arange(LMAX, dtype=jnp.int32) < length

        def per_block(query_block):
            scores = (
                jnp.einsum(
                    "qhe,khe->hqk", query_block, key_heads, preferred_element_type=jnp.float32
                )
                * score_scale
            )
            scores = jnp.where(live_keys[None, None, :], scores, -1e30)
            maximum = jnp.max(scores, axis=-1, keepdims=True)
            weights = jnp.exp(scores - maximum)
            totals = jnp.sum(weights, axis=-1, keepdims=True)
            probability = (weights / totals).astype(jnp.bfloat16)
            result = jnp.einsum(
                "hqk,khe->qhe", probability, value_heads, preferred_element_type=jnp.float32
            )
            return (result.astype(jnp.bfloat16), (maximum + jnp.log(totals))[:, :, 0])

        blocks = query_image.reshape(LMAX // block_rows, block_rows, heads_here, HEAD_DIM)
        result, log_sums = lax.map(per_block, blocks)
        return (result.reshape(LMAX, heads_here * HEAD_DIM), log_sums)

    stacked = (
        queries.reshape(image_count, LMAX, -1),
        key_rows.reshape(image_count, LMAX, -1),
        value_rows.reshape(image_count, LMAX, -1),
        lengths,
    )
    result, log_sums = lax.map(per_image, stacked)
    return (result.reshape(image_count * LMAX, -1), log_sums)


def attend_back(queries, key_rows, value_rows, grad_rows, log_sums, lengths):
    heads_here = queries.shape[1] // HEAD_DIM
    block_rows = min(512, LMAX)
    score_scale = HEAD_DIM ** (-0.5)
    image_count = lengths.shape[0]

    def per_image(packed):
        query_image, key_image, value_image, grad_image, logsum_image, length = packed
        key_heads = key_image.reshape(LMAX, heads_here, HEAD_DIM)
        value_heads = value_image.reshape(LMAX, heads_here, HEAD_DIM)
        live_keys = jnp.arange(LMAX, dtype=jnp.int32) < length

        def per_block(running, inputs):
            key_grad, value_grad = running
            query_block, grad_block, logsum_block = inputs
            scores = (
                jnp.einsum(
                    "qhe,khe->hqk", query_block, key_heads, preferred_element_type=jnp.float32
                )
                * score_scale
            )
            scores = jnp.where(live_keys[None, None, :], scores, -1e30)
            probability = jnp.exp(scores - logsum_block[:, :, None])
            grad_prob = jnp.einsum(
                "qhe,khe->hqk", grad_block, value_heads, preferred_element_type=jnp.float32
            )
            inner_sum = jnp.sum(probability * grad_prob, axis=-1, keepdims=True)
            grad_score = (probability * (grad_prob - inner_sum)).astype(jnp.bfloat16)
            query_grad = (
                jnp.einsum(
                    "hqk,khe->qhe", grad_score, key_heads, preferred_element_type=jnp.float32
                )
                * score_scale
            )
            key_grad = (
                key_grad
                + jnp.einsum(
                    "hqk,qhe->khe", grad_score, query_block, preferred_element_type=jnp.float32
                )
                * score_scale
            )
            value_grad = value_grad + jnp.einsum(
                "hqk,qhe->khe",
                probability.astype(jnp.bfloat16),
                grad_block,
                preferred_element_type=jnp.float32,
            )
            return ((key_grad, value_grad), query_grad.astype(jnp.bfloat16))

        initial = (
            jnp.zeros((LMAX, heads_here, HEAD_DIM), jnp.float32),
            jnp.zeros((LMAX, heads_here, HEAD_DIM), jnp.float32),
        )
        blocks = (
            query_image.reshape(LMAX // block_rows, block_rows, heads_here, HEAD_DIM),
            grad_image.reshape(LMAX // block_rows, block_rows, heads_here, HEAD_DIM),
            logsum_image,
        )
        (key_grad, value_grad), query_grad = lax.scan(per_block, initial, blocks)
        return (
            query_grad.reshape(LMAX, -1),
            key_grad.reshape(LMAX, -1).astype(jnp.bfloat16),
            value_grad.reshape(LMAX, -1).astype(jnp.bfloat16),
        )

    stacked = (
        queries.reshape(image_count, LMAX, -1),
        key_rows.reshape(image_count, LMAX, -1),
        value_rows.reshape(image_count, LMAX, -1),
        grad_rows.reshape(image_count, LMAX, -1),
        log_sums,
        lengths,
    )
    query_grad, key_grad, value_grad = lax.map(per_image, stacked)
    return (
        query_grad.reshape(image_count * LMAX, -1),
        key_grad.reshape(image_count * LMAX, -1),
        value_grad.reshape(image_count * LMAX, -1),
    )


def adam_update(master, first_moment, second_moment, gradient, learn_rate, clip_factor, correction):
    clipped = gradient * clip_factor
    first_new = 0.5 * first_moment + 0.5 * clipped
    second_new = 0.5 * second_moment + 0.5 * clipped * clipped
    direction = first_new / correction / (jnp.sqrt(second_new / correction) + 1e-08)
    return (master - learn_rate * (direction + 0.1 * master), first_new, second_new)


def on_device(
    tokens,
    cotangent,
    buckets,
    timesteps,
    labels,
    class_table,
    step_count,
    modulate_master,
    modulate_first,
    modulate_second,
    attend_master,
    attend_first,
    attend_second,
    project_master,
    project_first,
    project_second,
    expand_master,
    expand_first,
    expand_second,
    reduce_master,
    reduce_first,
    reduce_second,
    biases_master,
    biases_first,
    biases_second,
):
    head_index = lax.axis_index("head")
    head_count = lax.axis_size("head")
    tok_rows = tokens.shape[0]
    image_count = buckets.shape[0]
    unit_cells = SIDE // 8
    heights = table_pick(buckets, row_units) * unit_cells
    widths = table_pick(buckets, col_units) * unit_cells
    lengths = heights * widths
    row_index = head_index * tok_rows + jnp.arange(tok_rows, dtype=jnp.int32)
    image_of = row_index // LMAX
    position = row_index % LMAX
    choose = image_of[:, None] == jnp.arange(image_count, dtype=jnp.int32)[None, :]
    pick_rows = choose.astype(jnp.float32)
    row_wide = jnp.sum(jnp.where(choose, widths[None, :], 0), axis=1)
    row_length = jnp.sum(jnp.where(choose, lengths[None, :], 0), axis=1)
    live_rows = (position < row_length).astype(jnp.float32)
    grid_cells = grid_features(position, row_wide, D)
    class_pick = (
        labels[:, None] == jnp.arange(class_table.shape[0], dtype=jnp.int32)[None, :]
    ).astype(jnp.bfloat16)
    class_rows = jnp.dot(class_pick, class_table, preferred_element_type=jnp.float32)
    condition = jax.nn.silu(class_rows + time_features(timesteps, D)).astype(jnp.bfloat16)
    bias_low = biases_master.astype(jnp.bfloat16).astype(jnp.float32)
    offset_base = 6 * D
    bias_query = bias_low[offset_base : offset_base + D]
    bias_value = bias_low[offset_base + D : offset_base + 2 * D]
    bias_proj = bias_low[offset_base + 2 * D : offset_base + 3 * D]
    bias_hidden = bias_low[offset_base + 3 * D : offset_base + 3 * D + FF]
    bias_output = bias_low[offset_base + 3 * D + FF :]
    head_slabs = (
        lax.all_gather(attend_master.astype(jnp.bfloat16), "head", axis=1, tiled=True),
        lax.all_gather(project_master.astype(jnp.bfloat16), "head", axis=1, tiled=True),
        lax.all_gather(expand_master.astype(jnp.bfloat16), "head", axis=1, tiled=True),
        lax.all_gather(reduce_master.astype(jnp.bfloat16), "head", axis=1, tiled=True),
    )
    attend_slab, project_slab, expand_slab, reduce_slab = head_slabs
    mod_width = 6 * D // head_count
    mod_share = fold_rows(condition, modulate_master.astype(jnp.bfloat16))
    mod_share = mod_share + lax.dynamic_slice_in_dim(bias_low, head_index * mod_width, mod_width)
    modulation = lax.all_gather(mod_share, "head", axis=1, tiled=True)
    mod_rows = jnp.dot(pick_rows, modulation, precision=highest)
    shift_one, scale_one, gating_one, shift_two, scale_two, gating_two = jnp.split(
        mod_rows, 6, axis=1
    )
    residual_zero = tokens.astype(jnp.float32) + grid_cells
    hidden_attend = modulate(residual_zero, shift_one, scale_one).astype(jnp.bfloat16)
    packed = fold_rows(hidden_attend, attend_slab)
    queries = (packed[:, :D] + bias_query).astype(jnp.bfloat16)
    key_rows = packed[:, D : 2 * D].astype(jnp.bfloat16)
    value_rows = (packed[:, 2 * D :] + bias_value).astype(jnp.bfloat16)
    query_heads, key_heads, value_heads = (
        lax.all_to_all(queries, "head", split_axis=1, concat_axis=0, tiled=True),
        lax.all_to_all(key_rows, "head", split_axis=1, concat_axis=0, tiled=True),
        lax.all_to_all(value_rows, "head", split_axis=1, concat_axis=0, tiled=True),
    )
    head_out, log_sums = attend(query_heads, key_heads, value_heads, lengths)
    attention = lax.all_to_all(head_out, "head", split_axis=0, concat_axis=1, tiled=True)
    branch_attend = fold_rows(attention, project_slab) + bias_proj
    residual_one = residual_zero + gating_one * branch_attend
    hidden_expand = modulate(residual_one, shift_two, scale_two).astype(jnp.bfloat16)
    widened = fold_rows(hidden_expand, expand_slab) + bias_hidden
    activated = jax.nn.gelu(widened, approximate=True).astype(jnp.bfloat16)
    branch_expand = fold_rows(activated, reduce_slab) + bias_output
    output = (residual_one + gating_two * branch_expand).astype(jnp.bfloat16)
    outer_grad = cotangent.astype(jnp.float32) * live_rows[:, None]
    gating_later = outer_grad * branch_expand
    closing_grad = (outer_grad * gating_two).astype(jnp.bfloat16)
    active_grad = back_cols(closing_grad, reduce_slab)
    gelu_value, gelu_pullback = jax.vjp(lambda inner: jax.nn.gelu(inner, approximate=True), widened)
    widened_grad = gelu_pullback(active_grad)[0].astype(jnp.bfloat16)
    hidden_grad = back_cols(widened_grad, expand_slab)
    later_value, later_pullback = jax.vjp(modulate, residual_one, shift_two, scale_two)
    residual_part, shift_later, scale_later = later_pullback(hidden_grad)
    middle_grad = outer_grad + residual_part
    gating_early = middle_grad * branch_attend
    branch_grad = (middle_grad * gating_one).astype(jnp.bfloat16)
    attend_grad = back_cols(branch_grad, project_slab).astype(jnp.bfloat16)
    heads_grad = lax.all_to_all(attend_grad, "head", split_axis=1, concat_axis=0, tiled=True)
    query_grad, keyrow_grad, value_grad = attend_back(
        query_heads, key_heads, value_heads, heads_grad, log_sums, lengths
    )
    query_back, keys_back, values_back = (
        lax.all_to_all(query_grad, "head", split_axis=0, concat_axis=1, tiled=True),
        lax.all_to_all(keyrow_grad, "head", split_axis=0, concat_axis=1, tiled=True),
        lax.all_to_all(value_grad, "head", split_axis=0, concat_axis=1, tiled=True),
    )
    packed_grad = jnp.concatenate([query_back, keys_back, values_back], axis=1)
    normed_grad = back_cols(packed_grad, attend_slab)
    early_value, early_pullback = jax.vjp(modulate, residual_zero, shift_one, scale_one)
    input_part, shift_early, scale_early = early_pullback(normed_grad)
    input_grad = middle_grad + input_part
    mod_token_grad = jnp.concatenate(
        [shift_early, scale_early, gating_early, shift_later, scale_later, gating_later], axis=1
    )
    mod_grad = lax.dot_general(
        pick_rows, mod_token_grad, (((0,), (0,)), ((), ())), precision=highest
    )
    mod_summed = lax.psum_scatter(mod_grad, "head", scatter_dimension=1, tiled=True)
    mod_rounded = mod_summed.astype(jnp.bfloat16)
    grad_mod = rows_seq(condition, mod_rounded)
    mod_slot = lax.dynamic_update_slice_in_dim(
        jnp.zeros((6 * D,), jnp.float32),
        jnp.sum(mod_rounded.astype(jnp.float32), axis=0),
        head_index * mod_width,
        0,
    )
    bias_share = jnp.concatenate(
        [
            mod_slot,
            jnp.sum(query_back.astype(jnp.float32), axis=0),
            jnp.sum(values_back.astype(jnp.float32), axis=0),
            jnp.sum(branch_grad.astype(jnp.float32), axis=0),
            jnp.sum(widened_grad.astype(jnp.float32), axis=0),
            jnp.sum(closing_grad.astype(jnp.float32), axis=0),
        ]
    )
    operand_pairs = (
        (hidden_attend, packed_grad),
        (attention, branch_grad),
        (hidden_expand, widened_grad),
        (activated, closing_grad),
    )
    term_slabs = tuple((rows_seq(left_side, right_side) for left_side, right_side in operand_pairs))
    reduced = (
        lax.psum_scatter(
            term_slabs[0].astype(jnp.bfloat16), "head", scatter_dimension=1, tiled=True
        ).astype(jnp.float32),
        lax.psum_scatter(
            term_slabs[1].astype(jnp.bfloat16), "head", scatter_dimension=1, tiled=True
        ).astype(jnp.float32),
        lax.psum_scatter(
            term_slabs[2].astype(jnp.bfloat16), "head", scatter_dimension=1, tiled=True
        ).astype(jnp.float32),
        lax.psum_scatter(
            term_slabs[3].astype(jnp.bfloat16), "head", scatter_dimension=1, tiled=True
        ).astype(jnp.float32),
    )
    grad_attend, grad_project, grad_expand, grad_reduce = reduced
    local_squares = jnp.sum(grad_mod * grad_mod) + sum(
        (jnp.sum(gradient * gradient) for gradient in reduced)
    )
    bias_total, square_total = lax.psum((bias_share, local_squares), ("seq", "head"))
    grad_norm = jnp.sqrt(square_total + jnp.sum(bias_total * bias_total))
    clip_factor = jnp.minimum(1.0, 1.0 / (grad_norm + 1e-06))
    correction = 1.0 - jnp.power(0.5, step_count.astype(jnp.float32))
    modulate_new = adam_update(
        modulate_master,
        modulate_first,
        modulate_second,
        grad_mod,
        0.5 * D ** (-0.5),
        clip_factor,
        correction,
    )
    attend_new = adam_update(
        attend_master,
        attend_first,
        attend_second,
        grad_attend,
        0.5 * D ** (-0.5),
        clip_factor,
        correction,
    )
    project_new = adam_update(
        project_master,
        project_first,
        project_second,
        grad_project,
        0.5 * D ** (-0.5),
        clip_factor,
        correction,
    )
    expand_new = adam_update(
        expand_master,
        expand_first,
        expand_second,
        grad_expand,
        0.5 * D ** (-0.5),
        clip_factor,
        correction,
    )
    reduce_new = adam_update(
        reduce_master,
        reduce_first,
        reduce_second,
        grad_reduce,
        0.5 * FF ** (-0.5),
        clip_factor,
        correction,
    )
    biases_new = adam_update(
        biases_master, biases_first, biases_second, bias_total, 0.1, clip_factor, correction
    )
    return (
        output,
        input_grad,
        grad_norm,
        modulate_new[0],
        modulate_new[1],
        modulate_new[2],
        attend_new[0],
        attend_new[1],
        attend_new[2],
        project_new[0],
        project_new[1],
        project_new[2],
        expand_new[0],
        expand_new[1],
        expand_new[2],
        reduce_new[0],
        reduce_new[1],
        reduce_new[2],
        biases_new[0],
        biases_new[1],
        biases_new[2],
    )


ALPHA = HEAD_DIM ** (-0.5) * math.log2(math.e)
GELU_A = math.sqrt(2.0 / math.pi)
GELU_B = 0.044715
BLOCK = FF // 16
BF, F32 = jnp.bfloat16, jnp.float32
ANY, VM = pl.ANY, pltpu.VMEM
PIECES = {"q": (144, 864, 48), "p": (72, 576, None), "u": (144, 1152, 48), "d": (288, 576, 96)}
NAMES = ("q", "p", "u", "d")
MESH = pl.DeviceIdType.MESH


def place():
    return tuple(lax.axis_index(a) for a in ("z", "x", "c", "y"))


def at_z(k):
    z = lax.axis_index("z")
    return (z, z + 1 - 2 * (z % 2), (z + 2) % 4, 3 - z)[k]


def rdma(src, dst, send, recv, to):
    return pltpu.make_async_remote_copy(
        src_ref=src, dst_ref=dst, send_sem=send, recv_sem=recv, device_id=to, device_id_type=MESH
    )


def partners():
    z, x, c, y = place()
    xn, yn, twin = (z, 1 - x, c, y), (z, x, c, 1 - y), (z, x, 1 - c, y)
    return xn, yn, twin, [(at_z(k), x, c, y) for k in range(4)]


def flipped(f):
    z, x, c, y = place()
    return (z, 1 - x if f & 1 else x, 1 - c if f & 2 else c, 1 - y if f & 4 else y)


def greet():
    barrier = pltpu.get_barrier_semaphore()
    for to in [flipped(f) for f in range(1, 8)] + partners()[3][1:]:
        pl.semaphore_signal(barrier, inc=1, device_id=to, device_id_type=MESH)
    pl.semaphore_wait(barrier, 10)


CHUNKS = (
    (0, 0, 80, 16),
    (0, 80, 64, 16),
    (1, 0, 72, None),
    (2, 0, 80, 16),
    (2, 80, 64, 16),
    (3, 0, 144, 32),
    (3, 144, 144, 32),
)


def parts_of(chunk, k):
    _, _, rows, cut = CHUNKS[chunk]
    if cut is None:
        return ((0, rows), None) if k == 0 else (None, (0, rows))
    return (0, cut), (cut, rows - cut)


def piece_at(full, w, y, zk, x, first, count):
    rows = PIECES[NAMES[w]][0]
    if count == 72:
        return full.at[y, zk * 2 + x]
    return full.at[y, pl.ds(pl.multiple_of((zk * 2 + x) * rows + first, 16), count)]


def matmul(left, right):
    return jnp.dot(left, right, preferred_element_type=F32)


def matmul_nt(left, right):
    return lax.dot_general(left, right, (((1,), (1,)), ((), ())), preferred_element_type=F32)


def matmul_tn(left, right):
    return lax.dot_general(left, right, (((0,), (0,)), ((), ())), preferred_element_type=F32)


class Gather:
    def __init__(self, own, full, sems):
        self.own, self.full = own, full
        self.zs, self.zr, self.xs, self.xr, self.ys, self.yr, self.fs, self.fr, self.ps, self.pr = sems
        self.sent = []

    def piece(self, w, flip_y, k, flip_x):
        z, x, c, y = place()
        weight, first, count, _ = CHUNKS[w]
        return piece_at(
            self.full[weight], weight, 1 - y if flip_y else y, at_z(k), 1 - x if flip_x else x, first, count
        )

    def source(self, w):
        weight, first, count, _ = CHUNKS[w]
        return self.own[weight].at[pl.ds(first, count)]

    def send(self, make):
        make().start()
        self.sent.append(make)

    def arrived(self, ref, s, r):
        rdma(ref, ref, s, r, partners()[0]).wait_recv()

    def start(self, w):
        def to_x():
            return rdma(self.source(w), self.piece(w, 0, 0, 0), self.xs.at[w, 0], self.xr.at[w, 0], partners()[0])

        def to_y():
            return rdma(self.source(w), self.piece(w, 0, 0, 0), self.ys.at[w, 0], self.yr.at[w, 0], partners()[1])

        def to_z(k):
            to = partners()[3][k]
            return rdma(self.source(w), self.piece(w, 0, 0, 0), self.zs.at[w, k], self.zr.at[w, k], to)

        self.send(to_x)
        self.send(to_y)
        for k in (1, 2, 3):
            self.send(functools.partial(to_z, k))

    def column(self, w, k):
        self.arrived(self.piece(w, 0, k, 0), self.zs.at[w, k], self.zr.at[w, k])

        def to_x():
            piece = self.piece(w, 0, k, 0)
            return rdma(piece, piece, self.xs.at[w, k], self.xr.at[w, k], partners()[0])

        def to_y():
            piece = self.piece(w, 0, k, 0)
            return rdma(piece, piece, self.ys.at[w, k], self.yr.at[w, k], partners()[1])

        self.send(to_x)
        self.send(to_y)

    def plane(self, w, k):
        spans = parts_of(w, k)

        def pass_on(i):
            part = self.piece(w, i, k, 1 - i).at[pl.ds(*spans[i])]
            return rdma(part, part, self.fs.at[w, k, i], self.fr.at[w, k, i], partners()[1 - i])

        self.arrived(self.piece(w, 0, k, 1), self.xs.at[w, k], self.xr.at[w, k])
        if k in (0, 2) and spans[0] is not None:
            self.send(functools.partial(pass_on, 0))
        self.arrived(self.piece(w, 1, k, 0), self.ys.at[w, k], self.yr.at[w, k])
        if k in (0, 2) and spans[1] is not None:
            self.send(functools.partial(pass_on, 1))

    def corner(self, w, k):
        for i, span in enumerate(parts_of(w, k)):
            if span is not None:
                part = self.piece(w, 1, k, 1).at[pl.ds(*span)]
                self.arrived(part, self.fs.at[w, k, i], self.fr.at[w, k, i])

        def to_pair():
            piece = self.piece(w, 1, k, 1)
            return rdma(piece, piece, self.ps.at[w, k], self.pr.at[w, k], partners()[3][1])

        self.send(to_pair)

    def last(self, w, k):
        self.arrived(self.piece(w, 1, k ^ 1, 1), self.ps.at[w, k], self.pr.at[w, k])

    def finish(self):
        for make in self.sent:
            make().wait_send()

    def steps(self):
        def each(method, chunks, ks):
            return [(method, i, k) for i in chunks for k in ks]

        column, plane, corner, last = self.column, self.plane, self.corner, self.last
        one = (0, 1)
        plan = [(self.start, 0), (self.start, 1), (self.start, 2)]
        plan += each(column, one, (1,)) + each(plane, one, (0,))
        plan += each(column, one, (2,)) + each(column, one, (3,)) + [(self.start, 3)]
        plan += each(corner, one, (0,)) + each(plane, one, (2,))
        plan += each(column, (2,), (1,)) + [(self.start, 4)]
        plan += each(plane, one, (1,)) + each(corner, one, (2,))
        plan += each(plane, (2,), (0,)) + each(column, (2,), (2, 3)) + each(column, (3,), (1,))
        plan += each(plane, one, (3,)) + each(last, one, (0, 2))
        count = len(CHUNKS)
        for t in range(-2, count + 4):
            wave = [(self.start, t + 2)] if t + 2 < count else []
            if 0 <= t - 4 < count:
                wave += each(last, (t - 4,), (0, 2))
            for lag, make in enumerate(
                (
                    lambda i: each(column, (i,), (1,)),
                    lambda i: each(plane, (i,), (0,)) + each(column, (i,), (2, 3)),
                    lambda i: each(corner, (i,), (0,)) + each(plane, (i,), (2, 1)),
                    lambda i: each(corner, (i,), (2,)) + each(plane, (i,), (3,)),
                )
            ):
                if t >= 0 and 0 <= t - lag < count:
                    wave += make(t - lag)
            plan += [step for step in wave if step not in plan]
        return plan


def mod_steps(cond_ref, weight, bias, out_ref, lhs, bufs, s, r):
    conds, part, got_z, mid, box = bufs

    def hop(i):
        z, x, c, y = place()
        zn = partners()[3]
        if i == 0:
            pairs = [(conds.at[z, x, c], conds.at[z, x, c], flipped(f)) for f in (1, 2, 3)]
        elif i == 1:
            pairs = [(conds.at[z], conds.at[z], zn[k]) for k in (1, 2, 3)]
        elif i == 2:
            pairs = [(part.at[at_z(k)], got_z.at[k - 1], zn[k]) for k in (1, 2, 3)]
        else:
            pairs = []
            for f in range(1, 8):
                to = flipped(f)
                pairs.append((mid.at[to[1], to[3]], box.at[x, c, y], to))
        return [
            rdma(src, dst, s.at[i, n], r.at[i, n], to) for n, (src, dst, to) in enumerate(pairs)
        ]

    def step(i):
        z, x, c, y = place()
        if i > 0:
            for d in hop(i - 1):
                d.wait()
        if i == 0:
            conds[z, x, c] = cond_ref[...]
        elif i == 2:
            me = (z * 2 + x) * 2 + c
            for n in range(16):
                lhs[pl.ds(n, 1), :] = conds[n // 4, n // 2 % 2, n % 2, pl.ds(me, 1), :]
            for j in range(3):
                cols = slice(j * D, (j + 1) * D)
                result = matmul(lhs[:, :72].astype(BF), weight[:, cols].astype(BF))
                for n in range(16):
                    part[n // 4, n // 2 % 2, n % 2, :, cols] = result[n : n + 1]
        elif i == 3:
            mid[...] = part[z] + got_z[0] + got_z[1] + got_z[2]
            box[x, c, y] = mid[x, y]
        elif i == 4:
            for n in range(2):
                total = (box[0, 0, n] + box[0, 1, n]) + (box[1, 0, n] + box[1, 1, n])
                out_ref[n] = total + bias[:, n * 3456 : (n + 1) * 3456]
        if i < 4:
            for d in hop(i):
                d.start()

    return [functools.partial(step, i) for i in range(5)]


def normed_tile(value):
    average = jnp.mean(value, axis=-1, keepdims=True)
    centred = value - average
    spread = jnp.mean(centred * centred, axis=-1, keepdims=True)
    return centred * lax.rsqrt(spread + 1e-06)


SPACE = (8, 12)


def rounded(value):
    return value.astype(BF).astype(F32)


def pick(bucket, entries):
    return sum(
        jnp.where(bucket == float(i), float(e * (SIDE // 8)), 0.0) for i, e in enumerate(entries)
    )


def start_rows(tok, table, bucket, first, rows):
    wide = pick(bucket, col_units)
    spot = (first + lax.broadcasted_iota(jnp.int32, (rows, 1), 0)).astype(F32)
    lane = lax.broadcasted_iota(jnp.int32, (1, 64), 1).astype(F32)
    grid_row = jnp.where((spot >= lane * wide) & (spot < (lane + 1.0) * wide), 1.0, 0.0)
    left = spot - wide * jnp.sum(grid_row * lane, axis=1, keepdims=True)
    grid_col = jnp.where(left == lane, 1.0, 0.0)
    high = table.astype(BF)
    low = (table - high.astype(F32)).astype(BF)
    parts = [matmul(hot.astype(BF), high) + matmul(hot.astype(BF), low) for hot in (grid_row, grid_col)]
    return tok.astype(F32) + jnp.concatenate(parts, axis=1)


def forward_kernel(*refs):
    (tok, cot, bucket_in, table, att_m, proj_m, exp_m, red_m, mod_w, cond_in, bias_in) = refs[:11]
    gq, gp, gu, gd = full = refs[11:15]
    (mod_out, lhs, x0_out, dy_out, cl_out, h1_out, q_out, k_out, v_out) = refs[15:24]
    (attnt_out, lse_out, ba_out, x1_out, h2_out, der_out, bb_out, y_out, gred_out) = refs[24:33]
    (oq, op, ou, od, fq, tq, fu, tu) = refs[33:41]
    mod_bufs = refs[41:46]
    (xs, x0, dy, bucket, closing, h1, qa, ka, vt, attnt, attn) = refs[46:57]
    (ps, pr, ds, dr, acc, x1, h2, act, der, ba, bb, yo, gstage) = refs[57:70]
    (b_all, b_q, b_v, b_u) = refs[70:74]
    lsem = refs[74]
    gather_sems = refs[75:85]
    ms, mr, ws, wr, ts, tr, os, outs_sem, gsem = refs[85:94]
    z, x, c, y = place()
    xn, yn, twin, zn = partners()
    half = x0.shape[0]
    mine = pl.multiple_of(c * half, half)
    other = pl.multiple_of((1 - c) * half, half)
    gather = Gather((oq, op, ou, od), full, gather_sems)
    mods = mod_steps(cond_in, mod_w, b_all, mod_out, lhs, mod_bufs, ms, mr)
    greet()
    mods[0]()

    def split(master, width, f, t, i):
        count = master.shape[1] // (2 * width)
        sides = [
            jnp.concatenate(
                [master[:, (2 * j + p) * width : (2 * j + p + 1) * width] for j in range(count)], axis=1
            )
            for p in (0, 1)
        ]
        t[...] = jnp.where(c == 0, sides[1], sides[0])
        rdma(t, f.at[c], os.at[0, i], os.at[1, i], twin).start()
        f[c] = jnp.where(c == 0, sides[0], sides[1])

    def joined(f, t, i, piece):
        rdma(t, f.at[c], os.at[0, i], os.at[1, i], twin).wait()
        piece[...] = jnp.concatenate([f[0], f[1]], axis=0).astype(BF)

    steps = [step for step in gather.steps() if step[0] != gather.start or step[1] > 2]
    done = [0]

    def tick(n):
        for f, *a in steps[done[0] : done[0] + n]:
            f(*a)
        done[0] = min(done[0] + n, len(steps))

    def tick_until(chunk):
        last = max(i for i, s in enumerate(steps) if s[0] == gather.last and s[1] == chunk)
        tick(max(0, last + 1 - done[0]))

    swap_to = (z, x, y, c)
    PART = 128
    moves = [(bucket_in, bucket)]
    for i in range(half // PART):
        moves.append((xs.at[pl.ds(i * PART, PART)], x0.at[pl.ds(i * PART, PART)]))
    for i in range(half // PART):
        moves.append((cot.at[pl.ds(i * PART, PART)], dy.at[pl.ds(i * PART, PART)]))

    def move(i):
        @pl.when(c != y)
        def _():
            rdma(*moves[i], ws.at[i], wr.at[i], swap_to).start()

        @pl.when(c == y)
        def _():
            pltpu.make_async_copy(*moves[i], ws.at[i]).start()

    def moved(i):
        @pl.when(c != y)
        def _():
            rdma(*moves[i], ws.at[i], wr.at[i], swap_to).wait()

        @pl.when(c == y)
        def _():
            pltpu.make_async_copy(*moves[i], ws.at[i]).wait()

    def first_rows(i):
        rows = slice(i * PART, (i + 1) * PART)
        xs[rows, :] = start_rows(
            tok[rows, :], table[...], bucket_in[0:1, 0:1], y * half + i * PART, PART
        ).astype(BF)
        move(1 + i)

    move(0)
    split(att_m, HEAD_DIM, fq, tq, 0)
    mods[1]()
    op[...] = proj_m[...].astype(BF)
    gather.start(2)
    first_rows(0)
    joined(fq, tq, 0, oq)
    gather.start(0)
    gather.start(1)
    mods[2]()
    first_rows(1)
    split(exp_m, BLOCK, fu, tu, 1)
    first_rows(2)
    tick(2)
    first_rows(3)
    tick(2)
    joined(fu, tu, 1, ou)
    tick(3)
    mods[3]()
    od[...] = red_m[...].astype(BF)
    owns = [
        pltpu.make_async_copy(
            gather.own[w], piece_at(full[w], w, y, z, x, 0, PIECES[NAMES[w]][0]), lsem.at[w]
        )
        for w in range(4)
    ]
    for d in owns:
        d.start()
    b_all[...] = rounded(bias_in[...]).reshape(1, 14 * D)
    tick(SPACE[0])
    mods[4]()
    tick(SPACE[1])

    def of_core(base, width, count):
        return jnp.concatenate(
            [
                jnp.where(
                    c == 0,
                    b_all[:, base + 2 * j * width : base + (2 * j + 1) * width],
                    b_all[:, base + (2 * j + 1) * width : base + (2 * j + 2) * width],
                )
                for j in range(count)
            ],
            axis=1,
        )

    b_p = b_all.at[:, pl.ds(8 * D, D)]
    b_d = b_all.at[:, pl.ds(9 * D + FF, D)]
    for i in range(1 + half // PART):
        moved(i)

    def vec(i):
        return mod_out[i // 3, :, (i % 3) * D : (i % 3 + 1) * D]

    TILE, WIDE = 128, 256
    tiles = half // TILE

    def own_tile(ref, t):
        return ref.at[pl.ds(pl.multiple_of(mine + t * TILE, TILE), TILE)]

    def give(ref, t, i):
        part = own_tile(ref, t)
        return rdma(part, part, ts.at[i, t], tr.at[i, t], twin)

    def norm_one(t, _):
        rows = pl.ds(pl.multiple_of(t * TILE, TILE), TILE)
        value = normed_tile(x0[rows, :].astype(F32)) * (1.0 + vec(1)) + vec(0)
        own_tile(h1, t)[...] = value.astype(BF)
        give(h1, t, 0).start()
        return 0

    for t in range(tiles):
        norm_one(t, 0)
        tick(1)
    tick_until(1)
    for i in range(half // PART):
        move(1 + half // PART + i)

    def both_got(ref, i):
        for t in range(tiles):
            give(ref, t, i).wait_send()
            part = ref.at[pl.ds(pl.multiple_of(other + t * TILE, TILE), TILE)]
            rdma(part, part, ts.at[i, t], tr.at[i, t], twin).wait_recv()

    out_copies = []

    def put(src, dst):
        d = pltpu.make_async_copy(src, dst, outs_sem.at[len(out_copies)])
        d.start()
        out_copies.append(d)

    def load(src, dst, i):
        d = pltpu.make_async_copy(src, dst, lsem.at[i])
        d.start()
        d.wait()

    owns[0].wait()
    live = pick(bucket[0:1, 0:1], row_units) * pick(bucket[0:1, 0:1], col_units)
    lane = lax.broadcasted_iota(jnp.int32, (1, 128), 1)

    b_q[...] = of_core(6 * D, HEAD_DIM, 8)
    b_v[...] = of_core(7 * D, HEAD_DIM, 8)
    b_u[...] = of_core(9 * D, BLOCK, 8)

    def qkv(weight):
        load(gq, weight, 4)

        def rows_of(start):
            rows = pl.ds(start, half)
            left = h1[rows, :]
            spot = (start + lax.broadcasted_iota(jnp.int32, (half, 1), 0)).astype(F32)
            mask = jnp.where(lane == HEAD_DIM, jnp.where(spot < live, 0.0, -1e30), 0.0)
            ones = jnp.where(lane == HEAD_DIM, 1.0, 0.0)
            fill = jnp.zeros((half, 56), F32)

            def put_key(j, key):
                ka[j, rows, :] = (jnp.concatenate([key, fill], axis=1) + mask).astype(BF)

            one = matmul(left, weight[0])
            for j in range(8):
                cols = slice(j * HEAD_DIM, (j + 1) * HEAD_DIM)
                query = (one[:, cols] + b_q[:, cols]) * ALPHA
                qa[j, rows, :] = (jnp.concatenate([query, fill], axis=1) + ones).astype(BF)
            for j in range(4):
                put_key(j, one[:, 576 + j * 72 : 648 + j * 72])
            tick(2)
            two = matmul(left, weight[1])
            for j in range(4):
                put_key(4 + j, two[:, j * 72 : j * 72 + 72])
            for j in range(8):
                cols = slice(j * HEAD_DIM, (j + 1) * HEAD_DIM)
                value = two[:, 288 + j * 72 : 360 + j * 72] + b_v[:, cols]
                vt[j, :, rows] = value.T.astype(BF)
            tick(2)

        rows_of(mine)
        both_got(h1, 0)
        rows_of(other)

    pl.run_scoped(qkv, VM((2, D, 864), BF))
    put(h1, h1_out)
    tick(1)
    put(qa, q_out)
    put(ka, k_out)
    put(vt, v_out)

    def head(j, _):
        def queries(i, _):
            rows = pl.ds(pl.multiple_of(i * 512, 512), 512)
            scores = matmul_nt(ka[j], qa[j, rows, :])
            top = jnp.max(scores, axis=0, keepdims=True)
            prob = jnp.exp2(scores - top)
            total = jnp.sum(prob, axis=0, keepdims=True)
            result = matmul(vt[j], prob.astype(BF)) * (1.0 / total)
            attnt[j, :, rows] = result
            lse_out[j, :, rows] = top + jnp.log2(total)
            return 0

        lax.fori_loop(0, 2, queries, 0)
        return 0

    for j in range(8):
        head(j, 0)
        tick(3)

    for i in range(half // PART):
        moved(1 + half // PART + i)

    def close(t, _):
        rows = pl.ds(pl.multiple_of(t * TILE, TILE), TILE)
        spot = (mine + t * TILE + lax.broadcasted_iota(jnp.int32, (TILE, 1), 0)).astype(F32)
        outer = jnp.where(spot < live, dy[rows, :].astype(F32), 0.0)
        dy[rows, :] = outer.astype(BF)
        own_tile(closing, t)[...] = (outer * vec(5)).astype(BF)
        give(closing, t, 1).start()
        return 0

    lax.fori_loop(0, tiles, close, 0)
    put(attnt, attnt_out)
    tick_until(2)
    owns[1].wait()

    def proj(weight, stage, raw):
        load(gp, raw, 5)
        for i in (0, 1):
            for h in range(8):
                stage[h * 72 : h * 72 + 72, :] = raw[i, h].astype(F32)
            weight[i] = stage[...].astype(BF)

        def attn_rows(i, _):
            rows = pl.ds(pl.multiple_of(i * 256, 256), 256)
            value = jnp.concatenate([attnt[j, :, rows] for j in range(8)], axis=0)
            attn[rows, :] = value.T.astype(BF)
            return 0

        lax.fori_loop(0, 4, attn_rows, 0)

        def for_twin(t, _):
            rows = pl.ds(pl.multiple_of(t * WIDE, WIDE), WIDE)
            left = attn[pl.ds(pl.multiple_of(other + t * WIDE, WIDE), WIDE), :]
            for i in (0, 1):
                ps[rows, i * 576 : (i + 1) * 576] = matmul(left, weight[i]).astype(BF)
            rdma(ps.at[rows], pr.at[rows], ts.at[2, t], tr.at[2, t], twin).start()
            return 0

        for t in range(half // WIDE):
            for_twin(t, 0)
            tick(1)

        def for_me(t, _):
            rows = pl.ds(pl.multiple_of(t * WIDE, WIDE), WIDE)
            left = attn[pl.ds(pl.multiple_of(mine + t * WIDE, WIDE), WIDE), :]
            for i in (0, 1):
                acc[rows, i * 576 : (i + 1) * 576] = matmul(left, weight[i])
            return 0

        for t in range(half // WIDE):
            for_me(t, 0)
            tick(1)

    pl.run_scoped(proj, VM((2, 576, 576), BF), VM((576, 576), F32), VM((2, 8, 72, 576), BF))

    def middle(t, _):
        rows = pl.ds(pl.multiple_of(t * TILE, TILE), TILE)
        branch = acc[rows, :] + pr[rows, :].astype(F32) + b_p[...]
        ba[rows, :] = branch.astype(BF)
        value = x0[rows, :].astype(F32) + vec(2) * branch
        x1[rows, :] = value
        own_tile(h2, t)[...] = (normed_tile(value) * (1.0 + vec(4)) + vec(3)).astype(BF)
        give(h2, t, 3).start()
        return 0

    def half_got(src, dst, i, t):
        rows = pl.ds(t * WIDE, WIDE)
        rdma(src.at[rows], dst.at[rows], ts.at[i, t], tr.at[i, t], twin).wait()

    for t in range(tiles):
        if t % 2 == 0:
            half_got(ps, pr, 2, t // 2)
        middle(t, 0)
    put(ba, ba_out)
    put(x1, x1_out)
    put(x0, x0_out)
    put(dy, dy_out)
    tick_until(4)
    owns[2].wait()
    both_got(h2, 3)
    both_got(closing, 1)
    put(h2, h2_out)
    put(closing, cl_out)

    def up(weight):
        load(gu, weight, 6)

        def block_of(start, i, n):
            rows = pl.ds(start, half)
            part = slice(n * 384, (n + 1) * 384)
            cols = slice(i * D + n * 384, i * D + (n + 1) * 384)
            u = matmul(h2[rows, :], weight[i, :, part]) + b_u[:, cols]
            square = u * u
            inner = u * (GELU_A + GELU_A * GELU_B * square)
            bent = jnp.tanh(inner)
            half_up = 0.5 + 0.5 * bent
            act[rows, cols] = (u * half_up).astype(BF)
            slope = u * (GELU_A + 3.0 * GELU_A * GELU_B * square)
            der[rows, cols] = (half_up + slope * (half_up * (1.0 - bent))).astype(BF)

        for start in (mine, other):
            for i in (0, 1):
                for n in range(3):
                    block_of(start, i, n)
                    tick(n % 2)

    pl.run_scoped(up, VM((2, D, D), BF))
    put(der, der_out)

    gouts = []
    for t in range(6):
        slot = t % 2
        if t >= 2:
            gouts[t - 2].wait()
        value = matmul(act[:, t * 384 : (t + 1) * 384].T, closing[...])
        for i in (0, 1):
            gstage[slot, i] = value[:, i * 576 : (i + 1) * 576].astype(BF)
        d = pltpu.make_async_copy(
            gstage.at[slot], gred_out.at[:, pl.ds(t * 384, 384)], gsem.at[slot]
        )
        d.start()
        gouts.append(d)
        tick(1)
    for d in gouts[-2:]:
        d.wait()
    tick(len(steps))
    owns[3].wait()

    def down(weight):
        load(gd, weight, 7)

        for i in (0, 1):
            cols = slice(i * 576, (i + 1) * 576)
            ds[:, cols] = matmul(act[pl.ds(other, half), :], weight[i]).astype(BF)
        rdma(ds, dr, ts.at[4, 0], tr.at[4, 0], twin).start()
        for i in (0, 1):
            cols = slice(i * 576, (i + 1) * 576)
            acc[:, cols] = matmul(act[pl.ds(mine, half), :], weight[i])
        rdma(ds, dr, ts.at[4, 0], tr.at[4, 0], twin).wait()

    pl.run_scoped(down, VM((2, 2304, 576), BF))

    def finish(t, _):
        rows = pl.ds(pl.multiple_of(t * TILE, TILE), TILE)
        branch = acc[rows, :] + dr[rows, :].astype(F32) + b_d[...]
        bb[rows, :] = branch.astype(BF)
        yo[rows, :] = (x1[rows, :] + vec(5) * branch).astype(BF)
        return 0

    for t in range(tiles):
        finish(t, 0)
    put(bb, bb_out)
    put(yo, y_out)
    for d in out_copies:
        d.wait()
    gather.finish()


def forward_block(tokens, cotangent, bucket, table, masters, modulate_master, cond, biases):
    shapes = {
        "gq": (2, D, 864),
        "gp": (2, 8, 72, 576),
        "gu": (2, D, D),
        "gd": (2, 2304, 576),
    }
    half = tokens.shape[0]
    rows = 2 * half
    out_shape, out_specs = [], []

    def out(shape, dtype, space=ANY):
        out_shape.append(jax.ShapeDtypeStruct(shape, dtype))
        out_specs.append(pl.BlockSpec(memory_space=space))

    for s in shapes.values():
        out(s, BF)
    out((2, 1, 3456), F32, VM)
    out((16, 128), F32, VM)
    out((half, D), BF)
    out((half, D), BF)
    out((rows, D), BF)
    out((rows, D), BF)
    out((8, rows, 128), BF)
    out((8, rows, 128), BF)
    out((8, 72, rows), BF)
    out((8, 72, rows), F32)
    out((8, 1, rows), F32, VM)
    out((half, D), BF)
    out((half, D), F32)
    out((rows, D), BF)
    out((rows, 2304), BF)
    out((half, D), BF)
    out((half, D), BF)
    out((2, 2304, 576), BF)
    dma = pltpu.SemaphoreType.DMA
    scratch = [
        VM((144, 864), BF),
        VM((72, 576), BF),
        VM((144, D), BF),
        VM((288, 576), BF),
        VM((2, 72, 864), F32),
        VM((72, 864), F32),
        VM((2, 72, D), F32),
        VM((72, D), F32),
        VM((4, 2, 2, 16, 128), F32),
        VM((4, 2, 2, 1, 3456), F32),
        VM((3, 2, 2, 1, 3456), F32),
        VM((2, 2, 1, 3456), F32),
        VM((2, 2, 2, 1, 3456), F32),
        VM((half, D), BF),
        VM((half, D), BF),
        VM((half, D), BF),
        VM((8, 128), F32),
        VM((rows, D), BF),
        VM((rows, D), BF),
        VM((8, rows, 128), BF),
        VM((8, rows, 128), BF),
        VM((8, 72, rows), BF),
        VM((8, 72, rows), F32),
        VM((rows, 576), BF),
        VM((half, D), BF),
        VM((half, D), BF),
        VM((half, D), BF),
        VM((half, D), BF),
        VM((half, D), F32),
        VM((half, D), F32),
        VM((rows, D), BF),
        VM((rows, 2304), BF),
        VM((rows, 2304), BF),
        VM((half, D), BF),
        VM((half, D), BF),
        VM((half, D), BF),
        VM((2, 2, 384, 576), BF),
        VM((1, 14 * D), F32),
        VM((1, 576), F32),
        VM((1, 576), F32),
        VM((1, 2304), F32),
        dma((8,)),
    ]
    n = len(CHUNKS)
    scratch += [dma((n, 4))] * 6 + [dma((n, 4, 2))] * 2 + [dma((n, 4))] * 2
    scratch += [
        dma((4, 7)),
        dma((4, 7)),
        dma((9,)),
        dma((9,)),
        dma((5, 4)),
        dma((5, 4)),
        dma((2, 2)),
        dma((20,)),
        dma((2,)),
    ]
    vm = pl.BlockSpec(memory_space=VM)
    hbm = pl.BlockSpec(memory_space=ANY)
    return pl.pallas_call(
        forward_kernel,
        out_shape=out_shape,
        in_specs=[vm, hbm] + [vm] * 9,
        out_specs=out_specs,
        scratch_shapes=scratch,
        compiler_params=pltpu.CompilerParams(
            collective_id=0, has_side_effects=True, vmem_limit_bytes=60 * 2**20
        ),
        name="forward_block",
    )(tokens, cotangent, bucket, table, *masters, modulate_master, cond, biases)


class Scatter:
    def __init__(self, grads, boxes, outs, sems):
        self.grads, self.outs = grads, outs
        self.pair_box, self.diag_box, self.x_box, self.y_box, self.z_box = boxes
        self.ps, self.pr, self.fs, self.fr, self.xs, self.xr, self.ys, self.yr, self.zs, self.zr = sems
        self.sent = []

    def piece(self, i, flip_y, k, flip_x):
        z, x, c, y = place()
        weight, first, count, _ = CHUNKS[i]
        return piece_at(
            self.grads[weight], weight, 1 - y if flip_y else y, at_z(k), 1 - x if flip_x else x, first, count
        )

    def box(self, boxes, i, n):
        weight, first, count, _ = CHUNKS[i]
        return boxes[weight].at[n, pl.ds(first, count)]

    def send(self, make):
        make().start()
        self.sent.append(make)

    def arrived(self, ref, s, r):
        rdma(ref, ref, s, r, partners()[0]).wait_recv()

    def add(self, target, *others):
        total = target[...]
        for o in others:
            total = total + o[...]
        target[...] = total

    def across(self, i, k, by_y):
        if by_y:
            return rdma(
                self.piece(i, 1, k, 0), self.box(self.y_box, i, k), self.ys.at[i, k], self.yr.at[i, k], partners()[1]
            )
        return rdma(
            self.piece(i, 0, k, 1), self.box(self.x_box, i, k), self.xs.at[i, k], self.xr.at[i, k], partners()[0]
        )

    def start(self, i):
        def to_pair(k):
            return rdma(
                self.piece(i, 1, k ^ 1, 1),
                self.box(self.pair_box, i, k // 2),
                self.ps.at[i, k],
                self.pr.at[i, k],
                partners()[3][1],
            )

        for k in (0, 2):
            self.send(functools.partial(to_pair, k))
        for k in (1, 3):
            for by_y in (0, 1):
                self.send(functools.partial(self.across, i, k, by_y))

    def corner(self, i, k):
        box = self.box(self.pair_box, i, k // 2)
        self.arrived(box, self.ps.at[i, k], self.pr.at[i, k])
        self.add(self.piece(i, 1, k, 1), box)
        spans = parts_of(i, k)

        def part(n):
            return rdma(
                self.piece(i, 1, k, 1).at[pl.ds(*spans[n])],
                self.box(self.diag_box, i, k // 2).at[pl.ds(*spans[n])],
                self.fs.at[i, k, n],
                self.fr.at[i, k, n],
                partners()[1 - n],
            )

        for n in (0, 1):
            if spans[n] is not None:
                self.send(functools.partial(part, n))

    def plane(self, i, k):
        spans = parts_of(i, k)
        for n in (0, 1):
            if spans[n] is not None:
                part = self.box(self.diag_box, i, k // 2).at[pl.ds(*spans[n])]
                self.arrived(part, self.fs.at[i, k, n], self.fr.at[i, k, n])
                self.add(self.piece(i, n, k, 1 - n).at[pl.ds(*spans[n])], part)
            self.send(functools.partial(self.across, i, k, n))

    def both(self, i, k):
        boxes = []
        for boxes_of, s, r in ((self.x_box, self.xs, self.xr), (self.y_box, self.ys, self.yr)):
            box = self.box(boxes_of, i, k)
            self.arrived(box, s.at[i, k], r.at[i, k])
            boxes.append(box)
        return boxes

    def column(self, i, k):
        self.add(self.piece(i, 0, k, 0), *self.both(i, k))

        def along():
            return rdma(
                self.piece(i, 0, k, 0),
                self.box(self.z_box, i, k - 1),
                self.zs.at[i, k],
                self.zr.at[i, k],
                partners()[3][k],
            )

        self.send(along)

    def last(self, i):
        weight, first, count, _ = CHUNKS[i]
        boxes = self.both(i, 0)
        for k in (1, 2, 3):
            box = self.box(self.z_box, i, k - 1)
            self.arrived(box, self.zs.at[i, k], self.zr.at[i, k])
            boxes.append(box)
        total = self.piece(i, 0, 0, 0)[...].astype(F32)
        for box in boxes:
            total = total + box[...].astype(F32)
        self.outs[weight][first : first + count, :] = total

    def finish(self):
        for make in self.sent:
            make().wait_send()

    def steps(self, i):
        return (
            [(self.start, i), (self.corner, i, 0), (self.corner, i, 2)],
            [(self.plane, i, 0), (self.plane, i, 2), (self.column, i, 1)],
            [(self.column, i, 3), (self.column, i, 2)],
            [(self.last, i)],
        )


def total_steps(dm, bs, lhs, mods, bufs, gmod, bias_out, s, r):
    got_m, got_b, sb, got_z, near = bufs

    def hop(i):
        z, x, c, y = place()
        zn = partners()[3]
        pairs = []
        if i == 0:
            for f in range(1, 8):
                to = flipped(f)
                pairs.append((dm.at[to[3]], got_m.at[x, c, y], to))
                pairs.append((bs, got_b.at[f - 1], to))
        elif i == 1:
            for k in (1, 2, 3):
                pairs.append((mods.at[z], mods.at[z], zn[k]))
                pairs.append((sb, got_z.at[k - 1], zn[k]))
        else:
            pairs.append((near.at[0], near.at[1], flipped(4)))
        return [
            rdma(src, dst, s.at[i, n], r.at[i, n], to) for n, (src, dst, to) in enumerate(pairs)
        ]

    def step(i):
        z, x, c, y = place()
        if i > 0:
            for d in hop(i - 1):
                d.wait()
        if i == 0:
            got_m[x, c, y] = dm[y]
        elif i == 1:
            for n in range(4):
                mods[z, n // 2, n % 2] = rounded(got_m[n // 2, 0, n % 2] + got_m[n // 2, 1, n % 2])
            sb[...] = ((bs[...] + got_b[0]) + (got_b[1] + got_b[2])) + (
                (got_b[3] + got_b[4]) + (got_b[5] + got_b[6])
            )
        elif i == 2:
            rows = [mods[n // 4, n // 2 % 2, n % 2] for n in range(16)]
            total = rows[0]
            for row in rows[1:]:
                total = total + row
            near[0] = total
        elif i == 3:
            for n in (0, 1):
                bias_out[:, n * 3456 : (n + 1) * 3456] = jnp.where(y == n, near[0], near[1])
        if i < 3:
            for d in hop(i):
                d.start()
        if i == 2:
            bias_out[:, 6 * D :] = (sb[...] + got_z[0]) + (got_z[1] + got_z[2])
            left = lhs[:, :72].astype(BF)
            right = jnp.concatenate(rows, axis=0).astype(BF)
            for j in range(3):
                cols = slice(j * D, (j + 1) * D)
                gmod[:, cols] = matmul_tn(left, right[:, cols])

    return [functools.partial(step, i) for i in range(4)]


BEATS = {
    "down": "010101",
    "expand": "010101",
    "up": "010101",
    "middle": "1010",
    "project": "1010",
    "heads": "0001",
    "attend": "010101",
    "back": "000111",
    "input": "1111",
    "hops": "111111",
}


def backward_kernel(*refs):
    gq, gp, gu, gd, mod, lhs = refs[:6]
    (x0_in, dy_in, cl_in, h1_in, q_in, k_in, v_in, at_in, lse) = refs[6:15]
    (ba_in, x1_in, h2_in, der_in, bb_in, y_in, gred) = refs[15:22]
    (out, ig_out, s_att, s_proj, s_exp, s_red, gmod, bias_flat, norm_out) = refs[22:31]
    grads = refs[31:35]
    boxes = [refs[35 + 4 * i : 39 + 4 * i] for i in range(5)]
    fq, fu, gotq, gotu = refs[55:59]
    dba, dx1, ps, pr, dm, bs, mods = refs[59:66]
    total_bufs = refs[66:71]
    sq, here, bias_out = refs[71:74]
    lsem = refs[74]
    scatter_sems = refs[75:85]
    ts, tr, ws, wr, hs, hr, ns, nr = refs[85:93]
    z, x, c, y = place()
    xn, yn, twin, zn = partners()
    half = dx1.shape[0]
    mine = pl.multiple_of(c * half, half)
    other = pl.multiple_of((1 - c) * half, half)
    scatter = Scatter(grads, boxes, (fq, s_proj, fu, s_red), scatter_sems)
    hops = total_steps(dm, bs, lhs, mods, total_bufs, gmod, bias_out, hs, hr)
    pltpu.make_async_copy(gred, grads[3], lsem.at[0]).start()
    dm[...] = jnp.zeros_like(dm)
    bs[...] = jnp.zeros_like(bs)
    TILE = 128
    swap_to = (z, x, y, c)

    def vec(i):
        return mod[i // 3, :, (i % 3) * D : (i % 3 + 1) * D]

    def add_mod(i, value):
        cols = slice((i % 3) * D, (i % 3 + 1) * D)
        dm[i // 3, :, cols] = dm[i // 3, :, cols] + jnp.sum(value, axis=0, keepdims=True)

    def add_bias(at, value):
        cols = slice(at, at + value.shape[1])
        bs[:, cols] = bs[:, cols] + value

    def load(src, dst, i):
        d = pltpu.make_async_copy(src, dst, lsem.at[i])
        d.start()
        return d

    queue = []

    def tick(n):
        for _ in range(min(n, len(queue))):
            f, *a = queue.pop(0)
            f(*a)

    def beat(where, n):
        tick(int(BEATS[where][n]))

    def moves(i):
        if i == 0:
            return y_in, out
        rows = pl.ds((i - 1) * TILE, TILE)
        return dba.at[rows], ig_out.at[rows]

    def move(i):
        @pl.when(c != y)
        def _():
            rdma(*moves(i), ws.at[i], wr.at[i], swap_to).start()

        @pl.when(c == y)
        def _():
            pltpu.make_async_copy(*moves(i), ws.at[i]).start()

    def moved(i):
        @pl.when(c != y)
        def _():
            rdma(*moves(i), ws.at[i], wr.at[i], swap_to).wait()

        @pl.when(c == y)
        def _():
            pltpu.make_async_copy(*moves(i), ws.at[i]).wait()

    def begin():
        greet()
        pltpu.make_async_copy(gred, grads[3], lsem.at[0]).wait()
        scatter.start(5)
        scatter.start(6)
        five, six = scatter.steps(5), scatter.steps(6)
        queue.extend(five[0][1:] + six[0][1:] + five[1] + six[1] + five[2] + six[2] + five[3] + six[3])

    def own_tile(ref, t):
        return ref.at[pl.ds(pl.multiple_of(mine + t * TILE, TILE), TILE)]

    def widen(du):
        def through(weight, closing, der):
            loads = [load(gd, weight, 1), load(cl_in, closing, 2)]

            def slopes(n):
                return load(der_in.at[:, pl.ds(n * 384, 384)], der.at[n % 2], 3 + n % 2)

            coming = slopes(0)
            begin()
            for d in loads:
                d.wait()
            for n in range(6):
                cols = slice(n * 384, (n + 1) * 384)
                coming.wait()
                if n < 5:
                    coming = slopes(n + 1)
                right = jnp.concatenate([weight[0, cols, :], weight[1, cols, :]], axis=1)
                value = (matmul_nt(closing[...], right) * der[n % 2].astype(F32)).astype(BF)
                du[:, cols] = value
                sums = jnp.sum(value.astype(F32), axis=0, keepdims=True)
                here[:, cols] = sums
                beat("down", n)
            for j in range(8):
                block = here[:, j * BLOCK : (j + 1) * BLOCK]
                for p in (0, 1):
                    add_bias(3 * D + (2 * j + p) * BLOCK, jnp.where(c == p, block, 0.0))

        pl.run_scoped(through, VM((2, 2304, 576), BF), VM((2 * half, D), BF), VM((2, 2 * half, 384), BF))

        def expand(weight, h2):
            load(h2_in, h2, 2).wait()
            weight_load = load(gu, weight, 1)
            for t in range(3):
                left = h2[:, t * 384 : (t + 1) * 384].T
                for i in (0, 1):
                    grads[2][i, t * 384 : (t + 1) * 384, :] = matmul(
                        left, du[:, i * D : (i + 1) * D]
                    ).astype(BF)
                    beat("expand", 2 * t + i)

            scatter.start(3)
            scatter.start(4)
            three, four = scatter.steps(3), scatter.steps(4)
            queue.extend(
                three[0][1:] + four[0][1:] + three[1] + four[1] + three[2] + four[2] + three[3] + four[3]
            )
            move(0)

            def product(start, n):
                rows = pl.ds(start, half)
                part = slice(n * 384, (n + 1) * 384)
                return matmul_nt(du[rows, :D], weight[0, part, :]) + matmul_nt(du[rows, D:], weight[1, part, :])

            weight_load.wait()

            for n in range(3):
                ps[:, n * 384 : (n + 1) * 384] = product(other, n).astype(BF)
                beat("up", n)
            rdma(ps, pr, ts.at[0, 0], tr.at[0, 0], twin).start()
            for n in range(3):
                dx1[:, n * 384 : (n + 1) * 384] = product(mine, n)
                beat("up", 3 + n)

        pl.run_scoped(expand, VM((2, D, D), BF), VM((2 * half, D), BF))

    pl.run_scoped(widen, VM((2 * half, 2304), BF))

    def sums_got(i):
        rdma(ps, pr, ts.at[i, 0], tr.at[i, 0], twin).wait()

    def norm_back(value, scaling, gradient):
        average = jnp.mean(value, axis=-1, keepdims=True)
        centred = value - average
        inverse = lax.rsqrt(jnp.mean(centred * centred, axis=-1, keepdims=True) + 1e-06)
        normed = centred * inverse
        inner = gradient * (1.0 + scaling)
        part = inner - jnp.mean(inner, axis=-1, keepdims=True)
        part = part - normed * jnp.mean(inner * normed, axis=-1, keepdims=True)
        return part * inverse, normed

    def middle(x1, dy, ba, bb):
        loads = [load(x1_in, x1, 1), load(dy_in, dy, 2), load(ba_in, ba, 3), load(bb_in, bb, 4)]
        for d in loads:
            d.wait()
        sums_got(0)
        for t in range(half // TILE):
            rows = slice(t * TILE, (t + 1) * TILE)
            gradient = dx1[rows, :] + pr[rows, :].astype(F32)
            part, normed = norm_back(x1[rows, :], vec(4), gradient)
            add_mod(3, gradient)
            add_mod(4, gradient * normed)
            outer = dy[rows, :].astype(F32)
            add_mod(5, outer * bb[rows, :].astype(F32))
            add_bias(9216 - D, jnp.sum(rounded(outer * vec(5)), axis=0, keepdims=True))
            total = outer + part
            dx1[rows, :] = total
            add_mod(2, total * ba[rows, :].astype(F32))
            branch = (total * vec(2)).astype(BF)
            own_tile(dba, t)[...] = branch
            tile = own_tile(dba, t)
            rdma(tile, tile, ts.at[1, t], tr.at[1, t], twin).start()
            add_bias(2 * D, jnp.sum(branch.astype(F32), axis=0, keepdims=True))
            beat("middle", t)

    pl.run_scoped(middle, VM((half, D), F32), VM((half, D), BF), VM((half, D), BF), VM((half, D), BF))

    def attention(dot, dqkv):
        def project(weight, stage, raw, attnt, attn):
            loads = [load(gp, raw, 1), load(at_in, attnt, 2)]
            for d in loads:
                d.wait()
            for i in (0, 1):
                for h in range(8):
                    stage[h * 72 : h * 72 + 72, :] = raw[i, h].astype(F32)
                weight[i] = stage[...].astype(BF)
            attn[...] = jnp.concatenate([attnt[h] for h in range(8)], axis=0).astype(BF)
            for t in range(half // TILE):
                tile = own_tile(dba, t)
                rdma(tile, tile, ts.at[1, t], tr.at[1, t], twin).wait_send()
                part = dba.at[pl.ds(pl.multiple_of(other + t * TILE, TILE), TILE)]
                rdma(part, part, ts.at[1, t], tr.at[1, t], twin).wait_recv()
            for n in range(4):
                rows = slice(n * 256, (n + 1) * 256)
                right = dba[rows, :]
                value = matmul_nt(weight[0], right[:, :576]) + matmul_nt(weight[1], right[:, 576:])
                for h in range(8):
                    dot[h, :, rows] = value[h * 72 : h * 72 + 72, :].astype(BF)
                beat("project", n)
            for i in (0, 1):
                stage[...] = matmul(attn[...], dba[:, i * 576 : (i + 1) * 576])
                for h in range(8):
                    grads[1][i, h] = stage[h * 72 : h * 72 + 72, :].astype(BF)

        pl.run_scoped(
            project,
            VM((2, 576, 576), BF),
            VM((576, 576), F32),
            VM((2, 8, 72, 576), BF),
            VM((8, 72, 2 * half), F32),
            VM((576, 2 * half), BF),
        )
        scatter.start(2)
        two = scatter.steps(2)
        queue.extend(two[0][1:] + two[1] + two[2] + two[3])

        def heads(qa, ka, vt, at, dk, dv, dq):
            def fetch(h):
                n = h % 2
                return [
                    load(src.at[h], dst.at[n], 1 + 4 * n + m)
                    for m, (src, dst) in enumerate(((q_in, qa), (k_in, ka), (v_in, vt), (at_in, at)))
                ]

            coming = fetch(0)
            for h in range(8):
                n = h % 2
                for d in coming:
                    d.wait()
                if h < 7:
                    coming = fetch(h + 1)
                value = vt[n].T
                key_t = ka[n, :, :72].T
                inner = jnp.sum(at[n] * dot[h].astype(F32), axis=0, keepdims=True)
                dk[...] = jnp.zeros_like(dk)
                dv[...] = jnp.zeros_like(dv)
                for i in range(4):
                    rows = slice(i * 256, (i + 1) * 256)
                    query = qa[n, rows, :]
                    grad = dot[h, :, rows]
                    scores = matmul_nt(ka[n], query)
                    prob = jnp.exp2(scores - lse[h, :, rows])
                    change = matmul(value, grad) - inner[:, rows]
                    dscore = (prob * change).astype(BF)
                    dv[...] += matmul_nt(grad, prob.astype(BF))
                    dk[...] += matmul_nt(query[:, :72].T, dscore)
                    dq[:, rows] = matmul(key_t, dscore)
                    beat("heads", i)
                scale = HEAD_DIM ** (-0.5)
                dqkv[0, :, h * 72 : h * 72 + 72] = (dq[...] * scale).T.astype(BF)
                key_grad = (dk[...] * math.log(2.0)).T.astype(BF)
                if h < 4:
                    dqkv[0, :, 576 + h * 72 : 648 + h * 72] = key_grad
                else:
                    dqkv[1, :, h * 72 - 288 : h * 72 - 216] = key_grad
                dqkv[1, :, 288 + h * 72 : 360 + h * 72] = dv[...].T.astype(BF)

        pl.run_scoped(
            heads,
            VM((2, 2 * half, 128), BF),
            VM((2, 2 * half, 128), BF),
            VM((2, 72, 2 * half), BF),
            VM((2, 72, 2 * half), F32),
            VM((72, 2 * half), F32),
            VM((72, 2 * half), F32),
            VM((72, 2 * half), F32),
        )

        def attend(weight, x0):
            loads = [load(gq, weight, 2), load(x0_in, x0, 3)]
            pl.run_scoped(attend_grad, VM((2 * half, D), BF))
            scatter.start(0)
            scatter.start(1)
            zero, one = scatter.steps(0), scatter.steps(1)
            queue.extend(
                zero[0][1:] + one[0][1:] + zero[1] + one[1] + zero[2] + one[2] + zero[3] + one[3]
            )
            for d in loads:
                d.wait()
            pl.run_scoped(functools.partial(back, weight, x0), VM((half, D), F32))

        def attend_grad(h1):
            load(h1_in, h1, 1).wait()
            for t in range(3):
                left = h1[:, t * 384 : (t + 1) * 384].T
                for i in (0, 1):
                    grads[0][i, t * 384 : (t + 1) * 384, :] = matmul(left, dqkv[i]).astype(BF)
                    beat("attend", 2 * t + i)

        def back(weight, x0, acc):
            def product(start, n):
                rows = pl.ds(start, half)
                part = slice(n * 384, (n + 1) * 384)
                return matmul_nt(dqkv[0, rows, :], weight[0, part, :]) + matmul_nt(
                    dqkv[1, rows, :], weight[1, part, :]
                )

            for n in range(3):
                ps[:, n * 384 : (n + 1) * 384] = product(other, n).astype(BF)
                beat("back", n)
            rdma(ps, pr, ts.at[2, 0], tr.at[2, 0], twin).start()
            for n in range(3):
                acc[:, n * 384 : (n + 1) * 384] = product(mine, n)
                beat("back", 3 + n)
            sums_got(2)
            for t in range(half // TILE):
                rows = slice(t * TILE, (t + 1) * TILE)
                gradient = acc[rows, :] + pr[rows, :].astype(F32)
                part, normed = norm_back(x0[rows, :].astype(F32), vec(1), gradient)
                add_mod(0, gradient)
                add_mod(1, gradient * normed)
                dba[rows, :] = (dx1[rows, :] + part).astype(BF)
                move(1 + t)
                beat("input", t)

        pl.run_scoped(
            attend,
            VM((2, D, 864), BF),
            VM((half, D), BF),
        )
        for i in (0, 1):
            sums = jnp.sum(dqkv[i].astype(F32), axis=0, keepdims=True)
            for j in range(8):
                block = sums[:, i * 288 + j * 72 : i * 288 + j * 72 + 72]
                for p in (0, 1):
                    add_bias(i * D + (2 * j + p) * 72, jnp.where(c == p, block, 0.0))

    pl.run_scoped(attention, VM((8, 72, 2 * half), BF), VM((2, 2 * half, 864), BF))
    for n, hop in enumerate(hops):
        hop()
        beat("hops", n)
    tick(len(queue))

    last_half = 72
    def give(f, got, i):
        return rdma(f.at[pl.ds(pl.multiple_of((1 - c) * 72, 8), 72)], got, ts.at[3, i], tr.at[3, i], twin)

    give(fq, gotq, 0).start()
    give(fu, gotu, 1).start()

    def squares(value):
        return jnp.sum(jnp.sum(value * value, axis=0, keepdims=True), axis=1, keepdims=True)

    bias_squares = squares(bias_out[...])
    bias_flat[...] = bias_out[...].reshape(14 * D)
    total = squares(fq[...]) + squares(fu[...]) + squares(s_proj[...]) + squares(s_red[...]) + squares(gmod[...])
    total = jnp.broadcast_to(total, (8, 128))
    sq[0] = total
    near = [
        rdma(sq.at[0], sq.at[f], ns.at[f - 1], nr.at[f - 1], flipped(f)) for f in range(1, 8)
    ]
    for d in near:
        d.start()
    for d in near:
        d.wait()
    sq[8] = ((sq[0] + sq[1]) + (sq[2] + sq[3])) + ((sq[4] + sq[5]) + (sq[6] + sq[7]))
    last = [rdma(sq.at[8], sq.at[8 + k], ns.at[6 + k], nr.at[6 + k], zn[k]) for k in (1, 2, 3)]
    for d in last:
        d.start()

    def interleave(f, got, shard, width, i):
        give(f, got, i).wait()
        own = jnp.where(c == 0, f[:72, :], f[72:, :])
        sides = (jnp.where(c == 0, own, got[...]), jnp.where(c == 0, got[...], own))
        count = own.shape[1] // width
        shard[...] = jnp.concatenate(
            [sides[p][:, j * width : (j + 1) * width] for j in range(count) for p in (0, 1)], axis=1
        )

    interleave(fq, gotq, s_att, HEAD_DIM, 0)
    interleave(fu, gotu, s_exp, BLOCK, 1)
    for d in last:
        d.wait()
    norm_out[...] = (sq[8] + sq[9]) + (sq[10] + sq[11]) + bias_squares
    for i in range(1 + half // TILE):
        moved(i)
    scatter.finish()


def backward_block(kept):
    half = kept[6].shape[0]
    rows = 2 * half
    sd = jax.ShapeDtypeStruct
    vm = pl.BlockSpec(memory_space=VM)
    hbm = pl.BlockSpec(memory_space=ANY)
    sizes = ((D, 864), (72, 576), (D, D), (2304, 576))
    pieces = [PIECES[n][:2] for n in NAMES]
    dma = pltpu.SemaphoreType.DMA
    n = len(CHUNKS)
    scratch = [
        VM((2, D, 864), BF),
        VM((2, 8, 72, 576), BF),
        VM((2, D, D), BF),
        VM((2, 2304, 576), BF),
    ]
    for count in (2, 2, 4, 4, 3):
        scratch += [VM((count,) + p, BF) for p in pieces]
    scratch += [
        VM((144, 864), F32),
        VM((144, D), F32),
        VM((72, 864), F32),
        VM((72, D), F32),
        VM((rows, D), BF),
        VM((half, D), F32),
        VM((half, D), BF),
        VM((half, D), BF),
        VM((2, 1, 3456), F32),
        VM((1, 9216), F32),
        VM((4, 2, 2, 1, 3456), F32),
        VM((2, 2, 2, 1, 3456), F32),
        VM((7, 1, 9216), F32),
        VM((1, 9216), F32),
        VM((3, 1, 9216), F32),
        VM((2, 1, 3456), F32),
        VM((12, 8, 128), F32),
        VM((1, 2304), F32),
        VM((1, 14 * D), F32),
        dma((9,)),
    ]
    scratch += [dma((n, 4))] * 2 + [dma((n, 4, 2))] * 2 + [dma((n, 4))] * 6
    scratch += [dma((4, 4))] * 2 + [dma((5,))] * 2 + [dma((3, 14))] * 2 + [dma((10,))] * 2
    places = [hbm] * 4 + [vm, vm] + [hbm] * 8 + [vm] + [hbm] * 7
    return pl.pallas_call(
        backward_kernel,
        out_shape=[
            sd((half, D), BF),
            sd((half, D), BF),
            sd((72, 1728), F32),
            sd((72, 576), F32),
            sd((72, 2304), F32),
            sd((288, 576), F32),
            sd((72, 3456), F32),
            sd((14 * D,), F32),
            sd((8, 128), F32),
        ],
        in_specs=places,
        out_specs=[hbm, hbm] + [vm] * 7,
        scratch_shapes=scratch,
        compiler_params=pltpu.CompilerParams(
            collective_id=1, has_side_effects=True, vmem_limit_bytes=62 * 2**20
        ),
        name="backward_block",
    )(*kept)


def step_kernel(squares, correction, *refs):
    count = len(RATES)
    norm = jnp.sqrt(squares[0:1, 0:1])
    clip = jnp.minimum(1.0, 1.0 / (norm + 1e-06))
    fix = correction[0:1, 0:1]
    for i, rate in enumerate(RATES):
        master, first, second, gradient = (refs[4 * i + j][...] for j in range(4))
        new = adam_update(master, first, second, gradient, rate, clip, fix)
        for j in range(3):
            refs[4 * count + 4 + 3 * i + j][...] = new[j]

    @pl.when(pl.program_id(0) == 0)
    def _():
        master, first, second, gradient = (
            refs[4 * count + j][...].reshape(1, 14 * D) for j in range(4)
        )
        new = adam_update(master, first, second, gradient, 0.1, clip, fix)
        for j in range(3):
            refs[7 * count + 4 + j][...] = new[j].reshape(14 * D)


RATES = (0.5 * D ** (-0.5),) * 4 + (0.5 * FF ** (-0.5),)


def step_weights(squares, correction, states, biases):
    grid = 3

    def spec(shape):
        return pl.BlockSpec((shape[0] // grid, shape[1]), lambda i: (i, 0))

    whole = pl.BlockSpec((8, 128), lambda i: (0, 0))
    flat = [value for state in states for value in state]
    new = [value for state in states for value in state[:3]] + list(biases[:3])
    line = pl.BlockSpec(biases[0].shape, lambda i: (0,))
    return pl.pallas_call(
        step_kernel,
        grid=(grid,),
        out_shape=[jax.ShapeDtypeStruct(v.shape, v.dtype) for v in new],
        in_specs=[whole, whole] + [spec(v.shape) for v in flat] + [line] * 4,
        out_specs=[spec(v.shape) for v in new[:-3]] + [line] * 3,
        compiler_params=pltpu.CompilerParams(vmem_limit_bytes=62 * 2**20),
        name="step_weights",
    )(squares, correction, *flat, *biases)


def on_device_fast(
    tokens,
    cotangent,
    buckets,
    timesteps,
    labels,
    class_table,
    step_count,
    modulate_master,
    modulate_first,
    modulate_second,
    attend_master,
    attend_first,
    attend_second,
    project_master,
    project_first,
    project_second,
    expand_master,
    expand_first,
    expand_second,
    reduce_master,
    reduce_first,
    reduce_second,
    biases_master,
    biases_first,
    biases_second,
):

    z, x, c, y = place()
    bf16, f32 = jnp.bfloat16, jnp.float32
    block = FF // 16
    class_row = lax.dynamic_slice_in_dim(class_table, labels[0], 1).astype(f32)
    condition = jax.nn.silu(class_row + time_features(timesteps, D)).astype(bf16).astype(f32)
    cond_tiles = jnp.pad(condition.reshape(16, 72), ((0, 0), (0, 56)))
    bucket = jnp.broadcast_to(buckets.astype(f32)[:, None], (8, 128))
    steps = jnp.arange(64, dtype=f32)[:, None]
    omegas = jnp.exp(-math.log(10000.0) * jnp.arange(288, dtype=f32) / 288)[None, :]
    table = jnp.concatenate([jnp.sin(steps * omegas), jnp.cos(steps * omegas)], axis=1)
    kept = forward_block(
        tokens,
        cotangent,
        bucket,
        table,
        (attend_master, project_master, expand_master, reduce_master),
        modulate_master,
        cond_tiles,
        biases_master,
    )
    (output, input_grad, grad_attend, grad_project, grad_expand, grad_reduce, grad_mod, bias_total, squares) = (
        backward_block(kept)
    )
    correction = 1.0 - jnp.power(0.5, step_count.astype(f32))
    states = (
        (modulate_master, modulate_first, modulate_second, grad_mod),
        (attend_master, attend_first, attend_second, grad_attend),
        (project_master, project_first, project_second, grad_project),
        (expand_master, expand_first, expand_second, grad_expand),
        (reduce_master, reduce_first, reduce_second, grad_reduce),
    )
    updates = step_weights(
        squares,
        jnp.full((8, 128), correction),
        states,
        (biases_master, biases_first, biases_second, bias_total),
    )
    grad_norm = jnp.sqrt(squares[0, 0])
    return (output, input_grad.astype(f32), grad_norm, *updates)


def fast_solution(mesh):
    return jax.shard_map(
        on_device_fast,
        mesh=mesh,
        in_specs=(
            P(("z", "x", "c", "y"), None),
            P(("z", "x", "c", "y"), None),
            P(("z", "x", "c")),
            P(("z", "x", "c")),
            P(("z", "x", "c")),
            P(),
            P(),
            P(("z", "x", "c"), "y"),
            P(("z", "x", "c"), "y"),
            P(("z", "x", "c"), "y"),
            P(("z", "x", "c"), "y"),
            P(("z", "x", "c"), "y"),
            P(("z", "x", "c"), "y"),
            P(("z", "x", "c"), "y"),
            P(("z", "x", "c"), "y"),
            P(("z", "x", "c"), "y"),
            P(("z", "x", "c"), "y"),
            P(("z", "x", "c"), "y"),
            P(("z", "x", "c"), "y"),
            P(("z", "x", "c"), "y"),
            P(("z", "x", "c"), "y"),
            P(("z", "x", "c"), "y"),
            P(),
            P(),
            P(),
        ),
        out_specs=(
            P(("z", "x", "c", "y"), None),
            P(("z", "x", "c", "y"), None),
            P(),
            P(("z", "x", "c"), "y"),
            P(("z", "x", "c"), "y"),
            P(("z", "x", "c"), "y"),
            P(("z", "x", "c"), "y"),
            P(("z", "x", "c"), "y"),
            P(("z", "x", "c"), "y"),
            P(("z", "x", "c"), "y"),
            P(("z", "x", "c"), "y"),
            P(("z", "x", "c"), "y"),
            P(("z", "x", "c"), "y"),
            P(("z", "x", "c"), "y"),
            P(("z", "x", "c"), "y"),
            P(("z", "x", "c"), "y"),
            P(("z", "x", "c"), "y"),
            P(("z", "x", "c"), "y"),
            P(),
            P(),
            P(),
        ),
        check_vma=False,
    )


def plain_solution(mesh):
    return jax.shard_map(
        on_device,
        mesh=mesh,
        in_specs=(
            P(("seq", "head"), None),
            P(("seq", "head"), None),
            P("seq"),
            P("seq"),
            P("seq"),
            P(),
            P(),
            P("seq", "head"),
            P("seq", "head"),
            P("seq", "head"),
            P("seq", "head"),
            P("seq", "head"),
            P("seq", "head"),
            P("seq", "head"),
            P("seq", "head"),
            P("seq", "head"),
            P("seq", "head"),
            P("seq", "head"),
            P("seq", "head"),
            P("seq", "head"),
            P("seq", "head"),
            P("seq", "head"),
            P(),
            P(),
            P(),
        ),
        out_specs=(
            P(("seq", "head"), None),
            P(("seq", "head"), None),
            P(),
            P("seq", "head"),
            P("seq", "head"),
            P("seq", "head"),
            P("seq", "head"),
            P("seq", "head"),
            P("seq", "head"),
            P("seq", "head"),
            P("seq", "head"),
            P("seq", "head"),
            P("seq", "head"),
            P("seq", "head"),
            P("seq", "head"),
            P("seq", "head"),
            P("seq", "head"),
            P("seq", "head"),
            P(),
            P(),
            P(),
        ),
        check_vma=False,
    )


def solution(mesh):
    if dict(mesh.shape) == {"seq": 16, "head": 2}:
        grid = Mesh(mesh.devices.reshape(4, 2, 2, 2), ("z", "x", "c", "y"))
        return fast_solution(grid)
    return plain_solution(mesh)
```
